128 devices in a mesh: branch: 2 (over core), seq: 16 (over y, z), fsdp: 4 (over x).
Axes of the slice: x: 4, y: 4, z: 4, core: 2. Of those that a mesh axis runs over, the one named last changes fastest.
Arguments:
- tokens: bfloat16 [4, 2048, 1600], P('fsdp', 'seq'), may hold values from -6 to 6
- seq_lengths: int32 [4, 3], P('fsdp'), may hold values from 1 to 2046, as said below
- norm_gain: float32 [1600], P(('seq', 'fsdp')), may hold values from 0.25 to 1.75
- meta_tokens: float32 [128, 1600], P(None, ('seq', 'fsdp')), may hold values from -6 to 6
- w_query: float32 [1600, 1600], P(('seq', 'fsdp')), may hold values from -0.15625 to 0.15625
- w_key_value: float32 [1600, 640], P(('seq', 'fsdp')), may hold values from -0.15625 to 0.15625
- w_attn_out: float32 [1600, 1600], P(('seq', 'fsdp')), may hold values from -0.15625 to 0.15625
- attn_gain: float32 [1600], P(('seq', 'fsdp')), may hold values from 0.25 to 1.75
- w_mamba_in: float32 [1600, 6400], P(('seq', 'fsdp')), may hold values from -0.15625 to 0.15625
- conv_weight: float32 [4, 3200], P(None, ('seq', 'fsdp')), may hold values from -3 to 3
- conv_bias: float32 [3200], P(('seq', 'fsdp')), may hold values from -3 to 3
- w_ssm_x: float32 [3200, 132], P(('seq', 'fsdp')), may hold values from -0.109375 to 0.109375
- w_dt: float32 [100, 3200], P(None, ('seq', 'fsdp')), may hold values from -0.625 to 0.625
- dt_bias: float32 [3200], P(('seq', 'fsdp')), may hold values from -2 to 1
- a_log: float32 [16, 3200], P(None, ('seq', 'fsdp')), may hold values from -10 to -3
- skip_d: float32 [3200], P(('seq', 'fsdp')), may hold values from 0.5 to 1.5
- w_mamba_out: float32 [3200, 1600], P(('seq', 'fsdp')), may hold values from -0.109375 to 0.109375
- mamba_gain: float32 [1600], P(('seq', 'fsdp')), may hold values from 0.25 to 1.75
- ffn_gain: float32 [1600], P(('seq', 'fsdp')), may hold values from 0.25 to 1.75
- w_gate_up: float32 [1600, 11008], P(('seq', 'fsdp')), may hold values from -0.15625 to 0.15625
- w_down: float32 [5504, 1600], P(('seq', 'fsdp')), may hold values from -0.078125 to 0.078125
- cotangent: bfloat16 [4, 2048, 1600], P('fsdp', 'seq'), may hold values from -6 to 6
Outputs:
- mixed: bfloat16 [4, 2048, 1600], P('fsdp', 'seq')
- input_grad: float32 [4, 2048, 1600], P('fsdp', 'seq')
- grad_norm_gain: float32 [1600], P(('seq', 'fsdp'))
- grad_meta_tokens: float32 [128, 1600], P(None, ('seq', 'fsdp'))
- grad_w_query: float32 [1600, 1600], P(('seq', 'fsdp'))
- grad_w_key_value: float32 [1600, 640], P(('seq', 'fsdp'))
- grad_w_attn_out: float32 [1600, 1600], P(('seq', 'fsdp'))
- grad_attn_gain: float32 [1600], P(('seq', 'fsdp'))
- grad_w_mamba_in: float32 [1600, 6400], P(('seq', 'fsdp'))
- grad_conv_weight: float32 [4, 3200], P(None, ('seq', 'fsdp'))
- grad_conv_bias: float32 [3200], P(('seq', 'fsdp'))
- grad_w_ssm_x: float32 [3200, 132], P(('seq', 'fsdp'))
- grad_w_dt: float32 [100, 3200], P(None, ('seq', 'fsdp'))
- grad_dt_bias: float32 [3200], P(('seq', 'fsdp'))
- grad_a_log: float32 [16, 3200], P(None, ('seq', 'fsdp'))
- grad_skip_d: float32 [3200], P(('seq', 'fsdp'))
- grad_w_mamba_out: float32 [3200, 1600], P(('seq', 'fsdp'))
- grad_mamba_gain: float32 [1600], P(('seq', 'fsdp'))
- grad_ffn_gain: float32 [1600], P(('seq', 'fsdp'))
- grad_w_gate_up: float32 [1600, 11008], P(('seq', 'fsdp'))
- grad_w_down: float32 [5504, 1600], P(('seq', 'fsdp'))
The draws below stay inside these ranges and needn't reach their ends.
Inputs may be any that keep to these rules, and one draw needn't show every extreme that they name: `seq_lengths`: each row lists the lengths of 3 sequences packed in order into the 2048 rows of one batch; they sum to 2048, and exactly one of them is longer than 1920, at a place drawn from the seed.
All inputs are finite; a program needn't handle non-finite values.
Results may differ from the reference program's by a relative error of at most 0.015.
The reference program's roundings to bfloat16 on the way count: a program that leaves them out, or rounds other values in their place, can miss the bound.
Values may be sent and summed in bfloat16 or wider, within the bound.
A program may use at most 768 MiB of HBM per device.

```python
import math
import jax
import jax.numpy as jnp
from jax import lax

D = 1600
HEADS = 25
GROUPS = 5
HEAD = 64
INNER = 3200
STATE = 16
CONV = 4
RANK = 100
FF = 5504
META = 128
TOK_DEV = 128
SEQS = 3
GROUP = 2048
BATCHES = 4


def draw_seq_lengths(key, part):
    key = jax.random.fold_in(key, 11)
    first_key, last_key, place_key = jax.random.split(key, 3)
    half_dev = TOK_DEV // 2
    short_first = jax.random.randint(first_key, (BATCHES, 1), 1, half_dev)
    short_last = jax.random.randint(last_key, (BATCHES, 1), 1, half_dev)
    long_place = jax.random.randint(place_key, (BATCHES, 1), 0, SEQS)
    longest = GROUP - short_first - short_last
    slots = jnp.arange(SEQS, dtype=jnp.int32)[None, :]
    rank_other = slots - (slots > long_place).astype(jnp.int32)
    shorts = jnp.where(rank_other == 0, short_first, short_last)
    return jnp.where(slots == long_place, longest, shorts).astype(jnp.int32)


def levels(own_key, extent, cuts, smallest, high):
    def one(axis_at, parts):
        draws = jax.random.uniform(jax.random.fold_in(jax.random.fold_in(own_key, 6), axis_at), (parts,), jnp.float32, smallest / len(cuts), high / len(cuts))
        return jnp.repeat(jnp.exp(draws), extent[axis_at] // parts).reshape((-1,) + (1,) * (len(extent) - axis_at - 1))

    loudness = one(*cuts[0])
    for cut in cuts[1:]:
        loudness = loudness * one(*cut)
    return loudness


def scatter_about(own_key, extent, width, most, cuts=(), kind=jnp.bfloat16):
    loudness = levels(own_key, extent, cuts, -0.22, 0.18) if cuts else 1.0
    values = jax.random.normal(own_key, extent, jnp.float32) * width * loudness
    return jnp.minimum(jnp.maximum(values, -most), most).astype(kind)


def setup_inputs(seed: int = 0) -> dict:
    seeds = jax.random.split(jax.random.key(seed), 23)
    tokens = scatter_about(seeds[0], (BATCHES, GROUP, D), 1.0, 6.0, ((0, 4), (1, 16)))
    seq_lengths = draw_seq_lengths(jax.random.fold_in(seeds[22], 71), 0)
    norm_gain = jnp.clip(1.0 + 0.15 * jax.random.normal(seeds[2], (D,), jnp.float32), 0.25, 1.75)
    meta_tokens = scatter_about(seeds[3], (META, D), 1.0, 6.0, ((1, 64),), jnp.float32)
    w_query = scatter_about(seeds[4], (D, HEADS * HEAD), D ** -0.5, 0.15625, ((0, 64),), jnp.float32)
    w_key_value = scatter_about(seeds[5], (D, 2 * GROUPS * HEAD), D ** -0.5, 0.15625, ((0, 64),), jnp.float32)
    w_attn_out = scatter_about(seeds[6], (HEADS * HEAD, D), (HEADS * HEAD) ** -0.5, 0.15625, ((0, 64),), jnp.float32)
    attn_gain = jnp.clip(1.0 + 0.15 * jax.random.normal(seeds[7], (D,), jnp.float32), 0.25, 1.75)
    w_mamba_in = scatter_about(seeds[8], (D, 2 * INNER), D ** -0.5, 0.15625, ((0, 64),), jnp.float32)
    conv_weight = scatter_about(seeds[9], (CONV, INNER), CONV ** -0.5, 3.0, ((1, 64),), jnp.float32)
    conv_bias = scatter_about(seeds[10], (INNER,), 0.5, 3.0, ((0, 64),), jnp.float32)
    w_ssm_x = scatter_about(seeds[11], (INNER, RANK + 2 * STATE), INNER ** -0.5, 0.109375, ((0, 64),), jnp.float32)
    w_dt = scatter_about(seeds[12], (RANK, INNER), RANK ** -0.5, 0.625, ((1, 64),), jnp.float32)
    dt_bias = jnp.clip(-2.0 + 3.0 * jax.random.uniform(seeds[13], (INNER,), jnp.float32) ** levels(seeds[13], (INNER,), ((0, 64),), -0.2, 0.2), -2.0, 1.0)
    a_log = jnp.clip(-10.0 + 7.0 * jax.random.uniform(seeds[14], (STATE, INNER), jnp.float32) ** levels(seeds[14], (STATE, INNER), ((1, 64),), -0.2, 0.2), -10.0, -3.0)
    skip_d = jnp.clip(0.5 + 1.0 * jax.random.uniform(seeds[15], (INNER,), jnp.float32) ** levels(seeds[15], (INNER,), ((0, 64),), -0.2, 0.2), 0.5, 1.5)
    w_mamba_out = scatter_about(seeds[16], (INNER, D), INNER ** -0.5, 0.109375, ((0, 64),), jnp.float32)
    mamba_gain = jnp.clip(1.0 + 0.15 * jax.random.normal(seeds[17], (D,), jnp.float32), 0.25, 1.75)
    ffn_gain = jnp.clip(1.0 + 0.15 * jax.random.normal(seeds[18], (D,), jnp.float32), 0.25, 1.75)
    w_gate_up = scatter_about(seeds[19], (D, 2 * FF), D ** -0.5, 0.15625, ((0, 64),), jnp.float32)
    w_down = scatter_about(seeds[20], (FF, D), FF ** -0.5, 0.078125, ((0, 64),), jnp.float32)
    cotangent = scatter_about(seeds[21], (BATCHES, GROUP, D), 1.0, 6.0, ((0, 4), (1, 16)))
    return {"tokens": tokens, "seq_lengths": seq_lengths, "norm_gain": norm_gain, "meta_tokens": meta_tokens, "w_query": w_query, "w_key_value": w_key_value, "w_attn_out": w_attn_out, "attn_gain": attn_gain, "w_mamba_in": w_mamba_in, "conv_weight": conv_weight, "conv_bias": conv_bias, "w_ssm_x": w_ssm_x, "w_dt": w_dt, "dt_bias": dt_bias, "a_log": a_log, "skip_d": skip_d, "w_mamba_out": w_mamba_out, "mamba_gain": mamba_gain, "ffn_gain": ffn_gain, "w_gate_up": w_gate_up, "w_down": w_down, "cotangent": cotangent}


epsilon = 1e-05
negative_fill = -1e+30
score_scale = 0.125
highest = lax.Precision.HIGHEST

@jax.custom_vjp
def low(v):
    return lax.optimization_barrier(v.astype(jnp.bfloat16)).astype(jnp.float32)

@jax.custom_vjp
def low_back(v):
    return v

def low_keep(v):
    return (low(v), None)

def low_pass(kept, grad):
    return (grad,)

def back_keep(v):
    return (v, None)

def back_low(kept, grad):
    return (low(grad),)
low.defvjp(low_keep, low_pass)
low_back.defvjp(back_keep, back_low)

def rounded_both(values):
    return low(low_back(values))

def product(left, right):
    return jnp.dot(left, right, precision=highest)

def rms_norm(values, gain):
    return values * lax.rsqrt(lax.optimization_barrier(jnp.mean(values * values, axis=-1, keepdims=True)) + epsilon) * gain

def segment_info(lengths):
    row_ids = jnp.arange(GROUP, dtype=jnp.int32)
    end_rows = jnp.cumsum(lengths).astype(jnp.int32)
    start_rows = (end_rows - lengths).astype(jnp.int32)
    segment_ids = lax.optimization_barrier(jnp.sum((row_ids[:, None] >= end_rows[None, :]).astype(jnp.int32), axis=1)).astype(jnp.int32)
    keep_rows = 1.0 - jnp.any(row_ids[:, None] == start_rows[None, :], axis=1).astype(jnp.float32)
    return (row_ids, segment_ids, keep_rows)

def attention(queries, keyval, meta_keyval, row_ids, segment_ids):
    query_block = math.gcd(GROUP, 1024)
    key_rows = jnp.concatenate([meta_keyval[:, :GROUPS * HEAD], keyval[:, :GROUPS * HEAD]], axis=0).reshape(META + GROUP, GROUPS, HEAD)
    value_rows = jnp.concatenate([meta_keyval[:, GROUPS * HEAD:], keyval[:, GROUPS * HEAD:]], axis=0).reshape(META + GROUP, GROUPS, HEAD)
    query_heads = queries.reshape(GROUP // query_block, query_block, GROUPS, HEADS // GROUPS, HEAD)
    meta_allowed = jnp.zeros((query_block, META), jnp.int32) == 0

    def one_block(pieces):
        query_part, query_rows, query_segments = pieces
        scores = low_back(jnp.einsum('qgjd,kgd->qgjk', query_part, key_rows, precision=highest) * score_scale)
        allowed = (query_segments[:, None] == segment_ids[None, :]) & (row_ids[None, :] <= query_rows[:, None])
        allowed = jnp.concatenate([meta_allowed, allowed], axis=1)
        scores = jnp.where(allowed[:, None, None, :], scores, negative_fill)
        probs = jax.nn.softmax(scores, axis=-1)
        return jnp.einsum('qgjk,kgd->qgjd', low(probs), value_rows, precision=highest)
    attended = lax.map(jax.checkpoint(one_block), (query_heads, row_ids.reshape(-1, query_block), segment_ids.reshape(-1, query_block)))
    return attended.reshape(GROUP, HEADS * HEAD)

def conv_mix(conv_in, taps, offset, segment_ids):
    summed = taps[CONV - 1] * conv_in + offset
    for shift_by in range(1, CONV):
        earlier = jnp.concatenate([jnp.zeros((shift_by, INNER), jnp.float32), conv_in[:GROUP - shift_by]], axis=0)
        earlier_segments = jnp.concatenate([jnp.full((shift_by,), -1, jnp.int32), segment_ids[:GROUP - shift_by]])
        valid_rows = (earlier_segments == segment_ids).astype(jnp.float32)
        summed = summed + taps[CONV - 1 - shift_by] * earlier * valid_rows[:, None]
    return jax.nn.silu(summed)

def mamba_scan(inputs_m, steps, b_rows, c_rows, decay_rate, keep_rows):
    scan_block = math.gcd(GROUP, 64)

    def one_step(state_now, pieces):
        input_t, step_t, b_t, c_t, keep_t = pieces
        state_now = keep_t * jnp.exp(step_t[None, :] * decay_rate) * state_now + (step_t * input_t)[None, :] * b_t[:, None]
        return (state_now, lax.optimization_barrier(jnp.sum(c_t[:, None] * state_now, axis=0)))

    def one_block(state_now, pieces):
        return lax.scan(one_step, state_now, pieces)
    pieces = tuple((member.reshape((GROUP // scan_block, scan_block) + member.shape[1:]) for member in (inputs_m, steps, b_rows, c_rows, keep_rows)))
    _, outputs = lax.scan(jax.checkpoint(one_block), jnp.zeros((STATE, INNER), jnp.float32), pieces)
    return outputs.reshape(GROUP, INNER)

def layer_group(hidden_in, lengths, params, meta_keyval):
    gain_norm, meta_rows, weight_query, weight_keys, weight_attn, gain_attn, weight_mamba, conv_taps, conv_offset, weight_ssm, weight_step, step_bias, log_decay, skip_gain, weight_back, gain_mamba, gain_feed, weight_gate, weight_down = params
    row_ids, segment_ids, keep_rows = segment_info(lengths)
    normed = low(rms_norm(hidden_in, gain_norm))
    queries = rounded_both(product(normed, weight_query))
    keyval = rounded_both(product(normed, weight_keys))
    attended = rounded_both(attention(queries, keyval, meta_keyval, row_ids, segment_ids))
    attn_pre = low_back(product(attended, weight_attn))
    sent_attn = low(rms_norm(attn_pre, gain_attn))
    mamba_in = low_back(product(normed, weight_mamba))
    conv_in = low(mamba_in[:, :INNER])
    gate_z = mamba_in[:, INNER:]
    inputs_m = low(conv_mix(conv_in, conv_taps, conv_offset, segment_ids))
    ssm_proj = low_back(product(inputs_m, weight_ssm))
    step_low = low(ssm_proj[:, :RANK])
    b_rows = ssm_proj[:, RANK:RANK + STATE]
    c_rows = ssm_proj[:, RANK + STATE:]
    steps = jax.nn.softplus(low_back(product(step_low, weight_step)) + step_bias)
    ssm_out = mamba_scan(inputs_m, steps, b_rows, c_rows, -jnp.exp(log_decay), keep_rows)
    mixed_y = low((ssm_out + skip_gain * inputs_m) * jax.nn.silu(gate_z))
    mamba_pre = low_back(product(mixed_y, weight_back))
    sent_mamba = low(rms_norm(mamba_pre, gain_mamba))
    hidden = hidden_in + 0.5 * (sent_attn + sent_mamba)
    feed = low(rms_norm(hidden, gain_feed))
    gate_up = low_back(product(feed, weight_gate))
    active = low(jax.nn.silu(gate_up[:, :FF]) * gate_up[:, FF:])
    return hidden + low_back(product(active, weight_down))

def reference(tokens, seq_lengths, norm_gain, meta_tokens, w_query, w_key_value, w_attn_out, attn_gain, w_mamba_in, conv_weight, conv_bias, w_ssm_x, w_dt, dt_bias, a_log, skip_d, w_mamba_out, mamba_gain, ffn_gain, w_gate_up, w_down, cotangent):
    inputs_f = tokens.astype(jnp.float32)
    masters = (norm_gain, meta_tokens, w_query, w_key_value, w_attn_out, attn_gain, w_mamba_in, conv_weight, conv_bias, w_ssm_x, w_dt, dt_bias, a_log, skip_d, w_mamba_out, mamba_gain, ffn_gain, w_gate_up, w_down)

    def forward(hidden_all, *params):
        rounded = tuple((low(member) for member in params))
        meta_normed = low(rms_norm(rounded[1], rounded[0]))
        meta_keyval = low(product(meta_normed, rounded[3]))
        outputs = [layer_group(hidden_all[batch_id], seq_lengths[batch_id].astype(jnp.int32), rounded, meta_keyval) for batch_id in range(BATCHES)]
        return jnp.stack(outputs)
    result, pull_back = jax.vjp(forward, inputs_f, *masters)
    grads = pull_back(cotangent.astype(jnp.float32))
    return (result.astype(jnp.bfloat16), grads[0], grads[1], grads[2], grads[3], grads[4], grads[5], grads[6], grads[7], grads[8], grads[9], grads[10], grads[11], grads[12], grads[13], grads[14], grads[15], grads[16], grads[17], grads[18], grads[19])
```

```python
import functools
import types

import jax
import jax.numpy as jnp
from jax import lax
from jax.experimental import pallas as pl
from jax.experimental.pallas import tpu as pltpu
from jax.sharding import PartitionSpec as P

HEAD = 64
CONV = 4
SIDE = 4

epsilon = 1e-05
negative_fill = -1e30
score_scale = 0.125
log2_e = 1.4426950408889634
highest = lax.Precision.HIGHEST
MESH = pl.DeviceIdType.MESH
ANY = pl.BlockSpec(memory_space=pl.ANY)
VMEM = pl.BlockSpec(memory_space=pltpu.VMEM)
SEMS = 128
HOPS = (1, 3, 2)
X, Y, Z = range(3)


class Net:
    def __init__(self, core, coords, names, send, recv):
        self.core = core
        self.at = coords
        self.names = names
        self.send = send
        self.recv = recv
        self.begun = []

    def device(self, axis=None, hop=0, other_core=False):
        place = dict(self.at)
        if axis is not None:
            place[axis] = (place[axis] + hop) % SIDE
        core = 1 - self.core if other_core else self.core
        return (core, place[Y] * SIDE + place[Z], place[X])

    def slot(self, name):
        return self.names.setdefault(name, len(self.names))

    def copy(self, name, source, target, device):
        i = self.slot(name)
        return pltpu.make_async_remote_copy(
            source,
            target,
            self.send.at[i],
            self.recv.at[i],
            device_id=device,
            device_id_type=MESH,
        )

    def start(self, name, source, target, device):
        copy = self.copy(name, source, target, device)
        copy.start()
        self.begun.append(copy)
        return copy

    def local(self, name, source, target):
        copy = pltpu.make_async_copy(source, target, self.send.at[self.slot(name)])
        copy.start()
        return copy


def pick(axes, fixed):
    return tuple(fixed.get(axis, slice(None)) for axis in axes)


def gather(net, name, source, out, axes, order):
    at = net.at
    fixed = {axis: at[axis] for axis in axes}
    own = net.local((name, -1), source, out.at[pick(axes, fixed)])
    here = source
    for axis in order:
        place = pick(axes, fixed)
        copies = [
            net.start(
                (name, axis, hop),
                out.at[place] if here is None else here,
                out.at[place],
                net.device(axis, hop),
            )
            for hop in HOPS
        ]
        yield
        for copy in copies:
            copy.wait_recv()
        if here is not None:
            own.wait()
        here = None
        del fixed[axis]


def gather_two(net, name, source, out, order, after=None, patience=0):
    at = net.at
    first, second = order
    axes = (Y, Z)

    def place(back):
        spot = dict(at)
        spot[first] = (spot[first] - back + SIDE) % SIDE
        return (spot[Y], spot[Z])

    mine = place(0)
    own = net.local((name, -1), source, out.at[mine])
    ones = [
        net.start((name, 1, hop), source, out.at[mine], net.device(first, hop)) for hop in HOPS
    ]
    twos = []

    def forward(back):
        spot = place(back)
        for hop in HOPS:
            twos.append(
                net.start(
                    (name, 2, back, hop),
                    source if back == 0 else out.at[spot],
                    out.at[spot],
                    net.device(second, hop),
                )
            )

    forward(0)
    yield
    for copy, hop in zip(ones, HOPS):
        copy.wait_recv()
        forward(hop)
    own.wait()
    for _ in range(1 + patience):
        yield
    if after is None:
        for copy in twos:
            copy.wait_recv()
        return
    lines = [twos[3 * i : 3 * i + 3] for i in range(SIDE)]
    after(at[second])
    for h, hop in enumerate(HOPS):
        for line in lines:
            line[h].wait_recv()
        after((at[second] - hop + SIDE) % SIDE)


def scatter_sum(total, rows, own, others, out):
    chunk = 16 if rows % 16 == 0 else 8
    per = rows // chunk

    def step(i, carry):
        lead = i // per
        part = pl.ds(pl.multiple_of((i % per) * chunk, chunk), chunk)
        value = own(lead, part).astype(jnp.float32)
        for other in others:
            value = value + other(lead, part).astype(jnp.float32)
        out(lead, part, value)
        return carry

    lax.fori_loop(0, total * per, step, 0)


def reduce_two(net, name, source, pad, out, order):
    at = net.at
    first, second = order
    one, mid, two, kept = pad.one, pad.mid, pad.two, pad.own
    rows = source.shape[2]

    def part_of(line):
        return source.at[:, line] if first == Z else source.at[line]

    own = net.local((name, -4), part_of(at[first]), kept)
    ones = [
        net.start(
            (name, 1, hop),
            part_of((at[first] + hop) % SIDE),
            one.at[hop - 1],
            net.device(first, hop),
        )
        for hop in HOPS
    ]
    yield
    own.wait()
    for copy in ones:
        copy.wait_recv()

    def put_mid(lead, part, value):
        mid[lead, part, :] = value.astype(mid.dtype)

    scatter_sum(
        SIDE,
        rows,
        lambda lead, part: kept[lead, part, :],
        [lambda lead, part, k=k: one[k, lead, part, :] for k in range(3)],
        put_mid,
    )
    twos = [
        net.start(
            (name, 2, hop),
            mid.at[(at[second] + hop) % SIDE],
            two.at[hop - 1],
            net.device(second, hop),
        )
        for hop in HOPS
    ]
    yield
    for copy in twos:
        copy.wait_recv()
    spot = at[second]

    def put_out(lead, part, value):
        out[part, :] = value.astype(out.dtype)

    scatter_sum(
        1,
        rows,
        lambda lead, part: kept[spot, part, :],
        [lambda lead, part, k=k: one[k, spot, part, :] for k in range(3)]
        + [lambda lead, part, k=k: two[k, part, :] for k in range(3)],
        put_out,
    )


def swap_two(net, name, source, mid, out):
    at = net.at
    own = net.local((name, -1), source.at[:, at[Z]], mid.at[at[Z]])
    ones = [
        net.start(
            (name, 1, hop),
            source.at[:, (at[Z] + hop) % SIDE],
            mid.at[at[Z]],
            net.device(Z, hop),
        )
        for hop in HOPS
    ]
    yield
    for copy in ones:
        copy.wait_recv()
    own.wait()
    own = net.local((name, -2), mid.at[:, at[Y]], out.at[at[Y]])
    twos = [
        net.start(
            (name, 2, hop),
            mid.at[:, (at[Y] + hop) % SIDE],
            out.at[at[Y]],
            net.device(Y, hop),
        )
        for hop in HOPS
    ]
    yield
    for copy in twos:
        copy.wait_recv()
    own.wait()


def run_jobs(jobs):
    jobs = list(jobs)
    while jobs:
        jobs = [job for job in jobs if next(job, True) is None]


def flat(group):
    return [
        leaf
        for value in group.values()
        for leaf in (flat(value) if isinstance(value, dict) else [value])
    ]


def named(group, leaves):
    return types.SimpleNamespace(
        **{
            key: named(value, leaves) if isinstance(value, dict) else next(leaves)
            for key, value in group.items()
        }
    )


def exchange(name, number, program, inputs, outputs, scratch=None, vmem=None, cores=(0, 1)):
    scratch = scratch or {}
    parts = (inputs, outputs, scratch)
    counts = [len(flat(part)) for part in parts]

    def kernel(*refs):
        held = types.SimpleNamespace()
        begin = 0
        for part, count in zip(parts, counts):
            vars(held).update(vars(named(part, iter(refs[begin : begin + count]))))
            begin += count
        send, recv = refs[begin:]
        core = lax.axis_index("branch")
        seq = lax.axis_index("seq")
        coords = {X: lax.axis_index("fsdp"), Y: seq // SIDE, Z: seq % SIDE}
        names = {}
        for one_core in cores:

            @pl.when(core == one_core)
            def _():
                net = Net(one_core, coords, names, send, recv)
                barrier = pltpu.get_barrier_semaphore()
                peers = [net.device(axis, hop) for axis in (X, Y, Z) for hop in HOPS]
                if len(cores) == 2:
                    peers.append(net.device(other_core=True))
                for peer in peers:
                    pl.semaphore_signal(barrier, inc=1, device_id=peer, device_id_type=MESH)
                pl.semaphore_wait(barrier, len(peers))
                run_jobs(program(net, held))
                for copy in net.begun:
                    copy.wait_send()

        assert len(names) <= SEMS

    results = pl.pallas_call(
        kernel,
        out_shape=[jax.ShapeDtypeStruct(s, d) for s, d, _ in flat(outputs)],
        in_specs=[spec for _, spec in flat(inputs)],
        out_specs=[spec for _, _, spec in flat(outputs)],
        scratch_shapes=[pltpu.VMEM(s, d) for s, d in flat(scratch)]
        + [pltpu.SemaphoreType.DMA((SEMS,)), pltpu.SemaphoreType.DMA((SEMS,))],
        compiler_params=pltpu.CompilerParams(
            collective_id=number, has_side_effects=True, vmem_limit_bytes=vmem
        ),
        name=name,
    )(*[array for array, _ in flat(inputs)])
    return named(outputs, iter(results))


CHUNKS = 128
STEPS = 16
LINES = 8
WIDE = 40
far_away = 1e30


def to_lanes(source, target):
    for block in range(source.shape[0]):
        part = pl.ds(block * CHUNKS, CHUNKS)

        def move(l, carry):
            target[l, part, :] = source[block, pl.ds(l, CHUNKS, stride=STEPS), :].T
            return carry

        lax.fori_loop(0, STEPS, move, 0, unroll=2)


def to_rows(source, target):
    for block in range(target.shape[0]):
        part = pl.ds(block * CHUNKS, CHUNKS)

        def move(l, carry):
            target[block, pl.ds(l, CHUNKS, stride=STEPS), :] = source[l, part, :].T
            return carry

        lax.fori_loop(0, STEPS, move, 0, unroll=2)


def chunk_starts(ends, span, rates, reverse):
    lanes = lax.broadcasted_iota(jnp.int32, span.shape, 1)
    by = 1
    while by < CHUNKS:
        turn = CHUNKS - by if reverse else by
        inside = lanes < turn if reverse else lanes >= turn
        reach = jnp.where(inside, span, far_away)
        ends = [
            end + jnp.exp2(reach * rate) * pltpu.roll(end, turn, 1)
            for end, rate in zip(ends, rates)
        ]
        span = span + jnp.where(inside, pltpu.roll(span, turn, 1), 0.0)
        by *= 2
    turn = CHUNKS - 1 if reverse else 1
    inside = lanes < turn if reverse else lanes >= turn
    return [jnp.where(inside, pltpu.roll(end, turn, 1), 0.0) for end in ends]


def rate_lines(rate_ref, lines, states):
    tile = rate_ref[lines, :]
    return [jnp.broadcast_to(tile[:, s : s + 1], (lines.size, CHUNKS)) for s in range(states)]


def join_chunks(used, ends_ref, decay_t, rate_ref, reverse):
    states = rate_ref.shape[1]

    def channels(g, carry):
        lines = pl.ds(pl.multiple_of(g * WIDE, LINES), WIDE)
        span = decay_t[0, lines, :]
        for l in range(1, STEPS):
            span = span + decay_t[l, lines, :]
        starts = chunk_starts(
            [ends_ref[s, lines, :] for s in range(states)],
            span,
            rate_lines(rate_ref, lines, states),
            reverse,
        )
        for s in range(states):
            ends_ref[s, lines, :] = starts[s]
        return carry

    lax.fori_loop(0, used // WIDE, channels, 0)


def scan_forward_kernel(
    used, decay_ref, drive_ref, cols_ref, rate_ref, out_ref, start_ref, decay_t, drive_t, out_t
):
    states = rate_ref.shape[1]
    to_lanes(decay_ref, decay_t)
    to_lanes(drive_ref, drive_t)
    out_t[...] = jnp.zeros_like(out_t)

    def ends(g, carry):
        lines = pl.ds(pl.multiple_of(g * LINES, LINES), LINES)
        decays = [decay_t[l, lines, :] for l in range(STEPS)]
        drives = [drive_t[l, lines, :] for l in range(STEPS)]
        rates = rate_lines(rate_ref, lines, states)
        for s in range(states):
            state = drives[0] * cols_ref[s, 0:1, :]
            for l in range(1, STEPS):
                state = jnp.exp2(decays[l] * rates[s]) * state + drives[l] * cols_ref[s, l : l + 1, :]
            start_ref[s, lines, :] = state
        return carry

    lax.fori_loop(0, used // LINES, ends, 0)
    join_chunks(used, start_ref, decay_t, rate_ref, False)

    def channels(g, carry):
        lines = pl.ds(pl.multiple_of(g * LINES, LINES), LINES)
        decays = [decay_t[l, lines, :] for l in range(STEPS)]
        drives = [drive_t[l, lines, :] for l in range(STEPS)]
        rates = rate_lines(rate_ref, lines, states)
        outs = [jnp.zeros((LINES, CHUNKS), jnp.float32)] * STEPS
        for s in range(states):
            state = start_ref[s, lines, :]
            for l in range(STEPS):
                state = jnp.exp2(decays[l] * rates[s]) * state + drives[l] * cols_ref[s, l : l + 1, :]
                outs[l] = outs[l] + state * cols_ref[states + s, l : l + 1, :]
        for l in range(STEPS):
            out_t[l, lines, :] = outs[l]
        return carry

    lax.fori_loop(0, used // LINES, channels, 0)
    to_rows(out_t, out_ref)


def scan_forward(decay, drive, cols, rate, used):
    width = decay.shape[0] * CHUNKS
    states = rate.shape[1]
    turned = jax.ShapeDtypeStruct((STEPS, width, CHUNKS), jnp.float32)
    return pl.pallas_call(
        functools.partial(scan_forward_kernel, used),
        out_shape=[
            jax.ShapeDtypeStruct(decay.shape, jnp.float32),
            jax.ShapeDtypeStruct((states, width, CHUNKS), jnp.float32),
            turned,
            turned,
        ],
        in_specs=[VMEM] * 4,
        out_specs=[VMEM] * 4,
        scratch_shapes=[pltpu.VMEM(turned.shape, jnp.float32)],
        compiler_params=pltpu.CompilerParams(vmem_limit_bytes=32 * 2**20),
        name="scan_forward",
    )(decay, drive, cols, rate)


def scan_backward_kernel(
    used,
    decay_t,
    drive_t,
    cols_ref,
    rate_ref,
    start_ref,
    grad_ref,
    g_decay_ref,
    g_drive_ref,
    g_cols_ref,
    g_rate_ref,
    grad_t,
    g_decay_t,
    g_drive_t,
    sums_t,
    ends_t,
):
    states = rate_ref.shape[1]
    blank = jnp.zeros((LINES, CHUNKS), jnp.float32)
    to_lanes(grad_ref, grad_t)
    g_decay_t[...] = jnp.zeros_like(g_decay_t)
    g_drive_t[...] = jnp.zeros_like(g_drive_t)
    sums_t[...] = jnp.zeros_like(sums_t)
    g_rate_ref[...] = jnp.zeros_like(g_rate_ref)
    marks = lax.broadcasted_iota(jnp.int32, (LINES, states), 1)

    def ends(g, carry):
        lines = pl.ds(pl.multiple_of(g * LINES, LINES), LINES)
        rates = rate_lines(rate_ref, lines, states)
        decays = [decay_t[l, lines, :] for l in range(STEPS)]
        grads = [grad_t[l, lines, :] for l in range(STEPS)]
        for s in range(states):
            back = blank
            for l in reversed(range(STEPS)):
                back = jnp.exp2(decays[l] * rates[s]) * (
                    grads[l] * cols_ref[states + s, l : l + 1, :] + back
                )
            ends_t[s, lines, :] = back
        return carry

    lax.fori_loop(0, used // LINES, ends, 0)
    join_chunks(used, ends_t, decay_t, rate_ref, True)

    def channels(g, carry):
        lines = pl.ds(pl.multiple_of(g * LINES, LINES), LINES)
        tile = rate_ref[lines, :]

        def state_step(s, g_rate):
            rate = jnp.sum(jnp.where(marks == s, tile, 0.0), axis=1, keepdims=True)
            rate = jnp.broadcast_to(rate, (LINES, CHUNKS))
            state = start_ref[s, lines, :]
            befores, factors = [], []
            for l in range(STEPS):
                factor = jnp.exp2(decay_t[l, lines, :] * rate)
                befores.append(state)
                factors.append(factor)
                state = factor * state + drive_t[l, lines, :] * cols_ref[s, pl.ds(l, 1), :]
            back = ends_t[s, lines, :]
            total_rate = blank
            for l in reversed(range(STEPS)):
                grad = grad_t[l, lines, :]
                total = grad * cols_ref[states + s, pl.ds(l, 1), :] + back
                sums_t[s, l] += total * drive_t[l, lines, :]
                sums_t[states + s, l] += grad * state
                g_drive_t[l, lines, :] += total * cols_ref[s, pl.ds(l, 1), :]
                back = total * factors[l]
                moved = back * befores[l]
                g_decay_t[l, lines, :] += moved * rate
                total_rate = total_rate + moved * decay_t[l, lines, :]
                state = befores[l]
            total_rate = jnp.sum(total_rate, axis=1, keepdims=True)
            return jnp.where(marks == s, total_rate, g_rate)

        g_rate_ref[lines, :] = lax.fori_loop(
            0, states, state_step, jnp.zeros((LINES, states), jnp.float32), unroll=16
        )
        return carry

    lax.fori_loop(0, used // LINES, channels, 0)

    def collapse(i, carry):
        g_cols_ref[i] = jnp.sum(sums_t[i], axis=1)
        return carry

    lax.fori_loop(0, 2 * states, collapse, 0)
    to_rows(g_decay_t, g_decay_ref)
    to_rows(g_drive_t, g_drive_ref)


def scan_backward(decay_t, drive_t, cols, rate, starts, grad, used):
    states = rate.shape[1]
    turned = pltpu.VMEM(decay_t.shape, jnp.float32)
    return pl.pallas_call(
        functools.partial(scan_backward_kernel, used),
        out_shape=[
            jax.ShapeDtypeStruct(grad.shape, jnp.float32),
            jax.ShapeDtypeStruct(grad.shape, jnp.float32),
            jax.ShapeDtypeStruct(cols.shape, jnp.float32),
            jax.ShapeDtypeStruct(rate.shape, jnp.float32),
        ],
        in_specs=[VMEM] * 6,
        out_specs=[VMEM] * 4,
        scratch_shapes=[
            turned,
            turned,
            turned,
            pltpu.VMEM((2 * states, STEPS, LINES, CHUNKS), jnp.float32),
            pltpu.VMEM(starts.shape, jnp.float32),
        ],
        compiler_params=pltpu.CompilerParams(vmem_limit_bytes=48 * 2**20),
        name="scan_backward",
    )(decay_t, drive_t, cols, rate, starts, grad)


KEY_ROWS = 256
PIECE = 25
PADDED = 32
LANES = 128


def dot_on(left, right, left_dim, right_dim, **options):
    return lax.dot_general(
        left,
        right,
        (((left_dim,), (right_dim,)), ((), ())),
        preferred_element_type=jnp.float32,
        **options,
    )


def spread_matrix(low, high, wide_low, wide_high):
    shape = (high - low, wide_high - wide_low)
    column = low + lax.broadcasted_iota(jnp.int32, shape, 0)
    place = wide_low + lax.broadcasted_iota(jnp.int32, shape, 1)
    inside = place % PADDED
    match = (column == (place // PADDED) * PIECE + inside) & (inside < PIECE)
    return jnp.where(match, 1.0, 0.0).astype(jnp.bfloat16)


def spread_columns(values):
    width = values.shape[1]
    step = LANES // PADDED * PIECE
    parts = []
    for begin in range(0, width, step):
        low = begin // LANES * LANES
        high = min(low + 2 * LANES, width)
        wide = begin // PIECE * PADDED
        parts.append(dot_on(values[:, low:high], spread_matrix(low, high, wide, wide + LANES), 1, 0))
    return jnp.concatenate(parts, axis=1).astype(jnp.bfloat16)


def close_columns(values):
    width = values.shape[1] // PADDED * PIECE
    parts = []
    for begin in range(0, width, LANES):
        end = min(begin + LANES, width)
        low = begin // PIECE * PADDED // LANES * LANES
        high = -(-((end - 1) // PIECE + 1) * PADDED // LANES) * LANES
        matrix = spread_matrix(begin, end, low, high)
        value = values[:, low:high]
        most = value.astype(jnp.bfloat16)
        closed = dot_on(most, matrix, 1, 1)
        if values.dtype != jnp.bfloat16:
            rest = (value - most.astype(jnp.float32)).astype(jnp.bfloat16)
            closed = closed + dot_on(rest, matrix, 1, 1)
        parts.append(closed)
    return jnp.concatenate(parts, axis=1)


def unit_rows(values):
    return values * lax.rsqrt(jnp.mean(values * values, axis=-1, keepdims=True) + epsilon)


def whole_call(name, body, arrays, results, scratch=(), scalars=0, room=48):
    return pl.pallas_call(
        body,
        out_shape=[jax.ShapeDtypeStruct(shape, kind) for shape, kind in results],
        in_specs=[pl.BlockSpec(memory_space=pltpu.SMEM)] * scalars
        + [VMEM] * (len(arrays) - scalars),
        out_specs=[VMEM] * len(results),
        scratch_shapes=[pltpu.VMEM(shape, kind) for shape, kind in scratch],
        compiler_params=pltpu.CompilerParams(vmem_limit_bytes=room * 2**20),
        name=name,
    )(*arrays)


def attention_project_kernel(
    tokens_ref,
    meta_ref,
    gain_ref,
    first_ref,
    second_ref,
    wide_ref,
    query_ref,
    keyval_ref,
    meta_wide_ref,
    meta_kv_ref,
):
    gain = gain_ref[...]
    third = first_ref.shape[1]
    rest = query_ref.shape[1] - third
    begin = -(-rest // LANES) * LANES
    keys = pl.ds(begin, keyval_ref.shape[1])
    wide = spread_columns((unit_rows(tokens_ref[...].astype(jnp.float32)) * gain).astype(jnp.bfloat16))
    wide_ref[...] = wide
    query_ref[:, pl.ds(0, third)] = dot_on(wide, first_ref[...], 1, 0).astype(jnp.bfloat16)
    query_ref[:, pl.ds(third, rest)] = dot_on(wide, second_ref[:, pl.ds(0, rest)], 1, 0).astype(
        jnp.bfloat16
    )
    keyval_ref[...] = dot_on(wide, second_ref[:, keys], 1, 0).astype(jnp.bfloat16)
    meta_wide = spread_columns((unit_rows(meta_ref[...]) * gain).astype(jnp.bfloat16))
    meta_wide_ref[...] = meta_wide
    meta_kv_ref[...] = dot_on(meta_wide, second_ref[:, keys], 1, 0).astype(jnp.bfloat16)


def attention_project(tokens, meta, gain, first, second, query_width, keys_width):
    rows, metas, wide = tokens.shape[0], meta.shape[0], first.shape[0]
    low = jnp.bfloat16
    return whole_call(
        "attention_project",
        attention_project_kernel,
        (tokens, meta, gain, first, second),
        (
            ((rows, wide), low),
            ((rows, query_width), low),
            ((rows, keys_width), low),
            ((metas, wide), low),
            ((metas, keys_width), low),
        ),
    )


def attention_weights_kernel(
    wide_ref,
    out_wide_ref,
    g_query_ref,
    g_pre_ref,
    first_ref,
    second_ref,
    one_ref,
    two_ref,
    three_ref,
    gain_ref,
):
    third = first_ref.shape[1]
    one = dot_on(wide_ref[...], g_query_ref[...], 0, 0)
    cut = one_ref.shape[1]
    one_ref[...] = one[:, :cut].astype(jnp.bfloat16)
    gain = jnp.sum(one[:, :third] * first_ref[...].astype(jnp.float32), axis=1, keepdims=True)
    rest = one.shape[1] - third
    gain = gain + jnp.sum(
        one[:, third:] * second_ref[:, pl.ds(0, rest)].astype(jnp.float32), axis=1, keepdims=True
    )
    gain_ref[...] = gain
    two = dot_on(out_wide_ref[...], g_pre_ref[...], 0, 0)
    size = one.shape[1] - cut
    begin = -(-size // LANES) * LANES
    left = two_ref.shape[1] - begin
    two_ref[...] = jnp.zeros_like(two_ref)
    two_ref[:, pl.ds(0, size)] = one[:, cut:].astype(jnp.bfloat16)
    two_ref[:, pl.ds(begin, left)] = two[:, :left].astype(jnp.bfloat16)
    three_ref[...] = two[:, left:].astype(jnp.bfloat16)


def attention_weights(wide, out_wide, g_query, g_pre, first, second, cuts):
    rows, places = wide.shape
    size = 2 * LANES
    columns = pl.BlockSpec((rows, size), lambda i: (0, i))

    def lines(width):
        return pl.BlockSpec((size, width), lambda i: (i, 0))

    return pl.pallas_call(
        attention_weights_kernel,
        grid=(places // size,),
        out_shape=[jax.ShapeDtypeStruct((places, cut), jnp.bfloat16) for cut in cuts]
        + [jax.ShapeDtypeStruct((places, 1), jnp.float32)],
        in_specs=[columns, columns]
        + [pl.BlockSpec(part.shape, lambda i: (0, 0)) for part in (g_query, g_pre)]
        + [lines(first.shape[1]), lines(second.shape[1])],
        out_specs=[lines(cut) for cut in cuts] + [lines(1)],
        compiler_params=pltpu.CompilerParams(vmem_limit_bytes=32 * 2**20),
        name="attention_weights",
    )(wide, out_wide, g_query, g_pre, first, second)


def attention_inputs_kernel(
    keyval_ref,
    g_query_ref,
    wide_ref,
    meta_wide_ref,
    g_meta_ref,
    first_ref,
    second_ref,
    meta_ref,
    gain_ref,
    one_ref,
    two_ref,
    three_ref,
    g_normed_ref,
    part_ref,
    meta_gain_ref,
):
    third = first_ref.shape[1]
    rest = g_query_ref.shape[1] - third
    begin = -(-rest // LANES) * LANES
    keys = pl.ds(begin, keyval_ref.shape[1])
    keyval = keyval_ref[...].astype(jnp.bfloat16)
    weight = second_ref[:, keys]
    weight_f = weight.astype(jnp.float32)
    grad = dot_on(wide_ref[...], keyval, 0, 0)
    part_ref[...] = jnp.sum(grad * weight_f, axis=1, keepdims=True)
    g_meta = g_meta_ref[...]
    grad = grad + dot_on(
        meta_wide_ref[...].astype(jnp.float32), g_meta, 0, 0, precision=highest
    )
    half = one_ref.shape[1]
    one_ref[...] = grad[:, :half].astype(jnp.bfloat16)
    two_ref[...] = grad[:, half:].astype(jnp.bfloat16)
    g_normed = dot_on(g_query_ref[:, pl.ds(0, third)], first_ref[...], 1, 1)
    g_normed = g_normed + dot_on(
        g_query_ref[:, pl.ds(third, rest)], second_ref[:, pl.ds(0, rest)], 1, 1
    )
    g_normed_ref[...] = close_columns(g_normed + dot_on(keyval, weight, 1, 1))
    g_meta_normed = close_columns(dot_on(g_meta, weight_f, 1, 1, precision=highest))
    meta = meta_ref[...]
    scale = lax.rsqrt(jnp.mean(meta * meta, axis=-1, keepdims=True) + epsilon)
    unit = meta * scale
    meta_gain_ref[...] = jnp.sum(g_meta_normed * unit, axis=0, keepdims=True)
    g_unit = g_meta_normed * gain_ref[...]
    g_rows = scale * (g_unit - unit * jnp.mean(g_unit * unit, axis=-1, keepdims=True))
    three_ref[...] = spread_columns(g_rows.astype(jnp.bfloat16)).T


def attention_inputs(
    keyval_sum, g_query, wide, meta_wide, g_meta, first, second, meta, gain
):
    rows, places = wide.shape
    keys_width = keyval_sum.shape[1]
    metas, width = meta.shape
    low, full = jnp.bfloat16, jnp.float32
    return whole_call(
        "attention_inputs",
        attention_inputs_kernel,
        (keyval_sum, g_query, wide, meta_wide, g_meta, first, second, meta, gain),
        (
            ((places, keys_width // 2), low),
            ((places, keys_width // 2), low),
            ((places, metas), low),
            ((rows, width), full),
            ((places, 1), full),
            ((1, width), full),
        ),
        room=60,
    )


def stack_heads(source, target, scale, in_values):
    rows = source.shape[0]
    groups = target.shape[0]
    per = target.shape[1] // rows
    blank = jnp.zeros((rows, HEAD), target.dtype)
    for group in range(groups):
        for j in range(per):
            head = source[:, pl.ds((group * per + j) * HEAD, HEAD)].astype(jnp.float32) * scale
            head = head.astype(target.dtype)
            pair = [blank, head] if in_values else [head, blank]
            target[group, pl.ds(j * rows, rows), :] = jnp.concatenate(pair, axis=1)


def lay_keys(source, target):
    rows = source.shape[2]

    def move(place, carry):
        for half in range(2):
            begin = pl.multiple_of((place * 2 + half) * rows, rows)
            target[pl.ds(begin, rows), :] = source[half, place]
        return carry

    lax.fori_loop(0, source.shape[1], move, 0)


def key_bias(bounds_ref, begin, per):
    rows = bounds_ref.shape[0]
    keys = begin + lax.broadcasted_iota(jnp.int32, (rows, KEY_ROWS), 1)
    allowed = (keys >= bounds_ref[:, 0:1]) & (keys <= bounds_ref[:, 1:2])
    bias = jnp.where(allowed, 0.0, negative_fill)
    return jnp.concatenate([bias] * per, axis=0)


def attend_forward_kernel(
    count_ref,
    query_ref,
    keyval_ref,
    meta_ref,
    bounds_ref,
    second_ref,
    third_ref,
    out_ref,
    mass_ref,
    wide_ref,
    pre_ref,
    heads,
    keys,
    scores,
):
    rows = query_ref.shape[0]
    groups = heads.shape[0]
    per = heads.shape[1] // rows
    width = 2 * HEAD
    metas = meta_ref.shape[0]
    meta_part = pl.ds(scores.shape[1] - metas, metas)
    stack_heads(query_ref, heads, score_scale, False)
    lay_keys(keyval_ref, keys)
    count = count_ref[0]
    lanes = lax.broadcasted_iota(jnp.int32, mass_ref.shape, 1)
    for group in range(groups):
        part = pl.ds(group * width, width)
        query = heads[group]

        def score(b, top):
            begin = pl.multiple_of(b * KEY_ROWS, KEY_ROWS)
            value = dot_on(query, keys[pl.ds(begin, KEY_ROWS), part], 1, 1)
            value = value + key_bias(bounds_ref, begin, per)
            scores[:, pl.ds(begin, KEY_ROWS)] = value
            return jnp.maximum(top, jnp.max(value, axis=1, keepdims=True))

        value = dot_on(query, meta_ref[:, part], 1, 1)
        scores[:, meta_part] = value
        top = lax.fori_loop(0, count, score, jnp.max(value, axis=1, keepdims=True))

        def weigh(b, total):
            spot = pl.ds(pl.multiple_of(b * KEY_ROWS, KEY_ROWS), KEY_ROWS)
            value = jnp.exp(scores[:, spot] - top)
            scores[:, spot] = value
            return total + jnp.sum(value, axis=1, keepdims=True)

        value = jnp.exp(scores[:, meta_part] - top)
        scores[:, meta_part] = value
        total = lax.fori_loop(0, count, weigh, jnp.sum(value, axis=1, keepdims=True))
        share = 1.0 / total

        def gather_values(b, out):
            begin = pl.multiple_of(b * KEY_ROWS, KEY_ROWS)
            probs = (scores[:, pl.ds(begin, KEY_ROWS)] * share).astype(jnp.bfloat16)
            return out + dot_on(probs, keys[pl.ds(begin, KEY_ROWS), part], 1, 0)

        probs = (scores[:, meta_part] * share).astype(jnp.bfloat16)
        out = lax.fori_loop(0, count, gather_values, dot_on(probs, meta_ref[:, part], 1, 0))
        for j in range(per):
            out_ref[:, pl.ds((group * per + j) * HEAD, HEAD)] = out[
                j * rows : (j + 1) * rows, HEAD:
            ]
        mass = top + jnp.log(total)
        before = mass_ref[...] if group else jnp.zeros_like(mass_ref)
        mass_ref[...] = jnp.where(lanes == group, mass, before)
    wide = spread_columns(out_ref[...].astype(jnp.bfloat16))
    wide_ref[...] = wide
    most = third_ref.shape[1]
    part = pre_ref.shape[1] - most
    pre_ref[:, pl.ds(0, part)] = dot_on(
        wide, second_ref[:, pl.ds(second_ref.shape[1] - part, part)], 1, 0
    )
    pre_ref[:, pl.ds(part, most)] = dot_on(wide, third_ref[...], 1, 0)


def attend_forward(count, query, keyval, meta, bounds, second, third):
    rows, query_width = query.shape
    groups = meta.shape[1] // (2 * HEAD)
    stacked = query_width // HEAD // groups * rows
    key_rows = 2 * keyval.shape[1] * keyval.shape[2]
    places, low, full = second.shape[0], jnp.bfloat16, jnp.float32
    return whole_call(
        "attend_forward",
        attend_forward_kernel,
        (count, query, keyval, meta, bounds, second, third),
        (
            ((rows, query_width), full),
            ((stacked, 2 * HEAD), full),
            ((rows, places), low),
            ((rows, query_width), full),
        ),
        (
            ((groups, stacked, 2 * HEAD), low),
            ((key_rows, meta.shape[1]), low),
            ((stacked, key_rows + meta.shape[0]), full),
        ),
        scalars=1,
    )


def attend_backward_kernel(
    count_ref,
    query_ref,
    keyval_ref,
    meta_ref,
    bounds_ref,
    out_ref,
    mass_ref,
    g_pre_ref,
    second_ref,
    third_ref,
    g_query_ref,
    g_keyval_ref,
    g_meta_ref,
    heads,
    grads,
    keys,
    grad_ref,
):
    rows = query_ref.shape[0]
    groups = heads.shape[0]
    per = heads.shape[1] // rows
    width = 2 * HEAD
    most = third_ref.shape[1]
    left = g_pre_ref.shape[1] - most
    grad_wide = dot_on(
        g_pre_ref[:, pl.ds(0, left)],
        second_ref[:, pl.ds(second_ref.shape[1] - left, left)],
        1,
        1,
    )
    grad_wide = grad_wide + dot_on(g_pre_ref[:, pl.ds(left, most)], third_ref[...], 1, 1)
    grad_ref[...] = close_columns(grad_wide.astype(jnp.bfloat16)).astype(jnp.bfloat16)
    stack_heads(query_ref, heads, score_scale, False)
    stack_heads(grad_ref, grads, 1.0, True)
    lay_keys(keyval_ref, keys)
    g_keyval_ref[...] = jnp.zeros_like(g_keyval_ref)
    count = count_ref[0]
    lanes = lax.broadcasted_iota(jnp.int32, mass_ref.shape, 1)
    for group in range(groups):
        part = pl.ds(group * width, width)
        query, grad = heads[group], grads[group]
        mass = jnp.sum(jnp.where(lanes == group, mass_ref[...], 0.0), axis=1, keepdims=True)
        balance = []
        for j in range(per):
            head = pl.ds((group * per + j) * HEAD, HEAD)
            balance.append(
                jnp.sum(grad_ref[:, head].astype(jnp.float32) * out_ref[:, head], axis=1, keepdims=True)
            )
        balance = jnp.concatenate(balance, axis=0)

        def pieces(block, bias):
            value = dot_on(query, block, 1, 1)
            if bias is not None:
                value = value + bias
            probs = jnp.exp(value - mass)
            g_scores = (probs * (dot_on(grad, block, 1, 1) - balance)).astype(jnp.bfloat16)
            g_block = dot_on(g_scores, query, 0, 0) + dot_on(probs.astype(jnp.bfloat16), grad, 0, 0)
            return dot_on(g_scores, block, 1, 0), g_block

        g_query, g_meta = pieces(meta_ref[:, part], None)
        g_meta_ref[:, part] = g_meta

        def step(b, g_query):
            begin = pl.multiple_of(b * KEY_ROWS, KEY_ROWS)
            more, g_block = pieces(
                keys[pl.ds(begin, KEY_ROWS), part], key_bias(bounds_ref, begin, per)
            )
            g_keyval_ref[pl.ds(begin, KEY_ROWS), part] = g_block.astype(jnp.bfloat16)
            return g_query + more

        g_query = lax.fori_loop(0, count, step, g_query) * score_scale
        for j in range(per):
            g_query_ref[:, pl.ds((group * per + j) * HEAD, HEAD)] = g_query[
                j * rows : (j + 1) * rows, :HEAD
            ].astype(jnp.bfloat16)


def attend_backward(count, query, keyval, meta, bounds, out, mass, g_pre, second, third):
    rows, query_width = query.shape
    groups = meta.shape[1] // (2 * HEAD)
    stacked = mass.shape[0]
    key_rows = 2 * keyval.shape[1] * keyval.shape[2]
    low = jnp.bfloat16
    return whole_call(
        "attend_backward",
        attend_backward_kernel,
        (count, query, keyval, meta, bounds, out, mass, g_pre, second, third),
        (
            ((rows, query_width), low),
            ((key_rows, meta.shape[1]), low),
            (meta.shape, jnp.float32),
        ),
        (
            ((groups, stacked, 2 * HEAD), low),
            ((groups, stacked, 2 * HEAD), low),
            ((key_rows, meta.shape[1]), low),
            ((rows, query_width), low),
        ),
        scalars=1,
        room=56,
    )


def rms_norm(values, gain):
    return values * lax.rsqrt(jnp.mean(values * values, axis=-1, keepdims=True) + epsilon) * gain


def rms_unit(values):
    return values * lax.rsqrt(jnp.mean(values * values, axis=-1, keepdims=True) + epsilon)


def contract(left, right, left_dim, right_dim, **options):
    return lax.dot_general(
        left,
        right,
        (((left_dim,), (right_dim,)), ((), ())),
        **(options or {"preferred_element_type": jnp.float32}),
    )


def matmul(left, right):
    return contract(left, right, 1, 0)


def matmul_tn(left, right):
    return contract(left, right, 0, 0)


def matmul_nt(left, right):
    return contract(left, right, 1, 1)


def segment_of(row_ids, end_rows):
    return jnp.sum((row_ids[:, None] >= end_rows[None, :]).astype(jnp.int32), axis=1)


def conv_silu(conv_in, taps, offset, valid_rows):
    row_count = conv_in.shape[0]
    summed = taps[CONV - 1] * conv_in + offset
    for back in range(1, CONV):
        earlier = jnp.pad(conv_in, ((back, 0), (0, 0)))[:row_count]
        summed = summed + taps[CONV - 1 - back] * earlier * valid_rows[back - 1][:, None]
    return jax.nn.silu(summed)


def gate_mix(ssm_out, skip_gain, inputs_m, gate_z):
    return (ssm_out + skip_gain * inputs_m) * jax.nn.silu(gate_z)


def swiglu(gate, up):
    return jax.nn.silu(gate) * up


def pad_to(array, dim, size):
    widths = [(0, 0)] * array.ndim
    widths[dim] = (0, size - array.shape[dim])
    return jnp.pad(array, widths)


def zeros(shape, kind=jnp.float32):
    return jnp.zeros(shape, kind)


def halves_first(rows_by_place):
    width = rows_by_place.shape[-1]
    return rows_by_place.reshape(16, 2, -1, width).transpose(1, 0, 2, 3).reshape(-1, width)


def places_first(rows_by_half):
    width = rows_by_half.shape[-1]
    return rows_by_half.reshape(2, 16, -1, width).transpose(1, 0, 2, 3).reshape(-1, width)


def blank(shapes):
    leaves, nest = jax.tree.flatten(shapes)
    outs = pl.pallas_call(
        lambda *refs: None,
        out_shape=[jax.ShapeDtypeStruct(leaf.shape, leaf.dtype) for leaf in leaves],
        out_specs=[ANY] * len(leaves),
        name="blank",
    )()
    return jax.tree.unflatten(nest, outs)


def order_of(net):
    return (Z, Y) if net.core == 0 else (Y, Z)


def gather_halves(net, name, source, out, patience=0):
    if net.core == 0:
        count = []

        def after(line):
            net.start(
                (name, -3, len(count)),
                out.at[0, line],
                out.at[0, line],
                net.device(other_core=True),
            )
            count.append(line)

        yield from gather_two(net, name, source, out.at[0], (Z, Y), after, patience)
    else:
        yield from gather_two(net, name, source, out.at[1], (Y, Z), None, patience)
        for i in range(SIDE):
            net.copy(
                (name, -3, i), out.at[0, i], out.at[0, i], net.device(other_core=True)
            ).wait_recv()


def reduce_halves(net, name, source, pad, out):
    if net.core == 1:
        for y in range(SIDE):
            net.start(
                (name, -3, y), source.at[0, y], pad.half.at[y], net.device(other_core=True)
            )
        own = net.local((name, -1), source.at[1], pad.half)
        yield
        own.wait()
    else:
        yield
        for y in range(SIDE):
            net.copy(
                (name, -3, y), source.at[0, y], pad.half.at[y], net.device(other_core=True)
            ).wait_recv()
    yield from reduce_two(net, name, pad.half, pad, out, order_of(net))


def share_x(net, name, source, view):
    x = net.at[X]
    core, other = net.core, 1 - net.core
    own = net.local((name, -1), source, view(core, x))
    copies = [
        net.start((name, -2, hop), source, view(core, x), net.device(X, hop)) for hop in HOPS
    ]
    net.start((name, core, 0), source, view(core, x), net.device(other_core=True))
    yield
    for copy, hop in zip(copies, HOPS):
        copy.wait_recv()
        spot = (x - hop + SIDE) % SIDE
        net.start(
            (name, core, hop), view(core, spot), view(core, spot), net.device(other_core=True)
        )
    yield
    for i in (0,) + HOPS:
        net.copy(
            (name, other, i), source, view(other, x), net.device(other_core=True)
        ).wait_recv()
    own.wait()


def swap_cores(net, name, source, out):
    net.start((name, net.core), source, out.at[net.core], net.device(other_core=True))
    own = net.local((name, -1), source, out.at[net.core])
    yield
    net.copy(
        (name, 1 - net.core), source, out.at[1 - net.core], net.device(other_core=True)
    ).wait_recv()
    own.wait()


def hand(net, name, giver, source, target):
    if net.core == giver:
        net.start(name, source, target, net.device(other_core=True))
    else:
        net.copy(name, source, target, net.device(other_core=True)).wait_recv()


def keep_and_hand(net, name, giver, source, target):
    if net.core == giver:
        own = net.local((name, -1), source, target)
    hand(net, (name, 0), giver, source, target)
    yield
    if net.core == giver:
        own.wait()


def reduce_x(net, name, source, pad, out):
    x = net.at[X]
    recv, kept = pad.recv, pad.own
    own = net.local((name, -4), source.at[x], kept)
    copies = [
        net.start(
            (name, 5, hop), source.at[(x + hop) % SIDE], recv.at[hop - 1], net.device(X, hop)
        )
        for hop in HOPS
    ]
    yield
    own.wait()
    for copy in copies:
        copy.wait_recv()

    def put(lead, part, value):
        index = (lead,) if len(out.shape) == 3 else (lead // SIDE, lead % SIDE)
        out[index + (part, slice(None))] = value.astype(out.dtype)

    scatter_sum(
        source.shape[1],
        source.shape[2],
        lambda lead, part: kept[lead, part, :],
        [lambda lead, part, k=k: recv[k, lead, part, :] for k in range(3)],
        put,
    )


def reduce_three(net, name, source, pad, out, order):
    left = [Y, Z, X]
    held = source
    stages = ((pad.recv0, pad.mid0), (pad.recv1, pad.mid1), (pad.recv2, out))
    for stage, axis in enumerate(order):
        recv, mid = stages[stage]
        spot = left.index(axis)
        size = len(left)

        def part_of(place, held=held, spot=spot):
            return held.at[(slice(None),) * spot + (place,)]

        if stage == 0:
            fetch = net.local((name, -4), part_of(net.at[axis]), pad.own)
        copies = [
            net.start(
                (name, stage, hop),
                part_of((net.at[axis] + hop) % SIDE),
                recv.at[hop - 1],
                net.device(axis, hop),
            )
            for hop in HOPS
        ]
        yield
        if stage == 0:
            fetch.wait()
        for copy in copies:
            copy.wait_recv()

        def split(lead, size=size):
            return tuple((lead // SIDE**i) % SIDE for i in reversed(range(size - 1)))

        def own(lead, part, held=held, spot=spot, split=split, axis=axis):
            index = split(lead)
            if len(index) == 2:
                return pad.own[index + (part, slice(None))]
            index = index[:spot] + (net.at[axis],) + index[spot:]
            return held[index + (part, slice(None))]

        def put(lead, part, value, mid=mid, split=split):
            mid[split(lead) + (part, slice(None))] = value.astype(mid.dtype)

        scatter_sum(
            SIDE ** (size - 1),
            source.shape[3],
            own,
            [
                lambda lead, part, k=k, recv=recv, split=split: recv[
                    (k,) + split(lead) + (part, slice(None))
                ]
                for k in range(3)
            ],
            put,
        )
        held = mid
        del left[spot]


def three_pad(rows, width, kind=jnp.bfloat16):
    block = (rows, width)
    return dict(
        own=((SIDE, SIDE) + block, kind),
        recv0=((3, SIDE, SIDE) + block, kind),
        mid0=((SIDE, SIDE) + block, kind),
        recv1=((3, SIDE) + block, kind),
        mid1=((SIDE,) + block, kind),
        recv2=((3,) + block, kind),
    )


def two_pad(rows, width, kind=jnp.bfloat16):
    return dict(
        one=((3, SIDE, rows, width), kind),
        mid=((SIDE, rows, width), kind),
        two=((3, rows, width), kind),
        own=((SIDE, rows, width), kind),
    )


def half_pad(rows, width, kind=jnp.bfloat16):
    return dict(two_pad(rows, width, kind), half=((SIDE, SIDE, rows, width), kind))


def shrink_pad(lead, rows, width, kind=jnp.bfloat16):
    return dict(
        mine=((SIDE, lead, rows, width), kind),
        other=((SIDE, lead, rows, width), kind),
        mid=((SIDE, lead, rows, width), kind),
        **x_pad(lead, rows, width, kind),
    )


def x_pad(lead, rows, width, kind=jnp.bfloat16):
    return dict(recv=((3, lead, rows, width), kind), own=((lead, rows, width), kind))


def program_start(net, held):
    core = net.core
    rows = held.tokens.shape[0] // 2
    axes = (Y, Z, X)
    jobs = []
    if core == 1:

        def mamba():
            target = held.mamba_all.at[net.at[X]]
            yield from swap_two(net, 2, held.mamba, held.mamba_mid, target)
            copies = [
                net.start((2, 3, hop), target, target, net.device(X, hop)) for hop in HOPS
            ]
            yield
            for copy in copies:
                copy.wait_recv()

        jobs = [
            mamba(),
            gather(net, 3, held.back, held.back_all, (X,), (X,)),
            gather(net, 4, held.channel, held.channel_all, (X,), (X,)),
        ]
    return jobs + [
        gather(net, 1, held.small, held.small_all, axes, order_of(net) + (X,)),
        gather_halves(
            net, 0, held.tokens.at[pl.ds(core * rows, rows)], held.tokens_all, patience=2
        ),
    ]


def program_weights(net, held):
    axes = (Y, Z, X)
    jobs, begin = [], 0
    for i, (target, order) in enumerate(
        ((held.first, (X, Z, Y)), (held.second, (Z, Y, X)), (held.third, (Y, X, Z)))
    ):
        size = target.shape[-1]
        jobs.append(gather(net, i, held.whole.at[:, pl.ds(begin, size)], target, axes, order))
        begin += size
    return jobs


def program_keyval(net, held):
    rows = held.keyval.shape[0] // 2
    return [
        gather_two(
            net,
            i,
            held.keyval.at[pl.ds(i * rows, rows)],
            held.keyval_all.at[i],
            ((Z, Y), (Y, Z))[i],
        )
        for i in range(2)
    ] + [swap_two(net, 2, held.gate.at[0], held.gate_mid, held.gate_own)]


def program_project(net, held):
    jobs = []
    for i, order in enumerate(((Z, Y), (Y, Z))):
        source = (held.first, held.second)[i]
        pad = (held.first_pad, held.second_pad)[i]
        target = (held.first_all, held.second_all)[i]

        def job(source=source, pad=pad, target=target, order=order, i=i):
            yield from reduce_two(net, 2 * i, source, pad, pad.sum, order)
            yield from gather_two(net, 2 * i + 1, pad.sum, target, order)

        jobs.append(job())
    return jobs + [swap_two(net, 4, held.gate, held.gate_mid, held.gate_own)]


def program_mixers(net, held):
    core = net.core
    half = held.down.shape[0] // 2
    rows = held.attn_pre.shape[0] // 2

    def attn():
        if core == 0:
            own = net.local((1, -1), held.attn_pre.at[pl.ds(0, rows)], held.attn_half)
        hand(net, (1, 0), 0, held.attn_pre.at[pl.ds(rows, rows)], held.attn_half)
        yield
        if core == 0:
            own.wait()

    return [
        attn(),
        share_x(
            net,
            2,
            held.gate_first if core == 0 else held.gate_second,
            lambda b, x: held.gate_all.at[b, x],
        ),
        share_x(
            net,
            3,
            held.down.at[pl.ds(core * half, half)],
            lambda b, x: held.down_all.at[x, pl.ds(b * half, half)],
        ),
        reduce_halves(net, 0, held.partial, held.pad, held.mamba_pre),
    ]


def program_feed(net, held):
    return [gather_two(net, 0, held.feed, held.feed_all, order_of(net))]


def program_ffn(net, held):
    return [
        reduce_two(net, 0, held.out, held.out_pad, held.out_sum, order_of(net)),
        reduce_two(net, 1, held.grad, held.grad_pad, held.grad_sum, order_of(net)),
    ]


def shrink(net, name, source, pad, out):
    core = net.core
    lead, rows = source.shape[2:4]
    mine = net.local((name, -5), source.at[core], pad.mine)
    net.start((name, 6, core), source.at[1 - core], pad.other, net.device(other_core=True))
    yield
    net.copy(
        (name, 6, 1 - core), source.at[1 - core], pad.other, net.device(other_core=True)
    ).wait_recv()

    mine.wait()

    def put(i, part, value):
        pad.mid[i // lead, i % lead, part, :] = value.astype(pad.mid.dtype)

    scatter_sum(
        SIDE * lead,
        rows,
        lambda i, part: pad.mine[i // lead, i % lead, part, :],
        [lambda i, part: pad.other[i // lead, i % lead, part, :]],
        put,
    )
    yield from reduce_x(net, name, pad.mid, pad, out)


def program_back(net, held):
    core = net.core

    def attn():
        if core == 0:
            own = net.local((5, -1), held.g_attn, held.g_attn_both.at[0])
        hand(net, (5, 0), 1, held.g_attn, held.g_attn_both.at[1])
        yield
        if core == 0:
            own.wait()

    return [
        swap_cores(net, 3, held.mixed, held.mixed_both),
        swap_cores(net, 4, held.g_hidden, held.g_hidden_both),
        attn(),
        shrink(net, 1, held.g_gate, held.gate_pad, held.g_gate_sum),
        shrink(net, 2, held.g_down, held.down_pad, held.g_down_sum),
        gather_halves(net, 0, held.g_mamba, held.g_mamba_all, patience=1),
    ]


def three_sums(net, held):
    return [
        reduce_three(net, 10, held.one, held.one_pad, held.one_sum, (Y, Z, X)),
        reduce_three(net, 11, held.two, held.two_pad, held.two_sum, (X, Y, Z)),
        reduce_three(net, 12, held.three, held.three_pad, held.three_sum, (Z, X, Y)),
    ]


def program_attention(net, held):
    def last():
        for _ in range(4):
            yield
        begin = 0
        for part in (held.one_sum, held.two_sum, held.three_sum):
            held.sums[:, pl.ds(begin, part.shape[1])] = part[...]
            begin += part.shape[1]

    return [
        reduce_two(net, 0, held.keyval, held.keyval_pad, held.keyval_sum, (Z, Y)),
        *three_sums(net, held),
        swap_two(net, 3, held.gate, held.gate_mid, held.gate_own),
        last(),
    ]


def program_keys(net, held):
    return three_sums(net, held)


def program_end(net, held):
    core = net.core

    def normed():
        yield from reduce_halves(net, 0, held.partial, held.normed_pad, held.normed_sum)
        yield from swap_cores(net, 1, held.normed_sum, held.normed_both)

    def gains():
        yield from reduce_three(
            net, 2, held.gains, held.gains_pad, held.gains_sum, order_of(net) + (X,)
        )
        yield from swap_cores(net, 3, held.gains_sum, held.gains_both)

    def mamba():
        if core == 1:
            yield from reduce_x(net, 4, held.mamba, held.mamba_pad, held.mamba_part)
            yield from swap_two(net, 5, held.mamba_part, held.mamba_mid, held.mamba_sum)
        else:
            for _ in range(4):
                yield
        hand(net, (6, 0), 1, held.mamba_sum, held.mamba_sum)

    def channel(name, source, pad, total):
        if core == 1:
            yield from reduce_x(net, name, source, pad, total)
        else:
            for _ in range(2):
                yield
        hand(net, (name, 0), 1, total, total)

    return [
        normed(),
        mamba(),
        channel(7, held.back, held.back_pad, held.back_sum),
        channel(8, held.channel, held.channel_pad, held.channel_sum),
        gains(),
        keep_and_hand(net, 9, 0, held.g_attn, held.g_attn_both),
        keep_and_hand(net, 10, 0, held.sums_in, held.sums),
        keep_and_hand(net, 12, 0, held.keys, held.keys_sum),
        swap_cores(net, 13, held.gate, held.gate_both),
        swap_cores(net, 14, held.down, held.down_both),
    ]


def blocks_of(weight, splits):
    rows, columns = weight.shape
    cut = weight.reshape(rows, splits, 16, columns // splits // 16).transpose(1, 2, 0, 3)
    return pad_to(cut, 2, 32)


def rows_of(blocks, rows):
    width = blocks.shape[-1]
    return blocks.reshape(-1, blocks.shape[-2], width)[:, :rows].reshape(-1, width)


def padded_blocks(rows, count, size, kind=jnp.bfloat16):
    width = rows.shape[-1]
    return pad_to(rows.reshape(count, -1, width), 1, size).astype(kind)


def shards(
    tokens,
    seq_lengths,
    norm_gain,
    meta_tokens,
    w_query,
    w_key_value,
    w_attn_out,
    attn_gain,
    w_mamba_in,
    conv_weight,
    conv_bias,
    w_ssm_x,
    w_dt,
    dt_bias,
    a_log,
    skip_d,
    w_mamba_out,
    mamba_gain,
    ffn_gain,
    w_gate_up,
    w_down,
    cotangent,
):
    low = jnp.bfloat16
    full = jnp.float32
    core = lax.axis_index("branch")
    on_attention = core == 0
    tokens_b, cotangent_b = tokens[0], cotangent[0]
    rows, width = tokens_b.shape
    half = rows // 2
    group = rows * 16
    piece = w_query.shape[0]
    query_width = w_query.shape[1]
    keys_width = w_key_value.shape[1]
    inner_piece = w_mamba_out.shape[0]
    inner = inner_piece * SIDE
    rank = w_dt.shape[0]
    states = a_log.shape[0]
    proj = rank + 2 * states
    proj_pad = 136
    proj_cut = 72
    metas = meta_tokens.shape[0]
    down_piece = w_down.shape[0]
    units = down_piece * SIDE
    row_start = core * half

    lengths = seq_lengths[0]
    end_rows = jnp.cumsum(lengths)
    start_rows = end_rows - lengths
    all_rows = jnp.arange(group, dtype=jnp.int32)
    all_segments = segment_of(all_rows, end_rows)
    my_rows = lax.axis_index("seq") * rows + jnp.arange(rows, dtype=jnp.int32)
    keep_rows = jnp.logical_not(jnp.any(all_rows[:, None] == start_rows[None, :], axis=1))
    valid_rows = jnp.stack(
        [
            (
                (all_rows - back >= 0)
                & (segment_of(all_rows - back, end_rows) == all_segments)
            ).astype(jnp.float32)
            for back in range(1, CONV)
        ]
    )

    gains_in = jnp.stack([norm_gain, attn_gain, mamba_gain, ffn_gain], axis=1)
    small_in = jnp.concatenate([gains_in, meta_tokens.T], axis=1)
    small_in = pad_to(pad_to(small_in, 1, 256), 0, 32).astype(low)
    keys_in = w_key_value.reshape(piece, 2, -1, HEAD).transpose(0, 2, 1, 3).reshape(piece, -1)
    query_most = -(-query_width // LANES) * LANES
    attention_in = jnp.concatenate(
        [pad_to(w_query, 1, query_most).astype(low), keys_in.astype(low), w_attn_out.astype(low)], axis=1
    )
    attention_in = pad_to(attention_in, 0, 32)
    third = 10 * LANES
    last_third = attention_in.shape[1] - 2 * third
    mamba_in = blocks_of(w_mamba_in.astype(low), 2)
    mamba_in = jnp.concatenate([mamba_in[0], mamba_in[1]], axis=-1).reshape(SIDE, SIDE, 32, -1)
    back_in = pad_to(w_mamba_out, 0, 64).astype(low)
    channel_in = jnp.concatenate(
        [
            w_ssm_x,
            conv_weight.T,
            jnp.stack([conv_bias, dt_bias, skip_d], axis=1),
            a_log.T,
            w_dt.T,
        ],
        axis=1,
    )
    channel_in = pad_to(pad_to(channel_in, 0, 64), 1, 256).astype(low)
    gate_in = blocks_of(w_gate_up.astype(low), 2).reshape(2, SIDE, SIDE, 32, units)
    down_in = pad_to(w_down, 0, 96).astype(low)
    cube = (SIDE, SIDE, SIDE)

    begun = exchange(
        "exchange_start",
        0,
        program_start,
        dict(
            tokens=(tokens_b, ANY),
            small=(small_in, ANY),
            mamba=(mamba_in, ANY),
            back=(back_in, ANY),
            channel=(channel_in, ANY),
        ),
        dict(
            tokens_all=((2, SIDE, SIDE, half, width), low, ANY),
            small_all=(cube + small_in.shape, low, ANY),
            mamba_all=(cube + mamba_in.shape[2:], low, ANY),
            back_all=((SIDE,) + back_in.shape, low, ANY),
            channel_all=((SIDE,) + channel_in.shape, low, ANY),
        ),
        dict(mamba_mid=(mamba_in.shape, low)),
    )
    weights = exchange(
        "exchange_weights",
        1,
        program_weights,
        dict(whole=(attention_in, ANY)),
        dict(
            first=(cube + (32, third), low, ANY),
            second=(cube + (32, third), low, ANY),
            third=(cube + (32, last_third), low, ANY),
        ),
        cores=(0,),
    )
    weight_one, weight_two, weight_three = (
        part.reshape(64 * 32, -1) for part in (weights.first, weights.second, weights.third)
    )
    cotangent_part = lax.dynamic_slice_in_dim(cotangent_b, row_start, half, 0)
    cotangent_all = lax.all_gather(cotangent_part, "seq", axis=0, tiled=True)

    small = rows_of(begun.small_all, piece).astype(jnp.float32)
    gain_norm, gain_attn, gain_mamba, gain_feed = (small[:, i] for i in range(4))
    meta_f = small[:, 4 : 4 + metas].T
    channel = rows_of(begun.channel_all, inner_piece)
    weight_ssm = channel[:, :proj]
    conv_taps = channel[:, proj : proj + CONV].T.astype(jnp.float32)
    conv_offset, step_bias, skip_gain = (
        channel[:, proj + CONV + i].astype(jnp.float32) for i in range(3)
    )
    first_log = proj + CONV + 3
    log_decay = channel[:, first_log : first_log + states].T.astype(jnp.float32)
    weight_step = channel[:, first_log + states : first_log + states + rank]

    def on_core(which, work):
        shapes = jax.eval_shape(work)
        return lax.cond(core == which, work, lambda: blank(shapes))

    inputs_f = tokens_b.astype(jnp.float32)

    gain_row = gain_norm[None, :]
    normed_wide, query_b, keyval_b, meta_wide, meta_kv = on_core(
        0,
        lambda: attention_project(
            tokens_b, meta_f, gain_row, weight_one, weight_two, query_width, keys_width
        ),
    )
    keyval = exchange(
        "exchange_keyval",
        2,
        program_keyval,
        dict(keyval=(keyval_b, ANY), gate=(gate_in, ANY)),
        dict(
            keyval_all=((2, SIDE, SIDE, half, keys_width), low, ANY),
            gate_own=((SIDE, SIDE, 32, units), low, ANY),
        ),
        dict(gate_mid=((SIDE, SIDE, 32, units), low)),
        cores=(0,),
    )

    def mamba_first():
        normed_b = rms_norm(
            begun.tokens_all.reshape(group, width).astype(jnp.float32), gain_norm
        ).astype(low)
        weight_mamba = rows_of(begun.mamba_all.transpose(1, 2, 0, 3, 4), piece)
        mixed_in = places_first(matmul(normed_b, weight_mamba))
        conv_in = mixed_in[:, :inner].astype(low)
        inputs_b = conv_silu(
            conv_in.astype(jnp.float32), conv_taps, conv_offset, valid_rows
        ).astype(low)
        projected = contract(pad_to(weight_ssm, 1, proj_pad), inputs_b, 0, 1)
        projected = projected.reshape(proj_pad, SIDE, SIDE, rows).transpose(1, 2, 0, 3)
        return (
            normed_b,
            weight_mamba,
            conv_in,
            mixed_in[:, inner:],
            inputs_b,
            projected[:, :, :proj_cut],
            projected[:, :, proj_cut:],
        )

    normed_all, weight_mamba, conv_in, gate_z, inputs_b, proj_first, proj_second = on_core(
        1, mamba_first
    )

    def proj_pads(size):
        return dict(
            two_pad(size, rows, jnp.float32), sum=((size, rows), jnp.float32)
        )

    def spread_projection(name, number, first, second, gate):
        cuts = (proj_cut, proj_pad - proj_cut)
        results = exchange(
            name,
            number,
            program_project,
            dict(first=(first, ANY), second=(second, ANY), gate=(gate, ANY)),
            dict(
                first_all=((SIDE, SIDE, cuts[0], rows), jnp.float32, ANY),
                second_all=((SIDE, SIDE, cuts[1], rows), jnp.float32, ANY),
                gate_own=((SIDE, SIDE, 32, units), low, ANY),
            ),
            dict(
                first_pad=proj_pads(cuts[0]),
                second_pad=proj_pads(cuts[1]),
                gate_mid=((SIDE, SIDE, 32, units), low),
            ),
            vmem=32 * 2**20,
            cores=(1,),
        )
        return results

    def whole_projection(results):
        joined = jnp.concatenate([results.first_all, results.second_all], axis=2)
        return joined.transpose(2, 0, 1, 3).reshape(proj_pad, group)

    middle = spread_projection("exchange_project", 3, proj_first, proj_second, gate_in[1])
    keyval_all = keyval.keyval_all.reshape(2, 16, half, keys_width)

    my_starts = jnp.max(
        jnp.where(my_rows[:, None] >= start_rows[None, :], start_rows[None, :], 0), axis=1
    )
    bounds = jnp.stack([my_starts, my_rows], axis=1).astype(jnp.int32)
    key_blocks = (my_rows[-1:] // KEY_ROWS + 1).astype(jnp.int32)

    decay_rate = -jnp.exp(log_decay)
    scan_rate = pad_to(decay_rate * log2_e, 1, 2 * CHUNKS).T

    def blocked(lines):
        return jnp.stack([lines[:, :CHUNKS], pad_to(lines[:, CHUNKS:], 1, CHUNKS)])

    def unblocked(blocks):
        return jnp.concatenate([blocks[0], blocks[1][:, : inner - CHUNKS]], axis=1)

    attended, mass, attended_wide, attn_pre = on_core(
        0,
        lambda: attend_forward(
            key_blocks, query_b, keyval_all, meta_kv, bounds, weight_two, weight_three
        ),
    )

    def mamba_core():
        projected = whole_projection(middle)
        step_low = projected[:rank].astype(low)
        step_pre = contract(step_low, weight_step, 0, 1) + step_bias
        steps = jax.nn.softplus(step_pre)
        inputs_full = inputs_b.astype(jnp.float32)
        cols = projected[rank:proj].reshape(2 * states, CHUNKS, STEPS).transpose(0, 2, 1)
        scanned, starts, decay_t, drive_t = scan_forward(
            blocked(jnp.where(keep_rows[:, None], steps, far_away)),
            blocked(steps * inputs_full),
            cols,
            scan_rate,
            inner,
        )
        ssm_out = unblocked(scanned)
        mixed_y = halves_first(gate_mix(ssm_out, skip_gain, inputs_full, gate_z).astype(low))
        weight_back = rows_of(begun.back_all, inner_piece)
        return (
            matmul(mixed_y, weight_back).astype(low),
            step_low,
            step_pre,
            ssm_out,
            mixed_y,
            cols,
            starts,
            decay_t,
            drive_t,
        )

    partial, step_low, step_pre, ssm_out, mixed_y, cols, starts, decay_t, drive_t = on_core(
        1, mamba_core
    )

    mixers = exchange(
        "exchange_mixers",
        4,
        program_mixers,
        dict(
            partial=(partial.reshape(2, SIDE, SIDE, half, width), ANY),
            attn_pre=(attn_pre, ANY),
            gate_first=(keyval.gate_own, ANY),
            gate_second=(middle.gate_own, ANY),
            down=(down_in, ANY),
        ),
        dict(
            mamba_pre=((half, width), jnp.float32, VMEM),
            attn_half=((half, width), jnp.float32, ANY),
            gate_all=((2,) + cube + (32, units), low, ANY),
            down_all=((SIDE,) + down_in.shape, low, ANY),
        ),
        dict(pad=half_pad(half, width)),
        vmem=32 * 2**20,
    )
    weight_gate = mixers.gate_all.transpose(0, 2, 3, 1, 4, 5).reshape(2, 64, 32, units)
    weight_gate = weight_gate[:, :, :piece].reshape(2, width, units)
    weight_down = rows_of(mixers.down_all, down_piece)

    tokens_part = lax.dynamic_slice_in_dim(inputs_f, row_start, half, 0)
    sent = rms_norm(mixers.attn_half, gain_attn).astype(low).astype(jnp.float32)
    sent = sent + rms_norm(mixers.mamba_pre, gain_mamba).astype(low).astype(jnp.float32)
    hidden = tokens_part + 0.5 * sent
    feed = exchange(
        "exchange_feed",
        5,
        program_feed,
        dict(feed=(rms_norm(hidden, gain_feed).astype(low), ANY)),
        dict(feed_all=((SIDE, SIDE, half, width), low, ANY)),
    ).feed_all.reshape(16 * half, width)
    gate = matmul(feed, weight_gate[0])
    up = matmul(feed, weight_gate[1])
    active, pull_glu = jax.vjp(swiglu, gate, up)
    active_b = active.astype(low)
    out_partial = matmul(active_b, weight_down).astype(low)
    grad_gate, grad_up = pull_glu(matmul_nt(cotangent_all, weight_down))
    grad_gate, grad_up = grad_gate.astype(low), grad_up.astype(low)
    feed_partial = (matmul_nt(grad_gate, weight_gate[0]) + matmul_nt(grad_up, weight_gate[1])).astype(
        low
    )
    grad_down = matmul_tn(active_b, cotangent_all)
    grad_weight_gate = (matmul_tn(feed, grad_gate), matmul_tn(feed, grad_up))
    ffn = exchange(
        "exchange_ffn",
        6,
        program_ffn,
        dict(
            out=(out_partial.reshape(SIDE, SIDE, half, width), ANY),
            grad=(feed_partial.reshape(SIDE, SIDE, half, width), ANY),
        ),
        dict(
            out_sum=((half, width), jnp.float32, VMEM),
            grad_sum=((half, width), jnp.float32, VMEM),
        ),
        dict(out_pad=two_pad(half, width), grad_pad=two_pad(half, width)),
        vmem=48 * 2**20,
    )
    mixed_part = (hidden + ffn.out_sum).astype(low)
    cotangent_f = cotangent_part.astype(jnp.float32)
    _, pull_feed = jax.vjp(rms_norm, hidden, gain_feed)
    grad_hidden_norm, grad_gain_feed = pull_feed(ffn.grad_sum)
    grad_hidden = cotangent_f + grad_hidden_norm
    grad_sent = 0.5 * grad_hidden
    _, pull_attn = jax.vjp(rms_norm, mixers.attn_half, gain_attn)
    grad_attn_pre, grad_gain_attn = pull_attn(grad_sent)
    _, pull_mamba = jax.vjp(rms_norm, mixers.mamba_pre, gain_mamba)
    grad_mamba_pre, grad_gain_mamba = pull_mamba(grad_sent)

    g_gate = jnp.stack(grad_weight_gate).reshape(2, 16, SIDE, piece, units)
    g_gate = pad_to(g_gate.transpose(0, 2, 1, 3, 4), 3, 32).astype(low)
    g_down = pad_to(grad_down.reshape(SIDE, down_piece, width), 1, 96)
    g_down = g_down.reshape(SIDE, 2, 1, 48, width).transpose(1, 0, 2, 3, 4).astype(low)
    back = exchange(
        "exchange_back",
        7,
        program_back,
        dict(
            g_mamba=(grad_mamba_pre.astype(low), ANY),
            g_attn=(grad_attn_pre.astype(low), ANY),
            mixed=(mixed_part, ANY),
            g_hidden=(grad_hidden, ANY),
            g_gate=(g_gate, ANY),
            g_down=(g_down, ANY),
        ),
        dict(
            g_mamba_all=((2, SIDE, SIDE, half, width), low, ANY),
            g_attn_both=((2, half, width), low, ANY),
            mixed_both=((2, half, width), low, ANY),
            g_hidden_both=((2, half, width), jnp.float32, ANY),
            g_gate_sum=((16, 32, units), low, VMEM),
            g_down_sum=((1, 48, width), jnp.float32, VMEM),
        ),
        dict(gate_pad=shrink_pad(16, 32, units), down_pad=shrink_pad(1, 48, width)),
        vmem=32 * 2**20,
    )
    mixed = back.mixed_both.reshape(rows, width)
    grad_hidden_all = back.g_hidden_both.reshape(rows, width)
    g_gate_own = back.g_gate_sum.reshape(SIDE, SIDE, 32, units)

    cuts = (8 * LANES, 9 * LANES, query_most + width - 17 * LANES)

    def attention_back_one():
        g_pre = back.g_attn_both.reshape(rows, width)
        g_query, g_keyval, g_meta = attend_backward(
            key_blocks,
            query_b,
            keyval_all,
            meta_kv,
            bounds,
            attended,
            mass,
            g_pre,
            weight_two,
            weight_three,
        )
        pieces = attention_weights(
            normed_wide, attended_wide, g_query, g_pre, weight_one, weight_two, cuts
        )
        return [g_query, g_keyval, g_meta] + list(pieces)

    grad_query_b, grad_keyval, grad_meta_kv, sum_one, sum_two, sum_three, gain_query = on_core(
        0, attention_back_one
    )

    def cubed(blocks):
        return blocks.reshape(cube + (32, blocks.shape[-1]))

    attention = exchange(
        "exchange_attention",
        8,
        program_attention,
        dict(
            keyval=(grad_keyval.reshape(SIDE, SIDE, rows, keys_width), ANY),
            one=(cubed(sum_one), ANY),
            two=(cubed(sum_two), ANY),
            three=(cubed(sum_three), ANY),
            gate=(g_gate_own, ANY),
        ),
        dict(
            keyval_sum=((rows, keys_width), full, VMEM),
            sums=((32, query_most + width), full, VMEM),
            gate_own=((SIDE, SIDE, 32, units), low, ANY),
        ),
        dict(
            keyval_pad=two_pad(rows, keys_width),
            one_pad=three_pad(32, cuts[0]),
            two_pad=three_pad(32, cuts[1]),
            three_pad=three_pad(32, cuts[2]),
            one_sum=((32, cuts[0]), full),
            two_sum=((32, cuts[1]), full),
            three_sum=((32, cuts[2]), full),
            gate_mid=((SIDE, SIDE, 32, units), low),
        ),
        vmem=60 * 2**20,
        cores=(0,),
    )

    keys_one, keys_two, meta_out, grad_normed_attn, gain_keys, gain_meta = on_core(
        0,
        lambda: attention_inputs(
            attention.keyval_sum,
            grad_query_b,
            normed_wide,
            meta_wide,
            grad_meta_kv,
            weight_one,
            weight_two,
            meta_f,
            gain_row,
        ),
    )
    gain_attention = (gain_query + gain_keys).reshape(64, 32)[:, :piece].reshape(width)
    gain_attention = gain_attention / gain_norm + gain_meta[0]
    keys = exchange(
        "exchange_keys",
        9,
        program_keys,
        dict(
            one=(cubed(keys_one), ANY),
            two=(cubed(keys_two), ANY),
            three=(cubed(meta_out), ANY),
        ),
        dict(
            one_sum=((32, keys_width // 2), full, VMEM),
            two_sum=((32, keys_width // 2), full, VMEM),
            three_sum=((32, metas), full, VMEM),
        ),
        dict(
            one_pad=three_pad(32, keys_width // 2),
            two_pad=three_pad(32, keys_width // 2),
            three_pad=three_pad(32, metas),
        ),
        vmem=32 * 2**20,
        cores=(0,),
    )

    def mamba_back_one():
        grad_pre_b = back.g_mamba_all.reshape(group, width)
        grad_weight_back = matmul_tn(mixed_y, grad_pre_b)
        weight_back = rows_of(begun.back_all, inner_piece)
        grad_mixed = places_first(matmul_nt(grad_pre_b, weight_back))
        inputs_full = inputs_b.astype(jnp.float32)
        _, pull_gate = jax.vjp(gate_mix, ssm_out, skip_gain, inputs_full, gate_z)
        grad_ssm, grad_skip, grad_inputs, grad_gate_z = pull_gate(grad_mixed)
        steps = jax.nn.softplus(step_pre)
        grad_decay, grad_drive, grad_cols, grad_rate = scan_backward(
            decay_t, drive_t, cols, scan_rate, starts, blocked(grad_ssm), inner
        )
        grad_drive = unblocked(grad_drive)
        grad_steps = unblocked(grad_decay) * (1.0 / log2_e) + grad_drive * inputs_full
        grad_inputs = grad_inputs + grad_drive * steps
        grad_step_pre = grad_steps * jax.nn.sigmoid(step_pre)
        grad_step_b = grad_step_pre.astype(low)
        grad_step_low = contract(weight_step, grad_step_b, 0, 1)
        grad_cols = grad_cols.transpose(0, 2, 1).reshape(2 * states, group)
        grad_proj = pad_to(jnp.concatenate([grad_step_low, grad_cols], axis=0), 0, proj_pad)
        grad_proj = grad_proj.reshape(proj_pad, SIDE, SIDE, rows).transpose(1, 2, 0, 3)
        return (
            grad_proj[:, :, :proj_cut],
            grad_proj[:, :, proj_cut:],
            padded_blocks(grad_weight_back, SIDE, 64)[:, None],
            grad_inputs,
            grad_gate_z.astype(low),
            grad_skip,
            jnp.sum(grad_step_pre, axis=0),
            grad_rate[:inner] * decay_rate.T,
            contract(grad_step_b, step_low, 0, 1),
        )

    (
        proj_first,
        proj_second,
        back_out,
        grad_inputs,
        grad_gate_z,
        grad_skip,
        grad_step_bias,
        grad_log_decay,
        grad_weight_step,
    ) = on_core(1, mamba_back_one)
    last = spread_projection("exchange_last", 10, proj_first, proj_second, g_gate_own)

    def mamba_back_two():
        grad_proj_b = whole_projection(last)[:proj].astype(low)
        grad_weight_ssm = contract(inputs_b, grad_proj_b, 0, 1)
        grad_inputs_all = grad_inputs + contract(grad_proj_b, weight_ssm, 0, 1)

        def conv_only(conv_arg, taps_arg, offset_arg):
            return conv_silu(conv_arg, taps_arg, offset_arg, valid_rows)

        _, pull_conv = jax.vjp(conv_only, conv_in.astype(full), conv_taps, conv_offset)
        grad_conv, grad_taps, grad_offset = pull_conv(grad_inputs_all)
        grad_mixed_in = halves_first(jnp.concatenate([grad_conv.astype(low), grad_gate_z], axis=1))
        grad_weight_mamba = matmul_tn(normed_all, grad_mixed_in)
        grad_normed = matmul_nt(grad_mixed_in, weight_mamba).astype(low)
        channel_out = jnp.concatenate(
            [
                grad_weight_ssm,
                grad_taps.T,
                jnp.stack([grad_offset, grad_step_bias, grad_skip], axis=1),
                grad_log_decay,
                grad_weight_step,
            ],
            axis=1,
        )
        mamba_out = grad_weight_mamba.reshape(16, SIDE, piece, 2 * inner).transpose(1, 0, 2, 3)
        return (
            grad_normed,
            pad_to(mamba_out, 2, 32).astype(low),
            pad_to(padded_blocks(channel_out, SIDE, 64, full), 2, 256)[:, None],
            jnp.sum(grad_weight_mamba * weight_mamba.astype(full), axis=1) / gain_norm,
        )

    grad_normed_partial, mamba_out, channel_out, gain_mixer = on_core(1, mamba_back_two)
    grad_gain_norm = jnp.where(on_attention, gain_attention, gain_mixer)
    gains_out = jnp.stack([grad_gain_norm, grad_gain_attn, grad_gain_mamba, grad_gain_feed], axis=1)
    gains_out = padded_blocks(pad_to(gains_out, 1, 128), 64, 32)
    ended = exchange(
        "exchange_end",
        11,
        program_end,
        dict(
            partial=(grad_normed_partial.reshape(2, SIDE, SIDE, half, width), ANY),
            g_attn=(grad_normed_attn, ANY),
            sums_in=(attention.sums, ANY),
            keys=(jnp.concatenate([keys.one_sum, keys.two_sum, keys.three_sum], axis=1), ANY),
            gate=(jnp.where(on_attention, attention.gate_own, last.gate_own), ANY),
            down=(back.g_down_sum.reshape(48, width), ANY),
            mamba=(mamba_out, ANY),
            back=(back_out, ANY),
            channel=(channel_out, ANY),
            gains=(gains_out.reshape(cube + (32, 128)), ANY),
        ),
        dict(
            normed_both=((2, half, width), full, ANY),
            g_attn_both=((rows, width), full, ANY),
            sums=((32, query_most + width), full, ANY),
            keys_sum=((32, keys_width + metas), full, ANY),
            gate_both=((2, SIDE, SIDE, 32, units), low, ANY),
            down_both=((2, 48, width), full, ANY),
            mamba_sum=((SIDE, SIDE, 32, 2 * inner), low, ANY),
            back_sum=((1, 64, width), full, VMEM),
            channel_sum=((1, 64, 256), full, VMEM),
            gains_both=((2, 32, 128), full, ANY),
        ),
        dict(
            normed_pad=half_pad(half, width),
            normed_sum=((half, width), full),
            gains_pad=three_pad(32, 128),
            gains_sum=((32, 128), full),
            mamba_pad=x_pad(16, 32, 2 * inner),
            mamba_part=((SIDE, SIDE, 32, 2 * inner), low),
            mamba_mid=((SIDE, SIDE, 32, 2 * inner), low),
            back_pad=x_pad(1, 64, width),
            channel_pad=x_pad(1, 64, 256, full),
        ),
        vmem=48 * 2**20,
    )
    grad_normed = ended.normed_both.reshape(rows, width) + ended.g_attn_both
    _, pull_input = jax.vjp(lambda rows_in: rms_norm(rows_in, gain_norm), inputs_f)
    input_grad = grad_hidden_all + pull_input(grad_normed)[0]
    gains_sum = (ended.gains_both[0] + ended.gains_both[1])[:piece]
    keys_sum = ended.keys_sum[:piece]
    grad_keys = keys_sum[:, :keys_width].reshape(piece, -1, 2, HEAD).transpose(0, 2, 1, 3)
    grad_keys = grad_keys.reshape(piece, keys_width)
    grad_mamba_in = ended.mamba_sum.reshape(16, 32, 2, inner)[:, :piece]
    grad_mamba_in = grad_mamba_in.transpose(1, 2, 0, 3).reshape(piece, 2 * 16 * inner)
    grad_gate_up = ended.gate_both.reshape(2, 16, 32, units)[:, :, :piece]
    grad_gate_up = grad_gate_up.transpose(2, 0, 1, 3).reshape(piece, 2 * 16 * units)
    channel_sum = ended.channel_sum[0, :inner_piece]
    return (
        mixed[None],
        input_grad[None],
        gains_sum[:, 0],
        keys_sum[:, keys_width:].T,
        ended.sums[:piece, :query_width],
        grad_keys,
        ended.sums[:piece, query_most:],
        gains_sum[:, 1],
        grad_mamba_in.astype(full),
        channel_sum[:, proj : proj + CONV].T,
        channel_sum[:, proj + CONV],
        channel_sum[:, :proj],
        channel_sum[:, first_log + states : first_log + states + rank].T,
        channel_sum[:, proj + CONV + 1],
        channel_sum[:, first_log : first_log + states].T,
        channel_sum[:, proj + CONV + 2],
        ended.back_sum[0, :inner_piece],
        gains_sum[:, 2],
        gains_sum[:, 3],
        grad_gate_up.astype(full),
        ended.down_both.reshape(96, width)[:down_piece],
    )


def solution(mesh):
    spread = ("seq", "fsdp")
    rows = P("fsdp", "seq", None)
    flat, first, second = P(spread), P(spread, None), P(None, spread)
    weights = (
        flat,
        second,
        first,
        first,
        first,
        flat,
        first,
        second,
        flat,
        first,
        second,
        flat,
        second,
        flat,
        first,
        flat,
        flat,
        first,
        first,
    )
    return jax.shard_map(
        shards,
        mesh=mesh,
        in_specs=(rows, P("fsdp", None)) + weights + (rows,),
        out_specs=(rows, rows) + weights,
        check_vma=False,
    )
```

```python
import functools
import types

import jax
import jax.numpy as jnp
from jax import lax
from jax.experimental import pallas as pl
from jax.experimental.pallas import tpu as pltpu
from jax.sharding import PartitionSpec as P

HEAD = 64
CONV = 4
SIDE = 4

epsilon = 1e-05
negative_fill = -1e30
score_scale = 0.125
log2_e = 1.4426950408889634
highest = lax.Precision.HIGHEST
MESH = pl.DeviceIdType.MESH
ANY = pl.BlockSpec(memory_space=pl.ANY)
VMEM = pl.BlockSpec(memory_space=pltpu.VMEM)
SEMS = 128
HOPS = (1, 3, 2)
X, Y, Z = range(3)


class Net:
    def __init__(self, core, coords, names, send, recv):
        self.core = core
        self.at = coords
        self.names = names
        self.send = send
        self.recv = recv
        self.begun = []

    def device(self, axis=None, hop=0, other_core=False):
        place = dict(self.at)
        if axis is not None:
            place[axis] = (place[axis] + hop) % SIDE
        core = 1 - self.core if other_core else self.core
        return (core, place[Y] * SIDE + place[Z], place[X])

    def slot(self, name):
        return self.names.setdefault(name, len(self.names))

    def copy(self, name, source, target, device):
        i = self.slot(name)
        return pltpu.make_async_remote_copy(
            source,
            target,
            self.send.at[i],
            self.recv.at[i],
            device_id=device,
            device_id_type=MESH,
        )

    def start(self, name, source, target, device):
        copy = self.copy(name, source, target, device)
        copy.start()
        self.begun.append(copy)
        return copy

    def local(self, name, source, target):
        copy = pltpu.make_async_copy(source, target, self.send.at[self.slot(name)])
        copy.start()
        return copy


def pick(axes, fixed):
    return tuple(fixed.get(axis, slice(None)) for axis in axes)


def gather(net, name, source, out, axes, order, hold=0):
    at = net.at
    fixed = {axis: at[axis] for axis in axes}
    own = net.local((name, -1), source, out.at[pick(axes, fixed)])
    here = source
    for axis in order:
        if axis == order[-1]:
            for _ in range(hold):
                yield
        place = pick(axes, fixed)
        copies = [
            net.start(
                (name, axis, hop),
                out.at[place] if here is None else here,
                out.at[place],
                net.device(axis, hop),
            )
            for hop in HOPS
        ]
        yield
        for copy in copies:
            copy.wait_recv()
        if here is not None:
            own.wait()
        here = None
        del fixed[axis]


def gather_two(net, name, source, out, order, after=None, patience=0):
    at = net.at
    first, second = order

    def place(back):
        spot = dict(at)
        spot[first] = (spot[first] - back + SIDE) % SIDE
        return (spot[Y], spot[Z])

    mine = place(0)
    own = net.local((name, -1), source, out.at[mine])
    ones = [
        net.start((name, 1, hop), source, out.at[mine], net.device(first, hop)) for hop in HOPS
    ]
    twos = []

    def forward(back):
        spot = place(back)
        for hop in HOPS:
            twos.append(
                net.start(
                    (name, 2, back, hop),
                    source if back == 0 else out.at[spot],
                    out.at[spot],
                    net.device(second, hop),
                )
            )

    forward(0)
    yield
    for copy, hop in zip(ones, HOPS):
        copy.wait_recv()
        forward(hop)
    own.wait()
    for _ in range(1 + patience):
        yield
    if after is None:
        for copy in twos:
            copy.wait_recv()
        return
    lines = [twos[3 * i : 3 * i + 3] for i in range(SIDE)]
    after(at[second])
    for h, hop in enumerate(HOPS):
        for line in lines:
            line[h].wait_recv()
        after((at[second] - hop + SIDE) % SIDE)


NEAR = (1, 3)


def scatter_sum(total, rows, own, others, out):
    chunk = 16 if rows % 16 == 0 else 8
    per = rows // chunk

    def step(i, carry):
        lead = i // per
        part = pl.ds(pl.multiple_of((i % per) * chunk, chunk), chunk)
        value = own(lead, part).astype(jnp.float32)
        for other in others:
            value = value + other(lead, part).astype(jnp.float32)
        out(lead, part, value)
        return carry

    lax.fori_loop(0, total * per, step, 0)


def reduce_two(net, name, source, pad, out, order):
    at = net.at
    first, second = order
    one, mid, two, kept = pad.one, pad.mid, pad.two, pad.own
    rows = source.shape[2]

    def part_of(line):
        return source.at[:, line] if first == Z else source.at[line]

    own = net.local((name, -4), part_of(at[first]), kept)
    ones = [
        net.start(
            (name, 1, hop),
            part_of((at[first] + hop) % SIDE),
            one.at[hop - 1],
            net.device(first, hop),
        )
        for hop in HOPS
    ]
    yield
    own.wait()
    for copy in ones:
        copy.wait_recv()

    def put_mid(lead, part, value):
        mid[lead, part, :] = value.astype(mid.dtype)

    scatter_sum(
        SIDE,
        rows,
        lambda lead, part: kept[lead, part, :],
        [lambda lead, part, k=k: one[k, lead, part, :] for k in range(3)],
        put_mid,
    )
    twos = [
        net.start(
            (name, 2, hop),
            mid.at[(at[second] + hop) % SIDE],
            two.at[hop - 1],
            net.device(second, hop),
        )
        for hop in HOPS
    ]
    yield
    for copy in twos:
        copy.wait_recv()
    spot = at[second]

    def put_out(lead, part, value):
        out[part, :] = value.astype(out.dtype)

    scatter_sum(
        1,
        rows,
        lambda lead, part: kept[spot, part, :],
        [lambda lead, part, k=k: one[k, spot, part, :] for k in range(3)]
        + [lambda lead, part, k=k: two[k, part, :] for k in range(3)],
        put_out,
    )


def reduce_ring(net, name, source, pad, out, order):
    at = net.at
    rows = source.shape[2]
    half = rows // 2
    halves = {1: pl.ds(0, half), 3: pl.ds(half, half)}
    stages = (
        (order[0], pad.one, pad.via_one, pad.mix_one),
        (order[1], pad.two, pad.via_two, pad.mix_two),
    )

    def lines(stage, place, part):
        if stage == 1:
            return pad.mid.at[place, part]
        if order[0] == Z:
            return source.at[:, place, part]
        return source.at[place, :, part]

    whole = pl.ds(0, rows)
    own = net.local((name, -4), lines(0, at[order[0]], whole), pad.own)
    for stage, (axis, recv, via, mix) in enumerate(stages):

        def spot(hop, axis=axis):
            return (at[axis] + hop) % SIDE

        arrivals, fetched, passing = [], [], []
        for i, hop in enumerate(NEAR):
            device = net.device(axis, hop)
            across = lines(stage, spot(2), halves[hop])
            passing.append(net.start((name, stage, 0, hop), across, via.at[i], device))
            fetched.append(
                net.local((name, stage, 3, hop), lines(stage, spot(hop), halves[hop]), mix.at[i])
            )
        for i, hop in enumerate(NEAR):
            other = halves[4 - hop]
            target = recv.at[i, other] if stage else recv.at[i, :, other]
            arrivals.append(
                net.start(
                    (name, stage, 1, hop),
                    lines(stage, spot(hop), other),
                    target,
                    net.device(axis, hop),
                )
            )
        yield
        for i, hop in enumerate(NEAR):
            fetched[i].wait()
            passing[i].wait_recv()

            def put(lead, part, value, i=i, mix=mix, stage=stage):
                index = (i, part) if stage else (i, lead, part)
                mix[index + (slice(None),)] = value.astype(mix.dtype)

            def get(ref, i=i, stage=stage):
                if stage:
                    return lambda lead, part: ref[i, part, :]
                return lambda lead, part: ref[i, lead, part, :]

            scatter_sum(1 if stage else SIDE, half, get(mix), [get(via)], put)
            target = recv.at[i, halves[hop]] if stage else recv.at[i, :, halves[hop]]
            arrivals.append(
                net.start((name, stage, 2, hop), mix.at[i], target, net.device(axis, hop))
            )
        yield
        for copy in arrivals:
            copy.wait_recv()
        if stage == 0:
            own.wait()

            def put_mid(lead, part, value):
                pad.mid[lead, part, :] = value.astype(pad.mid.dtype)

            scatter_sum(
                SIDE,
                rows,
                lambda lead, part: pad.own[lead, part, :],
                [lambda lead, part, k=k: pad.one[k, lead, part, :] for k in range(2)],
                put_mid,
            )
    mine = at[order[1]]

    def put_out(lead, part, value):
        out[part, :] = value.astype(out.dtype)

    scatter_sum(
        1,
        rows,
        lambda lead, part: pad.own[mine, part, :],
        [lambda lead, part, k=k: pad.one[k, mine, part, :] for k in range(2)]
        + [lambda lead, part, k=k: pad.two[k, part, :] for k in range(2)],
        put_out,
    )


def swap_two(net, name, source, mid, out):
    at = net.at
    own = net.local((name, -1), source.at[:, at[Z]], mid.at[at[Z]])
    ones = [
        net.start(
            (name, 1, hop),
            source.at[:, (at[Z] + hop) % SIDE],
            mid.at[at[Z]],
            net.device(Z, hop),
        )
        for hop in HOPS
    ]
    yield
    for copy in ones:
        copy.wait_recv()
    own.wait()
    own = net.local((name, -2), mid.at[:, at[Y]], out.at[at[Y]])
    twos = [
        net.start(
            (name, 2, hop),
            mid.at[:, (at[Y] + hop) % SIDE],
            out.at[at[Y]],
            net.device(Y, hop),
        )
        for hop in HOPS
    ]
    yield
    for copy in twos:
        copy.wait_recv()
    own.wait()


def run_jobs(jobs):
    jobs = list(jobs)
    while jobs:
        jobs = [job for job in jobs if next(job, True) is None]


def flat(group):
    return [
        leaf
        for value in group.values()
        for leaf in (flat(value) if isinstance(value, dict) else [value])
    ]


def named(group, leaves):
    return types.SimpleNamespace(
        **{
            key: named(value, leaves) if isinstance(value, dict) else next(leaves)
            for key, value in group.items()
        }
    )


def exchange(name, number, program, inputs, outputs, scratch=None, vmem=None, cores=(0, 1)):
    scratch = scratch or {}
    parts = (inputs, outputs, scratch)
    counts = [len(flat(part)) for part in parts]

    def kernel(*refs):
        held = types.SimpleNamespace()
        begin = 0
        for part, count in zip(parts, counts):
            vars(held).update(vars(named(part, iter(refs[begin : begin + count]))))
            begin += count
        send, recv = refs[begin:]
        core = lax.axis_index("branch")
        seq = lax.axis_index("seq")
        coords = {X: lax.axis_index("fsdp"), Y: seq // SIDE, Z: seq % SIDE}
        names = {}
        for one_core in cores:

            @pl.when(core == one_core)
            def _():
                net = Net(one_core, coords, names, send, recv)
                barrier = pltpu.get_barrier_semaphore()
                peers = [net.device(axis, hop) for axis in (X, Y, Z) for hop in HOPS]
                if len(cores) == 2:
                    peers.append(net.device(other_core=True))
                for peer in peers:
                    pl.semaphore_signal(barrier, inc=1, device_id=peer, device_id_type=MESH)
                pl.semaphore_wait(barrier, len(peers))
                run_jobs(program(net, held))
                for copy in net.begun:
                    copy.wait_send()

        assert len(names) <= SEMS

    results = pl.pallas_call(
        kernel,
        out_shape=[jax.ShapeDtypeStruct(s, d) for s, d, _ in flat(outputs)],
        in_specs=[spec for _, spec in flat(inputs)],
        out_specs=[spec for _, _, spec in flat(outputs)],
        scratch_shapes=[pltpu.VMEM(s, d) for s, d in flat(scratch)]
        + [pltpu.SemaphoreType.DMA((SEMS,)), pltpu.SemaphoreType.DMA((SEMS,))],
        compiler_params=pltpu.CompilerParams(
            collective_id=number, has_side_effects=True, vmem_limit_bytes=vmem
        ),
        name=name,
    )(*[array for array, _ in flat(inputs)])
    return named(outputs, iter(results))


CHUNKS = 128
STEPS = 16
LINES = 8
WIDE = 40
far_away = 1e30


def to_lanes(source, target):
    for block in range(source.shape[0]):
        part = pl.ds(block * CHUNKS, CHUNKS)

        def move(l, carry):
            target[l, part, :] = source[block, pl.ds(l, CHUNKS, stride=STEPS), :].T
            return carry

        lax.fori_loop(0, STEPS, move, 0, unroll=2)


def to_rows(source, target):
    for block in range(target.shape[0]):
        part = pl.ds(block * CHUNKS, CHUNKS)

        def move(l, carry):
            target[block, pl.ds(l, CHUNKS, stride=STEPS), :] = source[l, part, :].T
            return carry

        lax.fori_loop(0, STEPS, move, 0, unroll=2)


def chunk_starts(ends, span, rates, reverse):
    lanes = lax.broadcasted_iota(jnp.int32, span.shape, 1)
    by = 1
    while by < CHUNKS:
        turn = CHUNKS - by if reverse else by
        inside = lanes < turn if reverse else lanes >= turn
        reach = jnp.where(inside, span, far_away)
        ends = [
            end + jnp.exp2(reach * rate) * pltpu.roll(end, turn, 1)
            for end, rate in zip(ends, rates)
        ]
        span = span + jnp.where(inside, pltpu.roll(span, turn, 1), 0.0)
        by *= 2
    turn = CHUNKS - 1 if reverse else 1
    inside = lanes < turn if reverse else lanes >= turn
    return [jnp.where(inside, pltpu.roll(end, turn, 1), 0.0) for end in ends]


def rate_lines(rate_ref, lines, states):
    tile = rate_ref[lines, :]
    return [jnp.broadcast_to(tile[:, s : s + 1], (lines.size, CHUNKS)) for s in range(states)]


def join_chunks(used, ends_ref, decay_t, rate_ref, reverse):
    states = rate_ref.shape[1]

    def channels(g, carry):
        lines = pl.ds(pl.multiple_of(g * WIDE, LINES), WIDE)
        span = decay_t[0, lines, :]
        for l in range(1, STEPS):
            span = span + decay_t[l, lines, :]
        starts = chunk_starts(
            [ends_ref[s, lines, :] for s in range(states)],
            span,
            rate_lines(rate_ref, lines, states),
            reverse,
        )
        for s in range(states):
            ends_ref[s, lines, :] = starts[s]
        return carry

    lax.fori_loop(0, used // WIDE, channels, 0)


def scan_forward_body(
    used, decay_ref, drive_ref, cols_ref, rate_ref, out_ref, start_ref, decay_t, drive_t, out_t
):
    states = rate_ref.shape[1]
    to_lanes(decay_ref, decay_t)
    to_lanes(drive_ref, drive_t)
    out_t[...] = jnp.zeros_like(out_t)

    def ends(g, carry):
        lines = pl.ds(pl.multiple_of(g * LINES, LINES), LINES)
        decays = [decay_t[l, lines, :] for l in range(STEPS)]
        drives = [drive_t[l, lines, :] for l in range(STEPS)]
        rates = rate_lines(rate_ref, lines, states)
        for s in range(states):
            state = drives[0] * cols_ref[s, 0:1, :]
            for l in range(1, STEPS):
                state = jnp.exp2(decays[l] * rates[s]) * state + drives[l] * cols_ref[s, l : l + 1, :]
            start_ref[s, lines, :] = state
        return carry

    lax.fori_loop(0, used // LINES, ends, 0)
    join_chunks(used, start_ref, decay_t, rate_ref, False)

    def channels(g, carry):
        lines = pl.ds(pl.multiple_of(g * LINES, LINES), LINES)
        decays = [decay_t[l, lines, :] for l in range(STEPS)]
        drives = [drive_t[l, lines, :] for l in range(STEPS)]
        rates = rate_lines(rate_ref, lines, states)
        outs = [jnp.zeros((LINES, CHUNKS), jnp.float32)] * STEPS
        for s in range(states):
            state = start_ref[s, lines, :]
            for l in range(STEPS):
                state = jnp.exp2(decays[l] * rates[s]) * state + drives[l] * cols_ref[s, l : l + 1, :]
                outs[l] = outs[l] + state * cols_ref[states + s, l : l + 1, :]
        for l in range(STEPS):
            out_t[l, lines, :] = outs[l]
        return carry

    lax.fori_loop(0, used // LINES, channels, 0)
    to_rows(out_t, out_ref)


def scan_backward_body(
    used,
    decay_t,
    drive_t,
    cols_ref,
    rate_ref,
    start_ref,
    grad_ref,
    g_decay_ref,
    g_drive_ref,
    g_cols_ref,
    g_rate_ref,
    grad_t,
    g_decay_t,
    g_drive_t,
    sums_t,
    ends_t,
):
    states = rate_ref.shape[1]
    blank = jnp.zeros((LINES, CHUNKS), jnp.float32)
    to_lanes(grad_ref, grad_t)
    g_decay_t[...] = jnp.zeros_like(g_decay_t)
    g_drive_t[...] = jnp.zeros_like(g_drive_t)
    sums_t[...] = jnp.zeros_like(sums_t)
    g_rate_ref[...] = jnp.zeros_like(g_rate_ref)
    marks = lax.broadcasted_iota(jnp.int32, (LINES, states), 1)

    def ends(g, carry):
        lines = pl.ds(pl.multiple_of(g * LINES, LINES), LINES)
        rates = rate_lines(rate_ref, lines, states)
        decays = [decay_t[l, lines, :] for l in range(STEPS)]
        grads = [grad_t[l, lines, :] for l in range(STEPS)]
        for s in range(states):
            back = blank
            for l in reversed(range(STEPS)):
                back = jnp.exp2(decays[l] * rates[s]) * (
                    grads[l] * cols_ref[states + s, l : l + 1, :] + back
                )
            ends_t[s, lines, :] = back
        return carry

    lax.fori_loop(0, used // LINES, ends, 0)
    join_chunks(used, ends_t, decay_t, rate_ref, True)

    def channels(g, carry):
        lines = pl.ds(pl.multiple_of(g * LINES, LINES), LINES)
        tile = rate_ref[lines, :]

        def state_step(s, g_rate):
            rate = jnp.sum(jnp.where(marks == s, tile, 0.0), axis=1, keepdims=True)
            rate = jnp.broadcast_to(rate, (LINES, CHUNKS))
            state = start_ref[s, lines, :]
            befores, factors = [], []
            for l in range(STEPS):
                factor = jnp.exp2(decay_t[l, lines, :] * rate)
                befores.append(state)
                factors.append(factor)
                state = factor * state + drive_t[l, lines, :] * cols_ref[s, pl.ds(l, 1), :]
            back = ends_t[s, lines, :]
            total_rate = blank
            for l in reversed(range(STEPS)):
                grad = grad_t[l, lines, :]
                total = grad * cols_ref[states + s, pl.ds(l, 1), :] + back
                sums_t[s, l] += total * drive_t[l, lines, :]
                sums_t[states + s, l] += grad * state
                g_drive_t[l, lines, :] += total * cols_ref[s, pl.ds(l, 1), :]
                back = total * factors[l]
                moved = back * befores[l]
                g_decay_t[l, lines, :] += moved * rate
                total_rate = total_rate + moved * decay_t[l, lines, :]
                state = befores[l]
            total_rate = jnp.sum(total_rate, axis=1, keepdims=True)
            return jnp.where(marks == s, total_rate, g_rate)

        g_rate_ref[lines, :] = lax.fori_loop(
            0, states, state_step, jnp.zeros((LINES, states), jnp.float32), unroll=16
        )
        return carry

    lax.fori_loop(0, used // LINES, channels, 0)

    def collapse(i, carry):
        g_cols_ref[i] = jnp.sum(sums_t[i], axis=1)
        return carry

    lax.fori_loop(0, 2 * states, collapse, 0)
    to_rows(g_decay_t, g_decay_ref)
    to_rows(g_drive_t, g_drive_ref)


KEY_ROWS = 256
PIECE = 25
PADDED = 32
LANES = 128


def dot_on(left, right, left_dim, right_dim, **options):
    return lax.dot_general(
        left,
        right,
        (((left_dim,), (right_dim,)), ((), ())),
        preferred_element_type=jnp.float32,
        **options,
    )


def spread_matrix(low, high, wide_low, wide_high):
    shape = (high - low, wide_high - wide_low)
    column = low + lax.broadcasted_iota(jnp.int32, shape, 0)
    place = wide_low + lax.broadcasted_iota(jnp.int32, shape, 1)
    inside = place % PADDED
    match = (column == (place // PADDED) * PIECE + inside) & (inside < PIECE)
    return jnp.where(match, 1.0, 0.0).astype(jnp.bfloat16)


def spread_columns(values):
    width = values.shape[1]
    step = LANES // PADDED * PIECE
    parts = []
    for begin in range(0, width, step):
        low = begin // LANES * LANES
        high = min(low + 2 * LANES, width)
        wide = begin // PIECE * PADDED
        parts.append(dot_on(values[:, low:high], spread_matrix(low, high, wide, wide + LANES), 1, 0))
    return jnp.concatenate(parts, axis=1).astype(jnp.bfloat16)


def close_columns(values):
    width = values.shape[1] // PADDED * PIECE
    parts = []
    for begin in range(0, width, LANES):
        end = min(begin + LANES, width)
        low = begin // PIECE * PADDED // LANES * LANES
        high = -(-((end - 1) // PIECE + 1) * PADDED // LANES) * LANES
        matrix = spread_matrix(begin, end, low, high)
        value = values[:, low:high]
        most = value.astype(jnp.bfloat16)
        closed = dot_on(most, matrix, 1, 1)
        if values.dtype != jnp.bfloat16:
            rest = (value - most.astype(jnp.float32)).astype(jnp.bfloat16)
            closed = closed + dot_on(rest, matrix, 1, 1)
        parts.append(closed)
    return jnp.concatenate(parts, axis=1)


def unit_rows(values):
    return values * lax.rsqrt(jnp.mean(values * values, axis=-1, keepdims=True) + epsilon)


def whole_call(name, body, arrays, results, scratch=(), scalars=0, room=48):
    return pl.pallas_call(
        body,
        out_shape=[jax.ShapeDtypeStruct(shape, kind) for shape, kind in results],
        in_specs=[pl.BlockSpec(memory_space=pltpu.SMEM)] * scalars
        + [VMEM] * (len(arrays) - scalars),
        out_specs=[VMEM] * len(results),
        scratch_shapes=[pltpu.VMEM(shape, kind) for shape, kind in scratch],
        compiler_params=pltpu.CompilerParams(vmem_limit_bytes=room * 2**20),
        name=name,
    )(*arrays)


def attention_project_kernel(
    tokens_ref,
    meta_ref,
    gain_ref,
    first_ref,
    second_ref,
    wide_ref,
    query_ref,
    keyval_ref,
    meta_wide_ref,
    meta_kv_ref,
):
    gain = gain_ref[...]
    third = first_ref.shape[1]
    rest = query_ref.shape[1] - third
    begin = -(-rest // LANES) * LANES
    keys = pl.ds(begin, keyval_ref.shape[1])
    wide = spread_columns((unit_rows(tokens_ref[...].astype(jnp.float32)) * gain).astype(jnp.bfloat16))
    wide_ref[...] = wide
    query_ref[:, pl.ds(0, third)] = dot_on(wide, first_ref[...], 1, 0).astype(jnp.bfloat16)
    query_ref[:, pl.ds(third, rest)] = dot_on(wide, second_ref[:, pl.ds(0, rest)], 1, 0).astype(
        jnp.bfloat16
    )
    keyval_ref[...] = dot_on(wide, second_ref[:, keys], 1, 0).astype(jnp.bfloat16)
    meta_wide = spread_columns((unit_rows(meta_ref[...]) * gain).astype(jnp.bfloat16))
    meta_wide_ref[...] = meta_wide
    meta_kv_ref[...] = dot_on(meta_wide, second_ref[:, keys], 1, 0).astype(jnp.bfloat16)


def attention_project(tokens, meta, gain, first, second, query_width, keys_width):
    rows, metas, wide = tokens.shape[0], meta.shape[0], first.shape[0]
    low = jnp.bfloat16
    return whole_call(
        "attention_project",
        attention_project_kernel,
        (tokens, meta, gain, first, second),
        (
            ((rows, wide), low),
            ((rows, query_width), low),
            ((rows, keys_width), low),
            ((metas, wide), low),
            ((metas, keys_width), low),
        ),
    )


def attention_weights_kernel(
    wide_ref,
    out_wide_ref,
    g_query_ref,
    g_pre_ref,
    first_ref,
    second_ref,
    one_ref,
    two_ref,
    three_ref,
    gain_ref,
):
    third = first_ref.shape[1]
    one = dot_on(wide_ref[...], g_query_ref[...], 0, 0)
    cut = one_ref.shape[1]
    one_ref[...] = one[:, :cut].astype(jnp.bfloat16)
    gain = jnp.sum(one[:, :third] * first_ref[...].astype(jnp.float32), axis=1, keepdims=True)
    rest = one.shape[1] - third
    gain = gain + jnp.sum(
        one[:, third:] * second_ref[:, pl.ds(0, rest)].astype(jnp.float32), axis=1, keepdims=True
    )
    gain_ref[...] = gain
    two = dot_on(out_wide_ref[...], g_pre_ref[...], 0, 0)
    size = one.shape[1] - cut
    begin = -(-size // LANES) * LANES
    left = two_ref.shape[1] - begin
    two_ref[...] = jnp.zeros_like(two_ref)
    two_ref[:, pl.ds(0, size)] = one[:, cut:].astype(jnp.bfloat16)
    two_ref[:, pl.ds(begin, left)] = two[:, :left].astype(jnp.bfloat16)
    three_ref[...] = two[:, left:].astype(jnp.bfloat16)


def attention_weights(wide, out_wide, g_query, g_pre, first, second, cuts):
    rows, places = wide.shape
    size = 2 * LANES
    columns = pl.BlockSpec((rows, size), lambda i: (0, i))

    def lines(width):
        return pl.BlockSpec((size, width), lambda i: (i, 0))

    return pl.pallas_call(
        attention_weights_kernel,
        grid=(places // size,),
        out_shape=[jax.ShapeDtypeStruct((places, cut), jnp.bfloat16) for cut in cuts]
        + [jax.ShapeDtypeStruct((places, 1), jnp.float32)],
        in_specs=[columns, columns]
        + [pl.BlockSpec(part.shape, lambda i: (0, 0)) for part in (g_query, g_pre)]
        + [lines(first.shape[1]), lines(second.shape[1])],
        out_specs=[lines(cut) for cut in cuts] + [lines(1)],
        compiler_params=pltpu.CompilerParams(vmem_limit_bytes=32 * 2**20),
        name="attention_weights",
    )(wide, out_wide, g_query, g_pre, first, second)


def attention_inputs_kernel(
    keyval_ref,
    g_query_ref,
    wide_ref,
    meta_wide_ref,
    g_meta_ref,
    first_ref,
    second_ref,
    meta_ref,
    gain_ref,
    one_ref,
    two_ref,
    three_ref,
    g_normed_ref,
    part_ref,
    meta_gain_ref,
):
    third = first_ref.shape[1]
    rest = g_query_ref.shape[1] - third
    begin = -(-rest // LANES) * LANES
    keys = pl.ds(begin, keyval_ref.shape[1])
    keyval = keyval_ref[...].astype(jnp.bfloat16)
    g_meta = g_meta_ref[...]
    half = one_ref.shape[1]
    places = wide_ref.shape[1]
    size = places // 4
    g_normed, g_meta_normed = [], []
    for i in range(4):
        spot = pl.ds(i * size, size)
        weight = second_ref[spot, keys]
        weight_f = weight.astype(jnp.float32)
        grad = dot_on(wide_ref[:, spot], keyval, 0, 0)
        part_ref[spot, :] = jnp.sum(grad * weight_f, axis=1, keepdims=True)
        grad = grad + dot_on(
            meta_wide_ref[:, spot].astype(jnp.float32), g_meta, 0, 0, precision=highest
        )
        one_ref[spot, :] = grad[:, :half].astype(jnp.bfloat16)
        two_ref[spot, :] = grad[:, half:].astype(jnp.bfloat16)
        total = dot_on(g_query_ref[:, pl.ds(0, third)], first_ref[spot, :], 1, 1)
        total = total + dot_on(
            g_query_ref[:, pl.ds(third, rest)], second_ref[spot, pl.ds(0, rest)], 1, 1
        )
        g_normed.append(total + dot_on(keyval, weight, 1, 1))
        g_meta_normed.append(dot_on(g_meta, weight_f, 1, 1, precision=highest))
    g_normed_ref[...] = close_columns(jnp.concatenate(g_normed, axis=1))
    g_meta_normed = close_columns(jnp.concatenate(g_meta_normed, axis=1))
    meta = meta_ref[...]
    scale = lax.rsqrt(jnp.mean(meta * meta, axis=-1, keepdims=True) + epsilon)
    unit = meta * scale
    meta_gain_ref[...] = jnp.sum(g_meta_normed * unit, axis=0, keepdims=True)
    g_unit = g_meta_normed * gain_ref[...]
    g_rows = scale * (g_unit - unit * jnp.mean(g_unit * unit, axis=-1, keepdims=True))
    three_ref[...] = spread_columns(g_rows.astype(jnp.bfloat16)).T


INSIDE = ("g_query", "wide", "meta_wide", "g_meta", "first", "second", "meta", "gain")


def stack_heads(source, target, scale, in_values):
    rows = source.shape[0]
    groups = target.shape[0]
    per = target.shape[1] // rows
    blank = jnp.zeros((rows, HEAD), target.dtype)
    for group in range(groups):
        for j in range(per):
            head = source[:, pl.ds((group * per + j) * HEAD, HEAD)].astype(jnp.float32) * scale
            head = head.astype(target.dtype)
            pair = [blank, head] if in_values else [head, blank]
            target[group, pl.ds(j * rows, rows), :] = jnp.concatenate(pair, axis=1)


def lay_keys(source, target):
    rows = source.shape[2]

    def move(place, carry):
        for half in range(2):
            begin = pl.multiple_of((place * 2 + half) * rows, rows)
            target[pl.ds(begin, rows), :] = source[half, place]
        return carry

    lax.fori_loop(0, source.shape[1], move, 0)


def key_bias(bounds_ref, begin, per):
    rows = bounds_ref.shape[0]
    keys = begin + lax.broadcasted_iota(jnp.int32, (rows, KEY_ROWS), 1)
    allowed = (keys >= bounds_ref[:, 0:1]) & (keys <= bounds_ref[:, 1:2])
    bias = jnp.where(allowed, 0.0, negative_fill)
    return jnp.concatenate([bias] * per, axis=0)


def key_bias_turned(bounds_ref, begin, per):
    rows = bounds_ref.shape[1]
    keys = begin + lax.broadcasted_iota(jnp.int32, (KEY_ROWS, rows), 0)
    allowed = (keys >= bounds_ref[0:1, :]) & (keys <= bounds_ref[1:2, :])
    bias = jnp.where(allowed, 0.0, negative_fill)
    return jnp.concatenate([bias] * per, axis=1)


def attend_forward_kernel(
    count_ref,
    query_ref,
    keyval_ref,
    meta_ref,
    bounds_ref,
    second_ref,
    third_ref,
    out_ref,
    mass_ref,
    wide_ref,
    pre_ref,
    heads,
    keys,
    scores,
):
    rows = query_ref.shape[0]
    groups = heads.shape[0]
    per = heads.shape[1] // rows
    width = 2 * HEAD
    metas = meta_ref.shape[0]
    meta_part = pl.ds(scores.shape[1] - metas, metas)
    stack_heads(query_ref, heads, score_scale, False)
    lay_keys(keyval_ref, keys)
    count = count_ref[0]
    lanes = lax.broadcasted_iota(jnp.int32, mass_ref.shape, 1)
    for group in range(groups):
        part = pl.ds(group * width, width)
        query = heads[group]

        def score(b, top):
            begin = pl.multiple_of(b * KEY_ROWS, KEY_ROWS)
            value = dot_on(query, keys[pl.ds(begin, KEY_ROWS), part], 1, 1)
            value = value + key_bias(bounds_ref, begin, per)
            scores[:, pl.ds(begin, KEY_ROWS)] = value
            return jnp.maximum(top, jnp.max(value, axis=1, keepdims=True))

        value = dot_on(query, meta_ref[:, part], 1, 1)
        scores[:, meta_part] = value
        top = lax.fori_loop(0, count, score, jnp.max(value, axis=1, keepdims=True))

        def weigh(b, carry):
            total, out = carry
            begin = pl.multiple_of(b * KEY_ROWS, KEY_ROWS)
            value = jnp.exp(scores[:, pl.ds(begin, KEY_ROWS)] - top)
            out = out + dot_on(
                value.astype(jnp.bfloat16), keys[pl.ds(begin, KEY_ROWS), part], 1, 0
            )
            return (total + jnp.sum(value, axis=1, keepdims=True), out)

        value = jnp.exp(scores[:, meta_part] - top)
        carry = (
            jnp.sum(value, axis=1, keepdims=True),
            dot_on(value.astype(jnp.bfloat16), meta_ref[:, part], 1, 0),
        )
        total, out = lax.fori_loop(0, count, weigh, carry)
        out = out * (1.0 / total)
        for j in range(per):
            out_ref[:, pl.ds((group * per + j) * HEAD, HEAD)] = out[
                j * rows : (j + 1) * rows, HEAD:
            ]
        mass = top + jnp.log(total)
        before = mass_ref[...] if group else jnp.zeros_like(mass_ref)
        mass_ref[...] = jnp.where(lanes == group, mass, before)
    wide = spread_columns(out_ref[...].astype(jnp.bfloat16))
    wide_ref[...] = wide
    most = third_ref.shape[1]
    part = pre_ref.shape[1] - most
    pre_ref[:, pl.ds(0, part)] = dot_on(
        wide, second_ref[:, pl.ds(second_ref.shape[1] - part, part)], 1, 0
    )
    pre_ref[:, pl.ds(part, most)] = dot_on(wide, third_ref[...], 1, 0)


def attend_forward(count, query, keyval, meta, bounds, second, third):
    rows, query_width = query.shape
    groups = meta.shape[1] // (2 * HEAD)
    stacked = query_width // HEAD // groups * rows
    key_rows = 2 * keyval.shape[1] * keyval.shape[2]
    places, low, full = second.shape[0], jnp.bfloat16, jnp.float32
    return whole_call(
        "attend_forward",
        attend_forward_kernel,
        (count, query, keyval, meta, bounds, second, third),
        (
            ((rows, query_width), full),
            ((stacked, 2 * HEAD), full),
            ((rows, places), low),
            ((rows, query_width), full),
        ),
        (
            ((groups, stacked, 2 * HEAD), low),
            ((key_rows, meta.shape[1]), low),
            ((stacked, key_rows + meta.shape[0]), full),
        ),
        scalars=1,
    )


def attend_backward_kernel(
    count_ref,
    query_ref,
    keyval_ref,
    meta_ref,
    bounds_ref,
    out_ref,
    mass_ref,
    g_pre_ref,
    second_ref,
    third_ref,
    g_query_ref,
    g_keyval_ref,
    g_meta_ref,
    heads,
    grads,
    keys,
    grad_ref,
):
    rows = query_ref.shape[0]
    groups = heads.shape[0]
    per = heads.shape[1] // rows
    width = 2 * HEAD
    most = third_ref.shape[1]
    left = g_pre_ref.shape[1] - most
    grad_wide = dot_on(
        g_pre_ref[:, pl.ds(0, left)],
        second_ref[:, pl.ds(second_ref.shape[1] - left, left)],
        1,
        1,
    )
    grad_wide = grad_wide + dot_on(g_pre_ref[:, pl.ds(left, most)], third_ref[...], 1, 1)
    grad_ref[...] = close_columns(grad_wide.astype(jnp.bfloat16)).astype(jnp.bfloat16)
    stack_heads(query_ref, heads, score_scale, False)
    stack_heads(grad_ref, grads, 1.0, True)
    lay_keys(keyval_ref, keys)
    g_keyval_ref[...] = jnp.zeros_like(g_keyval_ref)
    count = count_ref[0]
    lanes = lax.broadcasted_iota(jnp.int32, mass_ref.shape, 1)
    for group in range(groups):
        part = pl.ds(group * width, width)
        query, grad = heads[group], grads[group]
        mass = jnp.sum(jnp.where(lanes == group, mass_ref[...], 0.0), axis=1, keepdims=True)
        balance = []
        for j in range(per):
            head = pl.ds((group * per + j) * HEAD, HEAD)
            balance.append(
                jnp.sum(grad_ref[:, head].astype(jnp.float32) * out_ref[:, head], axis=1, keepdims=True)
            )
        balance = jnp.concatenate(balance, axis=0)

        mass_row, balance_row = mass.T, balance.T

        def pieces(block, bias):
            value = dot_on(block, query, 1, 1)
            if bias is not None:
                value = value + bias
            probs = jnp.exp(value - mass_row)
            g_scores = (probs * (dot_on(block, grad, 1, 1) - balance_row)).astype(jnp.bfloat16)
            g_block = dot_on(g_scores, query, 1, 0) + dot_on(probs.astype(jnp.bfloat16), grad, 1, 0)
            return dot_on(g_scores, block, 0, 0), g_block

        g_query, g_meta = pieces(meta_ref[:, part], None)
        g_meta_ref[:, part] = g_meta

        def step(b, g_query):
            begin = pl.multiple_of(b * KEY_ROWS, KEY_ROWS)
            more, g_block = pieces(
                keys[pl.ds(begin, KEY_ROWS), part], key_bias_turned(bounds_ref, begin, per)
            )
            g_keyval_ref[pl.ds(begin, KEY_ROWS), part] = g_block.astype(jnp.bfloat16)
            return g_query + more

        g_query = lax.fori_loop(0, count, step, g_query) * score_scale
        for j in range(per):
            g_query_ref[:, pl.ds((group * per + j) * HEAD, HEAD)] = g_query[
                j * rows : (j + 1) * rows, :HEAD
            ].astype(jnp.bfloat16)


def attend_backward(count, query, keyval, meta, bounds, out, mass, g_pre, second, third):
    rows, query_width = query.shape
    groups = meta.shape[1] // (2 * HEAD)
    stacked = mass.shape[0]
    key_rows = 2 * keyval.shape[1] * keyval.shape[2]
    low = jnp.bfloat16
    return whole_call(
        "attend_backward",
        attend_backward_kernel,
        (count, query, keyval, meta, bounds, out, mass, g_pre, second, third),
        (
            ((rows, query_width), low),
            ((key_rows, meta.shape[1]), low),
            (meta.shape, jnp.float32),
        ),
        (
            ((groups, stacked, 2 * HEAD), low),
            ((groups, stacked, 2 * HEAD), low),
            ((key_rows, meta.shape[1]), low),
            ((rows, query_width), low),
        ),
        scalars=1,
        room=56,
    )


def close_rows(source, target, places):
    width = target.shape[0]
    for begin in range(0, width, LANES):
        end = min(begin + LANES, width)
        low = begin // PIECE * PADDED // LANES * LANES
        high = min(-(-((end - 1) // PIECE + 1) * PADDED // LANES) * LANES, places)
        matrix = spread_matrix(begin, end, low, high)
        target[pl.ds(begin, end - begin), :] = dot_on(matrix, source(low, high), 1, 0).astype(
            target.dtype
        )


def spread_rows(source, put):
    step = LANES // PADDED * PIECE
    for n, begin in enumerate(range(0, 64 * PIECE, step)):
        low = begin // LANES * LANES
        high = min(low + 2 * LANES, 64 * PIECE)
        wide = begin // PIECE * PADDED
        matrix = spread_matrix(low, high, wide, wide + LANES)
        put(n, dot_on(matrix, source(low, high), 0, 0).astype(jnp.bfloat16))


def ffn_kernel(
    feed_ref,
    cot_ref,
    gate_ref,
    down_ref,
    out_ref,
    g_feed_ref,
    g_gate_ref,
    g_down_ref,
    gate_w,
    up_w,
    active_s,
    g_gate_s,
    g_up_s,
    sums,
):
    rows, size = feed_ref.shape[0], 256
    places = gate_ref.shape[1]
    for part, target in enumerate((gate_w, up_w)):
        close_rows(lambda low, high: gate_ref[part, pl.ds(low, high - low), :], target, places)

    def block(i, carry):
        spot = pl.ds(pl.multiple_of(i * size, size), size)
        feed = feed_ref[spot, :]
        gate = dot_on(feed, gate_w[...], 1, 0)
        up = dot_on(feed, up_w[...], 1, 0)
        share = jax.nn.sigmoid(gate)
        silu = gate * share
        active = (silu * up).astype(jnp.bfloat16)
        active_s[spot, :] = active
        out_ref[spot, :] = dot_on(active, down_ref[...], 1, 0).astype(jnp.bfloat16)
        g_active = dot_on(cot_ref[spot, :], down_ref[...], 1, 1)
        g_gate = (g_active * up * (share + silu * (1.0 - share))).astype(jnp.bfloat16)
        g_up = (g_active * silu).astype(jnp.bfloat16)
        g_gate_s[spot, :] = g_gate
        g_up_s[spot, :] = g_up
        g_feed = dot_on(g_gate, gate_w[...], 1, 1) + dot_on(g_up, up_w[...], 1, 1)
        g_feed_ref[spot, :] = g_feed.astype(jnp.bfloat16)
        return carry

    lax.fori_loop(0, rows // size, block, 0)
    for part, grad in enumerate((g_gate_s, g_up_s)):
        sums[...] = dot_on(feed_ref[...], grad[...], 0, 0).astype(jnp.bfloat16)

        def put(n, value):
            for x in range(SIDE):
                g_gate_ref[part, x, n] = value[x * PADDED : (x + 1) * PADDED]

        spread_rows(lambda low, high: sums[pl.ds(low, high - low), :], put)
    g_down = dot_on(active_s[...], cot_ref[...], 0, 0).astype(jnp.bfloat16)
    size = g_down_ref.shape[3]
    for x in range(SIDE):
        for part in range(2):
            begin = (2 * x + part) * size
            g_down_ref[part, x, 0] = g_down[begin : begin + size]


def feed_forward(feed, cot, gate, down):
    rows, width = feed.shape
    units = down.shape[0]
    low = jnp.bfloat16
    return whole_call(
        "feed_forward",
        ffn_kernel,
        (feed, cot, gate, down),
        (
            ((rows, width), low),
            ((rows, width), low),
            ((2, SIDE, 16, PADDED, units), low),
            ((2, SIDE, 1, units // 8, width), low),
        ),
        (
            ((width, units), low),
            ((width, units), low),
            ((rows, units), low),
            ((rows, units), low),
            ((rows, units), low),
            ((width, units), low),
        ),
        room=60,
    )


STEP_ROWS = 104
LOG_ROWS = slice(104, 120)
TAP_ROWS = slice(120, 124)
OFFSET_ROW = slice(124, 125)
BIAS_ROW = slice(125, 126)
SKIP_ROW = slice(126, 127)
FIRST_PROJ = 128
PROJ_CUT = 72


def channel_matrix(size):
    channel = lax.broadcasted_iota(jnp.int32, (size, size), 0)
    place = lax.broadcasted_iota(jnp.int32, (size, size), 1)
    match = (channel == (place // 64) * 50 + place % 64) & (place % 64 < 50)
    return jnp.where(match, 1.0, 0.0).astype(jnp.bfloat16)


def two_terms(values):
    most = values.astype(jnp.bfloat16)
    return most, (values - most.astype(jnp.float32)).astype(jnp.bfloat16)


def shifted_rows(before, rows, back):
    joined = jnp.concatenate([before, rows], axis=0)
    return joined[8 - back : 8 - back + rows.shape[0]]


def conv_sum(before, rows, dist, channel):
    taps = channel[TAP_ROWS]
    total = taps[CONV - 1 : CONV] * rows + channel[OFFSET_ROW]
    for back in range(1, CONV):
        earlier = shifted_rows(before, rows, back)
        valid = jnp.where(dist >= back, 1.0, 0.0)
        total = total + taps[CONV - 1 - back : CONV - back] * earlier * valid
    return total


def mixer_project_kernel(
    tokens_ref,
    gain_ref,
    weight_ref,
    channel_ref,
    dist_ref,
    normed_ref,
    conv_ref,
    gate_ref,
    inputs_ref,
    first_ref,
    second_ref,
    compact_ref,
    rows_ref,
    tail_ref,
):
    low = jnp.bfloat16
    lanes = conv_ref.shape[1]

    @pl.when(pl.program_id(0) == 0)
    def _():
        places = weight_ref.shape[0]
        close_rows(lambda a, b: weight_ref[pl.ds(a, b - a), :], compact_ref, places)
        rows_ref[...] = dot_on(channel_ref[...], channel_matrix(lanes), 0, 1)
        tail_ref[...] = jnp.zeros_like(tail_ref)

    tokens = jnp.concatenate([tokens_ref[0, 0], tokens_ref[1, 0]], axis=0).astype(jnp.float32)
    normed = (unit_rows(tokens) * gain_ref[...]).astype(low)
    normed_ref[...] = normed
    mixed = dot_on(normed, compact_ref[...], 1, 0)
    conv_in = mixed[:, :lanes].astype(low)
    conv_ref[...] = conv_in
    gate_ref[...] = mixed[:, lanes:]
    rows = conv_in.astype(jnp.float32)
    channel = rows_ref[...]
    total = conv_sum(tail_ref[...], rows, dist_ref[...], channel)
    tail_ref[...] = rows[-8:]
    inputs = (total * jax.nn.sigmoid(total)).astype(low)
    inputs_ref[...] = inputs
    proj = dot_on(channel[FIRST_PROJ : FIRST_PROJ + 136].astype(low), inputs, 1, 1)
    first_ref[0] = proj[:PROJ_CUT]
    second_ref[0] = proj[PROJ_CUT:]


def mixer_project(tokens, gain, weight, channel, dist):
    places, rows, width = tokens.shape[1], tokens.shape[2], tokens.shape[3]
    rows, lanes = 2 * rows, weight.shape[1] // 2
    group = places * rows
    low, full = jnp.bfloat16, jnp.float32

    def line(size):
        return pl.BlockSpec((rows, size), lambda i: (i, 0))

    def whole(*shape):
        return pl.BlockSpec(shape, lambda i: (0,) * len(shape))

    return pl.pallas_call(
        mixer_project_kernel,
        grid=(places,),
        out_shape=[
            jax.ShapeDtypeStruct((group, width), low),
            jax.ShapeDtypeStruct((group, lanes), low),
            jax.ShapeDtypeStruct((group, lanes), full),
            jax.ShapeDtypeStruct((group, lanes), low),
            jax.ShapeDtypeStruct((places, PROJ_CUT, rows), full),
            jax.ShapeDtypeStruct((places, 136 - PROJ_CUT, rows), full),
            jax.ShapeDtypeStruct((width, 2 * lanes), low),
            jax.ShapeDtypeStruct((channel.shape[1], lanes), full),
        ],
        in_specs=[
            pl.BlockSpec((2, 1, rows // 2, width), lambda i: (0, i, 0, 0)),
            whole(*gain.shape),
            whole(*weight.shape),
            whole(*channel.shape),
            line(1),
        ],
        out_specs=[
            line(width),
            line(lanes),
            line(lanes),
            line(lanes),
            pl.BlockSpec((1, PROJ_CUT, rows), lambda i: (i, 0, 0)),
            pl.BlockSpec((1, 136 - PROJ_CUT, rows), lambda i: (i, 0, 0)),
            whole(width, 2 * lanes),
            whole(channel.shape[1], lanes),
        ],
        scratch_shapes=[pltpu.VMEM((8, lanes), full)],
        compiler_params=pltpu.CompilerParams(vmem_limit_bytes=40 * 2**20),
        name="mixer_project",
    )(tokens, gain, weight, channel, dist)


def step_sum(first_ref, second_ref, channel_ref, p):
    low = jnp.bfloat16
    one = first_ref[p].astype(low)
    two = second_ref[p, pl.ds(0, STEP_ROWS - PROJ_CUT), :].astype(low)
    total = dot_on(one, channel_ref[pl.ds(0, PROJ_CUT), :].astype(low), 0, 0)
    total = total + dot_on(
        two, channel_ref[pl.ds(PROJ_CUT, STEP_ROWS - PROJ_CUT), :].astype(low), 0, 0
    )
    return total + channel_ref[BIAS_ROW], one, two


def put_blocks(target, spot, value):
    for block in range(target.shape[0]):
        target[block, spot, :] = value[:, block * CHUNKS : (block + 1) * CHUNKS]


def get_blocks(source, spot):
    return jnp.concatenate([source[block, spot, :] for block in range(source.shape[0])], axis=1)


def softplus(values):
    return jnp.maximum(values, 0.0) + jnp.log1p(jnp.exp(-jnp.abs(values)))


def mixer_forward_kernel(
    used,
    first_ref,
    second_ref,
    cols_ref,
    channel_ref,
    inputs_ref,
    reset_ref,
    gate_ref,
    back_ref,
    partial_ref,
    mixed_ref,
    out_ref,
    start_ref,
    decay_t,
    drive_t,
    rate_ref,
    decay_s,
    drive_s,
    out_t,
):
    places = first_ref.shape[0]
    rows = first_ref.shape[2]
    half = rows // 2
    lanes = channel_ref.shape[1]
    rate = -jnp.exp(channel_ref[LOG_ROWS]) * log2_e
    channel = lax.broadcasted_iota(jnp.int32, rate.shape, 1)
    rate_ref[...] = jnp.where(channel < used, rate, 0.0).T

    def prepare(p, carry):
        spot = pl.ds(pl.multiple_of(p * rows, rows), rows)
        steps = softplus(step_sum(first_ref, second_ref, channel_ref, p)[0])
        put_blocks(decay_s, spot, steps + reset_ref[spot, :])
        put_blocks(drive_s, spot, steps * inputs_ref[spot, :].astype(jnp.float32))
        return carry

    lax.fori_loop(0, places, prepare, 0)
    scan_forward_body(
        used, decay_s, drive_s, cols_ref, rate_ref, out_ref, start_ref, decay_t, drive_t, out_t
    )
    weight = dot_on(channel_matrix(lanes), back_ref[...], 1, 0).astype(jnp.bfloat16)

    def finish(p, carry):
        spot = pl.ds(pl.multiple_of(p * rows, rows), rows)
        gate = gate_ref[spot, :]
        inputs = inputs_ref[spot, :].astype(jnp.float32)
        mixed = (get_blocks(out_ref, spot) + channel_ref[SKIP_ROW] * inputs) * (
            gate * jax.nn.sigmoid(gate)
        )
        mixed = mixed.astype(jnp.bfloat16)
        mixed_ref[spot, :] = mixed
        value = dot_on(mixed, weight, 1, 0).astype(jnp.bfloat16)
        partial_ref[0, p] = value[:half]
        partial_ref[1, p] = value[half:]
        return carry

    lax.fori_loop(0, places, finish, 0)


def mixer_forward(used, first, second, cols, channel, inputs, reset, gate, back):
    group, lanes = inputs.shape
    places, rows = first.shape[0], first.shape[2]
    states = cols.shape[0] // 2
    low, full = jnp.bfloat16, jnp.float32
    blocks = (lanes // CHUNKS, group, CHUNKS)
    turned = (STEPS, lanes, CHUNKS)
    return whole_call(
        "mixer_forward",
        functools.partial(mixer_forward_kernel, used),
        (first, second, cols, channel, inputs, reset, gate, back),
        (
            ((2, places, rows // 2, back.shape[1]), low),
            ((group, lanes), low),
            (blocks, full),
            ((states, lanes, CHUNKS), full),
            (turned, full),
            (turned, full),
            ((lanes, states), full),
        ),
        ((blocks, full), (blocks, full), (turned, full)),
    )


def mixer_backward_kernel(
    used,
    first_ref,
    second_ref,
    cols_ref,
    channel_ref,
    inputs_ref,
    gate_ref,
    back_ref,
    grad_ref,
    mixed_ref,
    out_ref,
    start_ref,
    decay_t,
    drive_t,
    rate_ref,
    g_first_ref,
    g_second_ref,
    g_cols_ref,
    g_inputs_ref,
    g_gate_ref,
    g_back_ref,
    g_rows_ref,
    g_rate_ref,
    g_out_s,
    g_decay_s,
    g_drive_s,
    g_weight,
    grad_t,
    g_decay_t,
    g_drive_t,
    sums_t,
    ends_t,
):
    places = first_ref.shape[0]
    rows = first_ref.shape[2]
    lanes = channel_ref.shape[1]
    low, full = jnp.bfloat16, jnp.float32
    weight = dot_on(channel_matrix(lanes), back_ref[...], 1, 0).astype(low)
    skip = channel_ref[SKIP_ROW]
    g_weight[...] = jnp.zeros_like(g_weight)
    g_rows_ref[...] = jnp.zeros_like(g_rows_ref)

    def prepare(p, carry):
        spot = pl.ds(pl.multiple_of(p * rows, rows), rows)
        grad = jnp.concatenate([grad_ref[0, p], grad_ref[1, p]], axis=0)
        g_weight[...] += dot_on(mixed_ref[spot, :], grad, 0, 0)
        g_mixed = dot_on(grad, weight, 1, 1)
        gate = gate_ref[spot, :]
        inputs = inputs_ref[spot, :].astype(full)
        share = jax.nn.sigmoid(gate)
        g_out = g_mixed * (gate * share)
        put_blocks(g_out_s, spot, g_out)
        value = get_blocks(out_ref, spot) + skip * inputs
        g_gate = g_mixed * value * (share + gate * share * (1.0 - share))
        g_gate_ref[spot, :] = g_gate.astype(low)
        g_inputs_ref[spot, :] = g_out * skip
        g_rows_ref[SKIP_ROW] += jnp.sum(g_out * inputs, axis=0, keepdims=True)
        return carry

    lax.fori_loop(0, places, prepare, 0)
    scan_backward_body(
        used,
        decay_t,
        drive_t,
        cols_ref,
        rate_ref,
        start_ref,
        g_out_s,
        g_decay_s,
        g_drive_s,
        g_cols_ref,
        g_rate_ref,
        grad_t,
        g_decay_t,
        g_drive_t,
        sums_t,
        ends_t,
    )

    def finish(p, carry):
        spot = pl.ds(pl.multiple_of(p * rows, rows), rows)
        total, one, two = step_sum(first_ref, second_ref, channel_ref, p)
        steps = softplus(total)
        inputs = inputs_ref[spot, :].astype(full)
        g_drive = get_blocks(g_drive_s, spot)
        g_steps = get_blocks(g_decay_s, spot) * (1.0 / log2_e) + g_drive * inputs
        g_inputs_ref[spot, :] += g_drive * steps
        g_total = g_steps * jax.nn.sigmoid(total)
        g_rows_ref[BIAS_ROW] += jnp.sum(g_total, axis=0, keepdims=True)
        g_total = g_total.astype(low)
        g_rows_ref[pl.ds(0, PROJ_CUT), :] += dot_on(one, g_total, 1, 0)
        g_rows_ref[pl.ds(PROJ_CUT, STEP_ROWS - PROJ_CUT), :] += dot_on(two, g_total, 1, 0)
        g_low = dot_on(channel_ref[pl.ds(0, STEP_ROWS), :].astype(low), g_total, 1, 1)
        g_first_ref[p] = g_low[:PROJ_CUT]
        g_second_ref[p] = g_low[PROJ_CUT:]
        return carry

    lax.fori_loop(0, places, finish, 0)
    g_back = dot_on(channel_matrix(lanes), g_weight[...].astype(low), 0, 0).astype(low)
    size = g_back_ref.shape[2]
    for x in range(SIDE):
        g_back_ref[x, 0] = g_back[x * size : (x + 1) * size]


def mixer_backward(
    used,
    first,
    second,
    cols,
    channel,
    inputs,
    gate,
    back,
    grad,
    mixed,
    out,
    starts,
    decay_t,
    drive_t,
    rate,
):
    group, lanes = inputs.shape
    places, rows = first.shape[0], first.shape[2]
    low, full = jnp.bfloat16, jnp.float32
    width = back.shape[1]
    turned = (decay_t.shape, full)
    states = rate.shape[1]
    return whole_call(
        "mixer_backward",
        functools.partial(mixer_backward_kernel, used),
        (
            first,
            second,
            cols,
            channel,
            inputs,
            gate,
            back,
            grad,
            mixed,
            out,
            starts,
            decay_t,
            drive_t,
            rate,
        ),
        (
            ((places, PROJ_CUT, rows), full),
            ((places, STEP_ROWS - PROJ_CUT, rows), full),
            (cols.shape, full),
            ((group, lanes), full),
            ((group, lanes), low),
            ((SIDE, 1, lanes // SIDE, width), low),
            ((FIRST_PROJ, lanes), full),
            (rate.shape, full),
        ),
        (
            (out.shape, full),
            (out.shape, full),
            (out.shape, full),
            ((lanes, width), full),
            turned,
            turned,
            turned,
            ((2 * states, STEPS, LINES, CHUNKS), full),
            (starts.shape, full),
        ),
        room=60,
    )


def mixer_inputs_kernel(
    first_ref,
    second_ref,
    channel_ref,
    weight_ref,
    normed_ref,
    conv_ref,
    before_ref,
    inputs_ref,
    g_inputs_ref,
    g_gate_ref,
    dist_ref,
    later_ref,
    g_normed_ref,
    g_weight_ref,
    g_rows_ref,
    gain_ref,
    head_ref,
    sums,
):
    step = pl.program_id(0)
    steps = pl.num_programs(0)
    low, full = jnp.bfloat16, jnp.float32
    lanes = conv_ref.shape[1]

    @pl.when(step == 0)
    def _():
        head_ref[...] = jnp.zeros_like(head_ref)
        sums[...] = jnp.zeros_like(sums)
        g_rows_ref[...] = jnp.zeros_like(g_rows_ref)

    channel = channel_ref[...]
    proj = channel[FIRST_PROJ : FIRST_PROJ + 136].astype(low)
    g_proj = [
        jnp.concatenate([first_ref[i], second_ref[i]], axis=0) for i in range(first_ref.shape[0])
    ]
    g_proj = jnp.concatenate(g_proj, axis=1).astype(low)
    g_inputs = g_inputs_ref[...] + dot_on(g_proj, proj, 0, 0)
    g_rows_ref[pl.ds(FIRST_PROJ, 136), :] += dot_on(g_proj, inputs_ref[...], 1, 0)
    rows = conv_ref[...].astype(full)
    before = jnp.where(step == steps - 1, 0.0, 1.0) * before_ref[...].astype(full)[-8:]
    dist = dist_ref[...]
    total = conv_sum(before, rows, dist, channel)
    share = jax.nn.sigmoid(total)
    g_total = g_inputs * (share + total * share * (1.0 - share))
    taps = channel[TAP_ROWS]
    g_conv = taps[CONV - 1 : CONV] * g_total
    g_taps = [jnp.sum(g_total * rows, axis=0, keepdims=True)]
    after = jnp.concatenate([g_total, head_ref[...]], axis=0)
    size = rows.shape[0]
    later = later_ref[...]
    for back in range(1, CONV):
        earlier = shifted_rows(before, rows, back) * jnp.where(dist >= back, 1.0, 0.0)
        g_taps.append(jnp.sum(g_total * earlier, axis=0, keepdims=True))
        tap = taps[CONV - 1 - back : CONV - back]
        g_conv = g_conv + tap * after[back : back + size] * jnp.where(later >= back, 1.0, 0.0)
    head_ref[...] = g_total[:8]
    g_rows_ref[TAP_ROWS] += jnp.concatenate(g_taps[::-1], axis=0)
    g_rows_ref[OFFSET_ROW] += jnp.sum(g_total, axis=0, keepdims=True)
    g_mixed = jnp.concatenate([g_conv.astype(low), g_gate_ref[...]], axis=1)
    sums[...] += dot_on(normed_ref[...], g_mixed, 0, 0)
    g_normed = dot_on(g_mixed, weight_ref[...], 1, 1).astype(low)
    count, half = g_normed_ref.shape[1:3]
    for i in range(count):
        for part in range(2):
            begin = (2 * i + part) * half
            g_normed_ref[part, i] = g_normed[begin : begin + half]

    @pl.when(step == steps - 1)
    def _():
        gain_ref[...] = jnp.sum(sums[...] * weight_ref[...].astype(full), axis=1, keepdims=True)

        def put(n, value):
            for x in range(SIDE):
                g_weight_ref[x, n] = value[x * PADDED : (x + 1) * PADDED]

        spread_rows(lambda a, b: sums[pl.ds(a, b - a), :].astype(low), put)


def mixer_inputs(first, second, channel, weight, normed, conv, inputs, g_inputs, g_gate, dist, later):
    places, rows = first.shape[0], first.shape[2]
    group, lanes = conv.shape
    width = normed.shape[1]
    low, full = jnp.bfloat16, jnp.float32
    count = 2
    last = places // count - 1

    def line(size):
        return pl.BlockSpec((count * rows, size), lambda i: (last - i, 0))

    def cube(size):
        return pl.BlockSpec((count, size, rows), lambda i: (last - i, 0, 0))

    def whole(*shape):
        return pl.BlockSpec(shape, lambda i: (0,) * len(shape))

    return pl.pallas_call(
        mixer_inputs_kernel,
        grid=(places // count,),
        out_shape=[
            jax.ShapeDtypeStruct((2, places, rows // 2, width), low),
            jax.ShapeDtypeStruct((SIDE, 16, PADDED, 2 * lanes), low),
            jax.ShapeDtypeStruct(channel.shape, full),
            jax.ShapeDtypeStruct((width, 1), full),
        ],
        in_specs=[
            cube(PROJ_CUT),
            cube(136 - PROJ_CUT),
            whole(*channel.shape),
            whole(*weight.shape),
            line(width),
            line(lanes),
            pl.BlockSpec((count * rows, lanes), lambda i: (jnp.maximum(last - 1 - i, 0), 0)),
            line(lanes),
            line(lanes),
            line(lanes),
            line(1),
            line(1),
        ],
        out_specs=[
            pl.BlockSpec((2, count, rows // 2, width), lambda i: (0, last - i, 0, 0)),
            whole(SIDE, 16, PADDED, 2 * lanes),
            whole(*channel.shape),
            whole(width, 1),
        ],
        scratch_shapes=[pltpu.VMEM((8, lanes), full), pltpu.VMEM((width, 2 * lanes), full)],
        compiler_params=pltpu.CompilerParams(vmem_limit_bytes=48 * 2**20),
        name="mixer_inputs",
    )(first, second, channel, weight, normed, conv, conv, inputs, g_inputs, g_gate, dist, later)


def channel_grads_kernel(one_ref, two_ref, rate_ref, channel_ref, out_ref):
    lanes = channel_ref.shape[1]
    total = two_ref[...]
    states = rate_ref.shape[1]
    rows = lax.broadcasted_iota(jnp.int32, total.shape, 0)
    one = one_ref[...]
    one = jnp.concatenate([one, jnp.zeros((total.shape[0] - one.shape[0], lanes), one.dtype)], axis=0)
    logs = rate_ref[...].T * -jnp.exp(channel_ref[LOG_ROWS])
    blank = jnp.zeros((LOG_ROWS.start, lanes), logs.dtype)
    rest = jnp.zeros((total.shape[0] - LOG_ROWS.start - states, lanes), logs.dtype)
    total = total + jnp.where((rows >= LOG_ROWS.start) & (rows < LOG_ROWS.stop), 0.0, one)
    total = total + jnp.concatenate([blank, logs, rest], axis=0)
    matrix = channel_matrix(lanes)
    most, left = two_terms(total)
    wide = dot_on(matrix, most, 0, 1) + dot_on(matrix, left, 0, 1)
    size = out_ref.shape[2]
    for x in range(SIDE):
        out_ref[x, 0] = wide[x * size : (x + 1) * size]


def channel_grads(one, two, rate, channel):
    lanes = channel.shape[1]
    return whole_call(
        "channel_grads",
        channel_grads_kernel,
        (one, two, rate, channel),
        (((SIDE, 1, lanes // SIDE, channel.shape[0]), jnp.float32),),
    )[0]


def unpack_kernel(small_ref, meta_ref, gains_ref):
    width = meta_ref.shape[1]
    metas = meta_ref.shape[0]
    for begin in range(0, width, LANES):
        end = min(begin + LANES, width)
        low = begin // PIECE * PADDED // LANES * LANES
        high = -(-((end - 1) // PIECE + 1) * PADDED // LANES) * LANES
        matrix = spread_matrix(begin, end, low, high)
        value = dot_on(small_ref[pl.ds(low, high - low), :], matrix, 0, 1)
        meta_ref[:, pl.ds(begin, end - begin)] = value[:metas]
        gains_ref[:, pl.ds(begin, end - begin)] = value[metas : metas + gains_ref.shape[0]]


def unpack(small, metas, width):
    full = jnp.float32
    return whole_call(
        "unpack", unpack_kernel, (small,), (((metas, width), full), ((8, width), full))
    )


def padded_rows(value, rows):
    blank = jnp.zeros((rows - value.shape[0], value.shape[1]), value.dtype)
    return jnp.concatenate([value, blank], axis=0).astype(jnp.bfloat16)


def padded_lanes(value, lanes):
    return jnp.concatenate(
        [value, jnp.zeros((value.shape[0], lanes - value.shape[1]), value.dtype)], axis=1
    )


def stacked_rows(parts, rows):
    blank = jnp.zeros((rows - sum(part.shape[0] for part in parts), parts[0].shape[1]), jnp.float32)
    return jnp.concatenate(parts + [blank], axis=0)


def prepare_kernel(
    query_ref,
    keyval_ref,
    attn_ref,
    mamba_ref,
    back_ref,
    gate_ref,
    down_ref,
    meta_ref,
    norm_gain_ref,
    attn_gain_ref,
    mamba_gain_ref,
    feed_gain_ref,
    step_ref,
    log_ref,
    taps_ref,
    offset_ref,
    bias_ref,
    skip_ref,
    ssm_ref,
    attention_out,
    mamba_out,
    back_out,
    gate_out,
    down_out,
    small_out,
    channel_out,
):
    small = [meta_ref, norm_gain_ref, attn_gain_ref, mamba_gain_ref, feed_gain_ref]
    small = stacked_rows([ref[...] for ref in small], 2 * LANES)
    small_out[...] = padded_lanes(small, LANES).T[: small_out.shape[0]].astype(jnp.bfloat16)
    blank = jnp.zeros((STEP_ROWS - step_ref.shape[0], step_ref.shape[1]), jnp.float32)
    rows = [step_ref[...], blank]
    rows += [ref[...] for ref in (log_ref, taps_ref, offset_ref, bias_ref, skip_ref)]
    rows = padded_lanes(stacked_rows(rows, LANES), LANES).T[: channel_out.shape[0]]
    channel_out[:, pl.ds(0, LANES)] = rows.astype(jnp.bfloat16)
    channel_out[:, pl.ds(LANES, 2 * LANES)] = padded_rows(
        padded_lanes(ssm_ref[...], 2 * LANES), channel_out.shape[0]
    )
    width = query_ref.shape[1]
    begin = -(-width // LANES) * LANES
    attention_out[:, pl.ds(0, begin)] = padded_rows(padded_lanes(query_ref[...], begin), PADDED)
    half = keyval_ref.shape[1] // 2
    for group in range(half // HEAD):
        spot = group * HEAD
        pair = [keyval_ref[:, pl.ds(spot, HEAD)], keyval_ref[:, pl.ds(half + spot, HEAD)]]
        attention_out[:, pl.ds(begin + 2 * spot, 2 * HEAD)] = padded_rows(
            jnp.concatenate(pair, axis=1), PADDED
        )
    attention_out[:, pl.ds(begin + 2 * half, width)] = padded_rows(attn_ref[...], PADDED)
    places = mamba_out.shape[0]
    lanes = mamba_out.shape[2] // 2
    inner = mamba_ref.shape[1] // places // 2
    for place in range(places):
        parts = [
            padded_lanes(mamba_ref[:, pl.ds((part * places + place) * inner, inner)], lanes)
            for part in range(2)
        ]
        mamba_out[place] = padded_rows(jnp.concatenate(parts, axis=1), PADDED)
    back_out[...] = padded_rows(back_ref[...], back_out.shape[0])
    down_out[...] = padded_rows(down_ref[...], down_out.shape[0])
    size = down_ref.shape[0]
    room = gate_out.shape[3] // SIDE
    for part in range(2):
        for place in range(places):
            first = (part * places + place) * SIDE * size
            parts = [
                padded_lanes(gate_ref[:, pl.ds(first + x * size, size)], room) for x in range(SIDE)
            ]
            gate_out[part, place] = padded_rows(jnp.concatenate(parts, axis=1), PADDED)


def prepare(*arrays):
    low = jnp.bfloat16
    query, keyval, attn, _, back, _, down = arrays[:7]
    most = -(-query.shape[1] // LANES) * LANES
    return whole_call(
        "prepare",
        prepare_kernel,
        arrays,
        (
            ((PADDED, most + keyval.shape[1] + attn.shape[1]), low),
            ((16, PADDED, 4 * CHUNKS), low),
            ((64, back.shape[1]), low),
            ((2, 16, PADDED, 96 * SIDE), low),
            ((96, down.shape[1]), low),
            ((PADDED, 2 * LANES), low),
            ((64, 3 * LANES), low),
        ),
    )


def finish_kernel(
    tokens_ref,
    gain_ref,
    g_hidden_ref,
    normed_ref,
    g_attn_ref,
    sums_ref,
    keys_ref,
    mamba_ref,
    back_ref,
    channel_ref,
    gate_ref,
    down_ref,
    gains_ref,
    input_out,
    query_out,
    keyval_out,
    attn_out,
    mamba_out,
    back_out,
    gate_out,
    down_out,
    meta_out,
    ssm_out,
    step_out,
    log_out,
    taps_out,
    rows_out,
    gains_out,
):
    half = normed_ref.shape[1]
    for i in range(2):
        spot = pl.ds(i * half, half)
        rows = tokens_ref[spot, :].astype(jnp.float32)
        scale = lax.rsqrt(jnp.mean(rows * rows, axis=-1, keepdims=True) + epsilon)
        unit = rows * scale
        grad = (normed_ref[i] + g_attn_ref[spot, :]) * gain_ref[...]
        grad = scale * (grad - unit * jnp.mean(grad * unit, axis=-1, keepdims=True))
        input_out[spot, :] = g_hidden_ref[i] + grad
    piece, width = query_out.shape
    rows = pl.ds(0, piece)
    begin = sums_ref.shape[1] - width
    query_out[...] = sums_ref[rows, pl.ds(0, width)]
    attn_out[...] = sums_ref[rows, pl.ds(begin, width)]
    keys_half = keyval_out.shape[1] // 2
    for group in range(keys_half // HEAD):
        pair = keys_ref[rows, pl.ds(2 * group * HEAD, 2 * HEAD)]
        keyval_out[:, pl.ds(group * HEAD, HEAD)] = pair[:, :HEAD]
        keyval_out[:, pl.ds(keys_half + group * HEAD, HEAD)] = pair[:, HEAD:]
    meta = padded_lanes(keys_ref[:, pl.ds(2 * keys_half, meta_out.shape[0])].T, LANES)
    meta_out[...] = meta[:, :piece]
    places = mamba_ref.shape[0]
    lanes = mamba_ref.shape[2] // 2
    inner = mamba_out.shape[1] // places // 2
    for place in range(places):
        value = mamba_ref[place].astype(jnp.float32)
        for part in range(2):
            mamba_out[:, pl.ds((part * places + place) * inner, inner)] = value[
                :piece, part * lanes : part * lanes + inner
            ]
    back_out[...] = back_ref[0, pl.ds(0, back_out.shape[0]), :]
    count = back_out.shape[0]
    ssm_out[...] = channel_ref[0, pl.ds(0, count), pl.ds(FIRST_PROJ, ssm_out.shape[1])]
    channel = channel_ref[0, :, pl.ds(0, LANES)].T
    step_out[...] = channel[: step_out.shape[0], :count]
    log_out[...] = channel[LOG_ROWS, :count]
    taps_out[...] = channel[TAP_ROWS, :count]
    rows_out[...] = channel[TAP_ROWS.start : TAP_ROWS.start + 8, :count]
    gains = (gains_ref[0] + gains_ref[1]).T
    gains_out[...] = gains[: gains_out.shape[0], :piece]
    size = down_out.shape[0]
    top = down_ref.shape[1]
    down_out[pl.ds(0, top), :] = down_ref[0]
    down_out[pl.ds(top, size - top), :] = down_ref[1, pl.ds(0, size - top), :]
    room = gate_ref.shape[3] // SIDE
    for part in range(2):
        for place in range(places):
            value = gate_ref[part, place].astype(jnp.float32)
            first = (part * places + place) * SIDE * size
            parts = [value[:piece, x * room : x * room + size] for x in range(SIDE)]
            gate_out[:, pl.ds(first, SIDE * size)] = jnp.concatenate(parts, axis=1)


def finish(piece, inner_piece, down_piece, inner, proj, rank, *arrays):
    tokens = arrays[0]
    rows, width = tokens.shape
    full = jnp.float32
    keys = arrays[6]
    metas = LANES
    return whole_call(
        "finish",
        finish_kernel,
        arrays,
        (
            ((rows, width), full),
            ((piece, width), full),
            ((piece, keys.shape[1] - metas), full),
            ((piece, width), full),
            ((piece, 2 * 16 * inner), full),
            ((inner_piece, width), full),
            ((piece, 2 * 16 * SIDE * down_piece), full),
            ((down_piece, width), full),
            ((metas, piece), full),
            ((inner_piece, proj), full),
            ((rank, inner_piece), full),
            ((LOG_ROWS.stop - LOG_ROWS.start, inner_piece), full),
            ((CONV, inner_piece), full),
            ((8, inner_piece), full),
            ((8, piece), full),
        ),
    )


def rms_norm(values, gain):
    return values * lax.rsqrt(jnp.mean(values * values, axis=-1, keepdims=True) + epsilon) * gain


def pad_to(array, dim, size):
    widths = [(0, 0)] * array.ndim
    widths[dim] = (0, size - array.shape[dim])
    return jnp.pad(array, widths)


def blank(shapes):
    leaves, nest = jax.tree.flatten(shapes)
    outs = pl.pallas_call(
        lambda *refs: None,
        out_shape=[jax.ShapeDtypeStruct(leaf.shape, leaf.dtype) for leaf in leaves],
        out_specs=[ANY] * len(leaves),
        name="blank",
    )()
    return jax.tree.unflatten(nest, outs)


def order_of(net):
    return (Z, Y) if net.core == 0 else (Y, Z)


def gather_halves(net, name, source, out, patience=0):
    if net.core == 0:
        count = []

        def after(line):
            net.start(
                (name, -3, len(count)),
                out.at[0, line],
                out.at[0, line],
                net.device(other_core=True),
            )
            count.append(line)

        yield from gather_two(net, name, source, out.at[0], (Z, Y), after, patience)
    else:
        yield from gather_two(net, name, source, out.at[1], (Y, Z), None, patience)
        for i in range(SIDE):
            net.copy(
                (name, -3, i), out.at[0, i], out.at[0, i], net.device(other_core=True)
            ).wait_recv()


def reduce_halves(net, name, source, pad, out):
    if net.core == 1:
        for y in range(SIDE):
            net.start(
                (name, -3, y), source.at[0, y], pad.half.at[y], net.device(other_core=True)
            )
        own = net.local((name, -1), source.at[1], pad.half)
        yield
        own.wait()
    else:
        yield
        for y in range(SIDE):
            net.copy(
                (name, -3, y), source.at[0, y], pad.half.at[y], net.device(other_core=True)
            ).wait_recv()
    yield from reduce_two(net, name, pad.half, pad, out, order_of(net))


def share_x(net, name, source, view):
    x = net.at[X]
    core, other = net.core, 1 - net.core
    own = net.local((name, -1), source, view(core, x))
    copies = [
        net.start((name, -2, hop), source, view(core, x), net.device(X, hop)) for hop in HOPS
    ]
    net.start((name, core, 0), source, view(core, x), net.device(other_core=True))
    yield
    for copy, hop in zip(copies, HOPS):
        copy.wait_recv()
        spot = (x - hop + SIDE) % SIDE
        net.start(
            (name, core, hop), view(core, spot), view(core, spot), net.device(other_core=True)
        )
    yield
    for i in (0,) + HOPS:
        net.copy(
            (name, other, i), source, view(other, x), net.device(other_core=True)
        ).wait_recv()
    own.wait()


def swap_cores(net, name, source, out):
    net.start((name, net.core), source, out.at[net.core], net.device(other_core=True))
    own = net.local((name, -1), source, out.at[net.core])
    yield
    net.copy(
        (name, 1 - net.core), source, out.at[1 - net.core], net.device(other_core=True)
    ).wait_recv()
    own.wait()


def hand(net, name, giver, source, target):
    if net.core == giver:
        net.start(name, source, target, net.device(other_core=True))
    else:
        net.copy(name, source, target, net.device(other_core=True)).wait_recv()


def keep_and_hand(net, name, giver, source, target):
    if net.core == giver:
        own = net.local((name, -1), source, target)
    hand(net, (name, 0), giver, source, target)
    yield
    if net.core == giver:
        own.wait()


def reduce_x(net, name, source, pad, out):
    x = net.at[X]
    recv, kept = pad.recv, pad.own
    own = net.local((name, -4), source.at[x], kept)
    copies = [
        net.start(
            (name, 5, hop), source.at[(x + hop) % SIDE], recv.at[hop - 1], net.device(X, hop)
        )
        for hop in HOPS
    ]
    yield
    own.wait()
    for copy in copies:
        copy.wait_recv()

    def put(lead, part, value):
        index = (lead,) if len(out.shape) == 3 else (lead // SIDE, lead % SIDE)
        out[index + (part, slice(None))] = value.astype(out.dtype)

    scatter_sum(
        source.shape[1],
        source.shape[2],
        lambda lead, part: kept[lead, part, :],
        [lambda lead, part, k=k: recv[k, lead, part, :] for k in range(3)],
        put,
    )


def reduce_three(net, name, source, pad, out, order, hold=0):
    left = [Y, Z, X]
    held = source
    stages = ((pad.recv0, pad.mid0), (pad.recv1, pad.mid1), (pad.recv2, out))
    for stage, axis in enumerate(order):
        recv, mid = stages[stage]
        spot = left.index(axis)
        size = len(left)

        def part_of(place, held=held, spot=spot):
            return held.at[(slice(None),) * spot + (place,)]

        if stage == 0:
            fetch = net.local((name, -4), part_of(net.at[axis]), pad.own)
        copies = [
            net.start(
                (name, stage, hop),
                part_of((net.at[axis] + hop) % SIDE),
                recv.at[hop - 1],
                net.device(axis, hop),
            )
            for hop in HOPS
        ]
        yield
        if stage == 0:
            for _ in range(hold):
                yield
            fetch.wait()
        for copy in copies:
            copy.wait_recv()

        def split(lead, size=size):
            return tuple((lead // SIDE**i) % SIDE for i in reversed(range(size - 1)))

        def own(lead, part, held=held, spot=spot, split=split, axis=axis):
            index = split(lead)
            if len(index) == 2:
                return pad.own[index + (part, slice(None))]
            index = index[:spot] + (net.at[axis],) + index[spot:]
            return held[index + (part, slice(None))]

        def put(lead, part, value, mid=mid, split=split):
            mid[split(lead) + (part, slice(None))] = value.astype(mid.dtype)

        scatter_sum(
            SIDE ** (size - 1),
            source.shape[3],
            own,
            [
                lambda lead, part, k=k, recv=recv, split=split: recv[
                    (k,) + split(lead) + (part, slice(None))
                ]
                for k in range(3)
            ],
            put,
        )
        held = mid
        del left[spot]


def three_pad(rows, width, kind=jnp.bfloat16):
    block = (rows, width)
    return dict(
        own=((SIDE, SIDE) + block, kind),
        recv0=((3, SIDE, SIDE) + block, kind),
        mid0=((SIDE, SIDE) + block, kind),
        recv1=((3, SIDE) + block, kind),
        mid1=((SIDE,) + block, kind),
        recv2=((3,) + block, kind),
    )


def two_pad(rows, width, kind=jnp.bfloat16):
    return dict(
        one=((3, SIDE, rows, width), kind),
        mid=((SIDE, rows, width), kind),
        two=((3, rows, width), kind),
        own=((SIDE, rows, width), kind),
    )


def ring_pad(rows, width, kind=jnp.bfloat16):
    half = rows // 2
    return dict(
        one=((2, SIDE, rows, width), kind),
        via_one=((2, SIDE, half, width), kind),
        mix_one=((2, SIDE, half, width), kind),
        mid=((SIDE, rows, width), kind),
        two=((2, rows, width), kind),
        via_two=((2, half, width), kind),
        mix_two=((2, half, width), kind),
        own=((SIDE, rows, width), kind),
    )


def half_pad(rows, width, kind=jnp.bfloat16):
    return dict(two_pad(rows, width, kind), half=((SIDE, SIDE, rows, width), kind))


def shrink_pad(lead, rows, width, kind=jnp.bfloat16):
    return dict(
        mine=((SIDE, lead, rows, width), kind),
        other=((SIDE, lead, rows, width), kind),
        mid=((SIDE, lead, rows, width), kind),
        **x_pad(lead, rows, width, kind),
    )


def x_pad(lead, rows, width, kind=jnp.bfloat16):
    return dict(recv=((3, lead, rows, width), kind), own=((lead, rows, width), kind))


def gather_weights(net, held):
    axes = (Y, Z, X)
    jobs, begin = [], 0
    for i, (target, order) in enumerate(
        ((held.first, (X, Z, Y)), (held.second, (Z, Y, X)), (held.third, (Y, X, Z)))
    ):
        size = target.shape[-1]
        jobs.append(
            gather(net, 5 + i, held.whole.at[:, pl.ds(begin, size)], target, axes, order, hold=3)
        )
        begin += size
    return jobs


def program_start(net, held):
    core = net.core
    rows = held.tokens.shape[0] // 2
    axes = (Y, Z, X)
    jobs = []
    if core == 1:

        def mamba():
            target = held.mamba_all.at[:, :, net.at[X]]
            yield from swap_two(net, 2, held.mamba, held.mamba_mid, target)
            copies = [
                net.start((2, 3, hop), target, target, net.device(X, hop)) for hop in HOPS
            ]
            yield
            for copy in copies:
                copy.wait_recv()

        jobs = [
            mamba(),
            gather(net, 3, held.back, held.back_all, (X,), (X,)),
            gather(net, 4, held.channel, held.channel_all, (X,), (X,)),
        ]
    jobs.append(gather(net, 1, held.small, held.small_all, axes, order_of(net) + (X,)))
    jobs.append(
        gather_halves(net, 0, held.tokens.at[pl.ds(core * rows, rows)], held.tokens_all)
    )
    if core == 0:
        jobs += gather_weights(net, held)
    return jobs


def program_keyval(net, held):
    rows = held.keyval.shape[0] // 2
    return [
        gather_two(
            net,
            i,
            held.keyval.at[pl.ds(i * rows, rows)],
            held.keyval_all.at[i],
            ((Z, Y), (Y, Z))[i],
        )
        for i in range(2)
    ] + [swap_two(net, 2, held.gate.at[0], held.gate_mid, held.gate_own)]


def program_project(net, held):
    jobs = []
    for i, order in enumerate(((Z, Y), (Y, Z))):
        source = (held.first, held.second)[i]
        pad = (held.first_pad, held.second_pad)[i]
        target = (held.first_all, held.second_all)[i]

        def job(source=source, pad=pad, target=target, order=order, i=i):
            yield from reduce_two(net, 2 * i, source, pad, pad.sum, order)
            yield from gather_two(net, 2 * i + 1, pad.sum, target, order)

        jobs.append(job())
    return jobs + [swap_two(net, 4, held.gate, held.gate_mid, held.gate_own)]


def program_mixers(net, held):
    core = net.core
    half = held.down.shape[0] // 2
    rows = held.attn_pre.shape[0] // 2

    def attn():
        if core == 0:
            own = net.local((1, -1), held.attn_pre.at[pl.ds(0, rows)], held.attn_half)
        hand(net, (1, 0), 0, held.attn_pre.at[pl.ds(rows, rows)], held.attn_half)
        yield
        if core == 0:
            own.wait()

    return [
        attn(),
        reduce_halves(net, 0, held.partial, held.pad, held.mamba_pre),
        share_x(
            net,
            2,
            held.gate_first if core == 0 else held.gate_second,
            lambda b, x: held.gate_all.at[b, :, :, x],
        ),
        share_x(
            net,
            3,
            held.down.at[pl.ds(core * half, half)],
            lambda b, x: held.down_all.at[x, pl.ds(b * half, half)],
        ),
    ]


def program_feed(net, held):
    return [gather_two(net, 0, held.feed, held.feed_all, order_of(net))]


def program_ffn(net, held):
    return [
        reduce_ring(net, 0, held.out, held.out_pad, held.out_sum, order_of(net)),
        reduce_ring(net, 1, held.grad, held.grad_pad, held.grad_sum, order_of(net)),
    ]


def shrink(net, name, source, pad, out):
    core = net.core
    lead, rows = source.shape[2:4]
    mine = net.local((name, -5), source.at[core], pad.mine)
    net.start((name, 6, core), source.at[1 - core], pad.other, net.device(other_core=True))
    yield
    net.copy(
        (name, 6, 1 - core), source.at[1 - core], pad.other, net.device(other_core=True)
    ).wait_recv()

    mine.wait()

    def put(i, part, value):
        pad.mid[i // lead, i % lead, part, :] = value.astype(pad.mid.dtype)

    scatter_sum(
        SIDE * lead,
        rows,
        lambda i, part: pad.mine[i // lead, i % lead, part, :],
        [lambda i, part: pad.other[i // lead, i % lead, part, :]],
        put,
    )
    yield from reduce_x(net, name, pad.mid, pad, out)


def program_back(net, held):
    core = net.core

    def attn():
        if core == 0:
            own = net.local((5, -1), held.g_attn, held.g_attn_both.at[0])
        hand(net, (5, 0), 1, held.g_attn, held.g_attn_both.at[1])
        yield
        if core == 0:
            own.wait()

    return [
        swap_cores(net, 3, held.mixed, held.mixed_both),
        swap_cores(net, 4, held.g_hidden, held.g_hidden_both),
        attn(),
        shrink(net, 1, held.g_gate, held.gate_pad, held.g_gate_sum),
        shrink(net, 2, held.g_down, held.down_pad, held.g_down_sum),
        gather_halves(net, 0, held.g_mamba, held.g_mamba_all, patience=1),
    ]


SUMS = ("one", "two", "three", "four", "five", "six")
ORDERS = ((Y, Z, X), (X, Y, Z), (Z, X, Y), (Y, Z, X), (X, Y, Z), (Z, X, Y))


def program_attention(net, held):
    rows = held.keyval.shape[2] // 2
    parts = [getattr(held.parts, name) for name in SUMS]
    taken = [
        net.local((20, i), getattr(held.sources, name), getattr(held.inside, name))
        for i, name in enumerate(INSIDE)
    ]

    def weight(i, source, hold=0):
        pad = getattr(held.pads, SUMS[i])
        return reduce_three(net, 10 + i, source, pad, parts[i], ORDERS[i], hold)

    def keyval(i):
        pad = (held.upper_pad, held.lower_pad)[i]
        return reduce_two(
            net,
            i,
            held.keyval.at[:, :, pl.ds(i * rows, rows)],
            pad,
            held.keyval_sum.at[pl.ds(i * rows, rows)],
            ((Z, Y), (Y, Z))[i],
        )

    def follow():
        for _ in range(3):
            yield
        for copy in taken:
            copy.wait()
        inside = held.inside
        attention_inputs_kernel(
            held.keyval_sum,
            inside.g_query,
            inside.wide,
            inside.meta_wide,
            inside.g_meta,
            inside.first,
            inside.second,
            inside.meta,
            inside.gain,
            held.keys.four,
            held.keys.five,
            held.keys.six,
            held.g_normed,
            held.gain_part,
            held.meta_gain,
        )
        places = held.keys.four.shape[0] // SIDE**3

        def cubed(ref):
            return ref.reshape(SIDE, SIDE, SIDE, places, ref.shape[1])

        later = [weight(3 + i, cubed(ref)) for i, ref in enumerate(vars(held.keys).values())]
        while later:
            later = [job for job in later if next(job, True) is None]
            yield

    def last():
        for _ in range(9):
            yield
        begin = 0
        for part in parts[:3]:
            held.sums[:, pl.ds(begin, part.shape[1])] = part[...]
            begin += part.shape[1]
        begin = 0
        for part in parts[3:]:
            held.keys_sum[:, pl.ds(begin, part.shape[1])] = part[...]
            begin += part.shape[1]

    return [
        keyval(0),
        keyval(1),
        swap_two(net, 3, held.gate, held.gate_mid, held.gate_own),
        follow(),
        *(weight(i, getattr(held, SUMS[i]), 2) for i in range(3)),
        last(),
    ]


def program_end(net, held):
    core = net.core

    def normed():
        yield from reduce_halves(net, 0, held.partial, held.normed_pad, held.normed_sum)
        yield from swap_cores(net, 1, held.normed_sum, held.normed_both)

    def gains():
        yield from reduce_three(
            net, 2, held.gains, held.gains_pad, held.gains_sum, order_of(net) + (X,)
        )
        yield from swap_cores(net, 3, held.gains_sum, held.gains_both)

    def mamba():
        if core == 1:
            yield from reduce_x(net, 4, held.mamba, held.mamba_pad, held.mamba_part)
            yield from swap_two(net, 5, held.mamba_part, held.mamba_mid, held.mamba_sum)
        else:
            for _ in range(4):
                yield
        hand(net, (6, 0), 1, held.mamba_sum, held.mamba_sum)

    def channel(name, source, pad, total):
        if core == 1:
            yield from reduce_x(net, name, source, pad, total)
        else:
            for _ in range(2):
                yield
        hand(net, (name, 0), 1, total, total)

    return [
        normed(),
        mamba(),
        channel(7, held.back, held.back_pad, held.back_sum),
        channel(8, held.channel, held.channel_pad, held.channel_sum),
        gains(),
        keep_and_hand(net, 9, 0, held.g_attn, held.g_attn_both),
        keep_and_hand(net, 10, 0, held.sums_in, held.sums),
        keep_and_hand(net, 12, 0, held.keys, held.keys_sum),
        swap_cores(net, 13, held.gate, held.gate_both),
        swap_cores(net, 14, held.down, held.down_both),
    ]


def padded_blocks(rows, count, size, kind=jnp.bfloat16):
    width = rows.shape[-1]
    return pad_to(rows.reshape(count, -1, width), 1, size).astype(kind)


def shards(
    tokens,
    seq_lengths,
    norm_gain,
    meta_tokens,
    w_query,
    w_key_value,
    w_attn_out,
    attn_gain,
    w_mamba_in,
    conv_weight,
    conv_bias,
    w_ssm_x,
    w_dt,
    dt_bias,
    a_log,
    skip_d,
    w_mamba_out,
    mamba_gain,
    ffn_gain,
    w_gate_up,
    w_down,
    cotangent,
):
    low = jnp.bfloat16
    full = jnp.float32
    core = lax.axis_index("branch")
    on_attention = core == 0
    tokens_b, cotangent_b = tokens[0], cotangent[0]
    rows, width = tokens_b.shape
    half = rows // 2
    group = rows * 16
    piece = w_query.shape[0]
    query_width = w_query.shape[1]
    keys_width = w_key_value.shape[1]
    inner_piece = w_mamba_out.shape[0]
    inner = inner_piece * SIDE
    rank = w_dt.shape[0]
    states = a_log.shape[0]
    proj = rank + 2 * states
    proj_pad = 136
    metas = meta_tokens.shape[0]
    down_piece = w_down.shape[0]
    units = 96 * SIDE
    row_start = core * half

    lengths = seq_lengths[0]
    end_rows = jnp.cumsum(lengths)
    start_rows = end_rows - lengths
    all_rows = jnp.arange(group, dtype=jnp.int32)
    my_rows = lax.axis_index("seq") * rows + jnp.arange(rows, dtype=jnp.int32)

    def begins(row_ids):
        started = row_ids[:, None] >= start_rows[None, :]
        return jnp.max(jnp.where(started, start_rows[None, :], 0), axis=1)

    dist = (all_rows - begins(all_rows))[:, None]
    left = jnp.where(all_rows[:, None] < end_rows[None, :], end_rows[None, :], group)
    left = (jnp.min(left, axis=1) - 1 - all_rows)[:, None]
    reset = jnp.where(dist == 0, far_away, 0.0).astype(jnp.float32)

    attention_in, mamba_in, back_in, gate_in, down_in, small_in, channel_in = prepare(
        w_query,
        w_key_value,
        w_attn_out,
        w_mamba_in,
        w_mamba_out,
        w_gate_up,
        w_down,
        meta_tokens,
        *(gain[None] for gain in (norm_gain, attn_gain, mamba_gain, ffn_gain)),
        w_dt,
        a_log,
        conv_weight,
        *(row[None] for row in (conv_bias, dt_bias, skip_d)),
        w_ssm_x,
    )
    query_most = -(-query_width // LANES) * LANES
    third = 10 * LANES
    last_third = attention_in.shape[1] - 2 * third
    mamba_in = mamba_in.reshape(SIDE, SIDE, 32, -1)
    gate_in = gate_in.reshape(2, SIDE, SIDE, 32, units)
    cube = (SIDE, SIDE, SIDE)

    begun = exchange(
        "exchange_start",
        0,
        program_start,
        dict(
            tokens=(tokens_b, ANY),
            small=(small_in, ANY),
            mamba=(mamba_in, ANY),
            back=(back_in, ANY),
            channel=(channel_in, ANY),
            whole=(attention_in, ANY),
        ),
        dict(
            tokens_all=((2, SIDE, SIDE, half, width), low, ANY),
            small_all=(cube + small_in.shape, low, ANY),
            mamba_all=(cube + mamba_in.shape[2:], low, ANY),
            back_all=((SIDE,) + back_in.shape, low, ANY),
            channel_all=((SIDE,) + channel_in.shape, low, ANY),
            first=(cube + (32, third), low, ANY),
            second=(cube + (32, third), low, ANY),
            third=(cube + (32, last_third), low, ANY),
        ),
        dict(mamba_mid=(mamba_in.shape, low)),
    )
    weight_one, weight_two, weight_three = (
        part.reshape(64 * 32, -1) for part in (begun.first, begun.second, begun.third)
    )
    meta_f, gains = unpack(begun.small_all.reshape(64 * 32, -1), metas, width)
    gain_norm, gain_attn, gain_mamba, gain_feed = (gains[i] for i in range(4))
    gain_row = gains[:1]

    def on_core(which, work):
        shapes = jax.eval_shape(work)
        return lax.cond(core == which, work, lambda: blank(shapes))


    normed_wide, query_b, keyval_b, meta_wide, meta_kv = on_core(
        0,
        lambda: attention_project(
            tokens_b, meta_f, gain_row, weight_one, weight_two, query_width, keys_width
        ),
    )
    keyval = exchange(
        "exchange_keyval",
        2,
        program_keyval,
        dict(keyval=(keyval_b, ANY), gate=(gate_in, ANY)),
        dict(
            keyval_all=((2, SIDE, SIDE, half, keys_width), low, ANY),
            gate_own=((SIDE, SIDE, 32, units), low, ANY),
        ),
        dict(gate_mid=((SIDE, SIDE, 32, units), low)),
        cores=(0,),
    )

    mamba_wide = begun.mamba_all.reshape(64 * 32, -1)
    back_wide = begun.back_all.reshape(-1, width)
    normed_all, conv_in, gate_z, inputs_b, proj_first, proj_second, weight_mamba, channel = on_core(
        1,
        lambda: mixer_project(
            begun.tokens_all.reshape(2, 16, half, width),
            gain_row,
            mamba_wide,
            begun.channel_all.reshape(4 * 64, -1),
            dist,
        ),
    )

    def proj_pads(size):
        return dict(
            two_pad(size, rows, jnp.float32), sum=((size, rows), jnp.float32)
        )

    def spread_projection(name, number, first, second, gate):
        cuts = (PROJ_CUT, proj_pad - PROJ_CUT)
        results = exchange(
            name,
            number,
            program_project,
            dict(
                first=(first.reshape(SIDE, SIDE, cuts[0], rows), ANY),
                second=(second.reshape(SIDE, SIDE, cuts[1], rows), ANY),
                gate=(gate, ANY),
            ),
            dict(
                first_all=((SIDE, SIDE, cuts[0], rows), jnp.float32, ANY),
                second_all=((SIDE, SIDE, cuts[1], rows), jnp.float32, ANY),
                gate_own=((SIDE, SIDE, 32, units), low, ANY),
            ),
            dict(
                first_pad=proj_pads(cuts[0]),
                second_pad=proj_pads(cuts[1]),
                gate_mid=((SIDE, SIDE, 32, units), low),
            ),
            vmem=32 * 2**20,
            cores=(1,),
        )
        whole = [part.reshape(16, -1, rows) for part in (results.first_all, results.second_all)]
        return whole + [results.gate_own]

    step_first, step_second, gate_second = spread_projection("exchange_project", 3, proj_first, proj_second, gate_in[1])
    keyval_all = keyval.keyval_all.reshape(2, 16, half, keys_width)

    cotangent_b, step_second = lax.optimization_barrier((cotangent_b, step_second))
    cotangent_part = lax.dynamic_slice_in_dim(cotangent_b, row_start, half, 0)
    cotangent_all = lax.all_gather(cotangent_part, "seq", axis=0, tiled=True)

    my_starts = jnp.max(
        jnp.where(my_rows[:, None] >= start_rows[None, :], start_rows[None, :], 0), axis=1
    )
    bounds = jnp.stack([my_starts, my_rows], axis=1).astype(jnp.int32)
    key_blocks = (my_rows[-1:] // KEY_ROWS + 1).astype(jnp.int32)

    attended, mass, attended_wide, attn_pre = on_core(
        0,
        lambda: attend_forward(
            key_blocks, query_b, keyval_all, meta_kv, bounds, weight_two, weight_three
        ),
    )

    col_rows = slice(rank - PROJ_CUT, proj - PROJ_CUT)

    def mamba_core():
        cols = step_second[:, col_rows].transpose(1, 0, 2).reshape(-1, CHUNKS, STEPS)
        cols = cols.transpose(0, 2, 1)
        results = mixer_forward(
            inner, step_first, step_second, cols, channel, inputs_b, reset, gate_z, back_wide
        )
        return [cols] + list(results)

    cols, partial, mixed_y, ssm_out, starts, decay_t, drive_t, scan_rate = on_core(1, mamba_core)

    mixers = exchange(
        "exchange_mixers",
        4,
        program_mixers,
        dict(
            partial=(partial.reshape(2, SIDE, SIDE, half, width), ANY),
            attn_pre=(attn_pre, ANY),
            gate_first=(keyval.gate_own, ANY),
            gate_second=(gate_second, ANY),
            down=(down_in, ANY),
        ),
        dict(
            mamba_pre=((half, width), jnp.float32, VMEM),
            attn_half=((half, width), jnp.float32, ANY),
            gate_all=((2,) + cube + (32, units), low, ANY),
            down_all=((SIDE,) + down_in.shape, low, ANY),
        ),
        dict(pad=half_pad(half, width)),
        vmem=32 * 2**20,
    )
    tokens_part = lax.dynamic_slice_in_dim(tokens_b, row_start, half, 0).astype(full)
    sent = rms_norm(mixers.attn_half, gain_attn).astype(low).astype(jnp.float32)
    sent = sent + rms_norm(mixers.mamba_pre, gain_mamba).astype(low).astype(jnp.float32)
    hidden = tokens_part + 0.5 * sent
    feed = exchange(
        "exchange_feed",
        5,
        program_feed,
        dict(feed=(rms_norm(hidden, gain_feed).astype(low), ANY)),
        dict(feed_all=((SIDE, SIDE, half, width), low, ANY)),
    ).feed_all.reshape(16 * half, width)
    out_partial, feed_partial, g_gate, g_down = feed_forward(
        feed,
        cotangent_all,
        mixers.gate_all.reshape(2, 64 * 32, units),
        mixers.down_all.reshape(units, width),
    )
    ffn = exchange(
        "exchange_ffn",
        6,
        program_ffn,
        dict(
            out=(out_partial.reshape(SIDE, SIDE, half, width), ANY),
            grad=(feed_partial.reshape(SIDE, SIDE, half, width), ANY),
        ),
        dict(
            out_sum=((half, width), jnp.float32, VMEM),
            grad_sum=((half, width), jnp.float32, VMEM),
        ),
        dict(out_pad=ring_pad(half, width), grad_pad=ring_pad(half, width)),
        vmem=48 * 2**20,
    )
    mixed_part = (hidden + ffn.out_sum).astype(low)
    cotangent_f = cotangent_part.astype(jnp.float32)
    _, pull_feed = jax.vjp(rms_norm, hidden, gain_feed)
    grad_hidden_norm, grad_gain_feed = pull_feed(ffn.grad_sum)
    grad_hidden = cotangent_f + grad_hidden_norm
    grad_sent = 0.5 * grad_hidden
    _, pull_attn = jax.vjp(rms_norm, mixers.attn_half, gain_attn)
    grad_attn_pre, grad_gain_attn = pull_attn(grad_sent)
    _, pull_mamba = jax.vjp(rms_norm, mixers.mamba_pre, gain_mamba)
    grad_mamba_pre, grad_gain_mamba = pull_mamba(grad_sent)

    back = exchange(
        "exchange_back",
        7,
        program_back,
        dict(
            g_mamba=(grad_mamba_pre.astype(low), ANY),
            g_attn=(grad_attn_pre.astype(low), ANY),
            mixed=(mixed_part, ANY),
            g_hidden=(grad_hidden, ANY),
            g_gate=(g_gate, ANY),
            g_down=(g_down, ANY),
        ),
        dict(
            g_mamba_all=((2, SIDE, SIDE, half, width), low, ANY),
            g_attn_both=((2, half, width), low, ANY),
            mixed_both=((2, half, width), low, ANY),
            g_hidden_both=((2, half, width), jnp.float32, ANY),
            g_gate_sum=((16, 32, units), low, VMEM),
            g_down_sum=((1, 48, width), jnp.float32, VMEM),
        ),
        dict(gate_pad=shrink_pad(16, 32, units), down_pad=shrink_pad(1, 48, width)),
        vmem=32 * 2**20,
    )
    mixed = back.mixed_both.reshape(rows, width)
    g_gate_own = back.g_gate_sum.reshape(SIDE, SIDE, 32, units)

    cuts = (8 * LANES, 9 * LANES, query_most + width - 17 * LANES)

    def attention_back_one():
        g_pre = back.g_attn_both.reshape(rows, width)
        g_query, g_keyval, g_meta = attend_backward(
            key_blocks,
            query_b,
            keyval_all,
            meta_kv,
            bounds.T,
            attended,
            mass,
            g_pre,
            weight_two,
            weight_three,
        )
        pieces = attention_weights(
            normed_wide, attended_wide, g_query, g_pre, weight_one, weight_two, cuts
        )
        return [g_query, g_keyval, g_meta] + list(pieces)

    grad_query_b, grad_keyval, grad_meta_kv, sum_one, sum_two, sum_three, gain_query = on_core(
        0, attention_back_one
    )

    def cubed(blocks):
        return blocks.reshape(cube + (32, blocks.shape[-1]))

    small_cuts = (keys_width // 2, keys_width // 2, metas)
    sources = (
        grad_query_b,
        normed_wide,
        meta_wide,
        grad_meta_kv,
        weight_one,
        weight_two,
        meta_f,
        gain_row,
    )
    attention = exchange(
        "exchange_attention",
        8,
        program_attention,
        dict(
            keyval=(grad_keyval.reshape(SIDE, SIDE, rows, keys_width), ANY),
            gate=(g_gate_own, ANY),
            one=(cubed(sum_one), ANY),
            two=(cubed(sum_two), ANY),
            three=(cubed(sum_three), ANY),
            sources={name: (array, ANY) for name, array in zip(INSIDE, sources)},
        ),
        dict(
            gate_own=((SIDE, SIDE, 32, units), low, ANY),
            sums=((32, query_most + width), full, VMEM),
            keys_sum=((32, keys_width + metas), full, VMEM),
            g_normed=((rows, width), full, VMEM),
            gain_part=((64 * 32, 1), full, VMEM),
            meta_gain=((1, width), full, VMEM),
        ),
        dict(
            upper_pad=two_pad(half, keys_width),
            lower_pad=two_pad(half, keys_width),
            gate_mid=((SIDE, SIDE, 32, units), low),
            keyval_sum=((rows, keys_width), full),
            inside={name: (array.shape, array.dtype) for name, array in zip(INSIDE, sources)},
            keys=dict(zip(SUMS[3:], (((64 * 32, cut), low) for cut in small_cuts))),
            pads=dict(zip(SUMS, (three_pad(32, cut) for cut in cuts + small_cuts))),
            parts=dict(zip(SUMS, (((32, cut), full) for cut in cuts + small_cuts))),
        ),
        vmem=62 * 2**20,
        cores=(0,),
    )
    gain_attention = (gain_query + attention.gain_part).reshape(64, 32)[:, :piece].reshape(width)
    gain_attention = gain_attention / gain_norm + attention.meta_gain[0]

    def mamba_back_one():
        g_first, g_second, g_cols, *rest = mixer_backward(
            inner,
            step_first,
            step_second,
            cols,
            channel,
            inputs_b,
            gate_z,
            back_wide,
            back.g_mamba_all.reshape(2, 16, half, width),
            mixed_y,
            ssm_out,
            starts,
            decay_t,
            drive_t,
            scan_rate,
        )
        g_cols = g_cols.transpose(0, 2, 1).reshape(-1, 16, rows).transpose(1, 0, 2)
        g_second = jnp.concatenate([g_second[:, : rank - PROJ_CUT], g_cols], axis=1)
        return [g_first, pad_to(g_second, 1, proj_pad - PROJ_CUT)] + list(rest)

    g_first, g_second, grad_inputs, grad_gate_z, back_out, grad_rows, grad_rate = on_core(
        1, mamba_back_one
    )
    g_first, g_second, last_gate = spread_projection(
        "exchange_last", 9, g_first, g_second, g_gate_own
    )

    def mamba_back_two():
        g_normed, g_weight, g_rows, gain = mixer_inputs(
            g_first,
            g_second,
            channel,
            weight_mamba,
            normed_all,
            conv_in,
            inputs_b,
            grad_inputs,
            grad_gate_z,
            dist,
            left,
        )
        return g_normed, g_weight, channel_grads(grad_rows, g_rows, grad_rate, channel), gain

    grad_normed_partial, mamba_out, channel_out, gain_mixer = on_core(1, mamba_back_two)
    gain_mixer = gain_mixer[:, 0] / gain_norm
    grad_gain_norm = jnp.where(on_attention, gain_attention, gain_mixer)
    gains_out = jnp.stack([grad_gain_norm, grad_gain_attn, grad_gain_mamba, grad_gain_feed], axis=1)
    gains_out = padded_blocks(pad_to(gains_out, 1, 128), 64, 32)
    ended = exchange(
        "exchange_end",
        1,
        program_end,
        dict(
            partial=(grad_normed_partial.reshape(2, SIDE, SIDE, half, width), ANY),
            g_attn=(attention.g_normed, ANY),
            sums_in=(attention.sums, ANY),
            keys=(attention.keys_sum, ANY),
            gate=(jnp.where(on_attention, attention.gate_own, last_gate), ANY),
            down=(back.g_down_sum.reshape(48, width), ANY),
            mamba=(mamba_out, ANY),
            back=(back_out, ANY),
            channel=(channel_out, ANY),
            gains=(gains_out.reshape(cube + (32, 128)), ANY),
        ),
        dict(
            normed_both=((2, half, width), full, ANY),
            g_attn_both=((rows, width), full, ANY),
            sums=((32, query_most + width), full, ANY),
            keys_sum=((32, keys_width + metas), full, ANY),
            gate_both=((2, SIDE, SIDE, 32, units), low, ANY),
            down_both=((2, 48, width), full, ANY),
            mamba_sum=((SIDE, SIDE, 32, 4 * CHUNKS), low, ANY),
            back_sum=((1, 64, width), full, VMEM),
            channel_sum=((1, 64, 3 * LANES), full, VMEM),
            gains_both=((2, 32, 128), full, ANY),
        ),
        dict(
            normed_pad=half_pad(half, width),
            normed_sum=((half, width), full),
            gains_pad=three_pad(32, 128),
            gains_sum=((32, 128), full),
            mamba_pad=x_pad(16, 32, 4 * CHUNKS),
            mamba_part=((SIDE, SIDE, 32, 4 * CHUNKS), low),
            mamba_mid=((SIDE, SIDE, 32, 4 * CHUNKS), low),
            back_pad=x_pad(1, 64, width),
            channel_pad=x_pad(1, 64, 3 * LANES, full),
        ),
        vmem=48 * 2**20,
    )
    (
        input_grad,
        grad_query,
        grad_keyval_in,
        grad_attn,
        grad_mamba,
        grad_back,
        grad_gate,
        grad_down,
        grad_meta,
        grad_ssm,
        grad_step,
        grad_log,
        grad_taps,
        grad_rows,
        grad_gains,
    ) = finish(
        piece,
        inner_piece,
        down_piece,
        inner,
        proj,
        rank,
        tokens_b,
        gain_row,
        back.g_hidden_both,
        ended.normed_both,
        ended.g_attn_both,
        ended.sums,
        ended.keys_sum,
        ended.mamba_sum.reshape(16, 32, -1),
        ended.back_sum,
        ended.channel_sum,
        ended.gate_both.reshape(2, 16, 32, units),
        ended.down_both,
        ended.gains_both,
    )
    return (
        mixed[None],
        input_grad[None],
        grad_gains[0],
        grad_meta,
        grad_query,
        grad_keyval_in,
        grad_attn,
        grad_gains[1],
        grad_mamba,
        grad_taps,
        grad_rows[4],
        grad_ssm,
        grad_step,
        grad_rows[5],
        grad_log,
        grad_rows[6],
        grad_back,
        grad_gains[2],
        grad_gains[3],
        grad_gate,
        grad_down,
    )


def solution(mesh):
    spread = ("seq", "fsdp")
    rows = P("fsdp", "seq", None)
    flat, first, second = P(spread), P(spread, None), P(None, spread)
    weights = (
        flat,
        second,
        first,
        first,
        first,
        flat,
        first,
        second,
        flat,
        first,
        second,
        flat,
        second,
        flat,
        first,
        flat,
        flat,
        first,
        first,
    )
    return jax.shard_map(
        shards,
        mesh=mesh,
        in_specs=(rows, P("fsdp", None)) + weights + (rows,),
        out_specs=(rows, rows) + weights,
        check_vma=False,
    )
```

```python
import functools
import types

import jax
import jax.numpy as jnp
from jax import lax
from jax.experimental import pallas as pl
from jax.experimental.pallas import tpu as pltpu
from jax.sharding import PartitionSpec as P

HEAD = 64
CONV = 4
SIDE = 4

epsilon = 1e-05
negative_fill = -1e30
score_scale = 0.125
log2_e = 1.4426950408889634
highest = lax.Precision.HIGHEST
MESH = pl.DeviceIdType.MESH
ANY = pl.BlockSpec(memory_space=pl.ANY)
VMEM = pl.BlockSpec(memory_space=pltpu.VMEM)
SEMS = 128
HOPS = (1, 3, 2)
X, Y, Z, FIRST, SECOND = range(5)


class Net:
    def __init__(self, core, coords, names, send, recv):
        self.core = core
        self.at = coords
        self.names = names
        self.send = send
        self.recv = recv
        self.begun = []

    def device(self, axis=None, hop=0, other_core=False, partner=False):
        place = dict(self.at)
        if partner:
            place[Y], place[Z] = SIDE - 1 - place[Y], SIDE - 1 - place[Z]
        if axis in (FIRST, SECOND):
            along_z = self.core == (0 if axis == FIRST else 1)
            place[Y] = jnp.where(along_z, place[Y], (place[Y] + hop) % SIDE)
            place[Z] = jnp.where(along_z, (place[Z] + hop) % SIDE, place[Z])
        elif axis is not None:
            place[axis] = (place[axis] + hop) % SIDE
        core = 1 - self.core if other_core else self.core
        return (core, place[Y] * SIDE + place[Z], place[X])

    def slot(self, name):
        return self.names.setdefault(name, len(self.names))

    def copy(self, name, source, target, device):
        i = self.slot(name)
        return pltpu.make_async_remote_copy(
            source,
            target,
            self.send.at[i],
            self.recv.at[i],
            device_id=device,
            device_id_type=MESH,
        )

    def start(self, name, source, target, device):
        copy = self.copy(name, source, target, device)
        copy.start()
        self.begun.append(copy)
        return copy

    def local(self, name, source, target):
        copy = pltpu.make_async_copy(source, target, self.send.at[self.slot(name)])
        copy.start()
        return copy


def pick(axes, fixed):
    return tuple(fixed.get(axis, slice(None)) for axis in axes)


def gather(net, name, source, out, axes, order, hold=0):
    at = net.at
    fixed = {axis: at[axis] for axis in axes}
    own = net.local((name, -1), source, out.at[pick(axes, fixed)])
    here = source
    for axis in order:
        if axis == order[-1]:
            for _ in range(hold):
                yield
        place = pick(axes, fixed)
        copies = [
            net.start(
                (name, axis, hop),
                out.at[place] if here is None else here,
                out.at[place],
                net.device(axis, hop),
            )
            for hop in HOPS
        ]
        yield
        for copy in copies:
            copy.wait_recv()
        if here is not None:
            own.wait()
        here = None
        del fixed[axis]


def gather_two(net, name, source, out, order, after=None, patience=0):
    at = net.at
    first, second = order

    def place(back):
        spot = dict(at)
        spot[first] = (spot[first] - back + SIDE) % SIDE
        return (spot[Y], spot[Z])

    mine = place(0)
    own = net.local((name, -1), source, out.at[mine])
    ones = [
        net.start((name, 1, hop), source, out.at[mine], net.device(first, hop)) for hop in HOPS
    ]
    twos = []

    def forward(back):
        spot = place(back)
        for hop in HOPS:
            twos.append(
                net.start(
                    (name, 2, back, hop),
                    source if back == 0 else out.at[spot],
                    out.at[spot],
                    net.device(second, hop),
                )
            )

    forward(0)
    yield
    for copy, hop in zip(ones, HOPS):
        copy.wait_recv()
        forward(hop)
    own.wait()
    for _ in range(1 + patience):
        yield
    if after is None:
        for copy in twos:
            copy.wait_recv()
        return
    lines = [twos[3 * i : 3 * i + 3] for i in range(SIDE)]
    after(at[second])
    for h, hop in enumerate(HOPS):
        for line in lines:
            line[h].wait_recv()
        after((at[second] - hop + SIDE) % SIDE)


NEAR = (1, 3)


def scatter_sum(total, rows, own, others, out):
    chunk = 16 if rows % 16 == 0 else 8
    per = rows // chunk

    def step(i, carry):
        lead = i // per
        part = pl.ds(pl.multiple_of((i % per) * chunk, chunk), chunk)
        value = own(lead, part).astype(jnp.float32)
        for other in others:
            value = value + other(lead, part).astype(jnp.float32)
        out(lead, part, value)
        return carry

    lax.fori_loop(0, total * per, step, 0)


def reduce_two(net, name, source, pad, out, order):
    at = net.at
    first, second = order
    one, mid, two, kept = pad.one, pad.mid, pad.two, pad.own
    rows = source.shape[2]

    def part_of(line):
        return source.at[:, line] if first == Z else source.at[line]

    own = net.local((name, -4), part_of(at[first]), kept)
    ones = [
        net.start(
            (name, 1, hop),
            part_of((at[first] + hop) % SIDE),
            one.at[hop - 1],
            net.device(first, hop),
        )
        for hop in HOPS
    ]
    yield
    own.wait()
    for copy in ones:
        copy.wait_recv()

    def put_mid(lead, part, value):
        mid[lead, part, :] = value.astype(mid.dtype)

    scatter_sum(
        SIDE,
        rows,
        lambda lead, part: kept[lead, part, :],
        [lambda lead, part, k=k: one[k, lead, part, :] for k in range(3)],
        put_mid,
    )
    twos = [
        net.start(
            (name, 2, hop),
            mid.at[(at[second] + hop) % SIDE],
            two.at[hop - 1],
            net.device(second, hop),
        )
        for hop in HOPS
    ]
    yield
    for copy in twos:
        copy.wait_recv()
    spot = at[second]

    def put_out(lead, part, value):
        out[part, :] = value.astype(out.dtype)

    scatter_sum(
        1,
        rows,
        lambda lead, part: kept[spot, part, :],
        [lambda lead, part, k=k: one[k, spot, part, :] for k in range(3)]
        + [lambda lead, part, k=k: two[k, part, :] for k in range(3)],
        put_out,
    )


def reduce_ring(net, name, source, pad, out):
    at = net.at
    rows = source.shape[2]
    half = rows // 2
    halves = {1: pl.ds(0, half), 3: pl.ds(half, half)}
    stages = (
        (FIRST, pad.one, pad.via_one, pad.mix_one),
        (SECOND, pad.two, pad.via_two, pad.mix_two),
    )

    def lines(stage, place, part):
        return pad.mid.at[place, part] if stage else source.at[place, :, part]

    whole = pl.ds(0, rows)
    for stage, (axis, recv, via, mix) in enumerate(stages):

        def spot(hop, axis=axis):
            return (at[axis] + hop) % SIDE

        arrivals, fetched, passing = [], [], []
        if stage == 0:
            yield
        for i, hop in enumerate(NEAR):
            across = lines(stage, spot(2), halves[hop])
            passing.append(
                net.start((name, stage, 0, hop), across, via.at[i], net.device(axis, hop))
            )
        for i, hop in enumerate(NEAR):
            if stage == 0:
                yield
            other = halves[4 - hop]
            fetched.append(
                net.local((name, stage, 3, hop), lines(stage, spot(hop), halves[hop]), mix.at[i])
            )
            target = recv.at[i, other] if stage else recv.at[i, :, other]
            arrivals.append(
                net.start(
                    (name, stage, 1, hop),
                    lines(stage, spot(hop), other),
                    target,
                    net.device(axis, hop),
                )
            )
        if stage == 0:
            yield
            own = net.local((name, -4), lines(0, spot(0), whole), pad.own)
        yield
        for i, hop in enumerate(NEAR):
            fetched[i].wait()
            passing[i].wait_recv()

            def put(lead, part, value, i=i, mix=mix, stage=stage):
                index = (i, part) if stage else (i, lead, part)
                mix[index + (slice(None),)] = value.astype(mix.dtype)

            def get(ref, i=i, stage=stage):
                if stage:
                    return lambda lead, part: ref[i, part, :]
                return lambda lead, part: ref[i, lead, part, :]

            scatter_sum(1 if stage else SIDE, half, get(mix), [get(via)], put)
            target = recv.at[i, halves[hop]] if stage else recv.at[i, :, halves[hop]]
            arrivals.append(
                net.start((name, stage, 2, hop), mix.at[i], target, net.device(axis, hop))
            )
        yield
        for copy in arrivals:
            copy.wait_recv()
        if stage == 0:
            own.wait()

            def put_mid(lead, part, value):
                pad.mid[lead, part, :] = value.astype(pad.mid.dtype)

            scatter_sum(
                SIDE,
                rows,
                lambda lead, part: pad.own[lead, part, :],
                [lambda lead, part, k=k: pad.one[k, lead, part, :] for k in range(2)],
                put_mid,
            )
    mine = at[SECOND]

    def put_out(lead, part, value):
        out[part, :] = value.astype(out.dtype)

    scatter_sum(
        1,
        rows,
        lambda lead, part: pad.own[mine, part, :],
        [lambda lead, part, k=k: pad.one[k, mine, part, :] for k in range(2)]
        + [lambda lead, part, k=k: pad.two[k, part, :] for k in range(2)],
        put_out,
    )


def swap_two(net, name, source, mid, out):
    at = net.at
    own = net.local((name, -1), source.at[:, at[Z]], mid.at[at[Z]])
    ones = [
        net.start(
            (name, 1, hop),
            source.at[:, (at[Z] + hop) % SIDE],
            mid.at[at[Z]],
            net.device(Z, hop),
        )
        for hop in HOPS
    ]
    yield
    for copy in ones:
        copy.wait_recv()
    own.wait()
    own = net.local((name, -2), mid.at[:, at[Y]], out.at[at[Y]])
    twos = [
        net.start(
            (name, 2, hop),
            mid.at[:, (at[Y] + hop) % SIDE],
            out.at[at[Y]],
            net.device(Y, hop),
        )
        for hop in HOPS
    ]
    yield
    for copy in twos:
        copy.wait_recv()
    own.wait()


def run_jobs(jobs):
    jobs = list(jobs)
    while jobs:
        jobs = [job for job in jobs if next(job, True) is None]


def flat(group):
    return [
        leaf
        for value in group.values()
        for leaf in (flat(value) if isinstance(value, dict) else [value])
    ]


def named(group, leaves):
    return types.SimpleNamespace(
        **{
            key: named(value, leaves) if isinstance(value, dict) else next(leaves)
            for key, value in group.items()
        }
    )


def exchange(
    name,
    number,
    program,
    inputs,
    outputs,
    scratch=None,
    vmem=None,
    cores=(0, 1),
    shared=False,
    partners=(),
):
    scratch = scratch or {}
    parts = (inputs, outputs, scratch)
    counts = [len(flat(part)) for part in parts]

    def kernel(*refs):
        held = types.SimpleNamespace()
        begin = 0
        for part, count in zip(parts, counts):
            vars(held).update(vars(named(part, iter(refs[begin : begin + count]))))
            begin += count
        send, recv = refs[begin:]
        core = lax.axis_index("branch")
        seq = lax.axis_index("seq")
        coords = {X: lax.axis_index("fsdp"), Y: seq // SIDE, Z: seq % SIDE}
        names = {}

        def run(own_core):
            net = Net(own_core, coords, names, send, recv)
            barrier = pltpu.get_barrier_semaphore()
            peers = [net.device(axis, hop) for axis in (X, Y, Z) for hop in HOPS]
            if len(cores) == 2:
                peers.append(net.device(other_core=True))
            peers += [net.device(other_core=other, partner=True) for other in partners]
            for peer in peers:
                pl.semaphore_signal(barrier, inc=1, device_id=peer, device_id_type=MESH)
            pl.semaphore_wait(barrier, len(peers))
            run_jobs(program(net, held))
            for copy in net.begun:
                copy.wait_send()

        if shared:
            coords[FIRST] = jnp.where(core == 0, coords[Z], coords[Y])
            coords[SECOND] = jnp.where(core == 0, coords[Y], coords[Z])
            run(core)
        else:
            for one_core in cores:
                pl.when(core == one_core)(functools.partial(run, one_core))

        assert len(names) <= SEMS

    results = pl.pallas_call(
        kernel,
        out_shape=[jax.ShapeDtypeStruct(s, d) for s, d, _ in flat(outputs)],
        in_specs=[spec for _, spec in flat(inputs)],
        out_specs=[spec for _, _, spec in flat(outputs)],
        scratch_shapes=[pltpu.VMEM(s, d) for s, d in flat(scratch)]
        + [pltpu.SemaphoreType.DMA((SEMS,)), pltpu.SemaphoreType.DMA((SEMS,))],
        compiler_params=pltpu.CompilerParams(
            collective_id=number, has_side_effects=True, vmem_limit_bytes=vmem
        ),
        name=name,
    )(*[array for array, _ in flat(inputs)])
    return named(outputs, iter(results))


CHUNKS = 128
STEPS = 16
LINES = 8
WIDE = 40
far_away = 1e30


def to_lanes(source, target):
    for block in range(source.shape[0]):
        part = pl.ds(block * CHUNKS, CHUNKS)

        def move(l, carry):
            target[l, part, :] = source[block, pl.ds(l, CHUNKS, stride=STEPS), :].T
            return carry

        lax.fori_loop(0, STEPS, move, 0, unroll=2)


def to_rows(source, target):
    for block in range(target.shape[0]):
        part = pl.ds(block * CHUNKS, CHUNKS)

        def move(l, carry):
            target[block, pl.ds(l, CHUNKS, stride=STEPS), :] = source[l, part, :].T
            return carry

        lax.fori_loop(0, STEPS, move, 0, unroll=2)


def chunk_starts(ends, span, rates, reverse):
    lanes = lax.broadcasted_iota(jnp.int32, span.shape, 1)
    by = 1
    while by < CHUNKS:
        turn = CHUNKS - by if reverse else by
        inside = lanes < turn if reverse else lanes >= turn
        reach = jnp.where(inside, span, far_away)
        ends = [
            end + jnp.exp2(reach * rate) * pltpu.roll(end, turn, 1)
            for end, rate in zip(ends, rates)
        ]
        span = span + jnp.where(inside, pltpu.roll(span, turn, 1), 0.0)
        by *= 2
    turn = CHUNKS - 1 if reverse else 1
    inside = lanes < turn if reverse else lanes >= turn
    return [jnp.where(inside, pltpu.roll(end, turn, 1), 0.0) for end in ends]


def rate_lines(rate_ref, lines, states):
    tile = rate_ref[lines, :]
    return [jnp.broadcast_to(tile[:, s : s + 1], (lines.size, CHUNKS)) for s in range(states)]


def join_chunks(used, ends_ref, decay_t, rate_ref, reverse):
    states = rate_ref.shape[1]

    def channels(g, carry):
        lines = pl.ds(pl.multiple_of(g * WIDE, LINES), WIDE)
        span = decay_t[0, lines, :]
        for l in range(1, STEPS):
            span = span + decay_t[l, lines, :]
        starts = chunk_starts(
            [ends_ref[s, lines, :] for s in range(states)],
            span,
            rate_lines(rate_ref, lines, states),
            reverse,
        )
        for s in range(states):
            ends_ref[s, lines, :] = starts[s]
        return carry

    lax.fori_loop(0, used // WIDE, channels, 0)


def scan_forward_body(
    used, decay_ref, drive_ref, cols_ref, rate_ref, out_ref, start_ref, decay_t, drive_t, out_t
):
    states = rate_ref.shape[1]

    def col(l, s):
        return cols_ref[l, pl.ds(FIRST_COL + s, 1), :]

    to_lanes(decay_ref, decay_t)
    to_lanes(drive_ref, drive_t)
    out_t[...] = jnp.zeros_like(out_t)

    def ends(g, carry):
        lines = pl.ds(pl.multiple_of(g * LINES, LINES), LINES)
        decays = [decay_t[l, lines, :] for l in range(STEPS)]
        drives = [drive_t[l, lines, :] for l in range(STEPS)]
        rates = rate_lines(rate_ref, lines, states)
        for s in range(states):
            state = drives[0] * col(0, s)
            for l in range(1, STEPS):
                state = jnp.exp2(decays[l] * rates[s]) * state + drives[l] * col(l, s)
            start_ref[s, lines, :] = state
        return carry

    lax.fori_loop(0, used // LINES, ends, 0)
    join_chunks(used, start_ref, decay_t, rate_ref, False)

    def channels(g, carry):
        lines = pl.ds(pl.multiple_of(g * LINES, LINES), LINES)
        decays = [decay_t[l, lines, :] for l in range(STEPS)]
        drives = [drive_t[l, lines, :] for l in range(STEPS)]
        rates = rate_lines(rate_ref, lines, states)
        outs = [jnp.zeros((LINES, CHUNKS), jnp.float32)] * STEPS
        for s in range(states):
            state = start_ref[s, lines, :]
            for l in range(STEPS):
                state = jnp.exp2(decays[l] * rates[s]) * state + drives[l] * col(l, s)
                outs[l] = outs[l] + state * col(l, states + s)
        for l in range(STEPS):
            out_t[l, lines, :] = outs[l]
        return carry

    lax.fori_loop(0, used // LINES, channels, 0)
    to_rows(out_t, out_ref)


def scan_backward_body(
    used,
    decay_t,
    drive_t,
    cols_ref,
    rate_ref,
    start_ref,
    grad_ref,
    g_decay_ref,
    g_drive_ref,
    g_cols_ref,
    g_rate_ref,
    grad_t,
    g_decay_t,
    g_drive_t,
    sums_t,
    ends_t,
):
    states = rate_ref.shape[1]

    def col(l, s):
        return cols_ref[l, pl.ds(FIRST_COL + s, 1), :]

    blank = jnp.zeros((LINES, CHUNKS), jnp.float32)
    to_lanes(grad_ref, grad_t)
    g_decay_t[...] = jnp.zeros_like(g_decay_t)
    g_drive_t[...] = jnp.zeros_like(g_drive_t)
    sums_t[...] = jnp.zeros_like(sums_t)
    g_rate_ref[...] = jnp.zeros_like(g_rate_ref)
    marks = lax.broadcasted_iota(jnp.int32, (LINES, states), 1)

    def ends(g, carry):
        lines = pl.ds(pl.multiple_of(g * LINES, LINES), LINES)
        rates = rate_lines(rate_ref, lines, states)
        decays = [decay_t[l, lines, :] for l in range(STEPS)]
        grads = [grad_t[l, lines, :] for l in range(STEPS)]
        for s in range(states):
            back = blank
            for l in reversed(range(STEPS)):
                back = jnp.exp2(decays[l] * rates[s]) * (
                    grads[l] * col(l, states + s) + back
                )
            ends_t[s, lines, :] = back
        return carry

    lax.fori_loop(0, used // LINES, ends, 0)
    join_chunks(used, ends_t, decay_t, rate_ref, True)

    def channels(g, carry):
        lines = pl.ds(pl.multiple_of(g * LINES, LINES), LINES)
        tile = rate_ref[lines, :]

        def state_step(s, g_rate):
            rate = jnp.sum(jnp.where(marks == s, tile, 0.0), axis=1, keepdims=True)
            rate = jnp.broadcast_to(rate, (LINES, CHUNKS))
            state = start_ref[s, lines, :]
            befores, factors = [], []
            for l in range(STEPS):
                factor = jnp.exp2(decay_t[l, lines, :] * rate)
                befores.append(state)
                factors.append(factor)
                state = factor * state + drive_t[l, lines, :] * col(l, s)
            back = ends_t[s, lines, :]
            total_rate = blank
            for l in reversed(range(STEPS)):
                grad = grad_t[l, lines, :]
                total = grad * col(l, states + s) + back
                sums_t[s, l] += total * drive_t[l, lines, :]
                sums_t[states + s, l] += grad * state
                g_drive_t[l, lines, :] += total * col(l, s)
                back = total * factors[l]
                moved = back * befores[l]
                g_decay_t[l, lines, :] += moved * rate
                total_rate = total_rate + moved * decay_t[l, lines, :]
                state = befores[l]
            total_rate = jnp.sum(total_rate, axis=1, keepdims=True)
            return jnp.where(marks == s, total_rate, g_rate)

        g_rate_ref[lines, :] = lax.fori_loop(
            0, states, state_step, jnp.zeros((LINES, states), jnp.float32), unroll=16
        )
        return carry

    lax.fori_loop(0, used // LINES, channels, 0)

    for i in range(2 * states):
        g_cols_ref[:, FIRST_COL + i, :] = jnp.sum(sums_t[i], axis=1)
    to_rows(g_decay_t, g_decay_ref)
    to_rows(g_drive_t, g_drive_ref)


KEY_ROWS = 256
PIECE = 25
PADDED = 32
LANES = 128


def dot_on(left, right, left_dim, right_dim, **options):
    return lax.dot_general(
        left,
        right,
        (((left_dim,), (right_dim,)), ((), ())),
        preferred_element_type=jnp.float32,
        **options,
    )


def spread_matrix(low, high, wide_low, wide_high):
    shape = (high - low, wide_high - wide_low)
    column = low + lax.broadcasted_iota(jnp.int32, shape, 0)
    place = wide_low + lax.broadcasted_iota(jnp.int32, shape, 1)
    inside = place % PADDED
    match = (column == (place // PADDED) * PIECE + inside) & (inside < PIECE)
    return jnp.where(match, 1.0, 0.0).astype(jnp.bfloat16)


def spread_columns(values):
    width = values.shape[1]
    step = LANES // PADDED * PIECE
    parts = []
    for begin in range(0, width, step):
        low = begin // LANES * LANES
        high = min(low + 2 * LANES, width)
        wide = begin // PIECE * PADDED
        parts.append(dot_on(values[:, low:high], spread_matrix(low, high, wide, wide + LANES), 1, 0))
    return jnp.concatenate(parts, axis=1).astype(jnp.bfloat16)


def close_columns(values):
    width = values.shape[1] // PADDED * PIECE
    parts = []
    for begin in range(0, width, LANES):
        end = min(begin + LANES, width)
        low = begin // PIECE * PADDED // LANES * LANES
        high = -(-((end - 1) // PIECE + 1) * PADDED // LANES) * LANES
        matrix = spread_matrix(begin, end, low, high)
        value = values[:, low:high]
        most = value.astype(jnp.bfloat16)
        closed = dot_on(most, matrix, 1, 1)
        if values.dtype != jnp.bfloat16:
            rest = (value - most.astype(jnp.float32)).astype(jnp.bfloat16)
            closed = closed + dot_on(rest, matrix, 1, 1)
        parts.append(closed)
    return jnp.concatenate(parts, axis=1)


def unit_rows(values):
    return values * lax.rsqrt(jnp.mean(values * values, axis=-1, keepdims=True) + epsilon)


def whole_call(name, body, arrays, results, scratch=(), scalars=0, room=48, fetch=False):
    count = len(arrays)
    scratch_shapes = [pltpu.VMEM(shape, kind) for shape, kind in scratch]

    def fetching(*refs):
        sources, middle, held = refs[:count], refs[count : -count - 1], refs[-count - 1 : -1]
        copies = [
            pltpu.make_async_copy(source, target, refs[-1].at[i])
            for i, (source, target) in enumerate(zip(sources, held))
        ]
        for copy in copies:
            copy.start()
        for copy in copies:
            copy.wait()
        body(*held, *middle)

    if fetch:
        scratch_shapes += [pltpu.VMEM(array.shape, array.dtype) for array in arrays]
        scratch_shapes.append(pltpu.SemaphoreType.DMA((count,)))
    return pl.pallas_call(
        fetching if fetch else body,
        out_shape=[jax.ShapeDtypeStruct(shape, kind) for shape, kind in results],
        in_specs=[pl.BlockSpec(memory_space=pltpu.SMEM)] * scalars
        + [ANY if fetch else VMEM] * (count - scalars),
        out_specs=[VMEM] * len(results),
        scratch_shapes=scratch_shapes,
        compiler_params=pltpu.CompilerParams(vmem_limit_bytes=room * 2**20),
        name=name,
    )(*arrays)


def attention_project_kernel(
    tokens_ref,
    meta_ref,
    gain_ref,
    first_ref,
    second_ref,
    wide_ref,
    query_ref,
    keyval_ref,
    meta_wide_ref,
    meta_kv_ref,
):
    gain = gain_ref[...]
    third = first_ref.shape[1]
    rest = query_ref.shape[1] - third
    begin = -(-rest // LANES) * LANES
    keys = pl.ds(begin, keyval_ref.shape[1])
    wide = spread_columns((unit_rows(tokens_ref[...].astype(jnp.float32)) * gain).astype(jnp.bfloat16))
    wide_ref[...] = wide
    query_ref[:, pl.ds(0, third)] = dot_on(wide, first_ref[...], 1, 0).astype(jnp.bfloat16)
    query_ref[:, pl.ds(third, rest)] = dot_on(wide, second_ref[:, pl.ds(0, rest)], 1, 0).astype(
        jnp.bfloat16
    )
    keyval_ref[...] = dot_on(wide, second_ref[:, keys], 1, 0).astype(jnp.bfloat16)
    meta_wide = spread_columns((unit_rows(meta_ref[...]) * gain).astype(jnp.bfloat16))
    meta_wide_ref[...] = meta_wide
    meta_kv_ref[...] = dot_on(meta_wide, second_ref[:, keys], 1, 0).astype(jnp.bfloat16)


def attention_project(tokens, meta, gain, first, second, query_width, keys_width):
    rows, metas, wide = tokens.shape[0], meta.shape[0], first.shape[0]
    low = jnp.bfloat16
    return whole_call(
        "attention_project",
        attention_project_kernel,
        (tokens, meta, gain, first, second),
        (
            ((rows, wide), low),
            ((rows, query_width), low),
            ((rows, keys_width), low),
            ((metas, wide), low),
            ((metas, keys_width), low),
        ),
    )


def attention_weights_kernel(
    wide_ref,
    out_wide_ref,
    g_query_ref,
    g_pre_ref,
    first_ref,
    second_ref,
    one_ref,
    two_ref,
    three_ref,
    gain_ref,
):
    third = first_ref.shape[1]
    one = dot_on(wide_ref[...], g_query_ref[...], 0, 0)
    cut = one_ref.shape[1]
    one_ref[...] = one[:, :cut].astype(jnp.bfloat16)
    gain = jnp.sum(one[:, :third] * first_ref[...].astype(jnp.float32), axis=1, keepdims=True)
    rest = one.shape[1] - third
    gain = gain + jnp.sum(
        one[:, third:] * second_ref[:, pl.ds(0, rest)].astype(jnp.float32), axis=1, keepdims=True
    )
    gain_ref[...] = gain.T
    two = dot_on(out_wide_ref[...], g_pre_ref[...], 0, 0)
    size = one.shape[1] - cut
    begin = -(-size // LANES) * LANES
    left = two_ref.shape[1] - begin
    two_ref[...] = jnp.zeros_like(two_ref)
    two_ref[:, pl.ds(0, size)] = one[:, cut:].astype(jnp.bfloat16)
    two_ref[:, pl.ds(begin, left)] = two[:, :left].astype(jnp.bfloat16)
    three_ref[...] = two[:, left:].astype(jnp.bfloat16)


def attention_weights(wide, out_wide, g_query, g_pre, first, second, cuts):
    rows, places = wide.shape
    size = 2 * LANES
    columns = pl.BlockSpec((rows, size), lambda i: (0, i))

    def lines(width):
        return pl.BlockSpec((size, width), lambda i: (i, 0))

    return pl.pallas_call(
        attention_weights_kernel,
        grid=(places // size,),
        out_shape=[jax.ShapeDtypeStruct((places, cut), jnp.bfloat16) for cut in cuts]
        + [jax.ShapeDtypeStruct((1, places), jnp.float32)],
        in_specs=[columns, columns]
        + [pl.BlockSpec(part.shape, lambda i: (0, 0)) for part in (g_query, g_pre)]
        + [lines(first.shape[1]), lines(second.shape[1])],
        out_specs=[lines(cut) for cut in cuts] + [pl.BlockSpec((1, size), lambda i: (0, i))],
        compiler_params=pltpu.CompilerParams(vmem_limit_bytes=32 * 2**20),
        name="attention_weights",
    )(wide, out_wide, g_query, g_pre, first, second)


def attention_inputs_kernel(
    keyval_ref,
    g_query_ref,
    wide_ref,
    meta_wide_ref,
    g_meta_ref,
    first_ref,
    second_ref,
    meta_ref,
    gain_ref,
    one_ref,
    two_ref,
    three_ref,
    g_normed_ref,
    part_ref,
    meta_gain_ref,
    g_wide_ref,
    g_meta_wide_ref,
):
    third = first_ref.shape[1]
    rest = g_query_ref.shape[1] - third
    begin = -(-rest // LANES) * LANES
    keys = pl.ds(begin, keyval_ref.shape[1])
    keyval = keyval_ref[...].astype(jnp.bfloat16)
    g_meta = g_meta_ref[...]
    half = one_ref.shape[1]
    places = wide_ref.shape[1]
    size = places // 4

    def part_of(i, carry):
        spot = pl.ds(pl.multiple_of(i * size, size), size)
        weight = second_ref[spot, keys]
        weight_f = weight.astype(jnp.float32)
        grad = dot_on(wide_ref[:, spot], keyval, 0, 0)
        part_ref[:, spot] = jnp.sum(grad * weight_f, axis=1, keepdims=True).T
        grad = grad + dot_on(
            meta_wide_ref[:, spot].astype(jnp.float32), g_meta, 0, 0, precision=highest
        )
        one_ref[spot, :] = grad[:, :half].astype(jnp.bfloat16)
        two_ref[spot, :] = grad[:, half:].astype(jnp.bfloat16)
        total = dot_on(g_query_ref[:, pl.ds(0, third)], first_ref[spot, :], 1, 1)
        total = total + dot_on(
            g_query_ref[:, pl.ds(third, rest)], second_ref[spot, pl.ds(0, rest)], 1, 1
        )
        g_wide_ref[:, spot] = total + dot_on(keyval, weight, 1, 1)
        g_meta_wide_ref[:, spot] = dot_on(g_meta, weight_f, 1, 1, precision=highest)
        return carry

    lax.fori_loop(0, 4, part_of, 0)
    g_normed_ref[...] = close_columns(g_wide_ref[...])
    g_meta_normed = close_columns(g_meta_wide_ref[...])
    meta = meta_ref[...]
    scale = lax.rsqrt(jnp.mean(meta * meta, axis=-1, keepdims=True) + epsilon)
    unit = meta * scale
    meta_gain_ref[...] = jnp.sum(g_meta_normed * unit, axis=0, keepdims=True)
    g_unit = g_meta_normed * gain_ref[...]
    g_rows = scale * (g_unit - unit * jnp.mean(g_unit * unit, axis=-1, keepdims=True))
    three_ref[...] = spread_columns(g_rows.astype(jnp.bfloat16)).T


INSIDE = ("g_query", "wide", "meta_wide", "g_meta", "first", "second", "meta", "gain")


def stack_heads(source, target, scale, in_values):
    half = source.shape[0] // 2
    groups = target.shape[0]
    per = target.shape[1] // (2 * half)
    blank = jnp.zeros((half, HEAD), target.dtype)
    for group in range(groups):
        for j in range(per):
            head = source[:, pl.ds((group * per + j) * HEAD, HEAD)].astype(jnp.float32) * scale
            head = head.astype(target.dtype)
            for part in range(2):
                value = head[part * half : (part + 1) * half]
                pair = [blank, value] if in_values else [value, blank]
                target[group, pl.ds((part * per + j) * half, half), :] = jnp.concatenate(
                    pair, axis=1
                )


def lay_keys(source, target):
    places, rows = source.shape[1:3]

    def move(place, carry):
        for half in range(2):
            begin = pl.multiple_of((place * 2 + half) * rows, rows)
            target[pl.ds(begin, rows), :] = source[half, (places - 1 - place) if half else place]
        return carry

    lax.fori_loop(0, places, move, 0)


def key_bias(bounds_ref, part, begin, per):
    rows = bounds_ref.shape[0] // 2
    spot = pl.ds(part * rows, rows)
    keys = begin + lax.broadcasted_iota(jnp.int32, (rows, KEY_ROWS), 1)
    allowed = (keys >= bounds_ref[spot, 0:1]) & (keys <= bounds_ref[spot, 1:2])
    bias = jnp.where(allowed, 0.0, negative_fill)
    return jnp.concatenate([bias] * per, axis=0)


def key_bias_turned(bounds_ref, part, begin, per):
    rows = bounds_ref.shape[1] // 2
    keys = begin + lax.broadcasted_iota(jnp.int32, (KEY_ROWS, 2 * rows), 0)
    allowed = (keys >= bounds_ref[0:1, :]) & (keys <= bounds_ref[1:2, :])
    bias = jnp.where(allowed, 0.0, negative_fill)[:, part * rows : (part + 1) * rows]
    return jnp.concatenate([bias] * per, axis=1)


def attend_forward_kernel(
    count_ref,
    query_ref,
    keyval_ref,
    meta_ref,
    bounds_ref,
    second_ref,
    third_ref,
    out_ref,
    mass_ref,
    wide_ref,
    pre_ref,
    heads,
    keys,
    scores,
    tops,
    totals,
    outs,
):
    half = query_ref.shape[0] // 2
    groups = heads.shape[0]
    per = heads.shape[1] // (2 * half)
    stack = per * half
    width = 2 * HEAD
    metas = meta_ref.shape[0]
    meta_part = pl.ds(scores.shape[2] - metas, metas)
    stack_heads(query_ref, heads, score_scale, False)
    lay_keys(keyval_ref, keys)
    lanes = lax.broadcasted_iota(jnp.int32, (stack, mass_ref.shape[1]), 1)
    parts = [pl.ds(group * width, width) for group in range(groups)]

    def across(values):
        return [values[:, i : i + LANES] for i in range(0, values.shape[1], LANES)]

    for side in range(2):
        stacked = pl.ds(side * stack, stack)
        count = count_ref[side]
        for group in range(groups):
            value = dot_on(heads[group, stacked, :], meta_ref[:, parts[group]], 1, 1)
            scores[group, :, meta_part] = value
            tops[group] = value

        def score(b, carry):
            begin = pl.multiple_of(b * KEY_ROWS, KEY_ROWS)
            bias = key_bias(bounds_ref, side, begin, per)
            for group in range(groups):
                block = keys[pl.ds(begin, KEY_ROWS), parts[group]]
                value = dot_on(heads[group, stacked, :], block, 1, 1) + bias
                scores[group, :, pl.ds(begin, KEY_ROWS)] = value
                tops[group] = functools.reduce(jnp.maximum, across(value), tops[group])
            return carry

        lax.fori_loop(0, count, score, 0)
        for group in range(groups):
            top = jnp.max(tops[group], axis=1, keepdims=True)
            tops[group] = jnp.broadcast_to(top, tops.shape[1:])
            value = jnp.exp(scores[group, :, meta_part] - tops[group])
            totals[group] = value
            outs[group] = dot_on(value.astype(jnp.bfloat16), meta_ref[:, parts[group]], 1, 0)

        def weigh(b, carry):
            begin = pl.multiple_of(b * KEY_ROWS, KEY_ROWS)
            for group in range(groups):
                top = tops[group]
                value = [
                    jnp.exp(piece - top) for piece in across(scores[group, :, pl.ds(begin, KEY_ROWS)])
                ]
                totals[group] += sum(value)
                value = jnp.concatenate(value, axis=1).astype(jnp.bfloat16)
                outs[group] += dot_on(value, keys[pl.ds(begin, KEY_ROWS), parts[group]], 1, 0)
            return carry

        lax.fori_loop(0, count, weigh, 0)
        mass = jnp.zeros(lanes.shape, jnp.float32)
        for group in range(groups):
            total = jnp.sum(totals[group], axis=1, keepdims=True)
            out = outs[group] * (1.0 / total)
            for j in range(per):
                out_ref[pl.ds(side * half, half), pl.ds((group * per + j) * HEAD, HEAD)] = out[
                    j * half : (j + 1) * half, HEAD:
                ]
            mass = jnp.where(lanes == group, tops[group] + jnp.log(total), mass)
        mass_ref[stacked, :] = mass
    wide = spread_columns(out_ref[...].astype(jnp.bfloat16))
    wide_ref[...] = wide
    most = third_ref.shape[1]
    part = pre_ref.shape[1] - most
    pre_ref[:, pl.ds(0, part)] = dot_on(
        wide, second_ref[:, pl.ds(second_ref.shape[1] - part, part)], 1, 0
    )
    pre_ref[:, pl.ds(part, most)] = dot_on(wide, third_ref[...], 1, 0)


def attend_forward(count, query, keyval, meta, bounds, second, third):
    rows, query_width = query.shape
    groups = meta.shape[1] // (2 * HEAD)
    stacked = query_width // HEAD // groups * rows
    key_rows = 2 * keyval.shape[1] * keyval.shape[2]
    places, low, full = second.shape[0], jnp.bfloat16, jnp.float32
    return whole_call(
        "attend_forward",
        attend_forward_kernel,
        (count, query, keyval, meta, bounds, second, third),
        (
            ((rows, query_width), full),
            ((stacked, 2 * HEAD), full),
            ((rows, places), low),
            ((rows, query_width), full),
        ),
        (
            ((groups, stacked, 2 * HEAD), low),
            ((key_rows, meta.shape[1]), low),
            ((groups, stacked // 2, key_rows + meta.shape[0]), full),
            *[((groups, stacked // 2, LANES), full)] * 3,
        ),
        scalars=1,
        room=60,
    )


def attend_backward_kernel(
    count_ref,
    query_ref,
    keyval_ref,
    meta_ref,
    bounds_ref,
    out_ref,
    mass_ref,
    g_pre_ref,
    second_ref,
    third_ref,
    g_query_ref,
    g_keyval_ref,
    g_meta_ref,
    heads,
    grads,
    keys,
    grad_ref,
    g_keys,
    g_queries,
):
    half = query_ref.shape[0] // 2
    groups = heads.shape[0]
    per = heads.shape[1] // (2 * half)
    stack = per * half
    width = 2 * HEAD
    most = third_ref.shape[1]
    left = g_pre_ref.shape[1] - most
    grad_wide = dot_on(
        g_pre_ref[:, pl.ds(0, left)],
        second_ref[:, pl.ds(second_ref.shape[1] - left, left)],
        1,
        1,
    )
    grad_wide = grad_wide + dot_on(g_pre_ref[:, pl.ds(left, most)], third_ref[...], 1, 1)
    grad_ref[...] = close_columns(grad_wide.astype(jnp.bfloat16)).astype(jnp.bfloat16)
    stack_heads(query_ref, heads, score_scale, False)
    stack_heads(grad_ref, grads, 1.0, True)
    lay_keys(keyval_ref, keys)
    g_keys[...] = jnp.zeros_like(g_keys)
    lanes = lax.broadcasted_iota(jnp.int32, (stack, mass_ref.shape[1]), 1)
    parts = [pl.ds(group * width, width) for group in range(groups)]
    for side in range(2):
        stacked = pl.ds(side * stack, stack)
        rows = pl.ds(side * half, half)
        mass_rows, balance_rows = [], []
        for group in range(groups):
            mass = jnp.sum(
                jnp.where(lanes == group, mass_ref[stacked, :], 0.0), axis=1, keepdims=True
            )
            balance = []
            for j in range(per):
                head = pl.ds((group * per + j) * HEAD, HEAD)
                product = grad_ref[rows, head].astype(jnp.float32) * out_ref[rows, head]
                balance.append(jnp.sum(product, axis=1, keepdims=True))
            mass_rows.append(mass.T)
            balance_rows.append(jnp.concatenate(balance, axis=0).T)

        def pieces(group, block, bias):
            query, grad = heads[group, stacked, :], grads[group, stacked, :]
            value = dot_on(block, query, 1, 1)
            if bias is not None:
                value = value + bias
            probs = jnp.exp(value - mass_rows[group])
            g_scores = probs * (dot_on(block, grad, 1, 1) - balance_rows[group])
            g_scores = g_scores.astype(jnp.bfloat16)
            g_block = dot_on(g_scores, query, 1, 0) + dot_on(probs.astype(jnp.bfloat16), grad, 1, 0)
            return dot_on(g_scores, block, 0, 0), g_block

        for group in range(groups):
            g_queries[group], g_meta = pieces(group, meta_ref[:, parts[group]], None)
            if side:
                g_meta = g_meta + g_meta_ref[:, parts[group]]
            g_meta_ref[:, parts[group]] = g_meta

        def step(b, carry):
            begin = pl.multiple_of(b * KEY_ROWS, KEY_ROWS)
            bias = key_bias_turned(bounds_ref, side, begin, per)
            for group in range(groups):
                block = keys[pl.ds(begin, KEY_ROWS), parts[group]]
                more, g_block = pieces(group, block, bias)
                g_queries[group] += more
                g_keys[pl.ds(begin, KEY_ROWS), parts[group]] += g_block
            return carry

        lax.fori_loop(0, count_ref[side], step, 0)
        for group in range(groups):
            g_query = g_queries[group] * score_scale
            for j in range(per):
                g_query_ref[rows, pl.ds((group * per + j) * HEAD, HEAD)] = g_query[
                    j * half : (j + 1) * half, :HEAD
                ].astype(jnp.bfloat16)
    places = g_keyval_ref.shape[1]

    def spread(place, carry):
        for side in range(2):
            begin = pl.multiple_of((place * 2 + side) * half, half)
            g_keyval_ref[side, (places - 1 - place) if side else place] = g_keys[
                pl.ds(begin, half), :
            ].astype(jnp.bfloat16)
        return carry

    lax.fori_loop(0, places, spread, 0)


def attend_backward(count, query, keyval, meta, bounds, out, mass, g_pre, second, third):
    rows, query_width = query.shape
    groups = meta.shape[1] // (2 * HEAD)
    stacked = mass.shape[0]
    key_rows = 2 * keyval.shape[1] * keyval.shape[2]
    low = jnp.bfloat16
    return whole_call(
        "attend_backward",
        attend_backward_kernel,
        (count, query, keyval, meta, bounds, out, mass, g_pre, second, third),
        (
            ((rows, query_width), low),
            (keyval.shape, low),
            (meta.shape, jnp.float32),
        ),
        (
            ((groups, stacked, 2 * HEAD), low),
            ((groups, stacked, 2 * HEAD), low),
            ((key_rows, meta.shape[1]), low),
            ((rows, query_width), low),
            ((key_rows, meta.shape[1]), jnp.float32),
            ((groups, stacked // 2, 2 * HEAD), jnp.float32),
        ),
        scalars=1,
        room=56,
    )


def close_rows(source, target, places):
    width = target.shape[0]
    for begin in range(0, width, LANES):
        end = min(begin + LANES, width)
        low = begin // PIECE * PADDED // LANES * LANES
        high = min(-(-((end - 1) // PIECE + 1) * PADDED // LANES) * LANES, places)
        matrix = spread_matrix(begin, end, low, high)
        target[pl.ds(begin, end - begin), :] = dot_on(matrix, source(low, high), 1, 0).astype(
            target.dtype
        )


def spread_rows(source, put):
    step = LANES // PADDED * PIECE
    for n, begin in enumerate(range(0, 64 * PIECE, step)):
        low = begin // LANES * LANES
        high = min(low + 2 * LANES, 64 * PIECE)
        wide = begin // PIECE * PADDED
        matrix = spread_matrix(low, high, wide, wide + LANES)
        put(n, dot_on(matrix, source(low, high), 0, 0).astype(jnp.bfloat16))


def feed_forward_open(held):
    for part, target in enumerate((held.gate_w, held.up_w)):
        close_rows(
            lambda low, high: held.gate[part, pl.ds(low, high - low), :], target, held.gate.shape[1]
        )


def feed_forward_line(held, core, line):
    low = jnp.bfloat16
    size = held.feed.shape[2]

    def spot(i):
        return (jnp.where(core == 0, i, line), jnp.where(core == 0, line, i))

    feed = jnp.concatenate([held.feed[spot(i)] for i in range(SIDE)], axis=0)
    gate = dot_on(feed, held.gate_w[...], 1, 0)
    up = dot_on(feed, held.up_w[...], 1, 0)
    share = jax.nn.sigmoid(gate)
    silu = gate * share
    active = (silu * up).astype(low)
    out = dot_on(active, held.down[...], 1, 0).astype(low)
    cot = jnp.concatenate([held.cot[spot(i)] for i in range(SIDE)], axis=0)
    g_active = dot_on(cot, held.down[...], 1, 1)
    g_gate = (g_active * up * (share + silu * (1.0 - share))).astype(low)
    g_up = (g_active * silu).astype(low)
    g_feed = dot_on(g_gate, held.gate_w[...], 1, 1) + dot_on(g_up, held.up_w[...], 1, 1)
    g_feed = g_feed.astype(low)
    for i in range(SIDE):
        rows = slice(i * size, (i + 1) * size)
        held.out[line, i] = out[rows]
        held.g_feed[line, i] = g_feed[rows]
        held.active[spot(i)] = active[rows]
        held.g_parts[(0,) + spot(i)] = g_gate[rows]
        held.g_parts[(1,) + spot(i)] = g_up[rows]


def all_rows(ref):
    return ref.reshape(16 * ref.shape[2], ref.shape[3])[...]


def feed_forward_gate(held, part):
    held.products[...] = dot_on(all_rows(held.feed), all_rows(held.g_parts.at[part]), 0, 0).astype(
        jnp.bfloat16
    )

    def put(n, value):
        for x in range(SIDE):
            held.g_gate[part, x, n] = value[x * PADDED : (x + 1) * PADDED]

    spread_rows(lambda low, high: held.products[pl.ds(low, high - low), :], put)


def feed_forward_down(held):
    g_down = dot_on(all_rows(held.active), all_rows(held.cot), 0, 0).astype(jnp.bfloat16)
    size = held.g_down.shape[3]
    for x in range(SIDE):
        for part in range(2):
            begin = (2 * x + part) * size
            held.g_down[part, x, 0] = g_down[begin : begin + size]


STEP_ROWS = 104
LOG_ROWS = slice(104, 120)
TAP_ROWS = slice(120, 124)
OFFSET_ROW = slice(124, 125)
BIAS_ROW = slice(125, 126)
SKIP_ROW = slice(126, 127)
FIRST_PROJ = 128
PROJ_CUT = 80
PROJ_ROWS = 144
FIRST_COL = 20


def channel_matrix(size):
    channel = lax.broadcasted_iota(jnp.int32, (size, size), 0)
    place = lax.broadcasted_iota(jnp.int32, (size, size), 1)
    match = (channel == (place // 64) * 50 + place % 64) & (place % 64 < 50)
    return jnp.where(match, 1.0, 0.0).astype(jnp.bfloat16)


def two_terms(values):
    most = values.astype(jnp.bfloat16)
    return most, (values - most.astype(jnp.float32)).astype(jnp.bfloat16)


def row_places(starts_ref, begin, rows, group):
    row = begin + lax.broadcasted_iota(jnp.int32, (rows, 1), 0)
    first, after = jnp.zeros_like(row), jnp.full_like(row, group)
    for i in range(starts_ref.shape[0]):
        start = starts_ref[i]
        first = jnp.where(row >= start, jnp.maximum(first, start), first)
        after = jnp.where(row < start, jnp.minimum(after, start), after)
    return row - first, after - 1 - row


def shifted_rows(before, rows, back):
    joined = jnp.concatenate([before, rows], axis=0)
    return joined[8 - back : 8 - back + rows.shape[0]]


def conv_sum(before, rows, dist, channel):
    taps = channel[TAP_ROWS]
    total = taps[CONV - 1 : CONV] * rows + channel[OFFSET_ROW]
    for back in range(1, CONV):
        earlier = shifted_rows(before, rows, back)
        valid = jnp.where(dist >= back, 1.0, 0.0)
        total = total + taps[CONV - 1 - back : CONV - back] * earlier * valid
    return total


def mixer_project_kernel(
    starts_ref,
    tokens_ref,
    gain_ref,
    weight_ref,
    channel_ref,
    normed_ref,
    conv_ref,
    gate_ref,
    inputs_ref,
    first_ref,
    second_ref,
    compact_ref,
    rows_ref,
    tail_ref,
):
    low = jnp.bfloat16
    lanes = conv_ref.shape[1]

    @pl.when(pl.program_id(0) == 0)
    def _():
        places = weight_ref.shape[0]
        close_rows(lambda a, b: weight_ref[pl.ds(a, b - a), :], compact_ref, places)
        rows_ref[...] = dot_on(channel_ref[...], channel_matrix(lanes), 0, 1)
        tail_ref[...] = jnp.zeros_like(tail_ref)

    tokens = jnp.concatenate([tokens_ref[0, 0], tokens_ref[1, 0]], axis=0).astype(jnp.float32)
    normed = (unit_rows(tokens) * gain_ref[...]).astype(low)
    normed_ref[...] = normed
    mixed = dot_on(normed, compact_ref[...], 1, 0)
    conv_in = mixed[:, :lanes].astype(low)
    conv_ref[...] = conv_in
    gate_ref[...] = mixed[:, lanes:]
    rows = conv_in.astype(jnp.float32)
    channel = rows_ref[...]
    size = rows.shape[0]
    dist, _ = row_places(starts_ref, pl.program_id(0) * size, size, 0)
    total = conv_sum(tail_ref[...], rows, dist, channel)
    tail_ref[...] = rows[-8:]
    inputs = (total * jax.nn.sigmoid(total)).astype(low)
    inputs_ref[...] = inputs
    proj = dot_on(channel[FIRST_PROJ : FIRST_PROJ + PROJ_ROWS].astype(low), inputs, 1, 1)
    proj = proj.astype(low)
    first_ref[0] = proj[:PROJ_CUT]
    second_ref[0] = proj[PROJ_CUT:]


def mixer_project(starts, tokens, gain, weight, channel):
    places, rows, width = tokens.shape[1], tokens.shape[2], tokens.shape[3]
    rows, lanes = 2 * rows, weight.shape[1] // 2
    group = places * rows
    low, full = jnp.bfloat16, jnp.float32

    def line(size):
        return pl.BlockSpec((rows, size), lambda i: (i, 0))

    def whole(*shape):
        return pl.BlockSpec(shape, lambda i: (0,) * len(shape))

    return pl.pallas_call(
        mixer_project_kernel,
        grid=(places,),
        out_shape=[
            jax.ShapeDtypeStruct((group, width), low),
            jax.ShapeDtypeStruct((group, lanes), low),
            jax.ShapeDtypeStruct((group, lanes), full),
            jax.ShapeDtypeStruct((group, lanes), low),
            jax.ShapeDtypeStruct((places, PROJ_CUT, rows), low),
            jax.ShapeDtypeStruct((places, PROJ_ROWS - PROJ_CUT, rows), low),
            jax.ShapeDtypeStruct((width, 2 * lanes), low),
            jax.ShapeDtypeStruct((channel.shape[1], lanes), full),
        ],
        in_specs=[
            pl.BlockSpec(memory_space=pltpu.SMEM),
            pl.BlockSpec((2, 1, rows // 2, width), lambda i: (0, i, 0, 0)),
            whole(*gain.shape),
            whole(*weight.shape),
            whole(*channel.shape),
        ],
        out_specs=[
            line(width),
            line(lanes),
            line(lanes),
            line(lanes),
            pl.BlockSpec((1, PROJ_CUT, rows), lambda i: (i, 0, 0)),
            pl.BlockSpec((1, PROJ_ROWS - PROJ_CUT, rows), lambda i: (i, 0, 0)),
            whole(width, 2 * lanes),
            whole(channel.shape[1], lanes),
        ],
        scratch_shapes=[pltpu.VMEM((8, lanes), full)],
        compiler_params=pltpu.CompilerParams(vmem_limit_bytes=40 * 2**20),
        name="mixer_project",
    )(starts, tokens, gain, weight, channel)


def step_sum(first_ref, second_ref, channel_ref, p):
    low = jnp.bfloat16
    one = first_ref[p]
    two = second_ref[p][: STEP_ROWS - PROJ_CUT]
    total = dot_on(one, channel_ref[pl.ds(0, PROJ_CUT), :].astype(low), 0, 0)
    total = total + dot_on(
        two, channel_ref[pl.ds(PROJ_CUT, STEP_ROWS - PROJ_CUT), :].astype(low), 0, 0
    )
    return total + channel_ref[BIAS_ROW], one, two


def put_blocks(target, spot, value):
    for block in range(target.shape[0]):
        target[block, spot, :] = value[:, block * CHUNKS : (block + 1) * CHUNKS]


def get_blocks(source, spot):
    return jnp.concatenate([source[block, spot, :] for block in range(source.shape[0])], axis=1)


def softplus(values):
    return jnp.maximum(values, 0.0) + jnp.log1p(jnp.exp(-jnp.abs(values)))


def mixer_forward_kernel(
    used,
    starts_ref,
    first_ref,
    second_ref,
    channel_ref,
    inputs_ref,
    gate_ref,
    back_ref,
    partial_ref,
    mixed_ref,
    out_ref,
    start_ref,
    decay_t,
    drive_t,
    rate_ref,
    cols_t,
    decay_s,
    drive_s,
    out_t,
    cols_s,
):
    places = first_ref.shape[0]
    rows = first_ref.shape[2]
    half = rows // 2
    lanes = channel_ref.shape[1]
    rate = -jnp.exp(channel_ref[LOG_ROWS]) * log2_e
    channel = lax.broadcasted_iota(jnp.int32, rate.shape, 1)
    rate_ref[...] = jnp.where(channel < used, rate, 0.0).T

    def prepare(p, carry):
        spot = pl.ds(pl.multiple_of(p * rows, rows), rows)
        steps = softplus(step_sum(first_ref, second_ref, channel_ref, p)[0])
        dist, _ = row_places(starts_ref, p * rows, rows, 0)
        put_blocks(decay_s, spot, jnp.where(dist == 0, far_away, steps))
        cols = second_ref[p].astype(jnp.float32).T
        cols_s[0, spot, :] = jnp.concatenate([cols, jnp.zeros_like(cols)], axis=1)
        put_blocks(drive_s, spot, steps * inputs_ref[spot, :].astype(jnp.float32))
        return carry

    lax.fori_loop(0, places, prepare, 0)
    to_lanes(cols_s, cols_t)
    scan_forward_body(
        used, decay_s, drive_s, cols_t, rate_ref, out_ref, start_ref, decay_t, drive_t, out_t
    )
    weight = dot_on(channel_matrix(lanes), back_ref[...], 1, 0).astype(jnp.bfloat16)

    def finish(p, carry):
        spot = pl.ds(pl.multiple_of(p * rows, rows), rows)
        gate = gate_ref[spot, :]
        inputs = inputs_ref[spot, :].astype(jnp.float32)
        mixed = (get_blocks(out_ref, spot) + channel_ref[SKIP_ROW] * inputs) * (
            gate * jax.nn.sigmoid(gate)
        )
        mixed = mixed.astype(jnp.bfloat16)
        mixed_ref[spot, :] = mixed
        value = dot_on(mixed, weight, 1, 0).astype(jnp.bfloat16)
        partial_ref[0, p] = value[:half]
        partial_ref[1, p] = value[half:]
        return carry

    lax.fori_loop(0, places, finish, 0)


def mixer_forward(used, starts, first, second, channel, inputs, gate, back):
    group, lanes = inputs.shape
    places, rows = first.shape[0], first.shape[2]
    states = LOG_ROWS.stop - LOG_ROWS.start
    low, full = jnp.bfloat16, jnp.float32
    blocks = (lanes // CHUNKS, group, CHUNKS)
    turned = (STEPS, lanes, CHUNKS)
    return whole_call(
        "mixer_forward",
        functools.partial(mixer_forward_kernel, used),
        (starts, first, second, channel, inputs, gate, back),
        (
            ((2, places, rows // 2, back.shape[1]), low),
            ((group, lanes), low),
            (blocks, full),
            ((states, lanes, CHUNKS), full),
            (turned, full),
            (turned, full),
            ((lanes, states), full),
            ((STEPS, CHUNKS, CHUNKS), full),
        ),
        ((blocks, full), (blocks, full), (turned, full), ((1, group, CHUNKS), full)),
        scalars=1,
    )


def mixer_backward_kernel(
    used,
    first_ref,
    second_ref,
    cols_t,
    channel_ref,
    inputs_ref,
    gate_ref,
    back_ref,
    grad_ref,
    mixed_ref,
    out_ref,
    start_ref,
    decay_t,
    drive_t,
    rate_ref,
    g_first_ref,
    g_second_ref,
    g_inputs_ref,
    g_gate_ref,
    g_back_ref,
    g_rows_ref,
    g_rate_ref,
    g_out_s,
    g_decay_s,
    g_drive_s,
    g_weight,
    grad_t,
    g_decay_t,
    g_drive_t,
    sums_t,
    ends_t,
    g_cols_t,
    g_cols_s,
):
    places = first_ref.shape[0]
    rows = first_ref.shape[2]
    lanes = channel_ref.shape[1]
    low, full = jnp.bfloat16, jnp.float32
    weight = dot_on(channel_matrix(lanes), back_ref[...], 1, 0).astype(low)
    skip = channel_ref[SKIP_ROW]
    g_weight[...] = jnp.zeros_like(g_weight)
    g_rows_ref[...] = jnp.zeros_like(g_rows_ref)

    together = 4

    def prepare(q, carry):
        spot = pl.ds(pl.multiple_of(q * together * rows, together * rows), together * rows)
        grad = [grad_ref[i % 2, q * together + i // 2] for i in range(2 * together)]
        grad = jnp.concatenate(grad, axis=0)
        g_weight[...] += dot_on(mixed_ref[spot, :], grad, 0, 0)
        g_mixed = dot_on(grad, weight, 1, 1)
        gate = gate_ref[spot, :]
        inputs = inputs_ref[spot, :].astype(full)
        share = jax.nn.sigmoid(gate)
        g_out = g_mixed * (gate * share)
        put_blocks(g_out_s, spot, g_out)
        value = get_blocks(out_ref, spot) + skip * inputs
        g_gate = g_mixed * value * (share + gate * share * (1.0 - share))
        g_gate_ref[spot, :] = g_gate.astype(low)
        g_inputs_ref[spot, :] = g_out * skip
        g_rows_ref[SKIP_ROW] += jnp.sum(g_out * inputs, axis=0, keepdims=True)
        return carry

    lax.fori_loop(0, places // together, prepare, 0)
    g_cols_t[...] = jnp.zeros_like(g_cols_t)
    scan_backward_body(
        used,
        decay_t,
        drive_t,
        cols_t,
        rate_ref,
        start_ref,
        g_out_s,
        g_decay_s,
        g_drive_s,
        g_cols_t,
        g_rate_ref,
        grad_t,
        g_decay_t,
        g_drive_t,
        sums_t,
        ends_t,
    )

    to_rows(g_cols_t, g_cols_s)

    def finish(p, carry):
        spot = pl.ds(pl.multiple_of(p * rows, rows), rows)
        total, one, two = step_sum(first_ref, second_ref, channel_ref, p)
        steps = softplus(total)
        inputs = inputs_ref[spot, :].astype(full)
        g_drive = get_blocks(g_drive_s, spot)
        g_steps = get_blocks(g_decay_s, spot) * (1.0 / log2_e) + g_drive * inputs
        g_inputs_ref[spot, :] += g_drive * steps
        g_total = g_steps * jax.nn.sigmoid(total)
        g_rows_ref[BIAS_ROW] += jnp.sum(g_total, axis=0, keepdims=True)
        g_total = g_total.astype(low)
        g_rows_ref[pl.ds(0, PROJ_CUT), :] += dot_on(one, g_total, 1, 0)
        g_rows_ref[pl.ds(PROJ_CUT, STEP_ROWS - PROJ_CUT), :] += dot_on(two, g_total, 1, 0)
        g_low = dot_on(channel_ref[pl.ds(0, STEP_ROWS), :].astype(low), g_total, 1, 1)
        g_first_ref[p] = g_low[:PROJ_CUT].astype(low)
        g_cols = g_cols_s[0, spot, :].T[: PROJ_ROWS - PROJ_CUT]
        blank = jnp.zeros((PROJ_ROWS - STEP_ROWS, rows), full)
        g_second = g_cols + jnp.concatenate([g_low[PROJ_CUT:], blank], axis=0)
        g_second_ref[p] = g_second.astype(low)
        return carry

    lax.fori_loop(0, places, finish, 0)
    g_back = dot_on(channel_matrix(lanes), g_weight[...].astype(low), 0, 0).astype(low)
    size = g_back_ref.shape[2]
    for x in range(SIDE):
        g_back_ref[x, 0] = g_back[x * size : (x + 1) * size]


def mixer_backward(
    used,
    first,
    second,
    cols,
    channel,
    inputs,
    gate,
    back,
    grad,
    mixed,
    out,
    starts,
    decay_t,
    drive_t,
    rate,
):
    group, lanes = inputs.shape
    places, rows = first.shape[0], first.shape[2]
    low, full = jnp.bfloat16, jnp.float32
    width = back.shape[1]
    turned = (decay_t.shape, full)
    states = rate.shape[1]
    return whole_call(
        "mixer_backward",
        functools.partial(mixer_backward_kernel, used),
        (
            first,
            second,
            cols,
            channel,
            inputs,
            gate,
            back,
            grad,
            mixed,
            out,
            starts,
            decay_t,
            drive_t,
            rate,
        ),
        (
            ((places, PROJ_CUT, rows), low),
            ((places, PROJ_ROWS - PROJ_CUT, rows), low),
            ((group, lanes), full),
            ((group, lanes), low),
            ((SIDE, 1, lanes // SIDE, width), low),
            ((FIRST_PROJ, lanes), full),
            (rate.shape, full),
        ),
        (
            (out.shape, full),
            (out.shape, full),
            (out.shape, full),
            ((lanes, width), full),
            turned,
            turned,
            turned,
            ((2 * states, STEPS, LINES, CHUNKS), full),
            (starts.shape, full),
            (cols.shape, full),
            ((1, group, CHUNKS), full),
        ),
        room=60,
    )


def mixer_inputs_kernel(
    starts_ref,
    first_ref,
    second_ref,
    channel_ref,
    weight_ref,
    normed_ref,
    conv_ref,
    before_ref,
    inputs_ref,
    g_inputs_ref,
    g_gate_ref,
    g_normed_ref,
    g_weight_ref,
    g_rows_ref,
    gain_ref,
    head_ref,
    sums,
):
    step = pl.program_id(0)
    steps = pl.num_programs(0)
    low, full = jnp.bfloat16, jnp.float32
    lanes = conv_ref.shape[1]

    @pl.when(step == 0)
    def _():
        head_ref[...] = jnp.zeros_like(head_ref)
        sums[...] = jnp.zeros_like(sums)
        g_rows_ref[...] = jnp.zeros_like(g_rows_ref)

    channel = channel_ref[...]
    proj = channel[FIRST_PROJ : FIRST_PROJ + PROJ_ROWS].astype(low)
    g_proj = [
        jnp.concatenate([first_ref[i], second_ref[i]], axis=0) for i in range(first_ref.shape[0])
    ]
    g_proj = jnp.concatenate(g_proj, axis=1)
    g_inputs = g_inputs_ref[...] + dot_on(g_proj, proj, 0, 0)
    g_rows_ref[pl.ds(FIRST_PROJ, PROJ_ROWS), :] += dot_on(g_proj, inputs_ref[...], 1, 0)
    rows = conv_ref[...].astype(full)
    before = jnp.where(step == steps - 1, 0.0, 1.0) * before_ref[...].astype(full)[-8:]
    size = rows.shape[0]
    dist, later = row_places(starts_ref, (steps - 1 - step) * size, size, steps * size)
    total = conv_sum(before, rows, dist, channel)
    share = jax.nn.sigmoid(total)
    g_total = g_inputs * (share + total * share * (1.0 - share))
    taps = channel[TAP_ROWS]
    g_conv = taps[CONV - 1 : CONV] * g_total
    g_taps = [jnp.sum(g_total * rows, axis=0, keepdims=True)]
    after = jnp.concatenate([g_total, head_ref[...]], axis=0)
    for back in range(1, CONV):
        earlier = shifted_rows(before, rows, back) * jnp.where(dist >= back, 1.0, 0.0)
        g_taps.append(jnp.sum(g_total * earlier, axis=0, keepdims=True))
        tap = taps[CONV - 1 - back : CONV - back]
        g_conv = g_conv + tap * after[back : back + size] * jnp.where(later >= back, 1.0, 0.0)
    head_ref[...] = g_total[:8]
    g_rows_ref[TAP_ROWS] += jnp.concatenate(g_taps[::-1], axis=0)
    g_rows_ref[OFFSET_ROW] += jnp.sum(g_total, axis=0, keepdims=True)
    g_mixed = jnp.concatenate([g_conv.astype(low), g_gate_ref[...]], axis=1)
    sums[...] += dot_on(normed_ref[...], g_mixed, 0, 0)
    g_normed = dot_on(g_mixed, weight_ref[...], 1, 1).astype(low)
    count, half = g_normed_ref.shape[1:3]
    for i in range(count):
        for part in range(2):
            begin = (2 * i + part) * half
            g_normed_ref[part, i] = g_normed[begin : begin + half]

    @pl.when(step == steps - 1)
    def _():
        ones = jnp.ones((8, sums.shape[1]), full)
        gain_ref[...] = dot_on(ones, sums[...] * weight_ref[...].astype(full), 1, 1, precision=highest)

        def put(n, value):
            for x in range(SIDE):
                g_weight_ref[x, n] = value[x * PADDED : (x + 1) * PADDED]

        spread_rows(lambda a, b: sums[pl.ds(a, b - a), :].astype(low), put)


def mixer_inputs(starts, first, second, channel, weight, normed, conv, inputs, g_inputs, g_gate):
    places, rows = first.shape[0], first.shape[2]
    group, lanes = conv.shape
    width = normed.shape[1]
    low, full = jnp.bfloat16, jnp.float32
    count = 2
    last = places // count - 1

    def line(size):
        return pl.BlockSpec((count * rows, size), lambda i: (last - i, 0))

    def cube(size):
        return pl.BlockSpec((count, size, rows), lambda i: (last - i, 0, 0))

    def whole(*shape):
        return pl.BlockSpec(shape, lambda i: (0,) * len(shape))

    return pl.pallas_call(
        mixer_inputs_kernel,
        grid=(places // count,),
        out_shape=[
            jax.ShapeDtypeStruct((2, places, rows // 2, width), low),
            jax.ShapeDtypeStruct((SIDE, 16, PADDED, 2 * lanes), low),
            jax.ShapeDtypeStruct(channel.shape, full),
            jax.ShapeDtypeStruct((8, width), full),
        ],
        in_specs=[
            pl.BlockSpec(memory_space=pltpu.SMEM),
            cube(PROJ_CUT),
            cube(PROJ_ROWS - PROJ_CUT),
            whole(*channel.shape),
            whole(*weight.shape),
            line(width),
            line(lanes),
            pl.BlockSpec((count * rows, lanes), lambda i: (jnp.maximum(last - 1 - i, 0), 0)),
            line(lanes),
            line(lanes),
            line(lanes),
        ],
        out_specs=[
            pl.BlockSpec((2, count, rows // 2, width), lambda i: (0, last - i, 0, 0)),
            whole(SIDE, 16, PADDED, 2 * lanes),
            whole(*channel.shape),
            whole(8, width),
        ],
        scratch_shapes=[pltpu.VMEM((8, lanes), full), pltpu.VMEM((width, 2 * lanes), full)],
        compiler_params=pltpu.CompilerParams(vmem_limit_bytes=48 * 2**20),
        name="mixer_inputs",
    )(starts, first, second, channel, weight, normed, conv, conv, inputs, g_inputs, g_gate)


def channel_grads_kernel(one_ref, two_ref, rate_ref, channel_ref, out_ref):
    lanes = channel_ref.shape[1]
    total = two_ref[...]
    states = rate_ref.shape[1]
    rows = lax.broadcasted_iota(jnp.int32, total.shape, 0)
    one = one_ref[...]
    one = jnp.concatenate([one, jnp.zeros((total.shape[0] - one.shape[0], lanes), one.dtype)], axis=0)
    logs = rate_ref[...].T * -jnp.exp(channel_ref[LOG_ROWS])
    blank = jnp.zeros((LOG_ROWS.start, lanes), logs.dtype)
    rest = jnp.zeros((total.shape[0] - LOG_ROWS.start - states, lanes), logs.dtype)
    total = total + jnp.where((rows >= LOG_ROWS.start) & (rows < LOG_ROWS.stop), 0.0, one)
    total = total + jnp.concatenate([blank, logs, rest], axis=0)
    matrix = channel_matrix(lanes)
    most, left = two_terms(total)
    wide = dot_on(matrix, most, 0, 1) + dot_on(matrix, left, 0, 1)
    size = out_ref.shape[2]
    for x in range(SIDE):
        out_ref[x, 0] = wide[x * size : (x + 1) * size]


def channel_grads(one, two, rate, channel):
    lanes = channel.shape[1]
    return whole_call(
        "channel_grads",
        channel_grads_kernel,
        (one, two, rate, channel),
        (((SIDE, 1, lanes // SIDE, channel.shape[0]), jnp.float32),),
    )[0]


def unpack_kernel(small_ref, meta_ref, gains_ref):
    width = meta_ref.shape[1]
    metas = meta_ref.shape[0]
    for begin in range(0, width, LANES):
        end = min(begin + LANES, width)
        low = begin // PIECE * PADDED // LANES * LANES
        high = -(-((end - 1) // PIECE + 1) * PADDED // LANES) * LANES
        matrix = spread_matrix(begin, end, low, high)
        value = dot_on(small_ref[pl.ds(low, high - low), :], matrix, 0, 1)
        meta_ref[:, pl.ds(begin, end - begin)] = value[:metas]
        gains_ref[:, pl.ds(begin, end - begin)] = value[metas : metas + gains_ref.shape[0]]


def unpack(small, metas, width):
    full = jnp.float32
    return whole_call(
        "unpack",
        unpack_kernel,
        (small,),
        (((metas, width), full), ((8, width), full)),
        room=60,
        fetch=True,
    )


def padded_rows(value, rows):
    blank = jnp.zeros((rows - value.shape[0], value.shape[1]), value.dtype)
    return jnp.concatenate([value, blank], axis=0).astype(jnp.bfloat16)


def padded_lanes(value, lanes):
    return jnp.concatenate(
        [value, jnp.zeros((value.shape[0], lanes - value.shape[1]), value.dtype)], axis=1
    )


def stacked_rows(parts, rows):
    blank = jnp.zeros((rows - sum(part.shape[0] for part in parts), parts[0].shape[1]), jnp.float32)
    return jnp.concatenate(parts + [blank], axis=0)


def prepare_kernel(
    query_ref,
    keyval_ref,
    attn_ref,
    mamba_ref,
    back_ref,
    gate_ref,
    down_ref,
    meta_ref,
    norm_gain_ref,
    attn_gain_ref,
    mamba_gain_ref,
    feed_gain_ref,
    step_ref,
    log_ref,
    taps_ref,
    offset_ref,
    bias_ref,
    skip_ref,
    ssm_ref,
    attention_out,
    mamba_out,
    back_out,
    gate_out,
    down_out,
    small_out,
    channel_out,
):
    small = [meta_ref, norm_gain_ref, attn_gain_ref, mamba_gain_ref, feed_gain_ref]
    small = stacked_rows([ref[...] for ref in small], 2 * LANES)
    small_out[...] = padded_lanes(small, LANES).T[: small_out.shape[0]].astype(jnp.bfloat16)
    blank = jnp.zeros((STEP_ROWS - step_ref.shape[0], step_ref.shape[1]), jnp.float32)
    rows = [step_ref[...], blank]
    rows += [ref[...] for ref in (log_ref, taps_ref, offset_ref, bias_ref, skip_ref)]
    rows = padded_lanes(stacked_rows(rows, LANES), LANES).T[: channel_out.shape[0]]
    channel_out[:, pl.ds(0, LANES)] = rows.astype(jnp.bfloat16)
    channel_out[:, pl.ds(LANES, 2 * LANES)] = padded_rows(
        padded_lanes(ssm_ref[...], 2 * LANES), channel_out.shape[0]
    )
    width = query_ref.shape[1]
    begin = -(-width // LANES) * LANES
    attention_out[:, pl.ds(0, begin)] = padded_rows(padded_lanes(query_ref[...], begin), PADDED)
    half = keyval_ref.shape[1] // 2
    for group in range(half // HEAD):
        spot = group * HEAD
        pair = [keyval_ref[:, pl.ds(spot, HEAD)], keyval_ref[:, pl.ds(half + spot, HEAD)]]
        attention_out[:, pl.ds(begin + 2 * spot, 2 * HEAD)] = padded_rows(
            jnp.concatenate(pair, axis=1), PADDED
        )
    attention_out[:, pl.ds(begin + 2 * half, width)] = padded_rows(attn_ref[...], PADDED)
    places = mamba_out.shape[0]
    lanes = mamba_out.shape[2] // 2
    inner = mamba_ref.shape[1] // places // 2
    for place in range(places):
        parts = [
            padded_lanes(mamba_ref[:, pl.ds((part * places + place) * inner, inner)], lanes)
            for part in range(2)
        ]
        mamba_out[place] = padded_rows(jnp.concatenate(parts, axis=1), PADDED)
    back_out[...] = padded_rows(back_ref[...], back_out.shape[0])
    down_out[...] = padded_rows(down_ref[...], down_out.shape[0])
    size = down_ref.shape[0]
    room = gate_out.shape[3] // SIDE
    for part in range(2):
        for place in range(places):
            first = (part * places + place) * SIDE * size
            parts = [
                padded_lanes(gate_ref[:, pl.ds(first + x * size, size)], room) for x in range(SIDE)
            ]
            gate_out[part, place] = padded_rows(jnp.concatenate(parts, axis=1), PADDED)


def prepare(*arrays):
    low = jnp.bfloat16
    query, keyval, attn, _, back, _, down = arrays[:7]
    most = -(-query.shape[1] // LANES) * LANES
    return whole_call(
        "prepare",
        prepare_kernel,
        arrays,
        (
            ((PADDED, most + keyval.shape[1] + attn.shape[1]), low),
            ((16, PADDED, 4 * CHUNKS), low),
            ((64, back.shape[1]), low),
            ((2, 16, PADDED, 96 * SIDE), low),
            ((96, down.shape[1]), low),
            ((PADDED, 2 * LANES), low),
            ((64, 3 * LANES), low),
        ),
        room=60,
        fetch=True,
    )


def finish_kernel(
    tokens_ref,
    gain_ref,
    g_hidden_ref,
    normed_ref,
    sums_ref,
    keys_ref,
    mamba_ref,
    back_ref,
    channel_ref,
    gate_ref,
    down_ref,
    gains_ref,
    input_out,
    query_out,
    keyval_out,
    attn_out,
    mamba_out,
    back_out,
    gate_out,
    down_out,
    meta_out,
    ssm_out,
    step_out,
    log_out,
    taps_out,
    rows_out,
    gains_out,
):
    half = normed_ref.shape[1]
    for i in range(2):
        spot = pl.ds(i * half, half)
        rows = tokens_ref[spot, :].astype(jnp.float32)
        scale = lax.rsqrt(jnp.mean(rows * rows, axis=-1, keepdims=True) + epsilon)
        unit = rows * scale
        grad = normed_ref[i] * gain_ref[...]
        grad = scale * (grad - unit * jnp.mean(grad * unit, axis=-1, keepdims=True))
        input_out[spot, :] = g_hidden_ref[i] + grad
    piece, width = query_out.shape
    rows = pl.ds(0, piece)
    begin = sums_ref.shape[1] - width
    query_out[...] = sums_ref[rows, pl.ds(0, width)]
    attn_out[...] = sums_ref[rows, pl.ds(begin, width)]
    keys_half = keyval_out.shape[1] // 2
    for group in range(keys_half // HEAD):
        pair = keys_ref[rows, pl.ds(2 * group * HEAD, 2 * HEAD)]
        keyval_out[:, pl.ds(group * HEAD, HEAD)] = pair[:, :HEAD]
        keyval_out[:, pl.ds(keys_half + group * HEAD, HEAD)] = pair[:, HEAD:]
    meta = padded_lanes(keys_ref[:, pl.ds(2 * keys_half, meta_out.shape[0])].T, LANES)
    meta_out[...] = meta[:, :piece]
    places = mamba_ref.shape[0]
    lanes = mamba_ref.shape[2] // 2
    inner = mamba_out.shape[1] // places // 2
    for place in range(places):
        value = mamba_ref[place].astype(jnp.float32)
        for part in range(2):
            mamba_out[:, pl.ds((part * places + place) * inner, inner)] = value[
                :piece, part * lanes : part * lanes + inner
            ]
    back_out[...] = back_ref[0, pl.ds(0, back_out.shape[0]), :]
    count = back_out.shape[0]
    ssm_out[...] = channel_ref[0, pl.ds(0, count), pl.ds(FIRST_PROJ, ssm_out.shape[1])]
    channel = channel_ref[0, :, pl.ds(0, LANES)].T
    step_out[...] = channel[: step_out.shape[0], :count]
    log_out[...] = channel[LOG_ROWS, :count]
    taps_out[...] = channel[TAP_ROWS, :count]
    rows_out[...] = channel[TAP_ROWS.start : TAP_ROWS.start + 8, :count]
    gains = (gains_ref[0] + gains_ref[1]).T
    gains_out[...] = gains[: gains_out.shape[0], :piece]
    size = down_out.shape[0]
    top = down_ref.shape[1]
    down_out[pl.ds(0, top), :] = down_ref[0]
    down_out[pl.ds(top, size - top), :] = down_ref[1, pl.ds(0, size - top), :]
    room = gate_ref.shape[3] // SIDE
    for part in range(2):
        for place in range(places):
            value = gate_ref[part, place].astype(jnp.float32)
            first = (part * places + place) * SIDE * size
            parts = [value[:piece, x * room : x * room + size] for x in range(SIDE)]
            gate_out[:, pl.ds(first, SIDE * size)] = jnp.concatenate(parts, axis=1)


def finish(piece, inner_piece, down_piece, inner, proj, rank, *arrays):
    tokens = arrays[0]
    rows, width = tokens.shape
    full = jnp.float32
    keys = arrays[5]
    metas = LANES
    return whole_call(
        "finish",
        finish_kernel,
        arrays,
        (
            ((rows, width), full),
            ((piece, width), full),
            ((piece, keys.shape[1] - metas), full),
            ((piece, width), full),
            ((piece, 2 * 16 * inner), full),
            ((inner_piece, width), full),
            ((piece, 2 * 16 * SIDE * down_piece), full),
            ((down_piece, width), full),
            ((metas, piece), full),
            ((inner_piece, proj), full),
            ((rank, inner_piece), full),
            ((LOG_ROWS.stop - LOG_ROWS.start, inner_piece), full),
            ((CONV, inner_piece), full),
            ((8, inner_piece), full),
            ((8, piece), full),
        ),
    )


def pack_gains_kernel(norm_ref, attn_ref, mamba_ref, feed_ref, out_ref):
    width = norm_ref.shape[1]
    rows = [ref[...] for ref in (norm_ref, attn_ref, mamba_ref, feed_ref)]
    rows = jnp.concatenate(rows + [jnp.zeros((8 - len(rows), width), jnp.float32)], axis=0)
    wide = spread_columns(rows.astype(jnp.bfloat16)).astype(jnp.float32).T
    out_ref[...] = padded_lanes(wide, LANES).astype(jnp.bfloat16)


def pack_gains(*rows):
    places = rows[0].shape[1] // PIECE * PADDED
    return whole_call("pack_gains", pack_gains_kernel, rows, (((places, LANES), jnp.bfloat16),))[0]


def rms_norm(values, gain):
    return values * lax.rsqrt(jnp.mean(values * values, axis=-1, keepdims=True) + epsilon) * gain


def pad_to(array, dim, size):
    widths = [(0, 0)] * array.ndim
    widths[dim] = (0, size - array.shape[dim])
    return jnp.pad(array, widths)


def blank(shapes):
    leaves, nest = jax.tree.flatten(shapes)
    outs = pl.pallas_call(
        lambda *refs: None,
        out_shape=[jax.ShapeDtypeStruct(leaf.shape, leaf.dtype) for leaf in leaves],
        out_specs=[ANY] * len(leaves),
        name="blank",
    )()
    return jax.tree.unflatten(nest, outs)


def order_of(net):
    return (Z, Y) if net.core == 0 else (Y, Z)


def gather_halves(net, name, source, out, patience=0):
    if net.core == 0:
        count = []

        def after(line):
            net.start(
                (name, -3, len(count)),
                out.at[0, line],
                out.at[0, line],
                net.device(other_core=True),
            )
            count.append(line)

        yield from gather_two(net, name, source, out.at[0], (Z, Y), after, patience)
    else:
        yield from gather_two(net, name, source, out.at[1], (Y, Z), None, patience)
        for i in range(SIDE):
            net.copy(
                (name, -3, i), out.at[0, i], out.at[0, i], net.device(other_core=True)
            ).wait_recv()


def reduce_halves(net, name, source, pad, out):
    if net.core == 1:
        for y in range(SIDE):
            net.start(
                (name, -3, y), source.at[0, y], pad.half.at[y], net.device(other_core=True)
            )
        own = net.local((name, -1), source.at[1], pad.half)
        yield
        own.wait()
    else:
        yield
        for y in range(SIDE):
            net.copy(
                (name, -3, y), source.at[0, y], pad.half.at[y], net.device(other_core=True)
            ).wait_recv()
    yield from reduce_two(net, name, pad.half, pad, out, order_of(net))


def share_x(net, name, source, view):
    x = net.at[X]
    core, other = net.core, 1 - net.core
    own = net.local((name, -1), source, view(core, x))
    copies = [
        net.start((name, -2, hop), source, view(core, x), net.device(X, hop)) for hop in HOPS
    ]
    net.start((name, core, 0), source, view(core, x), net.device(other_core=True))
    yield
    for copy, hop in zip(copies, HOPS):
        copy.wait_recv()
        spot = (x - hop + SIDE) % SIDE
        net.start(
            (name, core, hop), view(core, spot), view(core, spot), net.device(other_core=True)
        )
    yield
    for i in (0,) + HOPS:
        net.copy(
            (name, other, i), source, view(other, x), net.device(other_core=True)
        ).wait_recv()
    own.wait()


def swap_cores(net, name, source, out):
    net.start((name, net.core), source, out.at[net.core], net.device(other_core=True))
    own = net.local((name, -1), source, out.at[net.core])
    yield
    net.copy(
        (name, 1 - net.core), source, out.at[1 - net.core], net.device(other_core=True)
    ).wait_recv()
    own.wait()


def hand(net, name, giver, source, target):
    if net.core == giver:
        net.start(name, source, target, net.device(other_core=True))
    else:
        net.copy(name, source, target, net.device(other_core=True)).wait_recv()


def keep_and_hand(net, name, giver, source, target):
    if net.core == giver:
        own = net.local((name, -1), source, target)
    hand(net, (name, 0), giver, source, target)
    yield
    if net.core == giver:
        own.wait()


def reduce_x(net, name, source, pad, out):
    x = net.at[X]
    recv, kept = pad.recv, pad.own
    own = net.local((name, -4), source.at[x], kept)
    copies = [
        net.start(
            (name, 5, hop), source.at[(x + hop) % SIDE], recv.at[hop - 1], net.device(X, hop)
        )
        for hop in HOPS
    ]
    yield
    own.wait()
    for copy in copies:
        copy.wait_recv()

    def put(lead, part, value):
        index = (lead,) if len(out.shape) == 3 else (lead // SIDE, lead % SIDE)
        out[index + (part, slice(None))] = value.astype(out.dtype)

    scatter_sum(
        source.shape[1],
        source.shape[2],
        lambda lead, part: kept[lead, part, :],
        [lambda lead, part, k=k: recv[k, lead, part, :] for k in range(3)],
        put,
    )


def reduce_three(net, name, source, pad, out, order, hold=0):
    left = [Y, Z, X]
    held = source
    stages = ((pad.recv0, pad.mid0), (pad.recv1, pad.mid1), (pad.recv2, out))
    for stage, axis in enumerate(order):
        recv, mid = stages[stage]
        spot = left.index(axis)
        size = len(left)

        def part_of(place, held=held, spot=spot):
            return held.at[(slice(None),) * spot + (place,)]

        if stage == 0:
            fetch = net.local((name, -4), part_of(net.at[axis]), pad.own)
        copies = [
            net.start(
                (name, stage, hop),
                part_of((net.at[axis] + hop) % SIDE),
                recv.at[hop - 1],
                net.device(axis, hop),
            )
            for hop in HOPS
        ]
        yield
        if stage == 0:
            for _ in range(hold):
                yield
            fetch.wait()
        for copy in copies:
            copy.wait_recv()

        def split(lead, size=size):
            return tuple((lead // SIDE**i) % SIDE for i in reversed(range(size - 1)))

        def own(lead, part, held=held, spot=spot, split=split, axis=axis):
            index = split(lead)
            if len(index) == 2:
                return pad.own[index + (part, slice(None))]
            index = index[:spot] + (net.at[axis],) + index[spot:]
            return held[index + (part, slice(None))]

        def put(lead, part, value, mid=mid, split=split):
            mid[split(lead) + (part, slice(None))] = value.astype(mid.dtype)

        scatter_sum(
            SIDE ** (size - 1),
            source.shape[3],
            own,
            [
                lambda lead, part, k=k, recv=recv, split=split: recv[
                    (k,) + split(lead) + (part, slice(None))
                ]
                for k in range(3)
            ],
            put,
        )
        held = mid
        del left[spot]


def three_pad(rows, width, kind=jnp.bfloat16):
    block = (rows, width)
    return dict(
        own=((SIDE, SIDE) + block, kind),
        recv0=((3, SIDE, SIDE) + block, kind),
        mid0=((SIDE, SIDE) + block, kind),
        recv1=((3, SIDE) + block, kind),
        mid1=((SIDE,) + block, kind),
        recv2=((3,) + block, kind),
    )


def two_pad(rows, width, kind=jnp.bfloat16):
    return dict(
        one=((3, SIDE, rows, width), kind),
        mid=((SIDE, rows, width), kind),
        two=((3, rows, width), kind),
        own=((SIDE, rows, width), kind),
    )


def ring_pad(rows, width, kind=jnp.bfloat16):
    half = rows // 2
    return dict(
        one=((2, SIDE, rows, width), kind),
        via_one=((2, SIDE, half, width), kind),
        mix_one=((2, SIDE, half, width), kind),
        mid=((SIDE, rows, width), kind),
        two=((2, rows, width), kind),
        via_two=((2, half, width), kind),
        mix_two=((2, half, width), kind),
        own=((SIDE, rows, width), kind),
    )


def half_pad(rows, width, kind=jnp.bfloat16):
    return dict(two_pad(rows, width, kind), half=((SIDE, SIDE, rows, width), kind))


def shrink_pad(lead, rows, width, kind=jnp.bfloat16):
    return dict(
        mine=((SIDE, lead, rows, width), kind),
        other=((SIDE, lead, rows, width), kind),
        mid=((SIDE, lead, rows, width), kind),
        **x_pad(lead, rows, width, kind),
    )


def x_pad(lead, rows, width, kind=jnp.bfloat16):
    return dict(recv=((3, lead, rows, width), kind), own=((lead, rows, width), kind))


def gather_weights(net, held):
    axes = (Y, Z, X)
    jobs, begin = [], 0
    for i, (target, order) in enumerate(
        ((held.first, (X, Z, Y)), (held.second, (Z, Y, X)), (held.third, (Y, X, Z)))
    ):
        size = target.shape[-1]
        jobs.append(
            gather(net, 5 + i, held.whole.at[:, pl.ds(begin, size)], target, axes, order, hold=3)
        )
        begin += size
    return jobs


def program_start(net, held):
    core = net.core
    rows = held.tokens.shape[0] // 2
    axes = (Y, Z, X)
    jobs = []
    if core == 1:

        def mamba():
            target = held.mamba_all.at[:, :, net.at[X]]
            yield from swap_two(net, 2, held.mamba, held.mamba_mid, target)
            copies = [
                net.start((2, 3, hop), target, target, net.device(X, hop)) for hop in HOPS
            ]
            yield
            for copy in copies:
                copy.wait_recv()

        jobs = [
            mamba(),
            gather(net, 3, held.back, held.back_all, (X,), (X,)),
            gather(net, 4, held.channel, held.channel_all, (X,), (X,)),
        ]
    jobs.append(gather(net, 1, held.small, held.small_all, axes, order_of(net) + (X,)))
    jobs.append(
        gather_halves(net, 0, held.tokens.at[pl.ds(core * rows, rows)], held.tokens_all)
    )
    if core == 0:

        def assigned():
            upper, lower = pl.ds(0, rows), pl.ds(rows, rows)
            own = net.local((9, -1), held.tokens.at[upper], held.assigned.at[upper])
            copy = net.start(
                (9, 0), held.tokens.at[lower], held.assigned.at[lower], net.device(partner=True)
            )
            yield
            copy.wait_recv()
            own.wait()

        jobs += [assigned()] + gather_weights(net, held)
    return jobs


def program_keyval(net, held):
    rows = held.keyval.shape[0] // 2
    return [
        gather_two(
            net,
            i,
            held.keyval.at[pl.ds(i * rows, rows)],
            held.keyval_all.at[i],
            ((Z, Y), (Y, Z))[i],
        )
        for i in range(2)
    ] + [swap_two(net, 2, held.gate.at[0], held.gate_mid, held.gate_own)]


def program_project(net, held):
    jobs = []
    for i, order in enumerate(((Z, Y), (Y, Z))):
        source = (held.first, held.second)[i]
        pad = (held.first_pad, held.second_pad)[i]
        target = (held.first_all, held.second_all)[i]

        def job(source=source, pad=pad, target=target, order=order, i=i):
            yield from reduce_two(net, 2 * i, source, pad, pad.sum, order)
            yield from gather_two(net, 2 * i + 1, pad.sum, target, order)

        jobs.append(job())
    return jobs + [swap_two(net, 4, held.gate, held.gate_mid, held.gate_own)]


def program_mixers(net, held):
    core = net.core
    half = held.down.shape[0] // 2
    rows = held.attn_pre.shape[0] // 2

    def attn():
        lower = held.attn_pre.at[pl.ds(rows, rows)]
        device = net.device(other_core=True, partner=True)
        if core == 0:
            own = net.local((1, -1), held.attn_pre.at[pl.ds(0, rows)], held.attn_half)
            net.start((1, 0), lower, held.attn_half, device)
        yield
        if core == 0:
            own.wait()
        else:
            net.copy((1, 0), lower, held.attn_half, device).wait_recv()

    return [
        attn(),
        reduce_halves(net, 0, held.partial, held.pad, held.mamba_pre),
        share_x(
            net,
            2,
            held.gate_first if core == 0 else held.gate_second,
            lambda b, x: held.gate_all.at[b, :, :, x],
        ),
        share_x(
            net,
            3,
            held.down.at[pl.ds(core * half, half)],
            lambda b, x: held.down_all.at[x, pl.ds(b * half, half)],
        ),
    ]


def program_feed(net, held):
    return [gather_two(net, 0, held.feed, held.feed_all, order_of(net))]


def program_ffn(net, held):
    feed_forward_open(held)
    jobs = [
        reduce_ring(net, 1, held.g_feed, held.grad_pad, held.grad_sum),
        reduce_ring(net, 0, held.out, held.out_pad, held.out_sum),
    ]
    for job in jobs:
        next(job)

    def line(hop):
        feed_forward_line(held, net.core, (net.at[FIRST] + hop) % SIDE)

    def weights():
        for part in range(2):
            feed_forward_gate(held, part)
            yield
        feed_forward_down(held)

    for hop in (2, 1, 3, 0):
        line(hop)
        for job in jobs:
            next(job)
    return jobs + [weights()]


def shrink(net, name, source, pad, out):
    core = net.core
    lead, rows = source.shape[2:4]
    mine = net.local((name, -5), source.at[core], pad.mine)
    net.start((name, 6, core), source.at[1 - core], pad.other, net.device(other_core=True))
    yield
    net.copy(
        (name, 6, 1 - core), source.at[1 - core], pad.other, net.device(other_core=True)
    ).wait_recv()

    mine.wait()

    def put(i, part, value):
        pad.mid[i // lead, i % lead, part, :] = value.astype(pad.mid.dtype)

    scatter_sum(
        SIDE * lead,
        rows,
        lambda i, part: pad.mine[i // lead, i % lead, part, :],
        [lambda i, part: pad.other[i // lead, i % lead, part, :]],
        put,
    )
    yield from reduce_x(net, name, pad.mid, pad, out)


def program_back(net, held):
    core = net.core

    def attn():
        device = net.device(other_core=True, partner=True)
        target = held.g_attn_both.at[1]
        if core == 0:
            own = net.local((5, -1), held.g_attn, held.g_attn_both.at[0])
        else:
            net.start((5, 0), held.g_attn, target, device)
        yield
        if core == 0:
            own.wait()
            net.copy((5, 0), held.g_attn, target, device).wait_recv()

    return [
        swap_cores(net, 3, held.mixed, held.mixed_both),
        swap_cores(net, 4, held.g_hidden, held.g_hidden_both),
        attn(),
        shrink(net, 1, held.g_gate, held.gate_pad, held.g_gate_sum),
        shrink(net, 2, held.g_down, held.down_pad, held.g_down_sum),
        gather_halves(net, 0, held.g_mamba, held.g_mamba_all, patience=1),
    ]


SUMS = ("one", "two", "three", "four", "five", "six")
ORDERS = ((Y, Z, X), (X, Y, Z), (Z, X, Y), (Y, Z, X), (X, Y, Z), (Z, X, Y))


def program_attention(net, held):
    rows = held.keyval.shape[3]
    parts = [getattr(held.parts, name) for name in SUMS]
    taken = [
        net.local((20, i), getattr(held.sources, name), getattr(held.inside, name))
        for i, name in enumerate(INSIDE)
    ]

    def weight(i, source, hold=0):
        pad = getattr(held.pads, SUMS[i])
        return reduce_three(net, 10 + i, source, pad, parts[i], ORDERS[i], hold)

    def keyval(i):
        pad = (held.upper_pad, held.lower_pad)[i]
        return reduce_two(
            net,
            i,
            held.keyval.at[i],
            pad,
            held.keyval_sum.at[pl.ds(i * rows, rows)],
            ((Z, Y), (Y, Z))[i],
        )

    def follow():
        for _ in range(3):
            yield
        for copy in taken:
            copy.wait()
        inside = held.inside
        attention_inputs_kernel(
            held.keyval_sum,
            inside.g_query,
            inside.wide,
            inside.meta_wide,
            inside.g_meta,
            inside.first,
            inside.second,
            inside.meta,
            inside.gain,
            held.keys.four,
            held.keys.five,
            held.keys.six,
            held.g_normed,
            held.gain_part,
            held.meta_gain,
            held.g_wide,
            held.g_meta_wide,
        )
        places = held.keys.four.shape[0] // SIDE**3

        def cubed(ref):
            return ref.reshape(SIDE, SIDE, SIDE, places, ref.shape[1])

        later = [weight(3 + i, cubed(ref)) for i, ref in enumerate(vars(held.keys).values())]
        while later:
            later = [job for job in later if next(job, True) is None]
            yield

    def last():
        for _ in range(9):
            yield
        begin = 0
        for part in parts[:3]:
            held.sums[:, pl.ds(begin, part.shape[1])] = part[...]
            begin += part.shape[1]
        begin = 0
        for part in parts[3:]:
            held.keys_sum[:, pl.ds(begin, part.shape[1])] = part[...]
            begin += part.shape[1]

    return [
        keyval(0),
        keyval(1),
        swap_two(net, 3, held.gate, held.gate_mid, held.gate_own),
        follow(),
        *(weight(i, getattr(held, SUMS[i]), 2) for i in range(3)),
        last(),
    ]


def program_end(net, held):
    core = net.core

    def normed():
        half = held.normed_sum.shape[0]
        device = net.device(other_core=True, partner=True)
        if core == 0:
            own = net.local((9, -1), held.g_attn.at[pl.ds(0, half)], held.attn_part)
            net.start((9, 0), held.g_attn.at[pl.ds(half, half)], held.attn_part, device)
        yield from reduce_halves(net, 0, held.partial, held.normed_pad, held.normed_sum)
        if core == 0:
            own.wait()
        else:
            lower = held.g_attn.at[pl.ds(half, half)]
            net.copy((9, 0), lower, held.attn_part, device).wait_recv()

        def put(lead, part, value):
            held.normed_sum[part, :] = value

        scatter_sum(
            1,
            half,
            lambda lead, part: held.normed_sum[part, :],
            [lambda lead, part: held.attn_part[part, :]],
            put,
        )
        yield from swap_cores(net, 1, held.normed_sum, held.normed_both)

    def gains():
        yield from reduce_three(
            net, 2, held.gains, held.gains_pad, held.gains_sum, order_of(net) + (X,)
        )
        yield from swap_cores(net, 3, held.gains_sum, held.gains_both)

    def mamba():
        if core == 1:
            yield from reduce_x(net, 4, held.mamba, held.mamba_pad, held.mamba_part)
            yield from swap_two(net, 5, held.mamba_part, held.mamba_mid, held.mamba_sum)
        else:
            for _ in range(4):
                yield
        hand(net, (6, 0), 1, held.mamba_sum, held.mamba_sum)

    def channel(name, source, pad, total):
        if core == 1:
            yield from reduce_x(net, name, source, pad, total)
        else:
            for _ in range(2):
                yield
        hand(net, (name, 0), 1, total, total)

    return [
        normed(),
        mamba(),
        channel(7, held.back, held.back_pad, held.back_sum),
        channel(8, held.channel, held.channel_pad, held.channel_sum),
        gains(),
        keep_and_hand(net, 10, 0, held.sums_in, held.sums),
        keep_and_hand(net, 12, 0, held.keys, held.keys_sum),
        swap_cores(net, 13, held.gate, held.gate_both),
        swap_cores(net, 14, held.down, held.down_both),
    ]


def shards(
    tokens,
    seq_lengths,
    norm_gain,
    meta_tokens,
    w_query,
    w_key_value,
    w_attn_out,
    attn_gain,
    w_mamba_in,
    conv_weight,
    conv_bias,
    w_ssm_x,
    w_dt,
    dt_bias,
    a_log,
    skip_d,
    w_mamba_out,
    mamba_gain,
    ffn_gain,
    w_gate_up,
    w_down,
    cotangent,
):
    low = jnp.bfloat16
    full = jnp.float32
    core = lax.axis_index("branch")
    on_attention = core == 0
    tokens_b, cotangent_b = tokens[0], cotangent[0]
    rows, width = tokens_b.shape
    half = rows // 2
    group = rows * 16
    piece = w_query.shape[0]
    query_width = w_query.shape[1]
    keys_width = w_key_value.shape[1]
    inner_piece = w_mamba_out.shape[0]
    inner = inner_piece * SIDE
    rank = w_dt.shape[0]
    states = a_log.shape[0]
    proj = rank + 2 * states
    metas = meta_tokens.shape[0]
    down_piece = w_down.shape[0]
    units = 96 * SIDE
    row_start = core * half

    lengths = seq_lengths[0]
    start_rows = (jnp.cumsum(lengths) - lengths).astype(jnp.int32)
    place = lax.axis_index("seq")
    counting = jnp.arange(half, dtype=jnp.int32)
    my_rows = jnp.concatenate([place * rows + counting, (16 - place) * rows - half + counting])

    attention_in, mamba_in, back_in, gate_in, down_in, small_in, channel_in = prepare(
        w_query,
        w_key_value,
        w_attn_out,
        w_mamba_in,
        w_mamba_out,
        w_gate_up,
        w_down,
        meta_tokens,
        *(gain[None] for gain in (norm_gain, attn_gain, mamba_gain, ffn_gain)),
        w_dt,
        a_log,
        conv_weight,
        *(row[None] for row in (conv_bias, dt_bias, skip_d)),
        w_ssm_x,
    )
    query_most = -(-query_width // LANES) * LANES
    third = 10 * LANES
    last_third = attention_in.shape[1] - 2 * third
    mamba_in = mamba_in.reshape(SIDE, SIDE, 32, -1)
    gate_in = gate_in.reshape(2, SIDE, SIDE, 32, units)
    cube = (SIDE, SIDE, SIDE)

    begun = exchange(
        "exchange_start",
        0,
        program_start,
        dict(
            tokens=(tokens_b, ANY),
            small=(small_in, ANY),
            mamba=(mamba_in, ANY),
            back=(back_in, ANY),
            channel=(channel_in, ANY),
            whole=(attention_in, ANY),
        ),
        dict(
            tokens_all=((2, SIDE, SIDE, half, width), low, ANY),
            assigned=((rows, width), low, ANY),
            small_all=(cube + small_in.shape, low, ANY),
            mamba_all=(cube + mamba_in.shape[2:], low, ANY),
            back_all=((SIDE,) + back_in.shape, low, ANY),
            channel_all=((SIDE,) + channel_in.shape, low, ANY),
            first=(cube + (32, third), low, ANY),
            second=(cube + (32, third), low, ANY),
            third=(cube + (32, last_third), low, ANY),
        ),
        dict(mamba_mid=(mamba_in.shape, low)),
        partners=(False,),
    )
    weight_one, weight_two, weight_three = (
        part.reshape(64 * 32, -1) for part in (begun.first, begun.second, begun.third)
    )
    meta_f, gains = unpack(begun.small_all.reshape(64 * 32, -1), metas, width)
    gain_norm, gain_attn, gain_mamba, gain_feed = (gains[i] for i in range(4))
    gain_row = gains[:1]

    def on_core(which, work):
        shapes = jax.eval_shape(work)
        return lax.cond(core == which, work, lambda: blank(shapes))


    normed_wide, query_b, keyval_b, meta_wide, meta_kv = on_core(
        0,
        lambda: attention_project(
            begun.assigned, meta_f, gain_row, weight_one, weight_two, query_width, keys_width
        ),
    )
    keyval = exchange(
        "exchange_keyval",
        2,
        program_keyval,
        dict(keyval=(keyval_b, ANY), gate=(gate_in, ANY)),
        dict(
            keyval_all=((2, SIDE, SIDE, half, keys_width), low, ANY),
            gate_own=((SIDE, SIDE, 32, units), low, ANY),
        ),
        dict(gate_mid=((SIDE, SIDE, 32, units), low)),
        cores=(0,),
    )

    mamba_wide = begun.mamba_all.reshape(64 * 32, -1)
    back_wide = begun.back_all.reshape(-1, width)
    normed_all, conv_in, gate_z, inputs_b, proj_first, proj_second, weight_mamba, channel = on_core(
        1,
        lambda: mixer_project(
            start_rows,
            begun.tokens_all.reshape(2, 16, half, width),
            gain_row,
            mamba_wide,
            begun.channel_all.reshape(4 * 64, -1),
        ),
    )

    def proj_pads(size):
        return dict(two_pad(size, rows), sum=((size, rows), low))

    def spread_projection(name, number, first, second, gate):
        cuts = (PROJ_CUT, PROJ_ROWS - PROJ_CUT)
        results = exchange(
            name,
            number,
            program_project,
            dict(
                first=(first.reshape(SIDE, SIDE, cuts[0], rows), ANY),
                second=(second.reshape(SIDE, SIDE, cuts[1], rows), ANY),
                gate=(gate, ANY),
            ),
            dict(
                first_all=((SIDE, SIDE, cuts[0], rows), low, ANY),
                second_all=((SIDE, SIDE, cuts[1], rows), low, ANY),
                gate_own=((SIDE, SIDE, 32, units), low, ANY),
            ),
            dict(
                first_pad=proj_pads(cuts[0]),
                second_pad=proj_pads(cuts[1]),
                gate_mid=((SIDE, SIDE, 32, units), low),
            ),
            vmem=32 * 2**20,
            cores=(1,),
        )
        whole = [part.reshape(16, -1, rows) for part in (results.first_all, results.second_all)]
        return whole + [results.gate_own]

    step_first, step_second, gate_second = spread_projection("exchange_project", 3, proj_first, proj_second, gate_in[1])
    keyval_all = keyval.keyval_all.reshape(2, 16, half, keys_width)

    cotangent_b, step_second = lax.optimization_barrier((cotangent_b, step_second))
    cotangent_part = lax.dynamic_slice_in_dim(cotangent_b, row_start, half, 0)
    cotangent_all = lax.all_gather(cotangent_part, "seq", axis=0, tiled=True)

    my_starts = jnp.max(
        jnp.where(my_rows[:, None] >= start_rows[None, :], start_rows[None, :], 0), axis=1
    )
    bounds = jnp.stack([my_starts, my_rows], axis=1).astype(jnp.int32)
    key_blocks = (my_rows[half - 1 :: half] // KEY_ROWS + 1).astype(jnp.int32)

    attended, mass, attended_wide, attn_pre = on_core(
        0,
        lambda: attend_forward(
            key_blocks, query_b, keyval_all, meta_kv, bounds, weight_two, weight_three
        ),
    )

    partial, mixed_y, ssm_out, starts, decay_t, drive_t, scan_rate, cols = on_core(
        1,
        lambda: mixer_forward(
            inner, start_rows, step_first, step_second, channel, inputs_b, gate_z, back_wide
        ),
    )

    mixers = exchange(
        "exchange_mixers",
        4,
        program_mixers,
        dict(
            partial=(partial.reshape(2, SIDE, SIDE, half, width), ANY),
            attn_pre=(attn_pre, ANY),
            gate_first=(keyval.gate_own, ANY),
            gate_second=(gate_second, ANY),
            down=(down_in, ANY),
        ),
        dict(
            mamba_pre=((half, width), jnp.float32, VMEM),
            attn_half=((half, width), jnp.float32, ANY),
            gate_all=((2,) + cube + (32, units), low, ANY),
            down_all=((SIDE,) + down_in.shape, low, ANY),
        ),
        dict(pad=half_pad(half, width)),
        vmem=32 * 2**20,
        partners=(True,),
    )
    tokens_part = lax.dynamic_slice_in_dim(tokens_b, row_start, half, 0).astype(full)
    sent = rms_norm(mixers.attn_half, gain_attn).astype(low).astype(jnp.float32)
    sent = sent + rms_norm(mixers.mamba_pre, gain_mamba).astype(low).astype(jnp.float32)
    hidden = tokens_part + 0.5 * sent
    feed = exchange(
        "exchange_feed",
        5,
        program_feed,
        dict(feed=(rms_norm(hidden, gain_feed).astype(low), ANY)),
        dict(feed_all=((SIDE, SIDE, half, width), low, ANY)),
    ).feed_all
    block = (SIDE, SIDE, half)
    ffn = exchange(
        "exchange_ffn",
        6,
        program_ffn,
        dict(
            feed=(feed, VMEM),
            cot=(cotangent_all.reshape(block + (width,)), VMEM),
            gate=(mixers.gate_all.reshape(2, 64 * 32, units), VMEM),
            down=(mixers.down_all.reshape(units, width), VMEM),
        ),
        dict(
            out_sum=((half, width), full, VMEM),
            grad_sum=((half, width), full, VMEM),
            g_gate=((2, SIDE, 16, 32, units), low, VMEM),
            g_down=((2, SIDE, 1, 48, width), low, VMEM),
        ),
        dict(
            out=(block + (width,), low),
            g_feed=(block + (width,), low),
            active=(block + (units,), low),
            g_parts=((2,) + block + (units,), low),
            gate_w=((width, units), low),
            up_w=((width, units), low),
            products=((width, units), low),
            out_pad=ring_pad(half, width),
            grad_pad=ring_pad(half, width),
        ),
        vmem=60 * 2**20,
        shared=True,
    )
    mixed_part = (hidden + ffn.out_sum).astype(low)
    cotangent_f = cotangent_part.astype(jnp.float32)
    _, pull_feed = jax.vjp(rms_norm, hidden, gain_feed)
    grad_hidden_norm, grad_gain_feed = pull_feed(ffn.grad_sum)
    grad_hidden = cotangent_f + grad_hidden_norm
    grad_sent = 0.5 * grad_hidden
    _, pull_attn = jax.vjp(rms_norm, mixers.attn_half, gain_attn)
    grad_attn_pre, grad_gain_attn = pull_attn(grad_sent)
    _, pull_mamba = jax.vjp(rms_norm, mixers.mamba_pre, gain_mamba)
    grad_mamba_pre, grad_gain_mamba = pull_mamba(grad_sent)

    back = exchange(
        "exchange_back",
        7,
        program_back,
        dict(
            g_mamba=(grad_mamba_pre.astype(low), ANY),
            g_attn=(grad_attn_pre.astype(low), ANY),
            mixed=(mixed_part, ANY),
            g_hidden=(grad_hidden, ANY),
            g_gate=(ffn.g_gate, ANY),
            g_down=(ffn.g_down, ANY),
        ),
        dict(
            g_mamba_all=((2, SIDE, SIDE, half, width), low, ANY),
            g_attn_both=((2, half, width), low, ANY),
            mixed_both=((2, half, width), low, ANY),
            g_hidden_both=((2, half, width), jnp.float32, ANY),
            g_gate_sum=((16, 32, units), low, VMEM),
            g_down_sum=((1, 48, width), jnp.float32, VMEM),
        ),
        dict(gate_pad=shrink_pad(16, 32, units), down_pad=shrink_pad(1, 48, width)),
        vmem=32 * 2**20,
        partners=(True,),
    )
    mixed = back.mixed_both.reshape(rows, width)
    g_gate_own = back.g_gate_sum.reshape(SIDE, SIDE, 32, units)

    cuts = (8 * LANES, 9 * LANES, query_most + width - 17 * LANES)

    def attention_back_one():
        g_pre = back.g_attn_both.reshape(rows, width)
        g_query, g_keyval, g_meta = attend_backward(
            key_blocks,
            query_b,
            keyval_all,
            meta_kv,
            bounds.T,
            attended,
            mass,
            g_pre,
            weight_two,
            weight_three,
        )
        pieces = attention_weights(
            normed_wide, attended_wide, g_query, g_pre, weight_one, weight_two, cuts
        )
        return [g_query, g_keyval, g_meta] + list(pieces)

    grad_query_b, grad_keyval, grad_meta_kv, sum_one, sum_two, sum_three, gain_query = on_core(
        0, attention_back_one
    )

    def cubed(blocks):
        return blocks.reshape(cube + (32, blocks.shape[-1]))

    small_cuts = (keys_width // 2, keys_width // 2, metas)
    sources = (
        grad_query_b,
        normed_wide,
        meta_wide,
        grad_meta_kv,
        weight_one,
        weight_two,
        meta_f,
        gain_row,
    )
    attention = exchange(
        "exchange_attention",
        8,
        program_attention,
        dict(
            keyval=(grad_keyval.reshape(2, SIDE, SIDE, half, keys_width), ANY),
            gate=(g_gate_own, ANY),
            one=(cubed(sum_one), ANY),
            two=(cubed(sum_two), ANY),
            three=(cubed(sum_three), ANY),
            sources={name: (array, ANY) for name, array in zip(INSIDE, sources)},
        ),
        dict(
            gate_own=((SIDE, SIDE, 32, units), low, ANY),
            sums=((32, query_most + width), full, VMEM),
            keys_sum=((32, keys_width + metas), full, VMEM),
            g_normed=((rows, width), full, VMEM),
            gain_part=((1, 64 * 32), full, VMEM),
            meta_gain=((1, width), full, VMEM),
        ),
        dict(
            upper_pad=two_pad(half, keys_width),
            lower_pad=two_pad(half, keys_width),
            gate_mid=((SIDE, SIDE, 32, units), low),
            keyval_sum=((rows, keys_width), full),
            g_wide=((rows, 64 * 32), full),
            g_meta_wide=((metas, 64 * 32), full),
            inside={name: (array.shape, array.dtype) for name, array in zip(INSIDE, sources)},
            keys=dict(zip(SUMS[3:], (((64 * 32, cut), low) for cut in small_cuts))),
            pads=dict(zip(SUMS, (three_pad(32, cut) for cut in cuts + small_cuts))),
            parts=dict(zip(SUMS, (((32, cut), full) for cut in cuts + small_cuts))),
        ),
        vmem=62 * 2**20,
        cores=(0,),
    )
    gain_attention = (gain_query + attention.gain_part).reshape(64, 32)[:, :piece].reshape(width)
    gain_attention = gain_attention / gain_norm + attention.meta_gain[0]

    g_first, g_second, grad_inputs, grad_gate_z, back_out, grad_rows, grad_rate = on_core(
        1,
        lambda: mixer_backward(
            inner,
            step_first,
            step_second,
            cols,
            channel,
            inputs_b,
            gate_z,
            back_wide,
            back.g_mamba_all.reshape(2, 16, half, width),
            mixed_y,
            ssm_out,
            starts,
            decay_t,
            drive_t,
            scan_rate,
        ),
    )
    g_first, g_second, last_gate = spread_projection(
        "exchange_last", 9, g_first, g_second, g_gate_own
    )

    def mamba_back_two():
        g_normed, g_weight, g_rows, gain = mixer_inputs(
            start_rows,
            g_first,
            g_second,
            channel,
            weight_mamba,
            normed_all,
            conv_in,
            inputs_b,
            grad_inputs,
            grad_gate_z,
        )
        return g_normed, g_weight, channel_grads(grad_rows, g_rows, grad_rate, channel), gain

    grad_normed_partial, mamba_out, channel_out, gain_mixer = on_core(1, mamba_back_two)
    gain_mixer = gain_mixer[0] / gain_norm
    grad_gain_norm = jnp.where(on_attention, gain_attention, gain_mixer)
    gains_out = pack_gains(
        *(grad[None] for grad in (grad_gain_norm, grad_gain_attn, grad_gain_mamba, grad_gain_feed))
    )
    ended = exchange(
        "exchange_end",
        1,
        program_end,
        dict(
            partial=(grad_normed_partial.reshape(2, SIDE, SIDE, half, width), ANY),
            g_attn=(attention.g_normed, ANY),
            sums_in=(attention.sums, ANY),
            keys=(attention.keys_sum, ANY),
            gate=(jnp.where(on_attention, attention.gate_own, last_gate), ANY),
            down=(back.g_down_sum.reshape(48, width), ANY),
            mamba=(mamba_out, ANY),
            back=(back_out, ANY),
            channel=(channel_out, ANY),
            gains=(gains_out.reshape(cube + (32, 128)), ANY),
        ),
        dict(
            normed_both=((2, half, width), full, ANY),
            sums=((32, query_most + width), full, ANY),
            keys_sum=((32, keys_width + metas), full, ANY),
            gate_both=((2, SIDE, SIDE, 32, units), low, ANY),
            down_both=((2, 48, width), full, ANY),
            mamba_sum=((SIDE, SIDE, 32, 4 * CHUNKS), low, ANY),
            back_sum=((1, 64, width), full, VMEM),
            channel_sum=((1, 64, 3 * LANES), full, VMEM),
            gains_both=((2, 32, 128), full, ANY),
        ),
        dict(
            normed_pad=half_pad(half, width),
            normed_sum=((half, width), full),
            attn_part=((half, width), full),
            gains_pad=three_pad(32, 128),
            gains_sum=((32, 128), full),
            mamba_pad=x_pad(16, 32, 4 * CHUNKS),
            mamba_part=((SIDE, SIDE, 32, 4 * CHUNKS), low),
            mamba_mid=((SIDE, SIDE, 32, 4 * CHUNKS), low),
            back_pad=x_pad(1, 64, width),
            channel_pad=x_pad(1, 64, 3 * LANES, full),
        ),
        vmem=48 * 2**20,
        partners=(True,),
    )
    (
        input_grad,
        grad_query,
        grad_keyval_in,
        grad_attn,
        grad_mamba,
        grad_back,
        grad_gate,
        grad_down,
        grad_meta,
        grad_ssm,
        grad_step,
        grad_log,
        grad_taps,
        grad_rows,
        grad_gains,
    ) = finish(
        piece,
        inner_piece,
        down_piece,
        inner,
        proj,
        rank,
        tokens_b,
        gain_row,
        back.g_hidden_both,
        ended.normed_both,
        ended.sums,
        ended.keys_sum,
        ended.mamba_sum.reshape(16, 32, -1),
        ended.back_sum,
        ended.channel_sum,
        ended.gate_both.reshape(2, 16, 32, units),
        ended.down_both,
        ended.gains_both,
    )
    return (
        mixed[None],
        input_grad[None],
        grad_gains[0],
        grad_meta,
        grad_query,
        grad_keyval_in,
        grad_attn,
        grad_gains[1],
        grad_mamba,
        grad_taps,
        grad_rows[4],
        grad_ssm,
        grad_step,
        grad_rows[5],
        grad_log,
        grad_rows[6],
        grad_back,
        grad_gains[2],
        grad_gains[3],
        grad_gate,
        grad_down,
    )


def solution(mesh):
    spread = ("seq", "fsdp")
    rows = P("fsdp", "seq", None)
    flat, first, second = P(spread), P(spread, None), P(None, spread)
    weights = (
        flat,
        second,
        first,
        first,
        first,
        flat,
        first,
        second,
        flat,
        first,
        second,
        flat,
        second,
        flat,
        first,
        flat,
        flat,
        first,
        first,
    )
    return jax.shard_map(
        shards,
        mesh=mesh,
        in_specs=(rows, P("fsdp", None)) + weights + (rows,),
        out_specs=(rows, rows) + weights,
        check_vma=False,
    )
```

```python
import functools
import types

import jax
import jax.numpy as jnp
from jax import lax
from jax.experimental import pallas as pl
from jax.experimental.pallas import tpu as pltpu
from jax.sharding import PartitionSpec as P

HEAD = 64
CONV = 4
SIDE = 4

epsilon = 1e-05
negative_fill = -1e30
score_scale = 0.125
log2_e = 1.4426950408889634
highest = lax.Precision.HIGHEST
MESH = pl.DeviceIdType.MESH
ANY = pl.BlockSpec(memory_space=pl.ANY)
VMEM = pl.BlockSpec(memory_space=pltpu.VMEM)
SEMS = 128
HOPS = (1, 3, 2)
X, Y, Z, FIRST, SECOND = range(5)


class Net:
    def __init__(self, core, coords, names, send, recv):
        self.core = core
        self.at = coords
        self.names = names
        self.send = send
        self.recv = recv
        self.begun = []

    def device(self, axis=None, hop=0, other_core=False, partner=False):
        place = dict(self.at)
        if partner:
            place[Y], place[Z] = SIDE - 1 - place[Y], SIDE - 1 - place[Z]
        if axis in (FIRST, SECOND):
            along_z = self.core == (0 if axis == FIRST else 1)
            place[Y] = jnp.where(along_z, place[Y], (place[Y] + hop) % SIDE)
            place[Z] = jnp.where(along_z, (place[Z] + hop) % SIDE, place[Z])
        elif axis is not None:
            place[axis] = (place[axis] + hop) % SIDE
        core = 1 - self.core if other_core else self.core
        return (core, place[Y] * SIDE + place[Z], place[X])

    def slot(self, name):
        return self.names.setdefault(name, len(self.names))

    def copy(self, name, source, target, device):
        i = self.slot(name)
        return pltpu.make_async_remote_copy(
            source,
            target,
            self.send.at[i],
            self.recv.at[i],
            device_id=device,
            device_id_type=MESH,
        )

    def start(self, name, source, target, device):
        copy = self.copy(name, source, target, device)
        copy.start()
        self.begun.append(copy)
        return copy

    def local(self, name, source, target):
        copy = pltpu.make_async_copy(source, target, self.send.at[self.slot(name)])
        copy.start()
        return copy


def pick(axes, fixed):
    return tuple(fixed.get(axis, slice(None)) for axis in axes)


def gather(net, name, source, out, axes, order, hold=0):
    at = net.at
    fixed = {axis: at[axis] for axis in axes}
    own = net.local((name, -1), source, out.at[pick(axes, fixed)])
    here = source
    for axis in order:
        if axis == order[-1]:
            for _ in range(hold):
                yield
        place = pick(axes, fixed)
        copies = [
            net.start(
                (name, axis, hop),
                out.at[place] if here is None else here,
                out.at[place],
                net.device(axis, hop),
            )
            for hop in HOPS
        ]
        yield
        for copy in copies:
            copy.wait_recv()
        if here is not None:
            own.wait()
        here = None
        del fixed[axis]


def gather_two(net, name, source, out, order, after=None, patience=0):
    at = net.at
    first, second = order

    def place(back):
        spot = dict(at)
        spot[first] = (spot[first] - back + SIDE) % SIDE
        return (spot[Y], spot[Z])

    mine = place(0)
    own = net.local((name, -1), source, out.at[mine])
    ones = [
        net.start((name, 1, hop), source, out.at[mine], net.device(first, hop)) for hop in HOPS
    ]
    twos = []

    def forward(back):
        spot = place(back)
        for hop in HOPS:
            twos.append(
                net.start(
                    (name, 2, back, hop),
                    source if back == 0 else out.at[spot],
                    out.at[spot],
                    net.device(second, hop),
                )
            )

    forward(0)
    yield
    for copy, hop in zip(ones, HOPS):
        copy.wait_recv()
        forward(hop)
    own.wait()
    for _ in range(1 + patience):
        yield
    if after is None:
        for copy in twos:
            copy.wait_recv()
        return
    lines = [twos[3 * i : 3 * i + 3] for i in range(SIDE)]
    after(at[second])
    for h, hop in enumerate(HOPS):
        for line in lines:
            line[h].wait_recv()
        after((at[second] - hop + SIDE) % SIDE)


NEAR = (1, 3)


def scatter_sum(total, rows, own, others, out):
    chunk = 16 if rows % 16 == 0 else 8
    per = rows // chunk

    def step(i, carry):
        lead = i // per
        part = pl.ds(pl.multiple_of((i % per) * chunk, chunk), chunk)
        value = own(lead, part).astype(jnp.float32)
        for other in others:
            value = value + other(lead, part).astype(jnp.float32)
        out(lead, part, value)
        return carry

    lax.fori_loop(0, total * per, step, 0)


def reduce_two(net, name, source, pad, out, order):
    at = net.at
    first, second = order
    one, mid, two, kept = pad.one, pad.mid, pad.two, pad.own
    rows = source.shape[2]

    def part_of(line):
        return source.at[:, line] if first == Z else source.at[line]

    own = net.local((name, -4), part_of(at[first]), kept)
    ones = [
        net.start(
            (name, 1, hop),
            part_of((at[first] + hop) % SIDE),
            one.at[hop - 1],
            net.device(first, hop),
        )
        for hop in HOPS
    ]
    yield
    own.wait()
    for copy in ones:
        copy.wait_recv()

    def put_mid(lead, part, value):
        mid[lead, part, :] = value.astype(mid.dtype)

    scatter_sum(
        SIDE,
        rows,
        lambda lead, part: kept[lead, part, :],
        [lambda lead, part, k=k: one[k, lead, part, :] for k in range(3)],
        put_mid,
    )
    twos = [
        net.start(
            (name, 2, hop),
            mid.at[(at[second] + hop) % SIDE],
            two.at[hop - 1],
            net.device(second, hop),
        )
        for hop in HOPS
    ]
    yield
    for copy in twos:
        copy.wait_recv()
    spot = at[second]

    def put_out(lead, part, value):
        out[part, :] = value.astype(out.dtype)

    scatter_sum(
        1,
        rows,
        lambda lead, part: kept[spot, part, :],
        [lambda lead, part, k=k: one[k, spot, part, :] for k in range(3)]
        + [lambda lead, part, k=k: two[k, part, :] for k in range(3)],
        put_out,
    )


def reduce_ring(net, name, source, pad, out):
    at = net.at
    rows = source.shape[2]
    half = rows // 2
    halves = {1: pl.ds(0, half), 3: pl.ds(half, half)}
    stages = (
        (FIRST, pad.one, pad.via_one, pad.mix_one),
        (SECOND, pad.two, pad.via_two, pad.mix_two),
    )

    def lines(stage, place, part):
        return pad.mid.at[place, part] if stage else source.at[place, :, part]

    whole = pl.ds(0, rows)
    for stage, (axis, recv, via, mix) in enumerate(stages):

        def spot(hop, axis=axis):
            return (at[axis] + hop) % SIDE

        arrivals, fetched, passing = [], [], []
        if stage == 0:
            yield
        for i, hop in enumerate(NEAR):
            across = lines(stage, spot(2), halves[hop])
            passing.append(
                net.start((name, stage, 0, hop), across, via.at[i], net.device(axis, hop))
            )
        for i, hop in enumerate(NEAR):
            if stage == 0:
                yield
            other = halves[4 - hop]
            fetched.append(
                net.local((name, stage, 3, hop), lines(stage, spot(hop), halves[hop]), mix.at[i])
            )
            target = recv.at[i, other] if stage else recv.at[i, :, other]
            arrivals.append(
                net.start(
                    (name, stage, 1, hop),
                    lines(stage, spot(hop), other),
                    target,
                    net.device(axis, hop),
                )
            )
        if stage == 0:
            yield
            own = net.local((name, -4), lines(0, spot(0), whole), pad.own)
        yield
        for i, hop in enumerate(NEAR):
            fetched[i].wait()
            passing[i].wait_recv()

            def put(lead, part, value, i=i, mix=mix, stage=stage):
                index = (i, part) if stage else (i, lead, part)
                mix[index + (slice(None),)] = value.astype(mix.dtype)

            def get(ref, i=i, stage=stage):
                if stage:
                    return lambda lead, part: ref[i, part, :]
                return lambda lead, part: ref[i, lead, part, :]

            scatter_sum(1 if stage else SIDE, half, get(mix), [get(via)], put)
            target = recv.at[i, halves[hop]] if stage else recv.at[i, :, halves[hop]]
            arrivals.append(
                net.start((name, stage, 2, hop), mix.at[i], target, net.device(axis, hop))
            )
        yield
        for copy in arrivals:
            copy.wait_recv()
        if stage == 0:
            own.wait()

            def put_mid(lead, part, value):
                pad.mid[lead, part, :] = value.astype(pad.mid.dtype)

            scatter_sum(
                SIDE,
                rows,
                lambda lead, part: pad.own[lead, part, :],
                [lambda lead, part, k=k: pad.one[k, lead, part, :] for k in range(2)],
                put_mid,
            )
    mine = at[SECOND]

    def put_out(lead, part, value):
        out[part, :] = value.astype(out.dtype)

    scatter_sum(
        1,
        rows,
        lambda lead, part: pad.own[mine, part, :],
        [lambda lead, part, k=k: pad.one[k, mine, part, :] for k in range(2)]
        + [lambda lead, part, k=k: pad.two[k, part, :] for k in range(2)],
        put_out,
    )


def swap_two(net, name, source, mid, out):
    at = net.at
    own = net.local((name, -1), source.at[:, at[Z]], mid.at[at[Z]])
    ones = [
        net.start(
            (name, 1, hop),
            source.at[:, (at[Z] + hop) % SIDE],
            mid.at[at[Z]],
            net.device(Z, hop),
        )
        for hop in HOPS
    ]
    yield
    for copy in ones:
        copy.wait_recv()
    own.wait()
    own = net.local((name, -2), mid.at[:, at[Y]], out.at[at[Y]])
    twos = [
        net.start(
            (name, 2, hop),
            mid.at[:, (at[Y] + hop) % SIDE],
            out.at[at[Y]],
            net.device(Y, hop),
        )
        for hop in HOPS
    ]
    yield
    for copy in twos:
        copy.wait_recv()
    own.wait()


def run_jobs(jobs):
    jobs = list(jobs)
    while jobs:
        jobs = [job for job in jobs if next(job, True) is None]


def flat(group):
    return [
        leaf
        for value in group.values()
        for leaf in (flat(value) if isinstance(value, dict) else [value])
    ]


def named(group, leaves):
    return types.SimpleNamespace(
        **{
            key: named(value, leaves) if isinstance(value, dict) else next(leaves)
            for key, value in group.items()
        }
    )


def exchange(
    name,
    number,
    program,
    inputs,
    outputs,
    scratch=None,
    vmem=None,
    cores=(0, 1),
    shared=False,
    partners=(),
):
    scratch = scratch or {}
    parts = (inputs, outputs, scratch)
    counts = [len(flat(part)) for part in parts]

    def kernel(*refs):
        held = types.SimpleNamespace()
        begin = 0
        for part, count in zip(parts, counts):
            vars(held).update(vars(named(part, iter(refs[begin : begin + count]))))
            begin += count
        send, recv = refs[begin:]
        core = lax.axis_index("branch")
        seq = lax.axis_index("seq")
        coords = {X: lax.axis_index("fsdp"), Y: seq // SIDE, Z: seq % SIDE}
        names = {}

        def run(own_core):
            net = Net(own_core, coords, names, send, recv)
            barrier = pltpu.get_barrier_semaphore()
            peers = [net.device(axis, hop) for axis in (X, Y, Z) for hop in HOPS]
            if len(cores) == 2:
                peers.append(net.device(other_core=True))
            peers += [net.device(other_core=other, partner=True) for other in partners]
            for peer in peers:
                pl.semaphore_signal(barrier, inc=1, device_id=peer, device_id_type=MESH)
            pl.semaphore_wait(barrier, len(peers))
            run_jobs(program(net, held))
            for copy in net.begun:
                copy.wait_send()

        if shared:
            coords[FIRST] = jnp.where(core == 0, coords[Z], coords[Y])
            coords[SECOND] = jnp.where(core == 0, coords[Y], coords[Z])
            run(core)
        else:
            for one_core in cores:
                pl.when(core == one_core)(functools.partial(run, one_core))

        assert len(names) <= SEMS

    results = pl.pallas_call(
        kernel,
        out_shape=[jax.ShapeDtypeStruct(s, d) for s, d, _ in flat(outputs)],
        in_specs=[spec for _, spec in flat(inputs)],
        out_specs=[spec for _, _, spec in flat(outputs)],
        scratch_shapes=[pltpu.VMEM(s, d) for s, d in flat(scratch)]
        + [pltpu.SemaphoreType.DMA((SEMS,)), pltpu.SemaphoreType.DMA((SEMS,))],
        compiler_params=pltpu.CompilerParams(
            collective_id=number, has_side_effects=True, vmem_limit_bytes=vmem
        ),
        name=name,
    )(*[array for array, _ in flat(inputs)])
    return named(outputs, iter(results))


CHUNKS = 128
STEPS = 16
LINES = 8
WIDE = 40
far_away = 1e30


def to_lanes(source, target):
    for block in range(source.shape[0]):
        part = pl.ds(block * CHUNKS, CHUNKS)

        def move(l, carry):
            target[l, part, :] = source[block, pl.ds(l, CHUNKS, stride=STEPS), :].T
            return carry

        lax.fori_loop(0, STEPS, move, 0, unroll=2)


def to_rows(source, target):
    for block in range(target.shape[0]):
        part = pl.ds(block * CHUNKS, CHUNKS)

        def move(l, carry):
            target[block, pl.ds(l, CHUNKS, stride=STEPS), :] = source[l, part, :].T
            return carry

        lax.fori_loop(0, STEPS, move, 0, unroll=2)


def chunk_starts(ends, span, rates, reverse):
    lanes = lax.broadcasted_iota(jnp.int32, span.shape, 1)
    by = 1
    while by < CHUNKS:
        turn = CHUNKS - by if reverse else by
        inside = lanes < turn if reverse else lanes >= turn
        reach = jnp.where(inside, span, far_away)
        ends = [
            end + jnp.exp2(reach * rate) * pltpu.roll(end, turn, 1)
            for end, rate in zip(ends, rates)
        ]
        span = span + jnp.where(inside, pltpu.roll(span, turn, 1), 0.0)
        by *= 2
    turn = CHUNKS - 1 if reverse else 1
    inside = lanes < turn if reverse else lanes >= turn
    return [jnp.where(inside, pltpu.roll(end, turn, 1), 0.0) for end in ends]


def rate_lines(rate_ref, lines, states):
    tile = rate_ref[lines, :]
    return [jnp.broadcast_to(tile[:, s : s + 1], (lines.size, CHUNKS)) for s in range(states)]


def join_chunks(used, ends_ref, decay_t, rate_ref, reverse):
    states = rate_ref.shape[1]

    def channels(g, carry):
        lines = pl.ds(pl.multiple_of(g * WIDE, LINES), WIDE)
        span = decay_t[0, lines, :]
        for l in range(1, STEPS):
            span = span + decay_t[l, lines, :]
        starts = chunk_starts(
            [ends_ref[s, lines, :] for s in range(states)],
            span,
            rate_lines(rate_ref, lines, states),
            reverse,
        )
        for s in range(states):
            ends_ref[s, lines, :] = starts[s]
        return carry

    lax.fori_loop(0, used // WIDE, channels, 0)


def scan_forward_body(
    used, decay_ref, drive_ref, cols_ref, rate_ref, out_ref, start_ref, decay_t, drive_t, out_t
):
    states = rate_ref.shape[1]

    def col(l, s):
        return cols_ref[l, pl.ds(FIRST_COL + s, 1), :]

    to_lanes(decay_ref, decay_t)
    to_lanes(drive_ref, drive_t)
    out_t[...] = jnp.zeros_like(out_t)

    def ends(g, carry):
        lines = pl.ds(pl.multiple_of(g * LINES, LINES), LINES)
        decays = [decay_t[l, lines, :] for l in range(STEPS)]
        drives = [drive_t[l, lines, :] for l in range(STEPS)]
        rates = rate_lines(rate_ref, lines, states)
        for s in range(states):
            state = drives[0] * col(0, s)
            for l in range(1, STEPS):
                state = jnp.exp2(decays[l] * rates[s]) * state + drives[l] * col(l, s)
            start_ref[s, lines, :] = state
        return carry

    lax.fori_loop(0, used // LINES, ends, 0)
    join_chunks(used, start_ref, decay_t, rate_ref, False)

    def channels(g, carry):
        lines = pl.ds(pl.multiple_of(g * LINES, LINES), LINES)
        decays = [decay_t[l, lines, :] for l in range(STEPS)]
        drives = [drive_t[l, lines, :] for l in range(STEPS)]
        rates = rate_lines(rate_ref, lines, states)
        outs = [jnp.zeros((LINES, CHUNKS), jnp.float32)] * STEPS
        for s in range(states):
            state = start_ref[s, lines, :]
            for l in range(STEPS):
                state = jnp.exp2(decays[l] * rates[s]) * state + drives[l] * col(l, s)
                outs[l] = outs[l] + state * col(l, states + s)
        for l in range(STEPS):
            out_t[l, lines, :] = outs[l]
        return carry

    lax.fori_loop(0, used // LINES, channels, 0)
    to_rows(out_t, out_ref)


def scan_backward_body(
    used,
    decay_t,
    drive_t,
    cols_ref,
    rate_ref,
    start_ref,
    grad_ref,
    g_decay_ref,
    g_drive_ref,
    g_cols_ref,
    g_rate_ref,
    grad_t,
    g_decay_t,
    g_drive_t,
    sums_t,
    ends_t,
):
    states = rate_ref.shape[1]

    def col(l, s):
        return cols_ref[l, pl.ds(FIRST_COL + s, 1), :]

    blank = jnp.zeros((LINES, CHUNKS), jnp.float32)
    to_lanes(grad_ref, grad_t)
    g_decay_t[...] = jnp.zeros_like(g_decay_t)
    g_drive_t[...] = jnp.zeros_like(g_drive_t)
    sums_t[...] = jnp.zeros_like(sums_t)
    g_rate_ref[...] = jnp.zeros_like(g_rate_ref)
    marks = lax.broadcasted_iota(jnp.int32, (LINES, states), 1)

    def ends(g, carry):
        lines = pl.ds(pl.multiple_of(g * LINES, LINES), LINES)
        rates = rate_lines(rate_ref, lines, states)
        decays = [decay_t[l, lines, :] for l in range(STEPS)]
        grads = [grad_t[l, lines, :] for l in range(STEPS)]
        for s in range(states):
            back = blank
            for l in reversed(range(STEPS)):
                back = jnp.exp2(decays[l] * rates[s]) * (
                    grads[l] * col(l, states + s) + back
                )
            ends_t[s, lines, :] = back
        return carry

    lax.fori_loop(0, used // LINES, ends, 0)
    join_chunks(used, ends_t, decay_t, rate_ref, True)

    def channels(g, carry):
        lines = pl.ds(pl.multiple_of(g * LINES, LINES), LINES)
        tile = rate_ref[lines, :]

        def state_step(s, g_rate):
            rate = jnp.sum(jnp.where(marks == s, tile, 0.0), axis=1, keepdims=True)
            rate = jnp.broadcast_to(rate, (LINES, CHUNKS))
            state = start_ref[s, lines, :]
            befores, factors = [], []
            for l in range(STEPS):
                factor = jnp.exp2(decay_t[l, lines, :] * rate)
                befores.append(state)
                factors.append(factor)
                state = factor * state + drive_t[l, lines, :] * col(l, s)
            back = ends_t[s, lines, :]
            total_rate = blank
            for l in reversed(range(STEPS)):
                grad = grad_t[l, lines, :]
                total = grad * col(l, states + s) + back
                sums_t[s, l] += total * drive_t[l, lines, :]
                sums_t[states + s, l] += grad * state
                g_drive_t[l, lines, :] += total * col(l, s)
                back = total * factors[l]
                moved = back * befores[l]
                g_decay_t[l, lines, :] += moved * rate
                total_rate = total_rate + moved * decay_t[l, lines, :]
                state = befores[l]
            total_rate = jnp.sum(total_rate, axis=1, keepdims=True)
            return jnp.where(marks == s, total_rate, g_rate)

        g_rate_ref[lines, :] = lax.fori_loop(
            0, states, state_step, jnp.zeros((LINES, states), jnp.float32), unroll=16
        )
        return carry

    lax.fori_loop(0, used // LINES, channels, 0)

    for i in range(2 * states):
        g_cols_ref[:, FIRST_COL + i, :] = jnp.sum(sums_t[i], axis=1)
    to_rows(g_decay_t, g_decay_ref)
    to_rows(g_drive_t, g_drive_ref)


KEY_ROWS = 256
PIECE = 25
PADDED = 32
LANES = 128


def dot_on(left, right, left_dim, right_dim, **options):
    return lax.dot_general(
        left,
        right,
        (((left_dim,), (right_dim,)), ((), ())),
        preferred_element_type=jnp.float32,
        **options,
    )


def spread_matrix(low, high, wide_low, wide_high):
    shape = (high - low, wide_high - wide_low)
    column = low + lax.broadcasted_iota(jnp.int32, shape, 0)
    place = wide_low + lax.broadcasted_iota(jnp.int32, shape, 1)
    inside = place % PADDED
    match = (column == (place // PADDED) * PIECE + inside) & (inside < PIECE)
    return jnp.where(match, 1.0, 0.0).astype(jnp.bfloat16)


def spread_columns(values):
    width = values.shape[1]
    step = LANES // PADDED * PIECE
    parts = []
    for begin in range(0, width, step):
        low = begin // LANES * LANES
        high = min(low + 2 * LANES, width)
        wide = begin // PIECE * PADDED
        parts.append(dot_on(values[:, low:high], spread_matrix(low, high, wide, wide + LANES), 1, 0))
    return jnp.concatenate(parts, axis=1).astype(jnp.bfloat16)


def close_columns(values):
    width = values.shape[1] // PADDED * PIECE
    parts = []
    for begin in range(0, width, LANES):
        end = min(begin + LANES, width)
        low = begin // PIECE * PADDED // LANES * LANES
        high = -(-((end - 1) // PIECE + 1) * PADDED // LANES) * LANES
        matrix = spread_matrix(begin, end, low, high)
        value = values[:, low:high]
        most = value.astype(jnp.bfloat16)
        closed = dot_on(most, matrix, 1, 1)
        if values.dtype != jnp.bfloat16:
            rest = (value - most.astype(jnp.float32)).astype(jnp.bfloat16)
            closed = closed + dot_on(rest, matrix, 1, 1)
        parts.append(closed)
    return jnp.concatenate(parts, axis=1)


def unit_rows(values):
    return values * lax.rsqrt(jnp.mean(values * values, axis=-1, keepdims=True) + epsilon)


def whole_call(name, body, arrays, results, scratch=(), scalars=0, room=48, fetch=False):
    count = len(arrays)
    scratch_shapes = [pltpu.VMEM(shape, kind) for shape, kind in scratch]

    def fetching(*refs):
        sources, middle, held = refs[:count], refs[count : -count - 1], refs[-count - 1 : -1]
        copies = [
            pltpu.make_async_copy(source, target, refs[-1].at[i])
            for i, (source, target) in enumerate(zip(sources, held))
        ]
        for copy in copies:
            copy.start()
        for copy in copies:
            copy.wait()
        body(*held, *middle)

    if fetch:
        scratch_shapes += [pltpu.VMEM(array.shape, array.dtype) for array in arrays]
        scratch_shapes.append(pltpu.SemaphoreType.DMA((count,)))
    return pl.pallas_call(
        fetching if fetch else body,
        out_shape=[jax.ShapeDtypeStruct(shape, kind) for shape, kind in results],
        in_specs=[pl.BlockSpec(memory_space=pltpu.SMEM)] * scalars
        + [ANY if fetch else VMEM] * (count - scalars),
        out_specs=[VMEM] * len(results),
        scratch_shapes=scratch_shapes,
        compiler_params=pltpu.CompilerParams(vmem_limit_bytes=room * 2**20),
        name=name,
    )(*arrays)


def attention_project_kernel(
    tokens_ref,
    meta_ref,
    gain_ref,
    first_ref,
    second_ref,
    wide_ref,
    query_ref,
    keyval_ref,
    meta_wide_ref,
    meta_kv_ref,
):
    gain = gain_ref[...]
    third = first_ref.shape[1]
    rest = query_ref.shape[1] - third
    begin = -(-rest // LANES) * LANES
    keys = pl.ds(begin, keyval_ref.shape[1])
    wide = spread_columns((unit_rows(tokens_ref[...].astype(jnp.float32)) * gain).astype(jnp.bfloat16))
    wide_ref[...] = wide
    query_ref[:, pl.ds(0, third)] = dot_on(wide, first_ref[...], 1, 0).astype(jnp.bfloat16)
    query_ref[:, pl.ds(third, rest)] = dot_on(wide, second_ref[:, pl.ds(0, rest)], 1, 0).astype(
        jnp.bfloat16
    )
    keyval_ref[...] = dot_on(wide, second_ref[:, keys], 1, 0).astype(jnp.bfloat16)
    meta_wide = spread_columns((unit_rows(meta_ref[...]) * gain).astype(jnp.bfloat16))
    meta_wide_ref[...] = meta_wide
    meta_kv_ref[...] = dot_on(meta_wide, second_ref[:, keys], 1, 0).astype(jnp.bfloat16)


def attention_project(tokens, meta, gain, first, second, query_width, keys_width):
    rows, metas, wide = tokens.shape[0], meta.shape[0], first.shape[0]
    low = jnp.bfloat16
    return whole_call(
        "attention_project",
        attention_project_kernel,
        (tokens, meta, gain, first, second),
        (
            ((rows, wide), low),
            ((rows, query_width), low),
            ((rows, keys_width), low),
            ((metas, wide), low),
            ((metas, keys_width), low),
        ),
    )


def attention_weights_kernel(
    wide_ref,
    out_wide_ref,
    g_query_ref,
    g_pre_ref,
    first_ref,
    second_ref,
    one_ref,
    two_ref,
    three_ref,
    gain_ref,
):
    third = first_ref.shape[1]
    one = dot_on(wide_ref[...], g_query_ref[...], 0, 0)
    cut = one_ref.shape[1]
    one_ref[...] = one[:, :cut].astype(jnp.bfloat16)
    gain = jnp.sum(one[:, :third] * first_ref[...].astype(jnp.float32), axis=1, keepdims=True)
    rest = one.shape[1] - third
    gain = gain + jnp.sum(
        one[:, third:] * second_ref[:, pl.ds(0, rest)].astype(jnp.float32), axis=1, keepdims=True
    )
    gain_ref[...] = gain.T
    two = dot_on(out_wide_ref[...], g_pre_ref[...], 0, 0)
    size = one.shape[1] - cut
    begin = -(-size // LANES) * LANES
    left = two_ref.shape[1] - begin
    two_ref[...] = jnp.zeros_like(two_ref)
    two_ref[:, pl.ds(0, size)] = one[:, cut:].astype(jnp.bfloat16)
    two_ref[:, pl.ds(begin, left)] = two[:, :left].astype(jnp.bfloat16)
    three_ref[...] = two[:, left:].astype(jnp.bfloat16)


def attention_weights(wide, out_wide, g_query, g_pre, first, second, cuts):
    rows, places = wide.shape
    size = 2 * LANES
    columns = pl.BlockSpec((rows, size), lambda i: (0, i))

    def lines(width):
        return pl.BlockSpec((size, width), lambda i: (i, 0))

    return pl.pallas_call(
        attention_weights_kernel,
        grid=(places // size,),
        out_shape=[jax.ShapeDtypeStruct((places, cut), jnp.bfloat16) for cut in cuts]
        + [jax.ShapeDtypeStruct((1, places), jnp.float32)],
        in_specs=[columns, columns]
        + [pl.BlockSpec(part.shape, lambda i: (0, 0)) for part in (g_query, g_pre)]
        + [lines(first.shape[1]), lines(second.shape[1])],
        out_specs=[lines(cut) for cut in cuts] + [pl.BlockSpec((1, size), lambda i: (0, i))],
        compiler_params=pltpu.CompilerParams(vmem_limit_bytes=32 * 2**20),
        name="attention_weights",
    )(wide, out_wide, g_query, g_pre, first, second)


def attention_inputs_kernel(
    keyval_ref,
    g_query_ref,
    wide_ref,
    meta_wide_ref,
    g_meta_ref,
    first_ref,
    second_ref,
    meta_ref,
    gain_ref,
    one_ref,
    two_ref,
    three_ref,
    g_normed_ref,
    part_ref,
    meta_gain_ref,
    g_wide_ref,
    g_meta_wide_ref,
):
    third = first_ref.shape[1]
    rest = g_query_ref.shape[1] - third
    begin = -(-rest // LANES) * LANES
    keys = pl.ds(begin, keyval_ref.shape[1])
    keyval = keyval_ref[...].astype(jnp.bfloat16)
    g_meta = g_meta_ref[...]
    half = one_ref.shape[1]
    places = wide_ref.shape[1]
    size = places // 4

    def part_of(i, carry):
        spot = pl.ds(pl.multiple_of(i * size, size), size)
        weight = second_ref[spot, keys]
        weight_f = weight.astype(jnp.float32)
        grad = dot_on(wide_ref[:, spot], keyval, 0, 0)
        part_ref[:, spot] = jnp.sum(grad * weight_f, axis=1, keepdims=True).T
        grad = grad + dot_on(
            meta_wide_ref[:, spot].astype(jnp.float32), g_meta, 0, 0, precision=highest
        )
        one_ref[spot, :] = grad[:, :half].astype(jnp.bfloat16)
        two_ref[spot, :] = grad[:, half:].astype(jnp.bfloat16)
        total = dot_on(g_query_ref[:, pl.ds(0, third)], first_ref[spot, :], 1, 1)
        total = total + dot_on(
            g_query_ref[:, pl.ds(third, rest)], second_ref[spot, pl.ds(0, rest)], 1, 1
        )
        g_wide_ref[:, spot] = total + dot_on(keyval, weight, 1, 1)
        g_meta_wide_ref[:, spot] = dot_on(g_meta, weight_f, 1, 1, precision=highest)
        return carry

    lax.fori_loop(0, 4, part_of, 0)
    g_normed_ref[...] = close_columns(g_wide_ref[...])
    g_meta_normed = close_columns(g_meta_wide_ref[...])
    meta = meta_ref[...]
    scale = lax.rsqrt(jnp.mean(meta * meta, axis=-1, keepdims=True) + epsilon)
    unit = meta * scale
    meta_gain_ref[...] = jnp.sum(g_meta_normed * unit, axis=0, keepdims=True)
    g_unit = g_meta_normed * gain_ref[...]
    g_rows = scale * (g_unit - unit * jnp.mean(g_unit * unit, axis=-1, keepdims=True))
    three_ref[...] = spread_columns(g_rows.astype(jnp.bfloat16)).T


INSIDE = ("g_query", "wide", "meta_wide", "g_meta", "first", "second", "meta", "gain")


def stack_heads(source, target, scale, in_values):
    half = source.shape[0] // 2
    groups = target.shape[0]
    per = target.shape[1] // (2 * half)
    blank = jnp.zeros((half, HEAD), target.dtype)
    for group in range(groups):
        for j in range(per):
            head = source[:, pl.ds((group * per + j) * HEAD, HEAD)].astype(jnp.float32) * scale
            head = head.astype(target.dtype)
            for part in range(2):
                value = head[part * half : (part + 1) * half]
                pair = [blank, value] if in_values else [value, blank]
                target[group, pl.ds((part * per + j) * half, half), :] = jnp.concatenate(
                    pair, axis=1
                )


def lay_keys(source, target):
    places, rows = source.shape[1:3]

    def move(place, carry):
        for half in range(2):
            begin = pl.multiple_of((place * 2 + half) * rows, rows)
            target[pl.ds(begin, rows), :] = source[half, (places - 1 - place) if half else place]
        return carry

    lax.fori_loop(0, places, move, 0)


def key_bias(bounds_ref, part, begin, per):
    rows = bounds_ref.shape[0] // 2
    spot = pl.ds(part * rows, rows)
    keys = begin + lax.broadcasted_iota(jnp.int32, (rows, KEY_ROWS), 1)
    allowed = (keys >= bounds_ref[spot, 0:1]) & (keys <= bounds_ref[spot, 1:2])
    bias = jnp.where(allowed, 0.0, negative_fill)
    return jnp.concatenate([bias] * per, axis=0)


def key_bias_turned(bounds_ref, part, begin, per):
    rows = bounds_ref.shape[1] // 2
    keys = begin + lax.broadcasted_iota(jnp.int32, (KEY_ROWS, 2 * rows), 0)
    allowed = (keys >= bounds_ref[0:1, :]) & (keys <= bounds_ref[1:2, :])
    bias = jnp.where(allowed, 0.0, negative_fill)[:, part * rows : (part + 1) * rows]
    return jnp.concatenate([bias] * per, axis=1)


def attend_forward_kernel(
    count_ref,
    query_ref,
    keyval_ref,
    meta_ref,
    bounds_ref,
    second_ref,
    third_ref,
    out_ref,
    mass_ref,
    wide_ref,
    pre_ref,
    heads,
    keys,
    scores,
    tops,
    totals,
    outs,
):
    half = query_ref.shape[0] // 2
    groups = heads.shape[0]
    per = heads.shape[1] // (2 * half)
    stack = per * half
    width = 2 * HEAD
    metas = meta_ref.shape[0]
    meta_part = pl.ds(scores.shape[2] - metas, metas)
    stack_heads(query_ref, heads, score_scale, False)
    lay_keys(keyval_ref, keys)
    lanes = lax.broadcasted_iota(jnp.int32, (stack, mass_ref.shape[1]), 1)
    parts = [pl.ds(group * width, width) for group in range(groups)]

    def across(values):
        return [values[:, i : i + LANES] for i in range(0, values.shape[1], LANES)]

    for side in range(2):
        stacked = pl.ds(side * stack, stack)
        count = count_ref[side]
        for group in range(groups):
            value = dot_on(heads[group, stacked, :], meta_ref[:, parts[group]], 1, 1)
            scores[group, :, meta_part] = value
            tops[group] = value

        def score(b, carry):
            begin = pl.multiple_of(b * KEY_ROWS, KEY_ROWS)
            bias = key_bias(bounds_ref, side, begin, per)
            for group in range(groups):
                block = keys[pl.ds(begin, KEY_ROWS), parts[group]]
                value = dot_on(heads[group, stacked, :], block, 1, 1) + bias
                scores[group, :, pl.ds(begin, KEY_ROWS)] = value
                tops[group] = functools.reduce(jnp.maximum, across(value), tops[group])
            return carry

        lax.fori_loop(0, count, score, 0)
        for group in range(groups):
            top = jnp.max(tops[group], axis=1, keepdims=True)
            tops[group] = jnp.broadcast_to(top, tops.shape[1:])
            value = jnp.exp(scores[group, :, meta_part] - tops[group])
            totals[group] = value
            outs[group] = dot_on(value.astype(jnp.bfloat16), meta_ref[:, parts[group]], 1, 0)

        def weigh(b, carry):
            begin = pl.multiple_of(b * KEY_ROWS, KEY_ROWS)
            for group in range(groups):
                top = tops[group]
                value = [
                    jnp.exp(piece - top) for piece in across(scores[group, :, pl.ds(begin, KEY_ROWS)])
                ]
                totals[group] += sum(value)
                value = jnp.concatenate(value, axis=1).astype(jnp.bfloat16)
                outs[group] += dot_on(value, keys[pl.ds(begin, KEY_ROWS), parts[group]], 1, 0)
            return carry

        lax.fori_loop(0, count, weigh, 0)
        mass = jnp.zeros(lanes.shape, jnp.float32)
        for group in range(groups):
            total = jnp.sum(totals[group], axis=1, keepdims=True)
            out = outs[group] * (1.0 / total)
            for j in range(per):
                out_ref[pl.ds(side * half, half), pl.ds((group * per + j) * HEAD, HEAD)] = out[
                    j * half : (j + 1) * half, HEAD:
                ]
            mass = jnp.where(lanes == group, tops[group] + jnp.log(total), mass)
        mass_ref[stacked, :] = mass
    wide = spread_columns(out_ref[...].astype(jnp.bfloat16))
    wide_ref[...] = wide
    most = third_ref.shape[1]
    part = pre_ref.shape[1] - most
    pre_ref[:, pl.ds(0, part)] = dot_on(
        wide, second_ref[:, pl.ds(second_ref.shape[1] - part, part)], 1, 0
    )
    pre_ref[:, pl.ds(part, most)] = dot_on(wide, third_ref[...], 1, 0)


def attend_forward(count, query, keyval, meta, bounds, second, third):
    rows, query_width = query.shape
    groups = meta.shape[1] // (2 * HEAD)
    stacked = query_width // HEAD // groups * rows
    key_rows = 2 * keyval.shape[1] * keyval.shape[2]
    places, low, full = second.shape[0], jnp.bfloat16, jnp.float32
    return whole_call(
        "attend_forward",
        attend_forward_kernel,
        (count, query, keyval, meta, bounds, second, third),
        (
            ((rows, query_width), full),
            ((stacked, 2 * HEAD), full),
            ((rows, places), low),
            ((rows, query_width), full),
        ),
        (
            ((groups, stacked, 2 * HEAD), low),
            ((key_rows, meta.shape[1]), low),
            ((groups, stacked // 2, key_rows + meta.shape[0]), full),
            *[((groups, stacked // 2, LANES), full)] * 3,
        ),
        scalars=1,
        room=60,
    )


def attend_backward_kernel(
    count_ref,
    query_ref,
    keyval_ref,
    meta_ref,
    bounds_ref,
    out_ref,
    mass_ref,
    g_pre_ref,
    second_ref,
    third_ref,
    g_query_ref,
    g_keyval_ref,
    g_meta_ref,
    heads,
    grads,
    keys,
    grad_ref,
    g_keys,
    g_queries,
):
    half = query_ref.shape[0] // 2
    groups = heads.shape[0]
    per = heads.shape[1] // (2 * half)
    stack = per * half
    width = 2 * HEAD
    most = third_ref.shape[1]
    left = g_pre_ref.shape[1] - most
    grad_wide = dot_on(
        g_pre_ref[:, pl.ds(0, left)],
        second_ref[:, pl.ds(second_ref.shape[1] - left, left)],
        1,
        1,
    )
    grad_wide = grad_wide + dot_on(g_pre_ref[:, pl.ds(left, most)], third_ref[...], 1, 1)
    grad_ref[...] = close_columns(grad_wide.astype(jnp.bfloat16)).astype(jnp.bfloat16)
    stack_heads(query_ref, heads, score_scale, False)
    stack_heads(grad_ref, grads, 1.0, True)
    lay_keys(keyval_ref, keys)
    g_keys[...] = jnp.zeros_like(g_keys)
    lanes = lax.broadcasted_iota(jnp.int32, (stack, mass_ref.shape[1]), 1)
    parts = [pl.ds(group * width, width) for group in range(groups)]
    for side in range(2):
        stacked = pl.ds(side * stack, stack)
        rows = pl.ds(side * half, half)
        mass_rows, balance_rows = [], []
        for group in range(groups):
            mass = jnp.sum(
                jnp.where(lanes == group, mass_ref[stacked, :], 0.0), axis=1, keepdims=True
            )
            balance = []
            for j in range(per):
                head = pl.ds((group * per + j) * HEAD, HEAD)
                product = grad_ref[rows, head].astype(jnp.float32) * out_ref[rows, head]
                balance.append(jnp.sum(product, axis=1, keepdims=True))
            mass_rows.append(mass.T)
            balance_rows.append(jnp.concatenate(balance, axis=0).T)

        def pieces(group, block, bias):
            query, grad = heads[group, stacked, :], grads[group, stacked, :]
            value = dot_on(block, query, 1, 1)
            if bias is not None:
                value = value + bias
            probs = jnp.exp(value - mass_rows[group])
            g_scores = probs * (dot_on(block, grad, 1, 1) - balance_rows[group])
            g_scores = g_scores.astype(jnp.bfloat16)
            g_block = dot_on(g_scores, query, 1, 0) + dot_on(probs.astype(jnp.bfloat16), grad, 1, 0)
            return dot_on(g_scores, block, 0, 0), g_block

        for group in range(groups):
            g_queries[group], g_meta = pieces(group, meta_ref[:, parts[group]], None)
            if side:
                g_meta = g_meta + g_meta_ref[:, parts[group]]
            g_meta_ref[:, parts[group]] = g_meta

        def step(b, carry):
            begin = pl.multiple_of(b * KEY_ROWS, KEY_ROWS)
            bias = key_bias_turned(bounds_ref, side, begin, per)
            for group in range(groups):
                block = keys[pl.ds(begin, KEY_ROWS), parts[group]]
                more, g_block = pieces(group, block, bias)
                g_queries[group] += more
                g_keys[pl.ds(begin, KEY_ROWS), parts[group]] += g_block
            return carry

        lax.fori_loop(0, count_ref[side], step, 0)
        for group in range(groups):
            g_query = g_queries[group] * score_scale
            for j in range(per):
                g_query_ref[rows, pl.ds((group * per + j) * HEAD, HEAD)] = g_query[
                    j * half : (j + 1) * half, :HEAD
                ].astype(jnp.bfloat16)
    places = g_keyval_ref.shape[1]

    def spread(place, carry):
        for side in range(2):
            begin = pl.multiple_of((place * 2 + side) * half, half)
            g_keyval_ref[side, (places - 1 - place) if side else place] = g_keys[
                pl.ds(begin, half), :
            ].astype(jnp.bfloat16)
        return carry

    lax.fori_loop(0, places, spread, 0)


def attend_backward(count, query, keyval, meta, bounds, out, mass, g_pre, second, third):
    rows, query_width = query.shape
    groups = meta.shape[1] // (2 * HEAD)
    stacked = mass.shape[0]
    key_rows = 2 * keyval.shape[1] * keyval.shape[2]
    low = jnp.bfloat16
    return whole_call(
        "attend_backward",
        attend_backward_kernel,
        (count, query, keyval, meta, bounds, out, mass, g_pre, second, third),
        (
            ((rows, query_width), low),
            (keyval.shape, low),
            (meta.shape, jnp.float32),
        ),
        (
            ((groups, stacked, 2 * HEAD), low),
            ((groups, stacked, 2 * HEAD), low),
            ((key_rows, meta.shape[1]), low),
            ((rows, query_width), low),
            ((key_rows, meta.shape[1]), jnp.float32),
            ((groups, stacked // 2, 2 * HEAD), jnp.float32),
        ),
        scalars=1,
        room=56,
    )


def close_rows(source, target, places):
    width = target.shape[0]
    for begin in range(0, width, LANES):
        end = min(begin + LANES, width)
        low = begin // PIECE * PADDED // LANES * LANES
        high = min(-(-((end - 1) // PIECE + 1) * PADDED // LANES) * LANES, places)
        matrix = spread_matrix(begin, end, low, high)
        target[pl.ds(begin, end - begin), :] = dot_on(matrix, source(low, high), 1, 0).astype(
            target.dtype
        )


def spread_rows(source, put):
    step = LANES // PADDED * PIECE
    for n, begin in enumerate(range(0, 64 * PIECE, step)):
        low = begin // LANES * LANES
        high = min(low + 2 * LANES, 64 * PIECE)
        wide = begin // PIECE * PADDED
        matrix = spread_matrix(low, high, wide, wide + LANES)
        put(n, dot_on(matrix, source(low, high), 0, 0).astype(jnp.bfloat16))


def feed_forward_open(held):
    for part, target in enumerate((held.gate_w, held.up_w)):
        close_rows(
            lambda low, high: held.gate[part, pl.ds(low, high - low), :], target, held.gate.shape[1]
        )


def feed_forward_line(held, core, line):
    low = jnp.bfloat16
    size = held.feed.shape[2]

    def spot(i):
        return (jnp.where(core == 0, i, line), jnp.where(core == 0, line, i))

    feed = jnp.concatenate([held.feed[spot(i)] for i in range(SIDE)], axis=0)
    gate = dot_on(feed, held.gate_w[...], 1, 0)
    up = dot_on(feed, held.up_w[...], 1, 0)
    share = jax.nn.sigmoid(gate)
    silu = gate * share
    active = (silu * up).astype(low)
    out = dot_on(active, held.down[...], 1, 0).astype(low)
    cot = jnp.concatenate([held.cot[spot(i)] for i in range(SIDE)], axis=0)
    g_active = dot_on(cot, held.down[...], 1, 1)
    g_gate = (g_active * up * (share + silu * (1.0 - share))).astype(low)
    g_up = (g_active * silu).astype(low)
    g_feed = dot_on(g_gate, held.gate_w[...], 1, 1) + dot_on(g_up, held.up_w[...], 1, 1)
    g_feed = g_feed.astype(low)
    for i in range(SIDE):
        rows = slice(i * size, (i + 1) * size)
        held.out[line, i] = out[rows]
        held.g_feed[line, i] = g_feed[rows]
        held.active[spot(i)] = active[rows]
        held.g_parts[(0,) + spot(i)] = g_gate[rows]
        held.g_parts[(1,) + spot(i)] = g_up[rows]


def all_rows(ref):
    return ref.reshape(16 * ref.shape[2], ref.shape[3])[...]


def feed_forward_gate(held, part):
    held.products[...] = dot_on(all_rows(held.feed), all_rows(held.g_parts.at[part]), 0, 0).astype(
        jnp.bfloat16
    )

    def put(n, value):
        for x in range(SIDE):
            held.g_gate[part, x, n] = value[x * PADDED : (x + 1) * PADDED]

    spread_rows(lambda low, high: held.products[pl.ds(low, high - low), :], put)


def feed_forward_down(held):
    g_down = dot_on(all_rows(held.active), all_rows(held.cot), 0, 0).astype(jnp.bfloat16)
    size = held.g_down.shape[3]
    for x in range(SIDE):
        for part in range(2):
            begin = (2 * x + part) * size
            held.g_down[part, x, 0] = g_down[begin : begin + size]


STEP_ROWS = 104
LOG_ROWS = slice(104, 120)
TAP_ROWS = slice(120, 124)
OFFSET_ROW = slice(124, 125)
BIAS_ROW = slice(125, 126)
SKIP_ROW = slice(126, 127)
FIRST_PROJ = 128
PROJ_CUT = 80
PROJ_ROWS = 144
FIRST_COL = 20


def channel_matrix(size):
    channel = lax.broadcasted_iota(jnp.int32, (size, size), 0)
    place = lax.broadcasted_iota(jnp.int32, (size, size), 1)
    match = (channel == (place // 64) * 50 + place % 64) & (place % 64 < 50)
    return jnp.where(match, 1.0, 0.0).astype(jnp.bfloat16)


def two_terms(values):
    most = values.astype(jnp.bfloat16)
    return most, (values - most.astype(jnp.float32)).astype(jnp.bfloat16)


def row_places(starts_ref, begin, rows, group):
    row = begin + lax.broadcasted_iota(jnp.int32, (rows, 1), 0)
    first, after = jnp.zeros_like(row), jnp.full_like(row, group)
    for i in range(starts_ref.shape[0]):
        start = starts_ref[i]
        first = jnp.where(row >= start, jnp.maximum(first, start), first)
        after = jnp.where(row < start, jnp.minimum(after, start), after)
    return row - first, after - 1 - row


def shifted_rows(before, rows, back):
    joined = jnp.concatenate([before, rows], axis=0)
    return joined[8 - back : 8 - back + rows.shape[0]]


def conv_sum(before, rows, dist, channel):
    taps = channel[TAP_ROWS]
    total = taps[CONV - 1 : CONV] * rows + channel[OFFSET_ROW]
    for back in range(1, CONV):
        earlier = shifted_rows(before, rows, back)
        valid = jnp.where(dist >= back, 1.0, 0.0)
        total = total + taps[CONV - 1 - back : CONV - back] * earlier * valid
    return total


def mixer_project_kernel(
    starts_ref,
    tokens_ref,
    gain_ref,
    weight_ref,
    channel_ref,
    normed_ref,
    conv_ref,
    gate_ref,
    inputs_ref,
    first_ref,
    second_ref,
    compact_ref,
    rows_ref,
    tail_ref,
):
    low = jnp.bfloat16
    lanes = conv_ref.shape[1]

    @pl.when(pl.program_id(0) == 0)
    def _():
        places = weight_ref.shape[0]
        close_rows(lambda a, b: weight_ref[pl.ds(a, b - a), :], compact_ref, places)
        rows_ref[...] = dot_on(channel_ref[...], channel_matrix(lanes), 0, 1)
        tail_ref[...] = jnp.zeros_like(tail_ref)

    count = tokens_ref.shape[1]
    tokens = [tokens_ref[part, i] for i in range(count) for part in range(2)]
    tokens = jnp.concatenate(tokens, axis=0).astype(jnp.float32)
    normed = (unit_rows(tokens) * gain_ref[...]).astype(low)
    normed_ref[...] = normed
    mixed = dot_on(normed, compact_ref[...], 1, 0)
    conv_in = mixed[:, :lanes].astype(low)
    conv_ref[...] = conv_in
    gate_ref[...] = mixed[:, lanes:]
    rows = conv_in.astype(jnp.float32)
    channel = rows_ref[...]
    size = rows.shape[0]
    dist, _ = row_places(starts_ref, pl.program_id(0) * size, size, 0)
    total = conv_sum(tail_ref[...], rows, dist, channel)
    tail_ref[...] = rows[-8:]
    inputs = (total * jax.nn.sigmoid(total)).astype(low)
    inputs_ref[...] = inputs
    proj = dot_on(channel[FIRST_PROJ : FIRST_PROJ + PROJ_ROWS].astype(low), inputs, 1, 1)
    proj = proj.astype(low)
    size = size // count
    for i in range(count):
        first_ref[i] = proj[:PROJ_CUT, i * size : (i + 1) * size]
        second_ref[i] = proj[PROJ_CUT:, i * size : (i + 1) * size]


def mixer_project(starts, tokens, gain, weight, channel):
    places, rows, width = tokens.shape[1], tokens.shape[2], tokens.shape[3]
    rows, lanes = 2 * rows, weight.shape[1] // 2
    group = places * rows
    low, full = jnp.bfloat16, jnp.float32

    count = 2

    def line(size):
        return pl.BlockSpec((count * rows, size), lambda i: (i, 0))

    def whole(*shape):
        return pl.BlockSpec(shape, lambda i: (0,) * len(shape))

    return pl.pallas_call(
        mixer_project_kernel,
        grid=(places // count,),
        out_shape=[
            jax.ShapeDtypeStruct((group, width), low),
            jax.ShapeDtypeStruct((group, lanes), low),
            jax.ShapeDtypeStruct((group, lanes), full),
            jax.ShapeDtypeStruct((group, lanes), low),
            jax.ShapeDtypeStruct((places, PROJ_CUT, rows), low),
            jax.ShapeDtypeStruct((places, PROJ_ROWS - PROJ_CUT, rows), low),
            jax.ShapeDtypeStruct((width, 2 * lanes), low),
            jax.ShapeDtypeStruct((channel.shape[1], lanes), full),
        ],
        in_specs=[
            pl.BlockSpec(memory_space=pltpu.SMEM),
            pl.BlockSpec((2, count, rows // 2, width), lambda i: (0, i, 0, 0)),
            whole(*gain.shape),
            whole(*weight.shape),
            whole(*channel.shape),
        ],
        out_specs=[
            line(width),
            line(lanes),
            line(lanes),
            line(lanes),
            pl.BlockSpec((count, PROJ_CUT, rows), lambda i: (i, 0, 0)),
            pl.BlockSpec((count, PROJ_ROWS - PROJ_CUT, rows), lambda i: (i, 0, 0)),
            whole(width, 2 * lanes),
            whole(channel.shape[1], lanes),
        ],
        scratch_shapes=[pltpu.VMEM((8, lanes), full)],
        compiler_params=pltpu.CompilerParams(vmem_limit_bytes=40 * 2**20),
        name="mixer_project",
    )(starts, tokens, gain, weight, channel)


def step_sum(first_ref, second_ref, channel_ref, p):
    low = jnp.bfloat16
    one = first_ref[p]
    two = second_ref[p][: STEP_ROWS - PROJ_CUT]
    total = dot_on(one, channel_ref[pl.ds(0, PROJ_CUT), :].astype(low), 0, 0)
    total = total + dot_on(
        two, channel_ref[pl.ds(PROJ_CUT, STEP_ROWS - PROJ_CUT), :].astype(low), 0, 0
    )
    return total + channel_ref[BIAS_ROW], one, two


def put_blocks(target, spot, value):
    for block in range(target.shape[0]):
        target[block, spot, :] = value[:, block * CHUNKS : (block + 1) * CHUNKS]


def get_blocks(source, spot):
    return jnp.concatenate([source[block, spot, :] for block in range(source.shape[0])], axis=1)


def softplus(values):
    return jnp.maximum(values, 0.0) + jnp.log1p(jnp.exp(-jnp.abs(values)))


def mixer_forward_kernel(
    used,
    starts_ref,
    first_ref,
    second_ref,
    channel_ref,
    inputs_ref,
    gate_ref,
    back_ref,
    partial_ref,
    mixed_ref,
    out_ref,
    start_ref,
    decay_t,
    drive_t,
    rate_ref,
    cols_t,
    decay_s,
    drive_s,
    out_t,
    cols_s,
):
    places = first_ref.shape[0]
    rows = first_ref.shape[2]
    half = rows // 2
    lanes = channel_ref.shape[1]
    rate = -jnp.exp(channel_ref[LOG_ROWS]) * log2_e
    channel = lax.broadcasted_iota(jnp.int32, rate.shape, 1)
    rate_ref[...] = jnp.where(channel < used, rate, 0.0).T

    def prepare(p, carry):
        spot = pl.ds(pl.multiple_of(p * rows, rows), rows)
        steps = softplus(step_sum(first_ref, second_ref, channel_ref, p)[0])
        dist, _ = row_places(starts_ref, p * rows, rows, 0)
        put_blocks(decay_s, spot, jnp.where(dist == 0, far_away, steps))
        cols = second_ref[p].astype(jnp.float32).T
        cols_s[0, spot, :] = jnp.concatenate([cols, jnp.zeros_like(cols)], axis=1)
        put_blocks(drive_s, spot, steps * inputs_ref[spot, :].astype(jnp.float32))
        return carry

    lax.fori_loop(0, places, prepare, 0)
    to_lanes(cols_s, cols_t)
    scan_forward_body(
        used, decay_s, drive_s, cols_t, rate_ref, out_ref, start_ref, decay_t, drive_t, out_t
    )
    weight = dot_on(channel_matrix(lanes), back_ref[...], 1, 0).astype(jnp.bfloat16)

    together = 4

    def finish(q, carry):
        spot = pl.ds(pl.multiple_of(q * together * rows, together * rows), together * rows)
        gate = gate_ref[spot, :]
        inputs = inputs_ref[spot, :].astype(jnp.float32)
        mixed = (get_blocks(out_ref, spot) + channel_ref[SKIP_ROW] * inputs) * (
            gate * jax.nn.sigmoid(gate)
        )
        mixed = mixed.astype(jnp.bfloat16)
        mixed_ref[spot, :] = mixed
        value = dot_on(mixed, weight, 1, 0).astype(jnp.bfloat16)
        for i in range(2 * together):
            partial_ref[i % 2, q * together + i // 2] = value[i * half : (i + 1) * half]
        return carry

    lax.fori_loop(0, places // together, finish, 0)


def mixer_forward(used, starts, first, second, channel, inputs, gate, back):
    group, lanes = inputs.shape
    places, rows = first.shape[0], first.shape[2]
    states = LOG_ROWS.stop - LOG_ROWS.start
    low, full = jnp.bfloat16, jnp.float32
    blocks = (lanes // CHUNKS, group, CHUNKS)
    turned = (STEPS, lanes, CHUNKS)
    return whole_call(
        "mixer_forward",
        functools.partial(mixer_forward_kernel, used),
        (starts, first, second, channel, inputs, gate, back),
        (
            ((2, places, rows // 2, back.shape[1]), low),
            ((group, lanes), low),
            (blocks, full),
            ((states, lanes, CHUNKS), full),
            (turned, full),
            (turned, full),
            ((lanes, states), full),
            ((STEPS, CHUNKS, CHUNKS), full),
        ),
        ((blocks, full), (blocks, full), (turned, full), ((1, group, CHUNKS), full)),
        scalars=1,
    )


def mixer_backward_kernel(
    used,
    first_ref,
    second_ref,
    cols_t,
    channel_ref,
    inputs_ref,
    gate_ref,
    back_ref,
    grad_ref,
    mixed_ref,
    out_ref,
    start_ref,
    decay_t,
    drive_t,
    rate_ref,
    g_first_ref,
    g_second_ref,
    g_inputs_ref,
    g_gate_ref,
    g_back_ref,
    g_rows_ref,
    g_rate_ref,
    g_out_s,
    g_decay_s,
    g_drive_s,
    g_weight,
    grad_t,
    g_decay_t,
    g_drive_t,
    sums_t,
    ends_t,
    g_cols_t,
    g_cols_s,
):
    places = first_ref.shape[0]
    rows = first_ref.shape[2]
    lanes = channel_ref.shape[1]
    low, full = jnp.bfloat16, jnp.float32
    weight = dot_on(channel_matrix(lanes), back_ref[...], 1, 0).astype(low)
    skip = channel_ref[SKIP_ROW]
    g_weight[...] = jnp.zeros_like(g_weight)
    g_rows_ref[...] = jnp.zeros_like(g_rows_ref)

    together = 4

    def prepare(q, carry):
        spot = pl.ds(pl.multiple_of(q * together * rows, together * rows), together * rows)
        grad = [grad_ref[i % 2, q * together + i // 2] for i in range(2 * together)]
        grad = jnp.concatenate(grad, axis=0)
        g_weight[...] += dot_on(mixed_ref[spot, :], grad, 0, 0)
        g_mixed = dot_on(grad, weight, 1, 1)
        gate = gate_ref[spot, :]
        inputs = inputs_ref[spot, :].astype(full)
        share = jax.nn.sigmoid(gate)
        g_out = g_mixed * (gate * share)
        put_blocks(g_out_s, spot, g_out)
        value = get_blocks(out_ref, spot) + skip * inputs
        g_gate = g_mixed * value * (share + gate * share * (1.0 - share))
        g_gate_ref[spot, :] = g_gate.astype(low)
        g_inputs_ref[spot, :] = g_out * skip
        g_rows_ref[SKIP_ROW] += jnp.sum(g_out * inputs, axis=0, keepdims=True)
        return carry

    lax.fori_loop(0, places // together, prepare, 0)
    g_cols_t[...] = jnp.zeros_like(g_cols_t)
    scan_backward_body(
        used,
        decay_t,
        drive_t,
        cols_t,
        rate_ref,
        start_ref,
        g_out_s,
        g_decay_s,
        g_drive_s,
        g_cols_t,
        g_rate_ref,
        grad_t,
        g_decay_t,
        g_drive_t,
        sums_t,
        ends_t,
    )

    to_rows(g_cols_t, g_cols_s)

    def finish(p, carry):
        spot = pl.ds(pl.multiple_of(p * rows, rows), rows)
        total, one, two = step_sum(first_ref, second_ref, channel_ref, p)
        steps = softplus(total)
        inputs = inputs_ref[spot, :].astype(full)
        g_drive = get_blocks(g_drive_s, spot)
        g_steps = get_blocks(g_decay_s, spot) * (1.0 / log2_e) + g_drive * inputs
        g_inputs_ref[spot, :] += g_drive * steps
        g_total = g_steps * jax.nn.sigmoid(total)
        g_rows_ref[BIAS_ROW] += jnp.sum(g_total, axis=0, keepdims=True)
        g_total = g_total.astype(low)
        g_rows_ref[pl.ds(0, PROJ_CUT), :] += dot_on(one, g_total, 1, 0)
        g_rows_ref[pl.ds(PROJ_CUT, STEP_ROWS - PROJ_CUT), :] += dot_on(two, g_total, 1, 0)
        g_low = dot_on(channel_ref[pl.ds(0, STEP_ROWS), :].astype(low), g_total, 1, 1)
        g_first_ref[p] = g_low[:PROJ_CUT].astype(low)
        g_cols = g_cols_s[0, spot, :].T[: PROJ_ROWS - PROJ_CUT]
        blank = jnp.zeros((PROJ_ROWS - STEP_ROWS, rows), full)
        g_second = g_cols + jnp.concatenate([g_low[PROJ_CUT:], blank], axis=0)
        g_second_ref[p] = g_second.astype(low)
        return carry

    lax.fori_loop(0, places, finish, 0)
    g_back = dot_on(channel_matrix(lanes), g_weight[...].astype(low), 0, 0).astype(low)
    size = g_back_ref.shape[2]
    for x in range(SIDE):
        g_back_ref[x, 0] = g_back[x * size : (x + 1) * size]


def mixer_backward(
    used,
    first,
    second,
    cols,
    channel,
    inputs,
    gate,
    back,
    grad,
    mixed,
    out,
    starts,
    decay_t,
    drive_t,
    rate,
):
    group, lanes = inputs.shape
    places, rows = first.shape[0], first.shape[2]
    low, full = jnp.bfloat16, jnp.float32
    width = back.shape[1]
    turned = (decay_t.shape, full)
    states = rate.shape[1]
    return whole_call(
        "mixer_backward",
        functools.partial(mixer_backward_kernel, used),
        (
            first,
            second,
            cols,
            channel,
            inputs,
            gate,
            back,
            grad,
            mixed,
            out,
            starts,
            decay_t,
            drive_t,
            rate,
        ),
        (
            ((places, PROJ_CUT, rows), low),
            ((places, PROJ_ROWS - PROJ_CUT, rows), low),
            ((group, lanes), full),
            ((group, lanes), low),
            ((SIDE, 1, lanes // SIDE, width), low),
            ((FIRST_PROJ, lanes), full),
            (rate.shape, full),
        ),
        (
            (out.shape, full),
            (out.shape, full),
            (out.shape, full),
            ((lanes, width), full),
            turned,
            turned,
            turned,
            ((2 * states, STEPS, LINES, CHUNKS), full),
            (starts.shape, full),
            (cols.shape, full),
            ((1, group, CHUNKS), full),
        ),
        room=60,
    )


def mixer_inputs_kernel(
    starts_ref,
    first_ref,
    second_ref,
    channel_ref,
    weight_ref,
    normed_ref,
    conv_ref,
    before_ref,
    inputs_ref,
    g_inputs_ref,
    g_gate_ref,
    g_normed_ref,
    g_weight_ref,
    g_rows_ref,
    gain_ref,
    head_ref,
    sums,
):
    step = pl.program_id(0)
    steps = pl.num_programs(0)
    low, full = jnp.bfloat16, jnp.float32
    lanes = conv_ref.shape[1]

    @pl.when(step == 0)
    def _():
        head_ref[...] = jnp.zeros_like(head_ref)
        sums[...] = jnp.zeros_like(sums)
        g_rows_ref[...] = jnp.zeros_like(g_rows_ref)

    channel = channel_ref[...]
    proj = channel[FIRST_PROJ : FIRST_PROJ + PROJ_ROWS].astype(low)
    g_proj = [
        jnp.concatenate([first_ref[i], second_ref[i]], axis=0) for i in range(first_ref.shape[0])
    ]
    g_proj = jnp.concatenate(g_proj, axis=1)
    g_inputs = g_inputs_ref[...] + dot_on(g_proj, proj, 0, 0)
    g_rows_ref[pl.ds(FIRST_PROJ, PROJ_ROWS), :] += dot_on(g_proj, inputs_ref[...], 1, 0)
    rows = conv_ref[...].astype(full)
    before = jnp.where(step == steps - 1, 0.0, 1.0) * before_ref[...].astype(full)[-8:]
    size = rows.shape[0]
    dist, later = row_places(starts_ref, (steps - 1 - step) * size, size, steps * size)
    total = conv_sum(before, rows, dist, channel)
    share = jax.nn.sigmoid(total)
    g_total = g_inputs * (share + total * share * (1.0 - share))
    taps = channel[TAP_ROWS]
    g_conv = taps[CONV - 1 : CONV] * g_total
    g_taps = [jnp.sum(g_total * rows, axis=0, keepdims=True)]
    after = jnp.concatenate([g_total, head_ref[...]], axis=0)
    for back in range(1, CONV):
        earlier = shifted_rows(before, rows, back) * jnp.where(dist >= back, 1.0, 0.0)
        g_taps.append(jnp.sum(g_total * earlier, axis=0, keepdims=True))
        tap = taps[CONV - 1 - back : CONV - back]
        g_conv = g_conv + tap * after[back : back + size] * jnp.where(later >= back, 1.0, 0.0)
    head_ref[...] = g_total[:8]
    g_rows_ref[TAP_ROWS] += jnp.concatenate(g_taps[::-1], axis=0)
    g_rows_ref[OFFSET_ROW] += jnp.sum(g_total, axis=0, keepdims=True)
    g_mixed = jnp.concatenate([g_conv.astype(low), g_gate_ref[...]], axis=1)
    sums[...] += dot_on(normed_ref[...], g_mixed, 0, 0)
    g_normed = dot_on(g_mixed, weight_ref[...], 1, 1).astype(low)
    count, half = g_normed_ref.shape[1:3]
    for i in range(count):
        for part in range(2):
            begin = (2 * i + part) * half
            g_normed_ref[part, i] = g_normed[begin : begin + half]

    @pl.when(step == steps - 1)
    def _():
        ones = jnp.ones((8, sums.shape[1]), full)
        gain_ref[...] = dot_on(ones, sums[...] * weight_ref[...].astype(full), 1, 1, precision=highest)

        def put(n, value):
            for x in range(SIDE):
                g_weight_ref[x, n] = value[x * PADDED : (x + 1) * PADDED]

        spread_rows(lambda a, b: sums[pl.ds(a, b - a), :].astype(low), put)


def mixer_inputs(starts, first, second, channel, weight, normed, conv, inputs, g_inputs, g_gate):
    places, rows = first.shape[0], first.shape[2]
    group, lanes = conv.shape
    width = normed.shape[1]
    low, full = jnp.bfloat16, jnp.float32
    count = 4
    last = places // count - 1

    def line(size):
        return pl.BlockSpec((count * rows, size), lambda i: (last - i, 0))

    def cube(size):
        return pl.BlockSpec((count, size, rows), lambda i: (last - i, 0, 0))

    def whole(*shape):
        return pl.BlockSpec(shape, lambda i: (0,) * len(shape))

    return pl.pallas_call(
        mixer_inputs_kernel,
        grid=(places // count,),
        out_shape=[
            jax.ShapeDtypeStruct((2, places, rows // 2, width), low),
            jax.ShapeDtypeStruct((SIDE, 16, PADDED, 2 * lanes), low),
            jax.ShapeDtypeStruct(channel.shape, full),
            jax.ShapeDtypeStruct((8, width), full),
        ],
        in_specs=[
            pl.BlockSpec(memory_space=pltpu.SMEM),
            cube(PROJ_CUT),
            cube(PROJ_ROWS - PROJ_CUT),
            whole(*channel.shape),
            whole(*weight.shape),
            line(width),
            line(lanes),
            pl.BlockSpec((count * rows, lanes), lambda i: (jnp.maximum(last - 1 - i, 0), 0)),
            line(lanes),
            line(lanes),
            line(lanes),
        ],
        out_specs=[
            pl.BlockSpec((2, count, rows // 2, width), lambda i: (0, last - i, 0, 0)),
            whole(SIDE, 16, PADDED, 2 * lanes),
            whole(*channel.shape),
            whole(8, width),
        ],
        scratch_shapes=[pltpu.VMEM((8, lanes), full), pltpu.VMEM((width, 2 * lanes), full)],
        compiler_params=pltpu.CompilerParams(vmem_limit_bytes=48 * 2**20),
        name="mixer_inputs",
    )(starts, first, second, channel, weight, normed, conv, conv, inputs, g_inputs, g_gate)


def channel_grads_kernel(one_ref, two_ref, rate_ref, channel_ref, out_ref):
    lanes = channel_ref.shape[1]
    total = two_ref[...]
    states = rate_ref.shape[1]
    rows = lax.broadcasted_iota(jnp.int32, total.shape, 0)
    one = one_ref[...]
    one = jnp.concatenate([one, jnp.zeros((total.shape[0] - one.shape[0], lanes), one.dtype)], axis=0)
    logs = rate_ref[...].T * -jnp.exp(channel_ref[LOG_ROWS])
    blank = jnp.zeros((LOG_ROWS.start, lanes), logs.dtype)
    rest = jnp.zeros((total.shape[0] - LOG_ROWS.start - states, lanes), logs.dtype)
    total = total + jnp.where((rows >= LOG_ROWS.start) & (rows < LOG_ROWS.stop), 0.0, one)
    total = total + jnp.concatenate([blank, logs, rest], axis=0)
    matrix = channel_matrix(lanes)
    most, left = two_terms(total)
    wide = dot_on(matrix, most, 0, 1) + dot_on(matrix, left, 0, 1)
    size = out_ref.shape[2]
    for x in range(SIDE):
        out_ref[x, 0] = wide[x * size : (x + 1) * size]


def channel_grads(one, two, rate, channel):
    lanes = channel.shape[1]
    return whole_call(
        "channel_grads",
        channel_grads_kernel,
        (one, two, rate, channel),
        (((SIDE, 1, lanes // SIDE, channel.shape[0]), jnp.float32),),
    )[0]


def unpack_kernel(small_ref, meta_ref, gains_ref):
    width = meta_ref.shape[1]
    metas = meta_ref.shape[0]
    for begin in range(0, width, LANES):
        end = min(begin + LANES, width)
        low = begin // PIECE * PADDED // LANES * LANES
        high = -(-((end - 1) // PIECE + 1) * PADDED // LANES) * LANES
        matrix = spread_matrix(begin, end, low, high)
        value = dot_on(small_ref[pl.ds(low, high - low), :], matrix, 0, 1)
        meta_ref[:, pl.ds(begin, end - begin)] = value[:metas]
        gains_ref[:, pl.ds(begin, end - begin)] = value[metas : metas + gains_ref.shape[0]]


def unpack(small, metas, width):
    full = jnp.float32
    return whole_call(
        "unpack",
        unpack_kernel,
        (small,),
        (((metas, width), full), ((8, width), full)),
        room=60,
        fetch=True,
    )


def padded_rows(value, rows):
    blank = jnp.zeros((rows - value.shape[0], value.shape[1]), value.dtype)
    return jnp.concatenate([value, blank], axis=0).astype(jnp.bfloat16)


def padded_lanes(value, lanes):
    return jnp.concatenate(
        [value, jnp.zeros((value.shape[0], lanes - value.shape[1]), value.dtype)], axis=1
    )


def stacked_rows(parts, rows):
    blank = jnp.zeros((rows - sum(part.shape[0] for part in parts), parts[0].shape[1]), jnp.float32)
    return jnp.concatenate(parts + [blank], axis=0)


def prepare_kernel(
    query_ref,
    keyval_ref,
    attn_ref,
    mamba_ref,
    back_ref,
    gate_ref,
    down_ref,
    meta_ref,
    norm_gain_ref,
    attn_gain_ref,
    mamba_gain_ref,
    feed_gain_ref,
    step_ref,
    log_ref,
    taps_ref,
    offset_ref,
    bias_ref,
    skip_ref,
    ssm_ref,
    attention_out,
    mamba_out,
    back_out,
    gate_out,
    down_out,
    small_out,
    channel_out,
):
    small = [meta_ref, norm_gain_ref, attn_gain_ref, mamba_gain_ref, feed_gain_ref]
    small = stacked_rows([ref[...] for ref in small], 2 * LANES)
    small_out[...] = padded_lanes(small, LANES).T[: small_out.shape[0]].astype(jnp.bfloat16)
    blank = jnp.zeros((STEP_ROWS - step_ref.shape[0], step_ref.shape[1]), jnp.float32)
    rows = [step_ref[...], blank]
    rows += [ref[...] for ref in (log_ref, taps_ref, offset_ref, bias_ref, skip_ref)]
    rows = padded_lanes(stacked_rows(rows, LANES), LANES).T[: channel_out.shape[0]]
    channel_out[:, pl.ds(0, LANES)] = rows.astype(jnp.bfloat16)
    channel_out[:, pl.ds(LANES, 2 * LANES)] = padded_rows(
        padded_lanes(ssm_ref[...], 2 * LANES), channel_out.shape[0]
    )
    width = query_ref.shape[1]
    begin = -(-width // LANES) * LANES
    attention_out[:, pl.ds(0, begin)] = padded_rows(padded_lanes(query_ref[...], begin), PADDED)
    half = keyval_ref.shape[1] // 2
    for group in range(half // HEAD):
        spot = group * HEAD
        pair = [keyval_ref[:, pl.ds(spot, HEAD)], keyval_ref[:, pl.ds(half + spot, HEAD)]]
        attention_out[:, pl.ds(begin + 2 * spot, 2 * HEAD)] = padded_rows(
            jnp.concatenate(pair, axis=1), PADDED
        )
    attention_out[:, pl.ds(begin + 2 * half, width)] = padded_rows(attn_ref[...], PADDED)
    places = mamba_out.shape[0]
    lanes = mamba_out.shape[2] // 2
    inner = mamba_ref.shape[1] // places // 2
    for place in range(places):
        parts = [
            padded_lanes(mamba_ref[:, pl.ds((part * places + place) * inner, inner)], lanes)
            for part in range(2)
        ]
        mamba_out[place] = padded_rows(jnp.concatenate(parts, axis=1), PADDED)
    back_out[...] = padded_rows(back_ref[...], back_out.shape[0])
    down_out[...] = padded_rows(down_ref[...], down_out.shape[0])
    size = down_ref.shape[0]
    room = gate_out.shape[3] // SIDE
    for part in range(2):
        for place in range(places):
            first = (part * places + place) * SIDE * size
            parts = [
                padded_lanes(gate_ref[:, pl.ds(first + x * size, size)], room) for x in range(SIDE)
            ]
            gate_out[part, place] = padded_rows(jnp.concatenate(parts, axis=1), PADDED)


def prepare(*arrays):
    low = jnp.bfloat16
    query, keyval, attn, _, back, _, down = arrays[:7]
    most = -(-query.shape[1] // LANES) * LANES
    return whole_call(
        "prepare",
        prepare_kernel,
        arrays,
        (
            ((PADDED, most + keyval.shape[1] + attn.shape[1]), low),
            ((16, PADDED, 4 * CHUNKS), low),
            ((64, back.shape[1]), low),
            ((2, 16, PADDED, 96 * SIDE), low),
            ((96, down.shape[1]), low),
            ((PADDED, 2 * LANES), low),
            ((64, 3 * LANES), low),
        ),
        room=60,
        fetch=True,
    )


def finish_kernel(
    tokens_ref,
    gain_ref,
    g_hidden_ref,
    normed_ref,
    sums_ref,
    keys_ref,
    mamba_ref,
    back_ref,
    channel_ref,
    gate_ref,
    down_ref,
    gains_ref,
    input_out,
    query_out,
    keyval_out,
    attn_out,
    mamba_out,
    back_out,
    gate_out,
    down_out,
    meta_out,
    ssm_out,
    step_out,
    log_out,
    taps_out,
    rows_out,
    gains_out,
):
    half = normed_ref.shape[1]
    for i in range(2):
        spot = pl.ds(i * half, half)
        rows = tokens_ref[spot, :].astype(jnp.float32)
        scale = lax.rsqrt(jnp.mean(rows * rows, axis=-1, keepdims=True) + epsilon)
        unit = rows * scale
        grad = normed_ref[i] * gain_ref[...]
        grad = scale * (grad - unit * jnp.mean(grad * unit, axis=-1, keepdims=True))
        input_out[spot, :] = g_hidden_ref[i] + grad
    piece, width = query_out.shape
    rows = pl.ds(0, piece)
    begin = sums_ref.shape[1] - width
    query_out[...] = sums_ref[rows, pl.ds(0, width)]
    attn_out[...] = sums_ref[rows, pl.ds(begin, width)]
    keys_half = keyval_out.shape[1] // 2
    for group in range(keys_half // HEAD):
        pair = keys_ref[rows, pl.ds(2 * group * HEAD, 2 * HEAD)]
        keyval_out[:, pl.ds(group * HEAD, HEAD)] = pair[:, :HEAD]
        keyval_out[:, pl.ds(keys_half + group * HEAD, HEAD)] = pair[:, HEAD:]
    meta = padded_lanes(keys_ref[:, pl.ds(2 * keys_half, meta_out.shape[0])].T, LANES)
    meta_out[...] = meta[:, :piece]
    places = mamba_ref.shape[0]
    lanes = mamba_ref.shape[2] // 2
    inner = mamba_out.shape[1] // places // 2
    for place in range(places):
        value = mamba_ref[place].astype(jnp.float32)
        for part in range(2):
            mamba_out[:, pl.ds((part * places + place) * inner, inner)] = value[
                :piece, part * lanes : part * lanes + inner
            ]
    back_out[...] = back_ref[0, pl.ds(0, back_out.shape[0]), :]
    count = back_out.shape[0]
    ssm_out[...] = channel_ref[0, pl.ds(0, count), pl.ds(FIRST_PROJ, ssm_out.shape[1])]
    channel = channel_ref[0, :, pl.ds(0, LANES)].T
    step_out[...] = channel[: step_out.shape[0], :count]
    log_out[...] = channel[LOG_ROWS, :count]
    taps_out[...] = channel[TAP_ROWS, :count]
    rows_out[...] = channel[TAP_ROWS.start : TAP_ROWS.start + 8, :count]
    gains = (gains_ref[0] + gains_ref[1]).T
    gains_out[...] = gains[: gains_out.shape[0], :piece]
    size = down_out.shape[0]
    top = down_ref.shape[1]
    down_out[pl.ds(0, top), :] = down_ref[0]
    down_out[pl.ds(top, size - top), :] = down_ref[1, pl.ds(0, size - top), :]
    room = gate_ref.shape[3] // SIDE
    for part in range(2):
        for place in range(places):
            value = gate_ref[part, place].astype(jnp.float32)
            first = (part * places + place) * SIDE * size
            parts = [value[:piece, x * room : x * room + size] for x in range(SIDE)]
            gate_out[:, pl.ds(first, SIDE * size)] = jnp.concatenate(parts, axis=1)


def finish(piece, inner_piece, down_piece, inner, proj, rank, *arrays):
    tokens = arrays[0]
    rows, width = tokens.shape
    full = jnp.float32
    keys = arrays[5]
    metas = LANES
    return whole_call(
        "finish",
        finish_kernel,
        arrays,
        (
            ((rows, width), full),
            ((piece, width), full),
            ((piece, keys.shape[1] - metas), full),
            ((piece, width), full),
            ((piece, 2 * 16 * inner), full),
            ((inner_piece, width), full),
            ((piece, 2 * 16 * SIDE * down_piece), full),
            ((down_piece, width), full),
            ((metas, piece), full),
            ((inner_piece, proj), full),
            ((rank, inner_piece), full),
            ((LOG_ROWS.stop - LOG_ROWS.start, inner_piece), full),
            ((CONV, inner_piece), full),
            ((8, inner_piece), full),
            ((8, piece), full),
        ),
    )


def pack_gains_kernel(norm_ref, attn_ref, mamba_ref, feed_ref, out_ref):
    width = norm_ref.shape[1]
    rows = [ref[...] for ref in (norm_ref, attn_ref, mamba_ref, feed_ref)]
    rows = jnp.concatenate(rows + [jnp.zeros((8 - len(rows), width), jnp.float32)], axis=0)
    wide = spread_columns(rows.astype(jnp.bfloat16)).astype(jnp.float32).T
    out_ref[...] = padded_lanes(wide, LANES).astype(jnp.bfloat16)


def pack_gains(*rows):
    places = rows[0].shape[1] // PIECE * PADDED
    return whole_call("pack_gains", pack_gains_kernel, rows, (((places, LANES), jnp.bfloat16),))[0]


def norm_back(values, gain, grad):
    scale = lax.rsqrt(jnp.mean(values * values, axis=-1, keepdims=True) + epsilon)
    unit = values * scale
    g_unit = grad * gain
    g_values = scale * (g_unit - unit * jnp.mean(g_unit * unit, axis=-1, keepdims=True))
    return g_values, jnp.sum(grad * unit, axis=0, keepdims=True)


def turn_kernel(
    gains_ref,
    hidden_ref,
    out_ref,
    grad_ref,
    cot_ref,
    attn_ref,
    mamba_ref,
    mixed_out,
    g_hidden_out,
    g_attn_out,
    g_mamba_out,
    attn_gain_out,
    mamba_gain_out,
    feed_gain_out,
):
    low = jnp.bfloat16
    hidden = hidden_ref[...]
    mixed_out[...] = (hidden + out_ref[...]).astype(low)
    g_norm, feed_gain_out[...] = norm_back(hidden, gains_ref[3:4, :], grad_ref[...])
    g_hidden = cot_ref[...].astype(jnp.float32) + g_norm
    g_hidden_out[...] = g_hidden
    g_sent = 0.5 * g_hidden
    g_attn, attn_gain_out[...] = norm_back(attn_ref[...], gains_ref[1:2, :], g_sent)
    g_mamba, mamba_gain_out[...] = norm_back(mamba_ref[...], gains_ref[2:3, :], g_sent)
    g_attn_out[...] = g_attn.astype(low)
    g_mamba_out[...] = g_mamba.astype(low)


def turn(gains, hidden, *arrays):
    shape, low, full = hidden.shape, jnp.bfloat16, jnp.float32
    row = ((1, shape[1]), full)
    return whole_call(
        "turn",
        turn_kernel,
        (gains, hidden) + arrays,
        ((shape, low), (shape, full), (shape, low), (shape, low), row, row, row),
    )


def rms_norm(values, gain):
    return values * lax.rsqrt(jnp.mean(values * values, axis=-1, keepdims=True) + epsilon) * gain


def pad_to(array, dim, size):
    widths = [(0, 0)] * array.ndim
    widths[dim] = (0, size - array.shape[dim])
    return jnp.pad(array, widths)


def blank(shapes):
    leaves, nest = jax.tree.flatten(shapes)
    outs = pl.pallas_call(
        lambda *refs: None,
        out_shape=[jax.ShapeDtypeStruct(leaf.shape, leaf.dtype) for leaf in leaves],
        out_specs=[ANY] * len(leaves),
        name="blank",
    )()
    return jax.tree.unflatten(nest, outs)


def order_of(net):
    return (Z, Y) if net.core == 0 else (Y, Z)


def gather_halves(net, name, source, out, patience=0):
    if net.core == 0:
        count = []

        def after(line):
            net.start(
                (name, -3, len(count)),
                out.at[0, line],
                out.at[0, line],
                net.device(other_core=True),
            )
            count.append(line)

        yield from gather_two(net, name, source, out.at[0], (Z, Y), after, patience)
    else:
        yield from gather_two(net, name, source, out.at[1], (Y, Z), None, patience)
        for i in range(SIDE):
            net.copy(
                (name, -3, i), out.at[0, i], out.at[0, i], net.device(other_core=True)
            ).wait_recv()


def reduce_halves(net, name, source, pad, out):
    if net.core == 1:
        for y in range(SIDE):
            net.start(
                (name, -3, y), source.at[0, y], pad.half.at[y], net.device(other_core=True)
            )
        own = net.local((name, -1), source.at[1], pad.half)
        yield
        own.wait()
    else:
        yield
        for y in range(SIDE):
            net.copy(
                (name, -3, y), source.at[0, y], pad.half.at[y], net.device(other_core=True)
            ).wait_recv()
    yield from reduce_two(net, name, pad.half, pad, out, order_of(net))


def share_x(net, name, source, view):
    x = net.at[X]
    core, other = net.core, 1 - net.core
    own = net.local((name, -1), source, view(core, x))
    copies = [
        net.start((name, -2, hop), source, view(core, x), net.device(X, hop)) for hop in HOPS
    ]
    net.start((name, core, 0), source, view(core, x), net.device(other_core=True))
    yield
    for copy, hop in zip(copies, HOPS):
        copy.wait_recv()
        spot = (x - hop + SIDE) % SIDE
        net.start(
            (name, core, hop), view(core, spot), view(core, spot), net.device(other_core=True)
        )
    yield
    for i in (0,) + HOPS:
        net.copy(
            (name, other, i), source, view(other, x), net.device(other_core=True)
        ).wait_recv()
    own.wait()


def swap_cores(net, name, source, out):
    net.start((name, net.core), source, out.at[net.core], net.device(other_core=True))
    own = net.local((name, -1), source, out.at[net.core])
    yield
    net.copy(
        (name, 1 - net.core), source, out.at[1 - net.core], net.device(other_core=True)
    ).wait_recv()
    own.wait()


def hand(net, name, giver, source, target):
    if net.core == giver:
        net.start(name, source, target, net.device(other_core=True))
    else:
        net.copy(name, source, target, net.device(other_core=True)).wait_recv()


def keep_and_hand(net, name, giver, source, target):
    if net.core == giver:
        own = net.local((name, -1), source, target)
    hand(net, (name, 0), giver, source, target)
    yield
    if net.core == giver:
        own.wait()


def reduce_x(net, name, source, pad, out):
    x = net.at[X]
    recv, kept = pad.recv, pad.own
    own = net.local((name, -4), source.at[x], kept)
    copies = [
        net.start(
            (name, 5, hop), source.at[(x + hop) % SIDE], recv.at[hop - 1], net.device(X, hop)
        )
        for hop in HOPS
    ]
    yield
    own.wait()
    for copy in copies:
        copy.wait_recv()

    def put(lead, part, value):
        index = (lead,) if len(out.shape) == 3 else (lead // SIDE, lead % SIDE)
        out[index + (part, slice(None))] = value.astype(out.dtype)

    scatter_sum(
        source.shape[1],
        source.shape[2],
        lambda lead, part: kept[lead, part, :],
        [lambda lead, part, k=k: recv[k, lead, part, :] for k in range(3)],
        put,
    )


def reduce_three(net, name, source, pad, out, order, hold=0):
    left = [Y, Z, X]
    held = source
    stages = ((pad.recv0, pad.mid0), (pad.recv1, pad.mid1), (pad.recv2, out))
    for stage, axis in enumerate(order):
        recv, mid = stages[stage]
        spot = left.index(axis)
        size = len(left)

        def part_of(place, held=held, spot=spot):
            return held.at[(slice(None),) * spot + (place,)]

        if stage == 0:
            fetch = net.local((name, -4), part_of(net.at[axis]), pad.own)
        copies = [
            net.start(
                (name, stage, hop),
                part_of((net.at[axis] + hop) % SIDE),
                recv.at[hop - 1],
                net.device(axis, hop),
            )
            for hop in HOPS
        ]
        yield
        if stage == 0:
            for _ in range(hold):
                yield
            fetch.wait()
        for copy in copies:
            copy.wait_recv()

        def split(lead, size=size):
            return tuple((lead // SIDE**i) % SIDE for i in reversed(range(size - 1)))

        def own(lead, part, held=held, spot=spot, split=split, axis=axis):
            index = split(lead)
            if len(index) == 2:
                return pad.own[index + (part, slice(None))]
            index = index[:spot] + (net.at[axis],) + index[spot:]
            return held[index + (part, slice(None))]

        def put(lead, part, value, mid=mid, split=split):
            mid[split(lead) + (part, slice(None))] = value.astype(mid.dtype)

        scatter_sum(
            SIDE ** (size - 1),
            source.shape[3],
            own,
            [
                lambda lead, part, k=k, recv=recv, split=split: recv[
                    (k,) + split(lead) + (part, slice(None))
                ]
                for k in range(3)
            ],
            put,
        )
        held = mid
        del left[spot]


def three_pad(rows, width, kind=jnp.bfloat16):
    block = (rows, width)
    return dict(
        own=((SIDE, SIDE) + block, kind),
        recv0=((3, SIDE, SIDE) + block, kind),
        mid0=((SIDE, SIDE) + block, kind),
        recv1=((3, SIDE) + block, kind),
        mid1=((SIDE,) + block, kind),
        recv2=((3,) + block, kind),
    )


def two_pad(rows, width, kind=jnp.bfloat16):
    return dict(
        one=((3, SIDE, rows, width), kind),
        mid=((SIDE, rows, width), kind),
        two=((3, rows, width), kind),
        own=((SIDE, rows, width), kind),
    )


def ring_pad(rows, width, kind=jnp.bfloat16):
    half = rows // 2
    return dict(
        one=((2, SIDE, rows, width), kind),
        via_one=((2, SIDE, half, width), kind),
        mix_one=((2, SIDE, half, width), kind),
        mid=((SIDE, rows, width), kind),
        two=((2, rows, width), kind),
        via_two=((2, half, width), kind),
        mix_two=((2, half, width), kind),
        own=((SIDE, rows, width), kind),
    )


def half_pad(rows, width, kind=jnp.bfloat16):
    return dict(two_pad(rows, width, kind), half=((SIDE, SIDE, rows, width), kind))


def shrink_pad(lead, rows, width, kind=jnp.bfloat16):
    return dict(
        mine=((SIDE, lead, rows, width), kind),
        other=((SIDE, lead, rows, width), kind),
        mid=((SIDE, lead, rows, width), kind),
        **x_pad(lead, rows, width, kind),
    )


def x_pad(lead, rows, width, kind=jnp.bfloat16):
    return dict(recv=((3, lead, rows, width), kind), own=((lead, rows, width), kind))


def gather_weights(net, held):
    axes = (Y, Z, X)
    jobs, begin = [], 0
    for i, (target, order) in enumerate(
        ((held.first, (X, Z, Y)), (held.second, (Z, Y, X)), (held.third, (Y, X, Z)))
    ):
        size = target.shape[-1]
        jobs.append(
            gather(net, 5 + i, held.whole.at[:, pl.ds(begin, size)], target, axes, order, hold=3)
        )
        begin += size
    return jobs


def program_start(net, held):
    core = net.core
    rows = held.tokens.shape[0] // 2
    axes = (Y, Z, X)
    jobs = []
    if core == 1:

        def mamba():
            target = held.mamba_all.at[:, :, net.at[X]]
            yield from swap_two(net, 2, held.mamba, held.mamba_mid, target)
            copies = [
                net.start((2, 3, hop), target, target, net.device(X, hop)) for hop in HOPS
            ]
            yield
            for copy in copies:
                copy.wait_recv()

        jobs = [
            mamba(),
            gather(net, 3, held.back, held.back_all, (X,), (X,)),
            gather(net, 4, held.channel, held.channel_all, (X,), (X,)),
        ]
    jobs.append(gather(net, 1, held.small, held.small_all, axes, order_of(net) + (X,)))
    jobs.append(
        gather_halves(net, 0, held.tokens.at[pl.ds(core * rows, rows)], held.tokens_all)
    )
    if core == 0:

        def assigned():
            upper, lower = pl.ds(0, rows), pl.ds(rows, rows)
            own = net.local((9, -1), held.tokens.at[upper], held.assigned.at[upper])
            copy = net.start(
                (9, 0), held.tokens.at[lower], held.assigned.at[lower], net.device(partner=True)
            )
            yield
            copy.wait_recv()
            own.wait()

        jobs += [assigned()] + gather_weights(net, held)
    return jobs


def program_keyval(net, held):
    rows = held.keyval.shape[0] // 2
    return [
        gather_two(
            net,
            i,
            held.keyval.at[pl.ds(i * rows, rows)],
            held.keyval_all.at[i],
            ((Z, Y), (Y, Z))[i],
        )
        for i in range(2)
    ] + [swap_two(net, 2, held.gate.at[0], held.gate_mid, held.gate_own)]


def program_project(net, held):
    jobs = []
    for i, order in enumerate(((Z, Y), (Y, Z))):
        source = (held.first, held.second)[i]
        pad = (held.first_pad, held.second_pad)[i]
        target = (held.first_all, held.second_all)[i]

        def job(source=source, pad=pad, target=target, order=order, i=i):
            yield from reduce_two(net, 2 * i, source, pad, pad.sum, order)
            yield from gather_two(net, 2 * i + 1, pad.sum, target, order)

        jobs.append(job())
    return jobs + [swap_two(net, 4, held.gate, held.gate_mid, held.gate_own)]


def program_mixers(net, held):
    core = net.core
    half = held.down.shape[0] // 2
    rows = held.attn_pre.shape[0] // 2

    def attn():
        lower = held.attn_pre.at[pl.ds(rows, rows)]
        device = net.device(other_core=True, partner=True)
        if core == 0:
            own = net.local((1, -1), held.attn_pre.at[pl.ds(0, rows)], held.attn_half)
            net.start((1, 0), lower, held.attn_half, device)
        yield
        if core == 0:
            own.wait()
        else:
            net.copy((1, 0), lower, held.attn_half, device).wait_recv()

    return [
        attn(),
        reduce_halves(net, 0, held.partial, held.pad, held.mamba_pre),
        share_x(
            net,
            2,
            held.gate_first if core == 0 else held.gate_second,
            lambda b, x: held.gate_all.at[b, :, :, x],
        ),
        share_x(
            net,
            3,
            held.down.at[pl.ds(core * half, half)],
            lambda b, x: held.down_all.at[x, pl.ds(b * half, half)],
        ),
    ]


def program_feed(net, held):
    return [gather_two(net, 0, held.feed, held.feed_all, order_of(net))]


def program_ffn(net, held):
    feed_forward_open(held)
    jobs = [
        reduce_ring(net, 1, held.g_feed, held.grad_pad, held.grad_sum),
        reduce_ring(net, 0, held.out, held.out_pad, held.out_sum),
    ]
    for job in jobs:
        next(job)

    def line(hop):
        feed_forward_line(held, net.core, (net.at[FIRST] + hop) % SIDE)

    def weights():
        for part in range(2):
            feed_forward_gate(held, part)
            yield
        feed_forward_down(held)

    for hop in (2, 1, 3, 0):
        line(hop)
        for job in jobs:
            next(job)
    return jobs + [weights()]


def shrink(net, name, source, pad, out):
    core = net.core
    lead, rows = source.shape[2:4]
    mine = net.local((name, -5), source.at[core], pad.mine)
    net.start((name, 6, core), source.at[1 - core], pad.other, net.device(other_core=True))
    yield
    net.copy(
        (name, 6, 1 - core), source.at[1 - core], pad.other, net.device(other_core=True)
    ).wait_recv()

    mine.wait()

    def put(i, part, value):
        pad.mid[i // lead, i % lead, part, :] = value.astype(pad.mid.dtype)

    scatter_sum(
        SIDE * lead,
        rows,
        lambda i, part: pad.mine[i // lead, i % lead, part, :],
        [lambda i, part: pad.other[i // lead, i % lead, part, :]],
        put,
    )
    yield from reduce_x(net, name, pad.mid, pad, out)


def program_back(net, held):
    core = net.core

    def attn():
        device = net.device(other_core=True, partner=True)
        target = held.g_attn_both.at[1]
        if core == 0:
            own = net.local((5, -1), held.g_attn, held.g_attn_both.at[0])
        else:
            net.start((5, 0), held.g_attn, target, device)
        yield
        if core == 0:
            own.wait()
            net.copy((5, 0), held.g_attn, target, device).wait_recv()

    return [
        swap_cores(net, 3, held.mixed, held.mixed_both),
        swap_cores(net, 4, held.g_hidden, held.g_hidden_both),
        attn(),
        shrink(net, 1, held.g_gate, held.gate_pad, held.g_gate_sum),
        shrink(net, 2, held.g_down, held.down_pad, held.g_down_sum),
        gather_halves(net, 0, held.g_mamba, held.g_mamba_all, patience=1),
    ]


SUMS = ("one", "two", "three", "four", "five", "six")
ORDERS = ((Y, Z, X), (X, Y, Z), (Z, X, Y), (Y, Z, X), (X, Y, Z), (Z, X, Y))


def program_attention(net, held):
    rows = held.keyval.shape[3]
    parts = [getattr(held.parts, name) for name in SUMS]
    taken = [
        net.local((20, i), getattr(held.sources, name), getattr(held.inside, name))
        for i, name in enumerate(INSIDE)
    ]

    def weight(i, source):
        pad = getattr(held.pads, SUMS[i])
        return reduce_three(net, 10 + i, source, pad, parts[i], ORDERS[i])

    def large(i):
        yield
        yield from reduce_three(
            net, 10 + i, getattr(held, SUMS[i]), getattr(held.pads, SUMS[i]), parts[i], ORDERS[i], 1
        )

    def keyval(i):
        pad = (held.upper_pad, held.lower_pad)[i]
        return reduce_two(
            net,
            i,
            held.keyval.at[i],
            pad,
            held.keyval_sum.at[pl.ds(i * rows, rows)],
            ((Z, Y), (Y, Z))[i],
        )

    def follow():
        for _ in range(3):
            yield
        for copy in taken:
            copy.wait()
        inside = held.inside
        attention_inputs_kernel(
            held.keyval_sum,
            inside.g_query,
            inside.wide,
            inside.meta_wide,
            inside.g_meta,
            inside.first,
            inside.second,
            inside.meta,
            inside.gain,
            held.keys.four,
            held.keys.five,
            held.keys.six,
            held.g_normed,
            held.gain_part,
            held.meta_gain,
            held.g_wide,
            held.g_meta_wide,
        )
        places = held.keys.four.shape[0] // SIDE**3

        def cubed(ref):
            return ref.reshape(SIDE, SIDE, SIDE, places, ref.shape[1])

        later = [weight(3 + i, cubed(ref)) for i, ref in enumerate(vars(held.keys).values())]
        while later:
            later = [job for job in later if next(job, True) is None]
            yield

    def last():
        for _ in range(9):
            yield
        begin = 0
        for part in parts[:3]:
            held.sums[:, pl.ds(begin, part.shape[1])] = part[...]
            begin += part.shape[1]
        begin = 0
        for part in parts[3:]:
            held.keys_sum[:, pl.ds(begin, part.shape[1])] = part[...]
            begin += part.shape[1]

    return [
        keyval(0),
        keyval(1),
        swap_two(net, 3, held.gate, held.gate_mid, held.gate_own),
        follow(),
        *(large(i) for i in range(3)),
        last(),
    ]


def program_end(net, held):
    core = net.core

    def normed():
        half = held.normed_sum.shape[0]
        device = net.device(other_core=True, partner=True)
        if core == 0:
            own = net.local((9, -1), held.g_attn.at[pl.ds(0, half)], held.attn_part)
            net.start((9, 0), held.g_attn.at[pl.ds(half, half)], held.attn_part, device)
        yield from reduce_halves(net, 0, held.partial, held.normed_pad, held.normed_sum)
        if core == 0:
            own.wait()
        else:
            lower = held.g_attn.at[pl.ds(half, half)]
            net.copy((9, 0), lower, held.attn_part, device).wait_recv()

        def put(lead, part, value):
            held.normed_sum[part, :] = value

        scatter_sum(
            1,
            half,
            lambda lead, part: held.normed_sum[part, :],
            [lambda lead, part: held.attn_part[part, :]],
            put,
        )
        yield from swap_cores(net, 1, held.normed_sum, held.normed_both)

    def gains():
        yield from reduce_three(
            net, 2, held.gains, held.gains_pad, held.gains_sum, order_of(net) + (X,)
        )
        yield from swap_cores(net, 3, held.gains_sum, held.gains_both)

    def mamba():
        if core == 1:
            yield from reduce_x(net, 4, held.mamba, held.mamba_pad, held.mamba_part)
            yield from swap_two(net, 5, held.mamba_part, held.mamba_mid, held.mamba_sum)
        else:
            for _ in range(4):
                yield
        hand(net, (6, 0), 1, held.mamba_sum, held.mamba_sum)

    def channel(name, source, pad, total):
        if core == 1:
            yield from reduce_x(net, name, source, pad, total)
        else:
            for _ in range(2):
                yield
        hand(net, (name, 0), 1, total, total)

    return [
        normed(),
        mamba(),
        channel(7, held.back, held.back_pad, held.back_sum),
        channel(8, held.channel, held.channel_pad, held.channel_sum),
        gains(),
        keep_and_hand(net, 10, 0, held.sums_in, held.sums),
        keep_and_hand(net, 12, 0, held.keys, held.keys_sum),
        swap_cores(net, 13, held.gate, held.gate_both),
        swap_cores(net, 14, held.down, held.down_both),
    ]


def shards(
    tokens,
    seq_lengths,
    norm_gain,
    meta_tokens,
    w_query,
    w_key_value,
    w_attn_out,
    attn_gain,
    w_mamba_in,
    conv_weight,
    conv_bias,
    w_ssm_x,
    w_dt,
    dt_bias,
    a_log,
    skip_d,
    w_mamba_out,
    mamba_gain,
    ffn_gain,
    w_gate_up,
    w_down,
    cotangent,
):
    low = jnp.bfloat16
    full = jnp.float32
    core = lax.axis_index("branch")
    on_attention = core == 0
    tokens_b, cotangent_b = tokens[0], cotangent[0]
    rows, width = tokens_b.shape
    half = rows // 2
    group = rows * 16
    piece = w_query.shape[0]
    query_width = w_query.shape[1]
    keys_width = w_key_value.shape[1]
    inner_piece = w_mamba_out.shape[0]
    inner = inner_piece * SIDE
    rank = w_dt.shape[0]
    states = a_log.shape[0]
    proj = rank + 2 * states
    metas = meta_tokens.shape[0]
    down_piece = w_down.shape[0]
    units = 96 * SIDE
    row_start = core * half

    lengths = seq_lengths[0]
    start_rows = (jnp.cumsum(lengths) - lengths).astype(jnp.int32)
    place = lax.axis_index("seq")
    counting = jnp.arange(half, dtype=jnp.int32)
    my_rows = jnp.concatenate([place * rows + counting, (16 - place) * rows - half + counting])

    attention_in, mamba_in, back_in, gate_in, down_in, small_in, channel_in = prepare(
        w_query,
        w_key_value,
        w_attn_out,
        w_mamba_in,
        w_mamba_out,
        w_gate_up,
        w_down,
        meta_tokens,
        *(gain[None] for gain in (norm_gain, attn_gain, mamba_gain, ffn_gain)),
        w_dt,
        a_log,
        conv_weight,
        *(row[None] for row in (conv_bias, dt_bias, skip_d)),
        w_ssm_x,
    )
    query_most = -(-query_width // LANES) * LANES
    third = 10 * LANES
    last_third = attention_in.shape[1] - 2 * third
    mamba_in = mamba_in.reshape(SIDE, SIDE, 32, -1)
    gate_in = gate_in.reshape(2, SIDE, SIDE, 32, units)
    cube = (SIDE, SIDE, SIDE)

    begun = exchange(
        "exchange_start",
        0,
        program_start,
        dict(
            tokens=(tokens_b, ANY),
            small=(small_in, ANY),
            mamba=(mamba_in, ANY),
            back=(back_in, ANY),
            channel=(channel_in, ANY),
            whole=(attention_in, ANY),
        ),
        dict(
            tokens_all=((2, SIDE, SIDE, half, width), low, ANY),
            assigned=((rows, width), low, ANY),
            small_all=(cube + small_in.shape, low, ANY),
            mamba_all=(cube + mamba_in.shape[2:], low, ANY),
            back_all=((SIDE,) + back_in.shape, low, ANY),
            channel_all=((SIDE,) + channel_in.shape, low, ANY),
            first=(cube + (32, third), low, ANY),
            second=(cube + (32, third), low, ANY),
            third=(cube + (32, last_third), low, ANY),
        ),
        dict(mamba_mid=(mamba_in.shape, low)),
        partners=(False,),
    )
    weight_one, weight_two, weight_three = (
        part.reshape(64 * 32, -1) for part in (begun.first, begun.second, begun.third)
    )
    meta_f, gains = unpack(begun.small_all.reshape(64 * 32, -1), metas, width)
    gain_row, gain_attn, gain_mamba, gain_feed = (gains[i : i + 1] for i in range(4))

    def on_core(which, work):
        shapes = jax.eval_shape(work)
        return lax.cond(core == which, work, lambda: blank(shapes))


    normed_wide, query_b, keyval_b, meta_wide, meta_kv = on_core(
        0,
        lambda: attention_project(
            begun.assigned, meta_f, gain_row, weight_one, weight_two, query_width, keys_width
        ),
    )
    keyval = exchange(
        "exchange_keyval",
        2,
        program_keyval,
        dict(keyval=(keyval_b, ANY), gate=(gate_in, ANY)),
        dict(
            keyval_all=((2, SIDE, SIDE, half, keys_width), low, ANY),
            gate_own=((SIDE, SIDE, 32, units), low, ANY),
        ),
        dict(gate_mid=((SIDE, SIDE, 32, units), low)),
        cores=(0,),
    )

    mamba_wide = begun.mamba_all.reshape(64 * 32, -1)
    back_wide = begun.back_all.reshape(-1, width)
    normed_all, conv_in, gate_z, inputs_b, proj_first, proj_second, weight_mamba, channel = on_core(
        1,
        lambda: mixer_project(
            start_rows,
            begun.tokens_all.reshape(2, 16, half, width),
            gain_row,
            mamba_wide,
            begun.channel_all.reshape(4 * 64, -1),
        ),
    )

    def proj_pads(size):
        return dict(two_pad(size, rows), sum=((size, rows), low))

    def spread_projection(name, number, first, second, gate):
        cuts = (PROJ_CUT, PROJ_ROWS - PROJ_CUT)
        results = exchange(
            name,
            number,
            program_project,
            dict(
                first=(first.reshape(SIDE, SIDE, cuts[0], rows), ANY),
                second=(second.reshape(SIDE, SIDE, cuts[1], rows), ANY),
                gate=(gate, ANY),
            ),
            dict(
                first_all=((SIDE, SIDE, cuts[0], rows), low, ANY),
                second_all=((SIDE, SIDE, cuts[1], rows), low, ANY),
                gate_own=((SIDE, SIDE, 32, units), low, ANY),
            ),
            dict(
                first_pad=proj_pads(cuts[0]),
                second_pad=proj_pads(cuts[1]),
                gate_mid=((SIDE, SIDE, 32, units), low),
            ),
            vmem=32 * 2**20,
            cores=(1,),
        )
        whole = [part.reshape(16, -1, rows) for part in (results.first_all, results.second_all)]
        return whole + [results.gate_own]

    step_first, step_second, gate_second = spread_projection("exchange_project", 3, proj_first, proj_second, gate_in[1])
    keyval_all = keyval.keyval_all.reshape(2, 16, half, keys_width)

    cotangent_b, step_second = lax.optimization_barrier((cotangent_b, step_second))
    cotangent_part = lax.dynamic_slice_in_dim(cotangent_b, row_start, half, 0)
    cotangent_all = lax.all_gather(cotangent_part, "seq", axis=0, tiled=True)

    my_starts = jnp.max(
        jnp.where(my_rows[:, None] >= start_rows[None, :], start_rows[None, :], 0), axis=1
    )
    bounds = jnp.stack([my_starts, my_rows], axis=1).astype(jnp.int32)
    key_blocks = (my_rows[half - 1 :: half] // KEY_ROWS + 1).astype(jnp.int32)

    attended, mass, attended_wide, attn_pre = on_core(
        0,
        lambda: attend_forward(
            key_blocks, query_b, keyval_all, meta_kv, bounds, weight_two, weight_three
        ),
    )

    partial, mixed_y, ssm_out, starts, decay_t, drive_t, scan_rate, cols = on_core(
        1,
        lambda: mixer_forward(
            inner, start_rows, step_first, step_second, channel, inputs_b, gate_z, back_wide
        ),
    )

    mixers = exchange(
        "exchange_mixers",
        4,
        program_mixers,
        dict(
            partial=(partial.reshape(2, SIDE, SIDE, half, width), ANY),
            attn_pre=(attn_pre, ANY),
            gate_first=(keyval.gate_own, ANY),
            gate_second=(gate_second, ANY),
            down=(down_in, ANY),
        ),
        dict(
            mamba_pre=((half, width), jnp.float32, VMEM),
            attn_half=((half, width), jnp.float32, ANY),
            gate_all=((2,) + cube + (32, units), low, ANY),
            down_all=((SIDE,) + down_in.shape, low, ANY),
        ),
        dict(pad=half_pad(half, width)),
        vmem=32 * 2**20,
        partners=(True,),
    )
    tokens_part = lax.dynamic_slice_in_dim(tokens_b, row_start, half, 0).astype(full)
    sent = rms_norm(mixers.attn_half, gain_attn).astype(low).astype(jnp.float32)
    sent = sent + rms_norm(mixers.mamba_pre, gain_mamba).astype(low).astype(jnp.float32)
    hidden = tokens_part + 0.5 * sent
    feed = exchange(
        "exchange_feed",
        5,
        program_feed,
        dict(feed=(rms_norm(hidden, gain_feed).astype(low), ANY)),
        dict(feed_all=((SIDE, SIDE, half, width), low, ANY)),
    ).feed_all
    block = (SIDE, SIDE, half)
    ffn = exchange(
        "exchange_ffn",
        6,
        program_ffn,
        dict(
            feed=(feed, VMEM),
            cot=(cotangent_all.reshape(block + (width,)), VMEM),
            gate=(mixers.gate_all.reshape(2, 64 * 32, units), VMEM),
            down=(mixers.down_all.reshape(units, width), VMEM),
        ),
        dict(
            out_sum=((half, width), full, VMEM),
            grad_sum=((half, width), full, VMEM),
            g_gate=((2, SIDE, 16, 32, units), low, VMEM),
            g_down=((2, SIDE, 1, 48, width), low, VMEM),
        ),
        dict(
            out=(block + (width,), low),
            g_feed=(block + (width,), low),
            active=(block + (units,), low),
            g_parts=((2,) + block + (units,), low),
            gate_w=((width, units), low),
            up_w=((width, units), low),
            products=((width, units), low),
            out_pad=ring_pad(half, width),
            grad_pad=ring_pad(half, width),
        ),
        vmem=60 * 2**20,
        shared=True,
    )
    (
        mixed_part,
        grad_hidden,
        grad_attn_pre,
        grad_mamba_pre,
        grad_gain_attn,
        grad_gain_mamba,
        grad_gain_feed,
    ) = turn(
        gains,
        hidden,
        ffn.out_sum,
        ffn.grad_sum,
        cotangent_part,
        mixers.attn_half,
        mixers.mamba_pre,
    )
    back = exchange(
        "exchange_back",
        7,
        program_back,
        dict(
            g_mamba=(grad_mamba_pre, ANY),
            g_attn=(grad_attn_pre, ANY),
            mixed=(mixed_part, ANY),
            g_hidden=(grad_hidden, ANY),
            g_gate=(ffn.g_gate, ANY),
            g_down=(ffn.g_down, ANY),
        ),
        dict(
            g_mamba_all=((2, SIDE, SIDE, half, width), low, ANY),
            g_attn_both=((2, half, width), low, ANY),
            mixed_both=((2, half, width), low, ANY),
            g_hidden_both=((2, half, width), jnp.float32, ANY),
            g_gate_sum=((16, 32, units), low, VMEM),
            g_down_sum=((1, 48, width), jnp.float32, VMEM),
        ),
        dict(gate_pad=shrink_pad(16, 32, units), down_pad=shrink_pad(1, 48, width)),
        vmem=32 * 2**20,
        partners=(True,),
    )
    mixed = back.mixed_both.reshape(rows, width)
    g_gate_own = back.g_gate_sum.reshape(SIDE, SIDE, 32, units)

    cuts = (8 * LANES, 9 * LANES, query_most + width - 17 * LANES)

    def attention_back_one():
        g_pre = back.g_attn_both.reshape(rows, width)
        g_query, g_keyval, g_meta = attend_backward(
            key_blocks,
            query_b,
            keyval_all,
            meta_kv,
            bounds.T,
            attended,
            mass,
            g_pre,
            weight_two,
            weight_three,
        )
        pieces = attention_weights(
            normed_wide, attended_wide, g_query, g_pre, weight_one, weight_two, cuts
        )
        return [g_query, g_keyval, g_meta] + list(pieces)

    grad_query_b, grad_keyval, grad_meta_kv, sum_one, sum_two, sum_three, gain_query = on_core(
        0, attention_back_one
    )

    def cubed(blocks):
        return blocks.reshape(cube + (32, blocks.shape[-1]))

    small_cuts = (keys_width // 2, keys_width // 2, metas)
    sources = (
        grad_query_b,
        normed_wide,
        meta_wide,
        grad_meta_kv,
        weight_one,
        weight_two,
        meta_f,
        gain_row,
    )
    attention = exchange(
        "exchange_attention",
        8,
        program_attention,
        dict(
            keyval=(grad_keyval.reshape(2, SIDE, SIDE, half, keys_width), ANY),
            gate=(g_gate_own, ANY),
            one=(cubed(sum_one), ANY),
            two=(cubed(sum_two), ANY),
            three=(cubed(sum_three), ANY),
            sources={name: (array, ANY) for name, array in zip(INSIDE, sources)},
        ),
        dict(
            gate_own=((SIDE, SIDE, 32, units), low, ANY),
            sums=((32, query_most + width), full, VMEM),
            keys_sum=((32, keys_width + metas), full, VMEM),
            g_normed=((rows, width), full, VMEM),
            gain_part=((1, 64 * 32), full, VMEM),
            meta_gain=((1, width), full, VMEM),
        ),
        dict(
            upper_pad=two_pad(half, keys_width),
            lower_pad=two_pad(half, keys_width),
            gate_mid=((SIDE, SIDE, 32, units), low),
            keyval_sum=((rows, keys_width), full),
            g_wide=((rows, 64 * 32), full),
            g_meta_wide=((metas, 64 * 32), full),
            inside={name: (array.shape, array.dtype) for name, array in zip(INSIDE, sources)},
            keys=dict(zip(SUMS[3:], (((64 * 32, cut), low) for cut in small_cuts))),
            pads=dict(zip(SUMS, (three_pad(32, cut) for cut in cuts + small_cuts))),
            parts=dict(zip(SUMS, (((32, cut), full) for cut in cuts + small_cuts))),
        ),
        vmem=62 * 2**20,
        cores=(0,),
    )
    gain_attention = (gain_query + attention.gain_part).reshape(64, 32)[:, :piece].reshape(1, width)
    gain_attention = gain_attention / gain_row + attention.meta_gain

    g_first, g_second, grad_inputs, grad_gate_z, back_out, grad_rows, grad_rate = on_core(
        1,
        lambda: mixer_backward(
            inner,
            step_first,
            step_second,
            cols,
            channel,
            inputs_b,
            gate_z,
            back_wide,
            back.g_mamba_all.reshape(2, 16, half, width),
            mixed_y,
            ssm_out,
            starts,
            decay_t,
            drive_t,
            scan_rate,
        ),
    )
    g_first, g_second, last_gate = spread_projection(
        "exchange_last", 9, g_first, g_second, g_gate_own
    )

    def mamba_back_two():
        g_normed, g_weight, g_rows, gain = mixer_inputs(
            start_rows,
            g_first,
            g_second,
            channel,
            weight_mamba,
            normed_all,
            conv_in,
            inputs_b,
            grad_inputs,
            grad_gate_z,
        )
        return g_normed, g_weight, channel_grads(grad_rows, g_rows, grad_rate, channel), gain

    grad_normed_partial, mamba_out, channel_out, gain_mixer = on_core(1, mamba_back_two)
    gain_mixer = gain_mixer[:1] / gain_row
    grad_gain_norm = jnp.where(on_attention, gain_attention, gain_mixer)
    gains_out = pack_gains(grad_gain_norm, grad_gain_attn, grad_gain_mamba, grad_gain_feed)
    ended = exchange(
        "exchange_end",
        1,
        program_end,
        dict(
            partial=(grad_normed_partial.reshape(2, SIDE, SIDE, half, width), ANY),
            g_attn=(attention.g_normed, ANY),
            sums_in=(attention.sums, ANY),
            keys=(attention.keys_sum, ANY),
            gate=(jnp.where(on_attention, attention.gate_own, last_gate), ANY),
            down=(back.g_down_sum.reshape(48, width), ANY),
            mamba=(mamba_out, ANY),
            back=(back_out, ANY),
            channel=(channel_out, ANY),
            gains=(gains_out.reshape(cube + (32, 128)), ANY),
        ),
        dict(
            normed_both=((2, half, width), full, ANY),
            sums=((32, query_most + width), full, ANY),
            keys_sum=((32, keys_width + metas), full, ANY),
            gate_both=((2, SIDE, SIDE, 32, units), low, ANY),
            down_both=((2, 48, width), full, ANY),
            mamba_sum=((SIDE, SIDE, 32, 4 * CHUNKS), low, ANY),
            back_sum=((1, 64, width), full, VMEM),
            channel_sum=((1, 64, 3 * LANES), full, VMEM),
            gains_both=((2, 32, 128), full, ANY),
        ),
        dict(
            normed_pad=half_pad(half, width),
            normed_sum=((half, width), full),
            attn_part=((half, width), full),
            gains_pad=three_pad(32, 128),
            gains_sum=((32, 128), full),
            mamba_pad=x_pad(16, 32, 4 * CHUNKS),
            mamba_part=((SIDE, SIDE, 32, 4 * CHUNKS), low),
            mamba_mid=((SIDE, SIDE, 32, 4 * CHUNKS), low),
            back_pad=x_pad(1, 64, width),
            channel_pad=x_pad(1, 64, 3 * LANES, full),
        ),
        vmem=48 * 2**20,
        partners=(True,),
    )
    (
        input_grad,
        grad_query,
        grad_keyval_in,
        grad_attn,
        grad_mamba,
        grad_back,
        grad_gate,
        grad_down,
        grad_meta,
        grad_ssm,
        grad_step,
        grad_log,
        grad_taps,
        grad_rows,
        grad_gains,
    ) = finish(
        piece,
        inner_piece,
        down_piece,
        inner,
        proj,
        rank,
        tokens_b,
        gain_row,
        back.g_hidden_both,
        ended.normed_both,
        ended.sums,
        ended.keys_sum,
        ended.mamba_sum.reshape(16, 32, -1),
        ended.back_sum,
        ended.channel_sum,
        ended.gate_both.reshape(2, 16, 32, units),
        ended.down_both,
        ended.gains_both,
    )
    return (
        mixed[None],
        input_grad[None],
        grad_gains[0],
        grad_meta,
        grad_query,
        grad_keyval_in,
        grad_attn,
        grad_gains[1],
        grad_mamba,
        grad_taps,
        grad_rows[4],
        grad_ssm,
        grad_step,
        grad_rows[5],
        grad_log,
        grad_rows[6],
        grad_back,
        grad_gains[2],
        grad_gains[3],
        grad_gate,
        grad_down,
    )


def solution(mesh):
    spread = ("seq", "fsdp")
    rows = P("fsdp", "seq", None)
    flat, first, second = P(spread), P(spread, None), P(None, spread)
    weights = (
        flat,
        second,
        first,
        first,
        first,
        flat,
        first,
        second,
        flat,
        first,
        second,
        flat,
        second,
        flat,
        first,
        flat,
        flat,
        first,
        first,
    )
    return jax.shard_map(
        shards,
        mesh=mesh,
        in_specs=(rows, P("fsdp", None)) + weights + (rows,),
        out_specs=(rows, rows) + weights,
        check_vma=False,
    )
```
